32 devices in a mesh: dp: 2 (over core), ctx: 16 (over z, y, x).
Axes of the slice: x: 2, y: 2, z: 4, core: 2. Of those that a mesh axis runs over, the one named last changes fastest.
Arguments:
- tokens: bfloat16 [8192, 4096], P(('dp', 'ctx')), parts along dimension 0, may hold values from -6 to 19
- positions: int32 [8192], P('dp'), parts along dimension 0, may hold values from 0 to 4095, as said below
- lengths: int32 [64], P('dp'), parts along dimension 0, may hold values from 1 to 384, 4096 in all
- gain: bfloat16 [4096], replicated, may hold values from 0.5 to 1.5
- w_query: bfloat16 [4096, 2048], replicated, may hold values from -0.09375 to 0.09375
- w_key: bfloat16 [4096, 512], replicated, may hold values from -0.09375 to 0.09375
- value_weight: bfloat16 [4096, 512], replicated, may hold values from -0.09375 to 0.09375
Outputs:
- attended: bfloat16 [8192, 2048], P(('dp', 'ctx')), parts along dimension 0
The draws below stay inside these ranges and needn't reach their ends.
There are 2 independent parts, one for each index of `dp`. The reference program is written for one: setup_inputs(seed, part) draws one part's arguments, and reference() takes and returns one part's arrays. A program takes and returns all parts, laid end to end along the dimension named above; an argument that names none is the same for every part. Nothing has to cross between parts.
Inputs may be any that keep to these rules, and one draw needn't show every extreme that they name: positions is a permutation; every aligned block of 256 rows holds exactly 16 positions of each owner j, whose positions are j * 128 to j * 128 + 127 and (2 * 16 - 1 - j) * 128 to (2 * 16 - j) * 128 - 1.
All inputs are finite; a program needn't handle non-finite values.
Results may differ from the reference program's by a relative error of at most 0.012.
The reference program's roundings to bfloat16 on the way count: a program that leaves them out, or rounds other values in their place, can miss the bound.
Values may be sent and summed in bfloat16 or wider, within the bound.
No kernel may reach another device: no remote copies, remote signals or barrier semaphores. Data moves between devices by JAX's collectives and lax.ppermute only.
A program may use at most 128 MiB of HBM per device.

```python
import math
import jax
import jax.numpy as jnp
import numpy as np
from jax import lax

MODEL_WIDTH = 4096
HEAD_SIZE = 128
QUERY_HEADS = 16
KEY_VALUE_HEADS = 4
TOK_DEV = 256
TOKENS = 4096
CH = 128
G = 16
NDOCS = 32
DOC_MOST = 384
N_CTX = 16


def zig_table():
    owner = jnp.arange(N_CTX, dtype=jnp.int32)[:, None]
    inner = jnp.arange(TOK_DEV, dtype=jnp.int32)[None, :]
    return jnp.where(inner < CH, owner * CH + inner, (2 * N_CTX - 1 - owner) * CH + inner - CH)


def position_law(key):
    table = zig_table()
    first_key, second_key = jax.random.split(jax.random.fold_in(key, 17))
    first_perm = jax.vmap(lambda sub: jax.random.permutation(sub, TOK_DEV))(jax.random.split(first_key, N_CTX))
    shuffled = jnp.take_along_axis(table, first_perm.astype(jnp.int32), axis=1)
    sources = shuffled.reshape(N_CTX, N_CTX, G).transpose(1, 0, 2).reshape(N_CTX, TOK_DEV)
    second_perm = jax.vmap(lambda sub: jax.random.permutation(sub, TOK_DEV))(jax.random.split(second_key, N_CTX))
    mixed = jnp.take_along_axis(sources, second_perm.astype(jnp.int32), axis=1)
    return mixed.reshape(TOKENS).astype(jnp.int32)


def draw_positions(key, part):
    return position_law(key)


def draw_tokens(key, part):
    unmodified_rows = jax.random.truncated_normal(jax.random.fold_in(key, 23), -6.0, 6.0, (TOKENS, MODEL_WIDTH), jnp.float32)
    return unmodified_rows.astype(jnp.bfloat16)


def draw_w_query(key, part):
    score_scale = MODEL_WIDTH ** (-0.5)
    unmodified_rows = jax.random.truncated_normal(jax.random.fold_in(key, 41), -6.0, 6.0, (MODEL_WIDTH, QUERY_HEADS * HEAD_SIZE), jnp.float32) * score_scale
    return unmodified_rows.astype(jnp.bfloat16)


def draw_w_key(key, part):
    score_scale = MODEL_WIDTH ** (-0.5)
    unmodified_rows = jax.random.truncated_normal(jax.random.fold_in(key, 43), -6.0, 6.0, (MODEL_WIDTH, KEY_VALUE_HEADS * HEAD_SIZE), jnp.float32) * score_scale
    return unmodified_rows.astype(jnp.bfloat16)


def split_up(amount, total, most, skew):
    portions = [(1 << 20) // math.isqrt(rank ** skew) + 1 for rank in range(2, amount + 1)]
    surplus, counts = total - most - (amount - 1), [1] * (amount - 1)
    while surplus > 0:
        candidates = [i for i in range(amount - 1) if counts[i] < most]
        pool, left = sum([portions[i] for i in candidates]), surplus
        for i in candidates:
            addition = min(most - counts[i], max(1, left * portions[i] // pool), surplus)
            counts[i] = counts[i] + addition
            surplus = surplus - addition
    return np.array([most] + counts)


def ragged(own_key, count, total, most, slope):
    if count == 2:
        one = jax.random.randint(own_key, (), max(1, total - most), min(most, total - 1) + 1)
        return jnp.stack([one, total - one])
    sizes = jnp.asarray(split_up(count, total, most, slope), jnp.int32)
    pairs = (count - 1) // 2
    giver, receiver = sizes[1:1 + 2 * pairs:2], sizes[2:2 + 2 * pairs:2]
    slack = jnp.minimum(giver - 1, most - receiver)
    shifted = jax.random.randint(jax.random.fold_in(own_key, 1), (pairs,), 0, 1 << 20) % (slack + 1)
    sizes = sizes.at[1:1 + 2 * pairs:2].set(giver - shifted).at[2:2 + 2 * pairs:2].set(receiver + shifted)
    return sizes[jax.random.permutation(jax.random.fold_in(own_key, 2), count)]


def bell_draw(key, shape, scale, most, kind=jnp.bfloat16):
    return jnp.clip(scale * jax.random.normal(key, shape, jnp.float32), -most, most).astype(kind)


def setup_inputs(seed: int = 0, part: int = 0) -> dict:
    seeds = jax.random.split(jax.random.key(seed), 8)
    own_keys = jax.random.split(jax.random.fold_in(seeds[7], part), 8)
    tokens = draw_tokens(jax.random.fold_in(jax.random.fold_in(seeds[7], part), 71), part)
    positions = draw_positions(jax.random.fold_in(jax.random.fold_in(seeds[7], part), 71), part)
    lengths = ragged(own_keys[2], NDOCS, TOKENS, DOC_MOST, 2).astype(jnp.int32)
    gain = jnp.clip(1.0 + 0.1 * jax.random.normal(seeds[3], (MODEL_WIDTH,), jnp.float32), 0.5, 1.5).astype(jnp.bfloat16)
    w_query = draw_w_query(jax.random.fold_in(seeds[7], 71), part)
    w_key = draw_w_key(jax.random.fold_in(seeds[7], 71), part)
    value_weight = bell_draw(seeds[6], (MODEL_WIDTH, KEY_VALUE_HEADS * HEAD_SIZE), MODEL_WIDTH ** -0.5, 0.09375)
    return dict(tokens=tokens, positions=positions, lengths=lengths, gain=gain, w_query=w_query, w_key=w_key, value_weight=value_weight)


ROPE_THETA = 500000.0
EPSILON = 1e-05

def rope(values, where_at):
    heads = values.shape[1] // HEAD_SIZE
    half = HEAD_SIZE // 2
    shaped = values.reshape(values.shape[0], heads, HEAD_SIZE)
    freq = ROPE_THETA ** (-(jnp.arange(half, dtype=jnp.float32) * 2.0 / HEAD_SIZE))
    angle = where_at.astype(jnp.float32)[:, None, None] * freq[None, None, :]
    cosine = jnp.cos(angle)
    sine = jnp.sin(angle)
    first = shaped[..., :half]
    second = shaped[..., half:]
    turned = jnp.concatenate([first * cosine - second * sine, second * cosine + first * sine], axis=-1)
    return turned.reshape(values.shape[0], heads * HEAD_SIZE)

def project(tokens, gain, w_query, w_key, value_weight, where_at):
    floats = tokens.astype(jnp.float32)
    score_scale = lax.rsqrt(lax.optimization_barrier(jnp.mean(floats * floats, axis=-1, keepdims=True)) + EPSILON)
    normed = (floats * score_scale * gain.astype(jnp.float32)).astype(jnp.bfloat16)
    query = rope(jnp.dot(normed, w_query, preferred_element_type=jnp.float32), where_at).astype(jnp.bfloat16)
    key = rope(jnp.dot(normed, w_key, preferred_element_type=jnp.float32), where_at).astype(jnp.bfloat16)
    value = jnp.dot(normed, value_weight, preferred_element_type=jnp.float32).astype(jnp.bfloat16)
    return (query, key, value)

def doc_of(where_at, lengths):
    ends = jnp.cumsum(lengths, dtype=jnp.int32)
    return lax.optimization_barrier(jnp.sum((ends[None, :] <= where_at[:, None]).astype(jnp.int32), axis=1))

def attend(query, key, value, query_at, key_at, key_valid, lengths):
    rows = query.shape[0]
    keys = key.shape[0]
    kv_heads = key.shape[1] // HEAD_SIZE
    group = query.shape[1] // HEAD_SIZE // kv_heads
    query_doc = doc_of(query_at, lengths)
    key_doc = doc_of(key_at, lengths)
    allowed = (key_doc[None, :] == query_doc[:, None]) & (key_at[None, :] <= query_at[:, None]) & key_valid[None, :]
    q_heads = query.astype(jnp.float32).reshape(rows, kv_heads, group, HEAD_SIZE)
    k_heads = key.astype(jnp.float32).reshape(keys, kv_heads, HEAD_SIZE)
    v_heads = value.astype(jnp.float32).reshape(keys, kv_heads, HEAD_SIZE)
    scores = jnp.einsum('rhgd,khd->hgrk', q_heads, k_heads) * (1.0 / HEAD_SIZE ** 0.5)
    scores = jnp.where(allowed[None, None], scores, jnp.float32(-1e+30))
    top = lax.optimization_barrier(jnp.max(scores, axis=-1, keepdims=True))
    weights = jnp.exp(scores - top)
    total = lax.optimization_barrier(jnp.sum(weights, axis=-1))
    rounded = weights.astype(jnp.bfloat16).astype(jnp.float32)
    mixed = jnp.einsum('hgrk,khd->rhgd', rounded, v_heads)
    mixed = mixed / jnp.transpose(total, (2, 0, 1))[..., None]
    return mixed.reshape(rows, kv_heads * group * HEAD_SIZE).astype(jnp.bfloat16)

def reference(tokens, positions, lengths, gain, w_query, w_key, value_weight):
    query, key, value = project(tokens, gain, w_query, w_key, value_weight, positions)
    total_rows = tokens.shape[0]
    loader_row = jnp.zeros((total_rows,), jnp.int32).at[positions].set(jnp.arange(total_rows, dtype=jnp.int32))
    query = query[loader_row]
    key = key[loader_row]
    value = value[loader_row]
    reach = 3 * CH
    block = min(512, total_rows)
    key_pad = jnp.concatenate([jnp.zeros((reach, key.shape[1]), key.dtype), key], axis=0)
    value_pad = jnp.concatenate([jnp.zeros((reach, value.shape[1]), value.dtype), value], axis=0)

    def one_block(index):
        start = (index * block).astype(jnp.int32)
        q_block = lax.dynamic_slice_in_dim(query, start, block, 0)
        k_block = lax.dynamic_slice_in_dim(key_pad, start, reach + block, 0)
        v_block = lax.dynamic_slice_in_dim(value_pad, start, reach + block, 0)
        query_at = start + jnp.arange(block, dtype=jnp.int32)
        key_at = start - reach + jnp.arange(reach + block, dtype=jnp.int32)
        return attend(q_block, k_block, v_block, query_at, key_at, key_at >= 0, lengths)
    blocks = lax.map(one_block, jnp.arange(total_rows // block, dtype=jnp.int32))
    ordered = blocks.reshape(total_rows, QUERY_HEADS * HEAD_SIZE)
    row = jnp.arange(total_rows, dtype=jnp.int32)
    owner = row // TOK_DEV
    inner = row % TOK_DEV
    zig = jnp.where(inner < CH, owner * CH + inner, (2 * N_CTX - 1 - owner) * CH + inner - CH)
    return ordered[zig]
```

```python
import functools

import jax
import jax.numpy as jnp
import numpy as np
from jax import lax
from jax.experimental import pallas as pl
from jax.experimental.pallas import tpu as pltpu
from jax.sharding import PartitionSpec as P

HEAD_SIZE = 128
REACH_BLOCKS = 3
ROPE_THETA = 500000.0
EPSILON = 1e-05

WHOLE = pl.BlockSpec(memory_space=pltpu.VMEM)
IN_PLACE = pl.BlockSpec(memory_space=pl.ANY)
SCALARS = pl.BlockSpec(memory_space=pltpu.SMEM)
MIB = 1024 * 1024


def dot(a, b):
    return jnp.dot(a, b, preferred_element_type=jnp.float32)


def project_kernel(kinds, group, tokens_hbm, gain_ref, rank_ref, cos_ref, sin_ref, *rest):
    count = len(kinds)
    weights_hbm, out_ref = rest[:count], rest[count]
    tokens, normed = rest[count + 1 : count + 3]
    weights, sems = rest[count + 3 : 2 * count + 3], rest[2 * count + 3]
    copies = [pltpu.make_async_copy(tokens_hbm, tokens, sems.at[0])]
    for i in range(count):
        copies.append(pltpu.make_async_copy(weights_hbm[i], weights[i], sems.at[i + 1]))
    for copy in copies:
        copy.start()
    rows, width = tokens.shape
    order = (lax.broadcasted_iota(jnp.int32, (rows, rows), 0) == rank_ref[...]).astype(jnp.bfloat16)
    gain = gain_ref[...].astype(jnp.float32)
    copies[0].wait()
    step = 32

    def norm(i, _):
        at = pl.ds(pl.multiple_of(i * step, step), step)
        floats = tokens[at, :].astype(jnp.float32)
        mean = jnp.sum(floats * floats, axis=1, keepdims=True) * (1.0 / width)
        normed[at, :] = (floats * lax.rsqrt(mean + EPSILON) * gain).astype(jnp.bfloat16)
        return 0

    lax.fori_loop(0, rows // step, norm, 0, unroll=True)
    groups, heads = out_ref.shape[0], out_ref.shape[1]
    cosine, sine = cos_ref[...], sin_ref[...]
    offset = 0
    for i in range(count):
        copies[i + 1].wait()
        per_head = weights[i].shape[1] // heads
        span = max(per_head, 256)
        for first in range(0, weights[i].shape[1], span):
            product = dot(normed[...], weights[i][:, first : first + span])
            parts = []
            for u in range(0, span, HEAD_SIZE):
                part = product[:, u : u + HEAD_SIZE]
                if kinds[i]:
                    part = part * cosine + pltpu.roll(part, HEAD_SIZE // 2, 1) * sine
                parts.append(part.astype(jnp.bfloat16))
            ordered = dot(order, jnp.concatenate(parts, axis=1)).astype(jnp.bfloat16)
            for u in range(0, span, per_head):
                out_ref[:, (first + u) // per_head, :, offset : offset + per_head] = ordered[
                    :, u : u + per_head
                ].reshape(groups, rows // groups, per_head)
        offset += per_head


def project(tokens, gain, rank, cosine, sine, weights, kinds, groups, heads):
    rows, width = tokens.shape
    columns = sum(w.shape[1] for w in weights)
    flops = 2 * rows * width * columns
    size = 2 * (width * columns + rows * width * 2 + rows * columns)
    return pl.pallas_call(
        functools.partial(project_kernel, kinds, groups),
        out_shape=jax.ShapeDtypeStruct((groups, heads, rows // groups, columns // heads), jnp.bfloat16),
        in_specs=[IN_PLACE] + [WHOLE] * 4 + [IN_PLACE] * len(weights),
        out_specs=WHOLE,
        scratch_shapes=[pltpu.VMEM((rows, width), jnp.bfloat16)] * 2
        + [pltpu.VMEM(w.shape, jnp.bfloat16) for w in weights]
        + [pltpu.SemaphoreType.DMA((len(weights) + 1,))],
        compiler_params=pltpu.CompilerParams(vmem_limit_bytes=size + 10 * MIB),
        cost_estimate=pl.CostEstimate(flops=flops, bytes_accessed=size, transcendentals=0),
    )(tokens, gain, rank, cosine, sine, *weights)


def place_kernel(arrived_ref, slot_ref, *outs):
    rows = arrived_ref.shape[0]
    first = 0
    for out_ref in outs:
        size = out_ref.shape[0]
        slots = lax.broadcasted_iota(jnp.int32, (size, rows), 0) + first
        chosen = (slots == slot_ref[...]).astype(jnp.bfloat16)
        out_ref[...] = dot(chosen, arrived_ref[...]).astype(jnp.bfloat16)
        first += size


def place(arrived, slot, sizes):
    width = arrived.shape[1]
    return pl.pallas_call(
        place_kernel,
        out_shape=[jax.ShapeDtypeStruct((size, width), jnp.bfloat16) for size in sizes],
        in_specs=[WHOLE, WHOLE],
        out_specs=[WHOLE] * len(sizes),
        compiler_params=pltpu.CompilerParams(vmem_limit_bytes=16 * MIB),
        cost_estimate=pl.CostEstimate(
            flops=2 * sum(sizes) * arrived.shape[0] * width,
            bytes_accessed=4 * arrived.size,
            transcendentals=0,
        ),
    )(arrived, slot)


def attend_kernel(block, scalar_ref, query_ref, slot_ref, ends_ref, *rest):
    pieces, out_ref, held = rest[:6], rest[6], rest[7]
    target, starts = scalar_ref[0], (scalar_ref[1], scalar_ref[2])
    heads = query_ref.shape[1] // HEAD_SIZE
    arrived = query_ref.shape[0]
    run = arrived // 2
    per_run = run // block
    reach = REACH_BLOCKS * block
    keys = reach + block
    slot = slot_ref[...]
    ends = ends_ref[...]
    factor = jnp.float32(np.log2(np.e) / HEAD_SIZE**0.5)
    for half in range(2):
        first = 0
        for piece in pieces[3 * half : 3 * half + 3]:
            held[half, first : first + piece.shape[0], :] = piece[...]
            first += piece.shape[0]
    for half in range(2):
        index = target if half == 0 else per_run - 1 - target
        at = pl.multiple_of(index * block, block)
        slots = lax.broadcasted_iota(jnp.int32, (block, arrived), 0) + (at + half * run)
        query = dot((slots == slot).astype(jnp.bfloat16), query_ref[...]).astype(jnp.bfloat16)
        key = held[half, pl.ds(at, keys), :HEAD_SIZE]
        value = held[half, pl.ds(at, keys), HEAD_SIZE:]
        begin = starts[half] + at
        query_at = lax.broadcasted_iota(jnp.int32, (block, 1), 0) + begin
        key_at = lax.broadcasted_iota(jnp.int32, (1, keys), 1) + (begin - reach)
        doc_start = jnp.max(jnp.where(ends <= query_at, ends, 0), axis=1, keepdims=True)
        allowed = (key_at >= doc_start) & (key_at <= query_at)
        for h in range(heads):
            columns = slice(h * HEAD_SIZE, (h + 1) * HEAD_SIZE)
            scores = lax.dot_general(
                query[:, columns], key, (((1,), (1,)), ((), ())), preferred_element_type=jnp.float32
            )
            scores = jnp.where(allowed, scores, jnp.float32(-1e30))
            top = jnp.max(scores, axis=1, keepdims=True)
            weights = jnp.exp2((scores - top) * factor)
            total = jnp.sum(weights, axis=1, keepdims=True)
            mixed = dot(weights.astype(jnp.bfloat16), value) / total
            out_ref[half * block : (half + 1) * block, columns] = mixed.astype(jnp.bfloat16)


def attend(scalars, query, slot, ends, pieces, block):
    width = query.shape[1]
    held = REACH_BLOCKS * block + query.shape[0] // 2
    heads = width // HEAD_SIZE
    reach = (REACH_BLOCKS + 1) * block
    return pl.pallas_call(
        functools.partial(attend_kernel, block),
        out_shape=jax.ShapeDtypeStruct((2 * block, width), jnp.bfloat16),
        in_specs=[SCALARS] + [WHOLE] * 9,
        out_specs=WHOLE,
        scratch_shapes=[pltpu.VMEM((2, held, 2 * HEAD_SIZE), jnp.bfloat16)],
        compiler_params=pltpu.CompilerParams(vmem_limit_bytes=16 * MIB),
        cost_estimate=pl.CostEstimate(
            flops=2 * 2 * heads * block * reach * HEAD_SIZE * 2 + 4 * block * query.size,
            bytes_accessed=2 * query.size + 8 * held * HEAD_SIZE,
            transcendentals=2 * heads * block * reach,
        ),
    )(scalars, query, slot, ends, *pieces)


def assemble_kernel(scalar_ref, *rest):
    pieces, out_ref = rest[:-1], rest[-1]
    width = pieces[0].shape[1]
    for k, piece in enumerate(pieces):
        at = pl.multiple_of((scalar_ref[0] ^ k) * width, width)
        out_ref[:, pl.ds(at, width)] = piece[...]


def assemble(scalars, pieces):
    rows, width = pieces[0].shape
    return pl.pallas_call(
        assemble_kernel,
        out_shape=jax.ShapeDtypeStruct((rows, width * len(pieces)), jnp.bfloat16),
        in_specs=[SCALARS] + [WHOLE] * len(pieces),
        out_specs=WHOLE,
        compiler_params=pltpu.CompilerParams(vmem_limit_bytes=8 * MIB),
        cost_estimate=pl.CostEstimate(
            flops=0, bytes_accessed=4 * rows * width * len(pieces), transcendentals=0
        ),
    )(scalars, *pieces)


def shards(tokens, positions, lengths, gain, w_query, w_key, value_weight):
    devices = lax.axis_size("ctx")
    device = lax.axis_index("ctx")
    rows = tokens.shape[0]
    block = rows // 2
    members = w_key.shape[1] // HEAD_SIZE
    groups = devices // members
    group = device // members
    member = device % members
    run = members * block
    group_rows = rows // groups

    def group_of(where_at):
        block_id = where_at // block
        return jnp.minimum(block_id, 2 * devices - 1 - block_id) // members

    mine = lax.dynamic_slice_in_dim(positions, device * rows, rows, 0)
    my_groups = group_of(mine)
    row = jnp.arange(rows, dtype=jnp.int32)
    earlier = (my_groups[:, None] == my_groups[None, :]) & (row[:, None] < row[None, :])
    rank = my_groups * group_rows + jnp.sum(earlier.astype(jnp.int32), axis=0)
    half = HEAD_SIZE // 2
    freq = ROPE_THETA ** (-(jnp.arange(half, dtype=jnp.float32) * 2.0 / HEAD_SIZE))
    angle = mine.astype(jnp.float32)[:, None] * freq[None, :]
    cosine, sine = jnp.cos(angle), jnp.sin(angle)
    cosine = jnp.concatenate([cosine, cosine], axis=1)
    sine = jnp.concatenate([-sine, sine], axis=1)
    gain = gain[None, :]
    rank = rank[None, :]

    def exchange(ordered):
        width = ordered.shape[3]
        flat = ordered.reshape(devices, group_rows, width)
        flat = lax.all_to_all(flat, "ctx", split_axis=0, concat_axis=0, tiled=True)
        return flat.reshape(devices * group_rows, width)

    kv = project(tokens, gain, rank, cosine, sine, (w_key, value_weight), (True, False), groups, members)
    kv = exchange(kv)
    query = project(tokens, gain, rank, cosine, sine, (w_query,), (True,), groups, members)

    table = positions.reshape(devices, rows)
    ours = group_of(table) == group
    first_run = group * run
    second_run = (2 * devices - members) * block - group * run
    slots = jnp.where(table // run == group, table - first_run, table - second_run + run)
    place_in = jnp.cumsum(ours.astype(jnp.int32), axis=1) - 1
    place_in = jnp.where(ours, place_in, -1)
    wanted = jnp.arange(group_rows, dtype=jnp.int32)[None, :, None] == place_in[:, None, :]
    slot = jnp.sum(jnp.where(wanted, slots[:, None, :], 0), axis=2).reshape(1, devices * group_rows)
    ends = jnp.cumsum(lengths, dtype=jnp.int32)[None, :]

    kv, query = lax.optimization_barrier((kv, query))
    query = exchange(query)
    reach = REACH_BLOCKS * block
    sizes = [run - reach, reach] * 2
    early_head, early_tail, late_head, late_tail = place(kv, slot, sizes)
    up = [(i, i + members) for i in range(devices - members)]
    down = [(i + members, i) for i in range(devices - members)]
    early_halo = lax.ppermute(early_tail, "ctx", up)
    late_halo = lax.ppermute(late_tail, "ctx", down)
    late_halo = jnp.where(group == groups - 1, early_tail, late_halo)
    pieces = (early_halo, early_head, early_tail, late_halo, late_head, late_tail)

    results = []
    for k in [3, 1, 2, 0][-members:]:
        target = member ^ k
        scalars = jnp.stack([target, first_run, second_run]).astype(jnp.int32)
        out = attend(scalars, query, slot, ends, pieces, block)
        if k:
            route = [(i, i // members * members + (i % members ^ k)) for i in range(devices)]
            out = lax.ppermute(out, "ctx", route)
        results.append((k, out))
    results = [out for _, out in sorted(results, key=lambda pair: pair[0])]
    return assemble(member.reshape(1).astype(jnp.int32), results)


def solution(mesh):
    in_specs = (P(("dp", "ctx"), None), P("dp"), P("dp"), P(), P(), P(), P())
    out_specs = P(("dp", "ctx"), None)
    return jax.shard_map(shards, mesh=mesh, in_specs=in_specs, out_specs=out_specs, check_vma=False)
```

```python
import functools

import jax
import jax.numpy as jnp
import numpy as np
from jax import lax
from jax.experimental import pallas as pl
from jax.experimental.pallas import tpu as pltpu
from jax.sharding import PartitionSpec as P

HEAD_SIZE = 128
REACH_BLOCKS = 3
ROPE_THETA = 500000.0
EPSILON = 1e-05

WHOLE = pl.BlockSpec(memory_space=pltpu.VMEM)
IN_PLACE = pl.BlockSpec(memory_space=pl.ANY)
SCALARS = pl.BlockSpec(memory_space=pltpu.SMEM)
MIB = 1024 * 1024


def dot(a, b):
    return jnp.dot(a, b, preferred_element_type=jnp.float32)


def transposed(row):
    size = row.shape[1]
    here = lax.broadcasted_iota(jnp.int32, (size, size), 0)
    there = lax.broadcasted_iota(jnp.int32, (size, size), 1)
    return jnp.sum(jnp.where(here == there, row, 0), axis=1, keepdims=True)


def group_of(where_at, block, devices, members):
    block_id = where_at // block
    return jnp.minimum(block_id, 2 * devices - 1 - block_id) // members


def project_kernel(kinds, devices, members, scalar_ref, positions_ref, freq_ref, gain_ref, tokens_hbm, *rest):
    count = len(kinds)
    weights_hbm, out_ref = rest[:count], rest[count]
    tokens, normed, weights, token_sems, sems = rest[count + 1 :]
    rows, width = tokens.shape
    chunks, _, span = weights.shape
    parts = token_sems.shape[0]
    part = rows // parts
    token_copies, copies, origin = [], [], []
    for i in range(parts):
        at = pl.ds(i * part, part)
        token_copies.append(pltpu.make_async_copy(tokens_hbm.at[at], tokens.at[at], token_sems.at[i]))
    for i in range(count):
        for first in range(0, weights_hbm[i].shape[1], span):
            j = len(copies)
            source = weights_hbm[i].at[:, pl.ds(first, span)]
            copies.append(pltpu.make_async_copy(source, weights.at[j], sems.at[j]))
            origin.append((i, first))
    for copy in token_copies + copies:
        copy.start()

    lanes = positions_ref.shape[1]
    stripes = rows // lanes
    mine = jnp.concatenate(
        [positions_ref[pl.ds(scalar_ref[0] * stripes + i, 1), :] for i in range(stripes)], axis=1
    )
    owner = group_of(mine, rows // 2, devices, members)
    here = lax.broadcasted_iota(jnp.int32, (rows, rows), 0)
    there = lax.broadcasted_iota(jnp.int32, (rows, rows), 1)
    earlier = jnp.where((transposed(owner) == owner) & (here < there), 1, 0)
    rank = owner * (rows * members // devices) + jnp.sum(earlier, axis=0, keepdims=True)
    order = here == rank
    ordered_at = jnp.sum(jnp.where(order, mine, 0), axis=1, keepdims=True)
    angle = ordered_at.astype(jnp.float32) * freq_ref[...]
    lane = lax.broadcasted_iota(jnp.int32, (rows, HEAD_SIZE), 1)
    cosine = jnp.cos(angle)
    sine = jnp.where(lane < HEAD_SIZE // 2, -1.0, 1.0) * jnp.sin(angle)
    order = jnp.where(order, 1.0, 0.0).astype(jnp.bfloat16)
    gain = gain_ref[...].astype(jnp.float32).reshape(1, width)
    step = 32

    for i in range(parts):
        token_copies[i].wait()

        def norm(j, _):
            at = pl.ds(pl.multiple_of(i * part + j * step, step), step)
            floats = tokens[at, :].astype(jnp.float32)
            mean = jnp.sum(floats * floats, axis=1, keepdims=True) * (1.0 / width)
            tokens[at, :] = (floats * lax.rsqrt(mean + EPSILON) * gain).astype(jnp.bfloat16)
            return 0

        lax.fori_loop(0, part // step, norm, 0, unroll=True)
    for first in range(0, width, 512):
        columns = slice(first, first + 512)
        normed[:, columns] = dot(order, tokens[:, columns]).astype(jnp.bfloat16)
    groups, heads = out_ref.shape[0], out_ref.shape[1]
    offsets = [0]
    for i in range(count):
        offsets.append(offsets[-1] + weights_hbm[i].shape[1] // heads)
    for j in range(chunks):
        i, first = origin[j]
        copies[j].wait()
        product = dot(normed[...], weights[j])
        per_head = offsets[i + 1] - offsets[i]
        for u in range(0, span, HEAD_SIZE):
            values = product[:, u : u + HEAD_SIZE]
            if kinds[i]:
                values = values * cosine + pltpu.roll(values, HEAD_SIZE // 2, 1) * sine
            head, inside = divmod(first + u, per_head)
            inside += offsets[i]
            out_ref[:, head, :, inside : inside + HEAD_SIZE] = values.astype(jnp.bfloat16).reshape(
                groups, rows // groups, HEAD_SIZE
            )


def project(scalars, positions, freq, gain, tokens, weights, kinds, devices, heads):
    rows, width = tokens.shape
    groups = devices // heads
    columns = sum(w.shape[1] for w in weights)
    span = 256
    parts = 4
    flops = 2 * rows * width * columns
    size = 2 * (width * columns + rows * width + rows * columns)
    return pl.pallas_call(
        functools.partial(project_kernel, kinds, devices, heads),
        out_shape=jax.ShapeDtypeStruct((groups, heads, rows // groups, columns // heads), jnp.bfloat16),
        in_specs=[SCALARS] + [WHOLE] * 3 + [IN_PLACE] * (len(weights) + 1),
        out_specs=WHOLE,
        scratch_shapes=[
            pltpu.VMEM((rows, width), jnp.bfloat16),
            pltpu.VMEM((rows, width), jnp.bfloat16),
            pltpu.VMEM((columns // span, width, span), jnp.bfloat16),
            pltpu.SemaphoreType.DMA((parts,)),
            pltpu.SemaphoreType.DMA((columns // span,)),
        ],
        compiler_params=pltpu.CompilerParams(vmem_limit_bytes=56 * MIB),
        cost_estimate=pl.CostEstimate(flops=flops, bytes_accessed=size, transcendentals=0),
    )(scalars, positions, freq, gain, tokens, *weights)


def place_kernel(arrived_ref, slot_ref, *outs):
    rows = arrived_ref.shape[0]
    first = 0
    for out_ref in outs:
        size = out_ref.shape[0]
        slots = lax.broadcasted_iota(jnp.int32, (size, rows), 0) + first
        chosen = (slots == slot_ref[...]).astype(jnp.bfloat16)
        out_ref[...] = dot(chosen, arrived_ref[...]).astype(jnp.bfloat16)
        first += size


def place(arrived, slot, sizes):
    width = arrived.shape[1]
    return pl.pallas_call(
        place_kernel,
        out_shape=[jax.ShapeDtypeStruct((size, width), jnp.bfloat16) for size in sizes],
        in_specs=[WHOLE, WHOLE],
        out_specs=[WHOLE] * len(sizes),
        compiler_params=pltpu.CompilerParams(vmem_limit_bytes=16 * MIB),
        cost_estimate=pl.CostEstimate(
            flops=2 * sum(sizes) * arrived.shape[0] * width,
            bytes_accessed=4 * arrived.size,
            transcendentals=0,
        ),
    )(arrived, slot)


def attend_kernel(block, scalar_ref, query_ref, slot_ref, ends_ref, *rest):
    pieces, out_ref, held = rest[:6], rest[6], rest[7]
    target, starts = scalar_ref[0], (scalar_ref[1], scalar_ref[2])
    heads = query_ref.shape[1] // HEAD_SIZE
    arrived = query_ref.shape[0]
    run = arrived // 2
    per_run = run // block
    reach = REACH_BLOCKS * block
    keys = reach + block
    slot = slot_ref[...]
    ends = ends_ref[...]
    factor = jnp.float32(np.log2(np.e) / HEAD_SIZE**0.5)
    for half in range(2):
        first = 0
        for piece in pieces[3 * half : 3 * half + 3]:
            held[half, first : first + piece.shape[0], :] = piece[...]
            first += piece.shape[0]
    indices = (target, per_run - 1 - target)
    at = [pl.multiple_of(index * block, block) for index in indices]
    iota = lax.broadcasted_iota(jnp.int32, (block, arrived), 0)
    chosen = [(iota + (at[half] + half * run) == slot).astype(jnp.bfloat16) for half in range(2)]
    queries = dot(jnp.concatenate(chosen, axis=0), query_ref[...]).astype(jnp.bfloat16)
    for half in range(2):
        here = slice(half * block, (half + 1) * block)
        key = held[half, pl.ds(at[half], keys), :HEAD_SIZE]
        value = held[half, pl.ds(at[half], keys), HEAD_SIZE:]
        begin = starts[half] + at[half]
        query_at = lax.broadcasted_iota(jnp.int32, (block, 1), 0) + begin
        key_at = lax.broadcasted_iota(jnp.int32, (1, keys), 1) + (begin - reach)
        doc_start = jnp.max(jnp.where(ends <= query_at, ends, 0), axis=1, keepdims=True)
        allowed = (key_at >= doc_start) & (key_at <= query_at)
        stacked = jnp.concatenate(
            [queries[here, h * HEAD_SIZE : (h + 1) * HEAD_SIZE] for h in range(heads)], axis=0
        )
        scores = lax.dot_general(stacked, key, (((1,), (1,)), ((), ())), preferred_element_type=jnp.float32)
        scores = jnp.where(allowed[None], scores.reshape(heads, block, keys), jnp.float32(-1e30))
        scores = scores.reshape(heads * block, keys)
        top = jnp.max(scores, axis=1, keepdims=True)
        weights = jnp.exp2((scores - top) * factor)
        total = jnp.sum(weights, axis=1, keepdims=True)
        mixed = (dot(weights.astype(jnp.bfloat16), value) / total).astype(jnp.bfloat16)
        for h in range(heads):
            out_ref[here, h * HEAD_SIZE : (h + 1) * HEAD_SIZE] = mixed[h * block : (h + 1) * block]


def attend(scalars, query, slot, ends, pieces, block):
    width = query.shape[1]
    held = REACH_BLOCKS * block + query.shape[0] // 2
    heads = width // HEAD_SIZE
    reach = (REACH_BLOCKS + 1) * block
    return pl.pallas_call(
        functools.partial(attend_kernel, block),
        out_shape=jax.ShapeDtypeStruct((2 * block, width), jnp.bfloat16),
        in_specs=[SCALARS] + [WHOLE] * 9,
        out_specs=WHOLE,
        scratch_shapes=[pltpu.VMEM((2, held, 2 * HEAD_SIZE), jnp.bfloat16)],
        compiler_params=pltpu.CompilerParams(vmem_limit_bytes=16 * MIB),
        cost_estimate=pl.CostEstimate(
            flops=2 * 2 * heads * block * reach * HEAD_SIZE * 2 + 4 * block * query.size,
            bytes_accessed=2 * query.size + 8 * held * HEAD_SIZE,
            transcendentals=2 * heads * block * reach,
        ),
    )(scalars, query, slot, ends, *pieces)


def assemble_kernel(scalar_ref, *rest):
    pieces, out_ref = rest[:-1], rest[-1]
    width = pieces[0].shape[1]
    for k, piece in enumerate(pieces):
        at = pl.multiple_of((scalar_ref[0] ^ k) * width, width)
        out_ref[:, pl.ds(at, width)] = piece[...]


def assemble(scalars, pieces):
    rows, width = pieces[0].shape
    return pl.pallas_call(
        assemble_kernel,
        out_shape=jax.ShapeDtypeStruct((rows, width * len(pieces)), jnp.bfloat16),
        in_specs=[SCALARS] + [WHOLE] * len(pieces),
        out_specs=WHOLE,
        compiler_params=pltpu.CompilerParams(vmem_limit_bytes=8 * MIB),
        cost_estimate=pl.CostEstimate(
            flops=0, bytes_accessed=4 * rows * width * len(pieces), transcendentals=0
        ),
    )(scalars, *pieces)


def shards(tokens, positions, lengths, gain, w_query, w_key, value_weight):
    devices = lax.axis_size("ctx")
    device = lax.axis_index("ctx")
    rows = tokens.shape[0]
    block = rows // 2
    members = w_key.shape[1] // HEAD_SIZE
    groups = devices // members
    group = device // members
    member = device % members
    run = members * block
    group_rows = rows // groups

    half = HEAD_SIZE // 2
    freq = ROPE_THETA ** (-(jnp.arange(HEAD_SIZE, dtype=jnp.float32) % half * 2.0 / HEAD_SIZE))
    operands = (device.reshape(1), positions.reshape(-1, 128), freq[None, :], gain, tokens)

    def exchange(ordered):
        width = ordered.shape[3]
        flat = ordered.reshape(devices, group_rows, width)
        flat = lax.all_to_all(flat, "ctx", split_axis=0, concat_axis=0, tiled=True)
        return flat.reshape(devices * group_rows, width)

    kv = project(*operands, (w_key, value_weight), (True, False), devices, members)
    kv = exchange(kv)
    query = project(*operands, (w_query,), (True,), devices, members)

    table = positions.reshape(devices, rows)
    ours = group_of(table, block, devices, members) == group
    first_run = group * run
    second_run = (2 * devices - members) * block - group * run
    slots = jnp.where(table // run == group, table - first_run, table - second_run + run)
    place_in = jnp.cumsum(ours.astype(jnp.int32), axis=1) - 1
    place_in = jnp.where(ours, place_in, -1)
    wanted = jnp.arange(group_rows, dtype=jnp.int32)[None, :, None] == place_in[:, None, :]
    slot = jnp.sum(jnp.where(wanted, slots[:, None, :], 0), axis=2).reshape(1, devices * group_rows)
    ends = jnp.cumsum(lengths, dtype=jnp.int32)[None, :]

    kv, query = lax.optimization_barrier((kv, query))
    query = exchange(query)
    reach = REACH_BLOCKS * block
    sizes = [run - reach, reach] * 2
    early_head, early_tail, late_head, late_tail = place(kv, slot, sizes)
    up = [(i, i + members) for i in range(devices - members)]
    down = [(i + members, i) for i in range(devices - members)]
    early_halo = lax.ppermute(early_tail, "ctx", up)
    late_halo = lax.ppermute(late_tail, "ctx", down)
    late_halo = jnp.where(group == groups - 1, early_tail, late_halo)
    pieces = (early_halo, early_head, early_tail, late_halo, late_head, late_tail)

    results = []
    for k in [3, 1, 2, 0][-members:]:
        target = member ^ k
        scalars = jnp.stack([target, first_run, second_run]).astype(jnp.int32)
        out = attend(scalars, query, slot, ends, pieces, block)
        if k:
            route = [(i, i // members * members + (i % members ^ k)) for i in range(devices)]
            out = lax.ppermute(out, "ctx", route)
        results.append((k, out))
    results = [out for _, out in sorted(results, key=lambda pair: pair[0])]
    return assemble(member.reshape(1).astype(jnp.int32), results)


def solution(mesh):
    in_specs = (P(("dp", "ctx"), None), P("dp"), P("dp"), P(), P(), P(), P())
    out_specs = P(("dp", "ctx"), None)
    return jax.shard_map(shards, mesh=mesh, in_specs=in_specs, out_specs=out_specs, check_vma=False)
```

```python
import functools

import jax
import jax.numpy as jnp
import numpy as np
from jax import lax
from jax.experimental import pallas as pl
from jax.experimental.pallas import tpu as pltpu
from jax.sharding import PartitionSpec as P

HEAD_SIZE = 128
REACH_BLOCKS = 3
ROPE_THETA = 500000.0
EPSILON = 1e-05

WHOLE = pl.BlockSpec(memory_space=pltpu.VMEM)
IN_PLACE = pl.BlockSpec(memory_space=pl.ANY)
SCALARS = pl.BlockSpec(memory_space=pltpu.SMEM)
MIB = 1024 * 1024


def dot(a, b):
    return jnp.dot(a, b, preferred_element_type=jnp.float32)


def transposed(row):
    size = row.shape[1]
    here = lax.broadcasted_iota(jnp.int32, (size, size), 0)
    there = lax.broadcasted_iota(jnp.int32, (size, size), 1)
    return jnp.sum(jnp.where(here == there, row, 0), axis=1, keepdims=True)


def group_of(where_at, block, devices, members):
    block_id = where_at // block
    return jnp.minimum(block_id, 2 * devices - 1 - block_id) // members


def project_kernel(kinds, devices, members, scalar_ref, positions_ref, freq_ref, gain_ref, tokens_hbm, *rest):
    count = len(kinds)
    weights_hbm, out_ref = rest[:count], rest[count]
    tokens, normed, weights, token_sems, sems = rest[count + 1 :]
    rows, width = tokens.shape
    chunks, _, span = weights.shape
    parts = token_sems.shape[0]
    part = rows // parts
    token_copies, copies, origin = [], [], []
    for i in range(parts):
        at = pl.ds(i * part, part)
        token_copies.append(pltpu.make_async_copy(tokens_hbm.at[at], tokens.at[at], token_sems.at[i]))
        token_copies[i].start()
    for i in range(count):
        for first in range(0, weights_hbm[i].shape[1], span):
            j = len(copies)
            source = weights_hbm[i].at[:, pl.ds(first, span)]
            copies.append(pltpu.make_async_copy(source, weights.at[j], sems.at[j]))
            origin.append((i, first))

    copies[0].start()
    lanes = positions_ref.shape[1]
    stripes = rows // lanes
    mine = jnp.concatenate(
        [positions_ref[pl.ds(scalar_ref[0] * stripes + i, 1), :] for i in range(stripes)], axis=1
    )
    owner = group_of(mine, rows // 2, devices, members)
    here = lax.broadcasted_iota(jnp.int32, (rows, rows), 0)
    there = lax.broadcasted_iota(jnp.int32, (rows, rows), 1)
    earlier = jnp.where((transposed(owner) == owner) & (here < there), 1, 0)
    rank = owner * (rows * members // devices) + jnp.sum(earlier, axis=0, keepdims=True)
    order = here == rank
    ordered_at = jnp.sum(jnp.where(order, mine, 0), axis=1, keepdims=True)
    angle = ordered_at.astype(jnp.float32) * freq_ref[...]
    lane = lax.broadcasted_iota(jnp.int32, (rows, HEAD_SIZE), 1)
    cosine = jnp.cos(angle)
    sine = jnp.where(lane < HEAD_SIZE // 2, -1.0, 1.0) * jnp.sin(angle)
    order = jnp.where(order, 1.0, 0.0).astype(jnp.bfloat16)
    gain = gain_ref[...].astype(jnp.float32).reshape(1, width)
    step = 32

    for i in range(parts):
        token_copies[i].wait()

        def norm(j, _):
            at = pl.ds(pl.multiple_of(i * part + j * step, step), step)
            floats = tokens[at, :].astype(jnp.float32)
            mean = jnp.sum(floats * floats, axis=1, keepdims=True) * (1.0 / width)
            tokens[at, :] = (floats * lax.rsqrt(mean + EPSILON) * gain).astype(jnp.bfloat16)
            return 0

        lax.fori_loop(0, part // step, norm, 0, unroll=True)
    if chunks > 1:
        copies[1].start()
    for first in range(0, width, 512):
        columns = slice(first, first + 512)
        normed[:, columns] = dot(order, tokens[:, columns]).astype(jnp.bfloat16)
    groups, heads = out_ref.shape[0], out_ref.shape[1]
    offsets = [0]
    for i in range(count):
        offsets.append(offsets[-1] + weights_hbm[i].shape[1] // heads)
    for j in range(chunks):
        i, first = origin[j]
        copies[j].wait()
        if j + 2 < chunks:
            copies[j + 2].start()
        product = dot(normed[...], weights[j])
        per_head = offsets[i + 1] - offsets[i]
        for u in range(0, span, HEAD_SIZE):
            values = product[:, u : u + HEAD_SIZE]
            if kinds[i]:
                values = values * cosine + pltpu.roll(values, HEAD_SIZE // 2, 1) * sine
            head, inside = divmod(first + u, per_head)
            inside += offsets[i]
            out_ref[:, head, :, inside : inside + HEAD_SIZE] = values.astype(jnp.bfloat16).reshape(
                groups, rows // groups, HEAD_SIZE
            )


def project(scalars, positions, freq, gain, tokens, weights, kinds, devices, heads):
    rows, width = tokens.shape
    groups = devices // heads
    columns = sum(w.shape[1] for w in weights)
    span = 512
    parts = 4
    flops = 2 * rows * width * columns
    size = 2 * (width * columns + rows * width + rows * columns)
    return pl.pallas_call(
        functools.partial(project_kernel, kinds, devices, heads),
        out_shape=jax.ShapeDtypeStruct((groups, heads, rows // groups, columns // heads), jnp.bfloat16),
        in_specs=[SCALARS] + [WHOLE] * 3 + [IN_PLACE] * (len(weights) + 1),
        out_specs=WHOLE,
        scratch_shapes=[
            pltpu.VMEM((rows, width), jnp.bfloat16),
            pltpu.VMEM((rows, width), jnp.bfloat16),
            pltpu.VMEM((columns // span, width, span), jnp.bfloat16),
            pltpu.SemaphoreType.DMA((parts,)),
            pltpu.SemaphoreType.DMA((columns // span,)),
        ],
        compiler_params=pltpu.CompilerParams(vmem_limit_bytes=56 * MIB),
        cost_estimate=pl.CostEstimate(flops=flops, bytes_accessed=size, transcendentals=0),
    )(scalars, positions, freq, gain, tokens, *weights)


def place_kernel(arrived_ref, slot_ref, *outs):
    rows = arrived_ref.shape[0]
    first = 0
    for out_ref in outs:
        size = out_ref.shape[0]
        slots = lax.broadcasted_iota(jnp.int32, (size, rows), 0) + first
        chosen = (slots == slot_ref[...]).astype(jnp.bfloat16)
        out_ref[...] = dot(chosen, arrived_ref[...]).astype(jnp.bfloat16)
        first += size


def place(arrived, slot, sizes):
    width = arrived.shape[1]
    return pl.pallas_call(
        place_kernel,
        out_shape=[jax.ShapeDtypeStruct((size, width), jnp.bfloat16) for size in sizes],
        in_specs=[WHOLE, WHOLE],
        out_specs=[WHOLE] * len(sizes),
        compiler_params=pltpu.CompilerParams(vmem_limit_bytes=16 * MIB),
        cost_estimate=pl.CostEstimate(
            flops=2 * sum(sizes) * arrived.shape[0] * width,
            bytes_accessed=4 * arrived.size,
            transcendentals=0,
        ),
    )(arrived, slot)


def attend_kernel(block, scalar_ref, query_ref, slot_ref, ends_ref, *rest):
    pieces, out_ref, held = rest[:6], rest[6], rest[7]
    target, starts = scalar_ref[0], (scalar_ref[1], scalar_ref[2])
    heads = query_ref.shape[1] // HEAD_SIZE
    arrived = query_ref.shape[0]
    run = arrived // 2
    per_run = run // block
    reach = REACH_BLOCKS * block
    keys = reach + block
    slot = slot_ref[...]
    ends = ends_ref[...]
    factor = jnp.float32(np.log2(np.e) / HEAD_SIZE**0.5)
    for half in range(2):
        first = 0
        for piece in pieces[3 * half : 3 * half + 3]:
            held[half, first : first + piece.shape[0], :] = piece[...]
            first += piece.shape[0]
    indices = (target, per_run - 1 - target)
    at = [pl.multiple_of(index * block, block) for index in indices]
    iota = lax.broadcasted_iota(jnp.int32, (block, arrived), 0)
    chosen = [(iota + (at[half] + half * run) == slot).astype(jnp.bfloat16) for half in range(2)]
    queries = dot(jnp.concatenate(chosen, axis=0), query_ref[...]).astype(jnp.bfloat16)
    for half in range(2):
        here = slice(half * block, (half + 1) * block)
        key = held[half, pl.ds(at[half], keys), :HEAD_SIZE]
        value = held[half, pl.ds(at[half], keys), HEAD_SIZE:]
        begin = starts[half] + at[half]
        query_at = lax.broadcasted_iota(jnp.int32, (block, 1), 0) + begin
        key_at = lax.broadcasted_iota(jnp.int32, (1, keys), 1) + (begin - reach)
        doc_start = jnp.max(jnp.where(ends <= query_at, ends, 0), axis=1, keepdims=True)
        allowed = (key_at >= doc_start) & (key_at <= query_at)
        stacked = jnp.concatenate(
            [queries[here, h * HEAD_SIZE : (h + 1) * HEAD_SIZE] for h in range(heads)], axis=0
        )
        scores = lax.dot_general(stacked, key, (((1,), (1,)), ((), ())), preferred_element_type=jnp.float32)
        scores = jnp.where(allowed[None], scores.reshape(heads, block, keys), jnp.float32(-1e30))
        scores = scores.reshape(heads * block, keys)
        top = jnp.max(scores, axis=1, keepdims=True)
        weights = jnp.exp2((scores - top) * factor)
        total = jnp.sum(weights, axis=1, keepdims=True)
        mixed = (dot(weights.astype(jnp.bfloat16), value) / total).astype(jnp.bfloat16)
        for h in range(heads):
            out_ref[here, h * HEAD_SIZE : (h + 1) * HEAD_SIZE] = mixed[h * block : (h + 1) * block]


def attend(scalars, query, slot, ends, pieces, block):
    width = query.shape[1]
    held = REACH_BLOCKS * block + query.shape[0] // 2
    heads = width // HEAD_SIZE
    reach = (REACH_BLOCKS + 1) * block
    return pl.pallas_call(
        functools.partial(attend_kernel, block),
        out_shape=jax.ShapeDtypeStruct((2 * block, width), jnp.bfloat16),
        in_specs=[SCALARS] + [WHOLE] * 9,
        out_specs=WHOLE,
        scratch_shapes=[pltpu.VMEM((2, held, 2 * HEAD_SIZE), jnp.bfloat16)],
        compiler_params=pltpu.CompilerParams(vmem_limit_bytes=16 * MIB),
        cost_estimate=pl.CostEstimate(
            flops=2 * 2 * heads * block * reach * HEAD_SIZE * 2 + 4 * block * query.size,
            bytes_accessed=2 * query.size + 8 * held * HEAD_SIZE,
            transcendentals=2 * heads * block * reach,
        ),
    )(scalars, query, slot, ends, *pieces)


def assemble_kernel(scalar_ref, *rest):
    pieces, out_ref = rest[:-1], rest[-1]
    width = pieces[0].shape[1]
    for k, piece in enumerate(pieces):
        at = pl.multiple_of((scalar_ref[0] ^ k) * width, width)
        out_ref[:, pl.ds(at, width)] = piece[...]


def assemble(scalars, pieces):
    rows, width = pieces[0].shape
    return pl.pallas_call(
        assemble_kernel,
        out_shape=jax.ShapeDtypeStruct((rows, width * len(pieces)), jnp.bfloat16),
        in_specs=[SCALARS] + [WHOLE] * len(pieces),
        out_specs=WHOLE,
        compiler_params=pltpu.CompilerParams(vmem_limit_bytes=8 * MIB),
        cost_estimate=pl.CostEstimate(
            flops=0, bytes_accessed=4 * rows * width * len(pieces), transcendentals=0
        ),
    )(scalars, *pieces)


def shards(tokens, positions, lengths, gain, w_query, w_key, value_weight):
    devices = lax.axis_size("ctx")
    device = lax.axis_index("ctx")
    rows = tokens.shape[0]
    block = rows // 2
    members = w_key.shape[1] // HEAD_SIZE
    groups = devices // members
    group = device // members
    member = device % members
    run = members * block
    group_rows = rows // groups

    half = HEAD_SIZE // 2
    freq = ROPE_THETA ** (-(jnp.arange(HEAD_SIZE, dtype=jnp.float32) % half * 2.0 / HEAD_SIZE))
    operands = (device.reshape(1), positions.reshape(-1, 128), freq[None, :], gain, tokens)

    def exchange(ordered):
        width = ordered.shape[3]
        flat = ordered.reshape(devices, group_rows, width)
        flat = lax.all_to_all(flat, "ctx", split_axis=0, concat_axis=0, tiled=True)
        return flat.reshape(devices * group_rows, width)

    kv = project(*operands, (w_key, value_weight), (True, False), devices, members)
    kv = exchange(kv)
    query = project(*operands, (w_query,), (True,), devices, members)

    table = positions.reshape(devices, rows)
    ours = group_of(table, block, devices, members) == group
    first_run = group * run
    second_run = (2 * devices - members) * block - group * run
    slots = jnp.where(table // run == group, table - first_run, table - second_run + run)
    place_in = jnp.cumsum(ours.astype(jnp.int32), axis=1) - 1
    place_in = jnp.where(ours, place_in, -1)
    wanted = jnp.arange(group_rows, dtype=jnp.int32)[None, :, None] == place_in[:, None, :]
    slot = jnp.sum(jnp.where(wanted, slots[:, None, :], 0), axis=2).reshape(1, devices * group_rows)
    ends = jnp.cumsum(lengths, dtype=jnp.int32)[None, :]

    kv, query = lax.optimization_barrier((kv, query))
    query = exchange(query)
    reach = REACH_BLOCKS * block
    sizes = [run - reach, reach] * 2
    early_head, early_tail, late_head, late_tail = place(kv, slot, sizes)
    up = [(i, i + members) for i in range(devices - members)]
    down = [(i + members, i) for i in range(devices - members)]
    early_halo = lax.ppermute(early_tail, "ctx", up)
    late_halo = lax.ppermute(late_tail, "ctx", down)
    late_halo = jnp.where(group == groups - 1, early_tail, late_halo)
    pieces = (early_halo, early_head, early_tail, late_halo, late_head, late_tail)

    results = []
    for k in [3, 1, 2, 0][-members:]:
        target = member ^ k
        scalars = jnp.stack([target, first_run, second_run]).astype(jnp.int32)
        out = attend(scalars, query, slot, ends, pieces, block)
        if k:
            route = [(i, i // members * members + (i % members ^ k)) for i in range(devices)]
            out = lax.ppermute(out, "ctx", route)
        results.append((k, out))
    results = [out for _, out in sorted(results, key=lambda pair: pair[0])]
    return assemble(member.reshape(1).astype(jnp.int32), results)


def solution(mesh):
    in_specs = (P(("dp", "ctx"), None), P("dp"), P("dp"), P(), P(), P(), P())
    out_specs = P(("dp", "ctx"), None)
    return jax.shard_map(shards, mesh=mesh, in_specs=in_specs, out_specs=out_specs, check_vma=False)
```

```python
import functools

import jax
import jax.numpy as jnp
import numpy as np
from jax import lax
from jax.experimental import pallas as pl
from jax.experimental.pallas import tpu as pltpu
from jax.sharding import PartitionSpec as P

HEAD_SIZE = 128
REACH_BLOCKS = 3
ROPE_THETA = 500000.0
EPSILON = 1e-05

WHOLE = pl.BlockSpec(memory_space=pltpu.VMEM)
IN_PLACE = pl.BlockSpec(memory_space=pl.ANY)
SCALARS = pl.BlockSpec(memory_space=pltpu.SMEM)
MIB = 1024 * 1024


def dot(a, b):
    return jnp.dot(a, b, preferred_element_type=jnp.float32)


def transposed(row):
    size = row.shape[1]
    here = lax.broadcasted_iota(jnp.int32, (size, size), 0)
    there = lax.broadcasted_iota(jnp.int32, (size, size), 1)
    return jnp.sum(jnp.where(here == there, row, 0), axis=1, keepdims=True)


def group_of(where_at, block, devices, members):
    block_id = where_at // block
    return jnp.minimum(block_id, 2 * devices - 1 - block_id) // members


def project_kernel(plan, devices, members, scalar_ref, positions_ref, freq_ref, gain_ref, tokens_hbm, *rest):
    weights_hbm, (out_ref, tokens, normed, weights, token_sems, sems) = rest[:-6], rest[-6:]
    rows, width = tokens.shape
    chunks = len(plan)
    parts = token_sems.shape[0]
    part = rows // parts
    token_copies, copies = [], []
    for i in range(parts):
        at = pl.ds(i * part, part)
        token_copies.append(pltpu.make_async_copy(tokens_hbm.at[at], tokens.at[at], token_sems.at[i]))
        token_copies[i].start()
    for j, tiles in enumerate(plan):
        joined = []
        for i, (array, column, _, _, _) in enumerate(tiles):
            if joined and joined[-1][:2] == [array, column - joined[-1][2]]:
                joined[-1][2] += HEAD_SIZE
            else:
                joined.append([array, column, HEAD_SIZE, i * HEAD_SIZE])
        copies.append(
            [
                pltpu.make_async_copy(
                    weights_hbm[array].at[:, pl.ds(column, size)],
                    weights.at[j, :, pl.ds(to, size)],
                    sems.at[j, i],
                )
                for i, (array, column, size, to) in enumerate(joined)
            ]
        )

    def start(j):
        for copy in copies[j]:
            copy.start()

    start(0)
    lanes = positions_ref.shape[1]
    stripes = rows // lanes
    mine = jnp.concatenate(
        [positions_ref[pl.ds(scalar_ref[0] * stripes + i, 1), :] for i in range(stripes)], axis=1
    )
    owner = group_of(mine, rows // 2, devices, members)
    here = lax.broadcasted_iota(jnp.int32, (rows, rows), 0)
    there = lax.broadcasted_iota(jnp.int32, (rows, rows), 1)
    earlier = jnp.where((transposed(owner) == owner) & (here < there), 1, 0)
    rank = owner * (rows * members // devices) + jnp.sum(earlier, axis=0, keepdims=True)
    order = here == rank
    ordered_at = jnp.sum(jnp.where(order, mine, 0), axis=1, keepdims=True)
    angle = ordered_at.astype(jnp.float32) * freq_ref[...]
    lane = lax.broadcasted_iota(jnp.int32, (rows, HEAD_SIZE), 1)
    cosine = jnp.cos(angle)
    sine = jnp.where(lane < HEAD_SIZE // 2, -1.0, 1.0) * jnp.sin(angle)
    order = jnp.where(order, 1.0, 0.0).astype(jnp.bfloat16)
    gain = gain_ref[...].astype(jnp.float32).reshape(1, width)
    step = 32

    for i in range(parts):
        token_copies[i].wait()

        def norm(j, _):
            at = pl.ds(pl.multiple_of(i * part + j * step, step), step)
            floats = tokens[at, :].astype(jnp.float32)
            mean = jnp.sum(floats * floats, axis=1, keepdims=True) * (1.0 / width)
            tokens[at, :] = (floats * lax.rsqrt(mean + EPSILON) * gain).astype(jnp.bfloat16)
            return 0

        lax.fori_loop(0, part // step, norm, 0, unroll=True)
    if chunks > 1:
        start(1)
    for first in range(0, width, 512):
        columns = slice(first, first + 512)
        normed[:, columns] = dot(order, tokens[:, columns]).astype(jnp.bfloat16)
    groups = out_ref.shape[0]
    for j, tiles in enumerate(plan):
        for copy in copies[j]:
            copy.wait()
        if j + 2 < chunks:
            start(j + 2)
        product = dot(normed[...], weights[j])
        for i, (_, _, head, to, roped) in enumerate(tiles):
            values = product[:, i * HEAD_SIZE : (i + 1) * HEAD_SIZE]
            if roped:
                values = values * cosine + pltpu.roll(values, HEAD_SIZE // 2, 1) * sine
            values = values.astype(jnp.bfloat16).reshape(groups, rows // groups, HEAD_SIZE)
            out_ref[:, head, :, to : to + HEAD_SIZE] = values


def project(scalars, positions, freq, gain, tokens, weights, tiles, devices, heads):
    rows, width = tokens.shape
    groups = devices // heads
    columns = len(tiles) * HEAD_SIZE
    per_chunk = 4
    plan = [tiles[i : i + per_chunk] for i in range(0, len(tiles), per_chunk)]
    parts = 4
    flops = 2 * rows * width * columns
    size = 2 * (width * columns + rows * width + rows * columns)
    return pl.pallas_call(
        functools.partial(project_kernel, plan, devices, heads),
        out_shape=jax.ShapeDtypeStruct((groups, heads, rows // groups, columns // heads), jnp.bfloat16),
        in_specs=[SCALARS] + [WHOLE] * 3 + [IN_PLACE] * (len(weights) + 1),
        out_specs=WHOLE,
        scratch_shapes=[
            pltpu.VMEM((rows, width), jnp.bfloat16),
            pltpu.VMEM((rows, width), jnp.bfloat16),
            pltpu.VMEM((len(plan), width, per_chunk * HEAD_SIZE), jnp.bfloat16),
            pltpu.SemaphoreType.DMA((parts,)),
            pltpu.SemaphoreType.DMA((len(plan), per_chunk)),
        ],
        compiler_params=pltpu.CompilerParams(vmem_limit_bytes=56 * MIB),
        cost_estimate=pl.CostEstimate(flops=flops, bytes_accessed=size, transcendentals=0),
    )(scalars, positions, freq, gain, tokens, *weights)


def place_kernel(arrived_ref, slot_ref, *outs):
    rows = arrived_ref.shape[0]
    first = 0
    for out_ref in outs:
        size = out_ref.shape[0]
        slots = lax.broadcasted_iota(jnp.int32, (size, rows), 0) + first
        chosen = (slots == slot_ref[...]).astype(jnp.bfloat16)
        out_ref[...] = dot(chosen, arrived_ref[:, : out_ref.shape[1]]).astype(jnp.bfloat16)
        first += size


def place(arrived, slot, sizes, width):
    return pl.pallas_call(
        place_kernel,
        out_shape=[jax.ShapeDtypeStruct((size, width), jnp.bfloat16) for size in sizes],
        in_specs=[WHOLE, WHOLE],
        out_specs=[WHOLE] * len(sizes),
        compiler_params=pltpu.CompilerParams(vmem_limit_bytes=16 * MIB),
        cost_estimate=pl.CostEstimate(
            flops=2 * sum(sizes) * arrived.shape[0] * width,
            bytes_accessed=4 * arrived.size,
            transcendentals=0,
        ),
    )(arrived, slot)


def attend_kernel(block, columns, scalar_ref, query_ref, slot_ref, ends_ref, *rest):
    pieces, out_ref, held = rest[:6], rest[6], rest[7]
    target, starts, last = scalar_ref[0], (scalar_ref[1], scalar_ref[2]), scalar_ref[3]
    heads = out_ref.shape[1] // HEAD_SIZE
    arrived = query_ref.shape[0]
    run = arrived // 2
    per_run = run // block
    reach = REACH_BLOCKS * block
    keys = reach + block
    slot = slot_ref[...]
    ends = ends_ref[...]
    factor = jnp.float32(np.log2(np.e) / HEAD_SIZE**0.5)
    for half in range(2):
        first = 0
        for piece in pieces[3 * half : 3 * half + 3]:
            values = piece[...]
            if half == 1 and first == 0:
                values = jnp.where(last == 1, pieces[2][...], values)
            held[half, first : first + piece.shape[0], :] = values
            first += piece.shape[0]
    indices = (target, per_run - 1 - target)
    at = [pl.multiple_of(index * block, block) for index in indices]
    iota = lax.broadcasted_iota(jnp.int32, (block, arrived), 0)
    chosen = [(iota + (at[half] + half * run) == slot).astype(jnp.bfloat16) for half in range(2)]
    queries = dot(jnp.concatenate(chosen, axis=0), query_ref[:, columns]).astype(jnp.bfloat16)
    for half in range(2):
        here = slice(half * block, (half + 1) * block)
        key = held[half, pl.ds(at[half], keys), :HEAD_SIZE]
        value = held[half, pl.ds(at[half], keys), HEAD_SIZE:]
        begin = starts[half] + at[half]
        query_at = lax.broadcasted_iota(jnp.int32, (block, 1), 0) + begin
        key_at = lax.broadcasted_iota(jnp.int32, (1, keys), 1) + (begin - reach)
        doc_start = jnp.max(jnp.where(ends <= query_at, ends, 0), axis=1, keepdims=True)
        allowed = (key_at >= doc_start) & (key_at <= query_at)
        stacked = jnp.concatenate(
            [queries[here, h * HEAD_SIZE : (h + 1) * HEAD_SIZE] for h in range(heads)], axis=0
        )
        scores = lax.dot_general(stacked, key, (((1,), (1,)), ((), ())), preferred_element_type=jnp.float32)
        scores = jnp.where(allowed[None], scores.reshape(heads, block, keys), jnp.float32(-1e30))
        scores = scores.reshape(heads * block, keys)
        top = jnp.max(scores, axis=1, keepdims=True)
        weights = jnp.exp2((scores - top) * factor)
        total = jnp.sum(weights, axis=1, keepdims=True)
        mixed = (dot(weights.astype(jnp.bfloat16), value) / total).astype(jnp.bfloat16)
        for h in range(heads):
            out_ref[here, h * HEAD_SIZE : (h + 1) * HEAD_SIZE] = mixed[h * block : (h + 1) * block]


def attend(scalars, query, columns, slot, ends, pieces, block):
    width = columns.stop - columns.start
    rows = query.shape[0]
    held = REACH_BLOCKS * block + rows // 2
    heads = width // HEAD_SIZE
    reach = (REACH_BLOCKS + 1) * block
    return pl.pallas_call(
        functools.partial(attend_kernel, block, columns),
        out_shape=jax.ShapeDtypeStruct((2 * block, width), jnp.bfloat16),
        in_specs=[SCALARS] + [WHOLE] * 9,
        out_specs=WHOLE,
        scratch_shapes=[pltpu.VMEM((2, held, 2 * HEAD_SIZE), jnp.bfloat16)],
        compiler_params=pltpu.CompilerParams(vmem_limit_bytes=16 * MIB),
        cost_estimate=pl.CostEstimate(
            flops=2 * 2 * heads * block * reach * HEAD_SIZE * 2 + 4 * block * rows * width,
            bytes_accessed=2 * query.size + 8 * held * HEAD_SIZE,
            transcendentals=2 * heads * block * reach,
        ),
    )(scalars, query, slot, ends, *pieces)


def assemble_kernel(parts, scalar_ref, *rest):
    pieces, out_ref = rest[:-1], rest[-1]
    width = pieces[0].shape[1]
    for i, piece in enumerate(pieces):
        k, part = divmod(i, parts)
        at = pl.multiple_of(((scalar_ref[0] ^ k) * parts + part) * width, width)
        out_ref[:, pl.ds(at, width)] = piece[...]


def assemble(scalars, pieces, parts):
    rows, width = pieces[0].shape
    return pl.pallas_call(
        functools.partial(assemble_kernel, parts),
        out_shape=jax.ShapeDtypeStruct((rows, width * len(pieces)), jnp.bfloat16),
        in_specs=[SCALARS] + [WHOLE] * len(pieces),
        out_specs=WHOLE,
        compiler_params=pltpu.CompilerParams(vmem_limit_bytes=8 * MIB),
        cost_estimate=pl.CostEstimate(
            flops=0, bytes_accessed=4 * rows * width * len(pieces), transcendentals=0
        ),
    )(scalars, *pieces)


def shards(tokens, positions, lengths, gain, w_query, w_key, value_weight):
    devices = lax.axis_size("ctx")
    device = lax.axis_index("ctx")
    rows = tokens.shape[0]
    block = rows // 2
    members = w_key.shape[1] // HEAD_SIZE
    groups = devices // members
    group = device // members
    member = device % members
    run = members * block
    group_rows = rows // groups

    half = HEAD_SIZE // 2
    freq = ROPE_THETA ** (-(jnp.arange(HEAD_SIZE, dtype=jnp.float32) % half * 2.0 / HEAD_SIZE))
    operands = (device.reshape(1), positions.reshape(-1, 128), freq[None, :], gain, tokens)

    def exchange(ordered):
        width = ordered.shape[3]
        flat = ordered.reshape(devices, group_rows, width)
        flat = lax.all_to_all(flat, "ctx", split_axis=0, concat_axis=0, tiled=True)
        return flat.reshape(devices * group_rows, width)

    per_group = w_query.shape[1] // w_key.shape[1]
    first_heads = per_group // 2

    def tiles(array, heads_each, taken, to, roped):
        return [
            (array, (head * heads_each + i) * HEAD_SIZE, head, to + (i - taken[0]) * HEAD_SIZE, roped)
            for head in range(members)
            for i in taken
        ]

    first_tiles = tiles(0, 1, range(1), 0, True) + tiles(1, 1, range(1), HEAD_SIZE, False)
    first_tiles += tiles(2, per_group, range(first_heads), 2 * HEAD_SIZE, True)
    second_tiles = tiles(0, per_group, range(first_heads, per_group), 0, True)
    first = project(*operands, (w_key, value_weight, w_query), first_tiles, devices, members)
    first = exchange(first)
    second = project(*operands, (w_query,), second_tiles, devices, members)

    table = positions.reshape(devices, rows)
    ours = group_of(table, block, devices, members) == group
    first_run = group * run
    second_run = (2 * devices - members) * block - group * run
    slots = jnp.where(table // run == group, table - first_run, table - second_run + run)
    place_in = jnp.cumsum(ours.astype(jnp.int32), axis=1) - 1
    place_in = jnp.where(ours, place_in, -1)
    wanted = jnp.arange(group_rows, dtype=jnp.int32)[None, :, None] == place_in[:, None, :]
    slot = jnp.sum(jnp.where(wanted, slots[:, None, :], 0), axis=2).reshape(1, devices * group_rows)
    ends = jnp.cumsum(lengths, dtype=jnp.int32)[None, :]

    reach = REACH_BLOCKS * block
    sizes = [run - reach, reach] * 2
    placed = place(first, slot, sizes, 2 * HEAD_SIZE)
    placed, second = lax.optimization_barrier((placed, second))
    early_head, early_tail, late_head, late_tail = placed
    up = [(i, i + members) for i in range(devices - members)]
    down = [(i + members, i) for i in range(devices - members)]
    early_halo = lax.ppermute(early_tail, "ctx", up)
    late_halo = lax.ppermute(late_tail, "ctx", down)
    pieces = (early_halo, early_head, early_tail, late_halo, late_head, late_tail)
    second = exchange(second)

    last = (group == groups - 1).astype(jnp.int32)
    first_columns = slice(2 * HEAD_SIZE, (2 + first_heads) * HEAD_SIZE)
    second_columns = slice(0, (per_group - first_heads) * HEAD_SIZE)
    results = {}
    for part, (query, columns) in enumerate([(first, first_columns), (second, second_columns)]):
        for k in [3, 1, 2, 0][-members:]:
            scalars = jnp.stack([member ^ k, first_run, second_run, last]).astype(jnp.int32)
            out = attend(scalars, query, columns, slot, ends, pieces, block)
            if k:
                route = [(i, i // members * members + (i % members ^ k)) for i in range(devices)]
                out = lax.ppermute(out, "ctx", route)
            results[k, part] = out
    results = [results[key] for key in sorted(results)]
    return assemble(member.reshape(1).astype(jnp.int32), results, 2)


def solution(mesh):
    in_specs = (P(("dp", "ctx"), None), P("dp"), P("dp"), P(), P(), P(), P())
    out_specs = P(("dp", "ctx"), None)
    return jax.shard_map(shards, mesh=mesh, in_specs=in_specs, out_specs=out_specs, check_vma=False)
```

```python
import functools

import jax
import jax.numpy as jnp
import numpy as np
from jax import lax
from jax.experimental import pallas as pl
from jax.experimental.pallas import tpu as pltpu
from jax.sharding import PartitionSpec as P

HEAD_SIZE = 128
REACH_BLOCKS = 3
ROPE_THETA = 500000.0
EPSILON = 1e-05

WHOLE = pl.BlockSpec(memory_space=pltpu.VMEM)
IN_PLACE = pl.BlockSpec(memory_space=pl.ANY)
SCALARS = pl.BlockSpec(memory_space=pltpu.SMEM)
MIB = 1024 * 1024


def dot(a, b):
    return jnp.dot(a, b, preferred_element_type=jnp.float32)


def transposed(row):
    size = row.shape[1]
    here = lax.broadcasted_iota(jnp.int32, (size, size), 0)
    there = lax.broadcasted_iota(jnp.int32, (size, size), 1)
    return jnp.sum(jnp.where(here == there, row, 0), axis=1, keepdims=True)


def group_of(where_at, block, devices, members):
    block_id = where_at // block
    return jnp.minimum(block_id, 2 * devices - 1 - block_id) // members


def project_kernel(kinds, devices, members, scalar_ref, positions_ref, freq_ref, gain_ref, tokens_hbm, *rest):
    count = len(kinds)
    weights_hbm, out_ref = rest[:count], rest[count]
    tokens, normed, weights, token_sems, sems = rest[count + 1 :]
    rows, width = tokens.shape
    chunks, _, span = weights.shape
    parts = token_sems.shape[0]
    part = rows // parts
    token_copies, copies, origin = [], [], []
    for i in range(parts):
        at = pl.ds(i * part, part)
        token_copies.append(pltpu.make_async_copy(tokens_hbm.at[at], tokens.at[at], token_sems.at[i]))
        token_copies[i].start()
    for i in range(count):
        for first in range(0, weights_hbm[i].shape[1], span):
            j = len(copies)
            source = weights_hbm[i].at[:, pl.ds(first, span)]
            copies.append(pltpu.make_async_copy(source, weights.at[j], sems.at[j]))
            origin.append((i, first))

    copies[0].start()
    lanes = positions_ref.shape[1]
    stripes = rows // lanes
    mine = jnp.concatenate(
        [positions_ref[pl.ds(scalar_ref[0] * stripes + i, 1), :] for i in range(stripes)], axis=1
    )
    owner = group_of(mine, rows // 2, devices, members)
    here = lax.broadcasted_iota(jnp.int32, (rows, rows), 0)
    there = lax.broadcasted_iota(jnp.int32, (rows, rows), 1)
    earlier = jnp.where((transposed(owner) == owner) & (here < there), 1, 0)
    rank = owner * (rows * members // devices) + jnp.sum(earlier, axis=0, keepdims=True)
    order = here == rank
    ordered_at = jnp.sum(jnp.where(order, mine, 0), axis=1, keepdims=True)
    angle = ordered_at.astype(jnp.float32) * freq_ref[...]
    lane = lax.broadcasted_iota(jnp.int32, (rows, HEAD_SIZE), 1)
    cosine = jnp.cos(angle)
    sine = jnp.where(lane < HEAD_SIZE // 2, -1.0, 1.0) * jnp.sin(angle)
    order = jnp.where(order, 1.0, 0.0).astype(jnp.bfloat16)
    gain = gain_ref[...].astype(jnp.float32).reshape(1, width)
    step = 32

    for i in range(parts):
        token_copies[i].wait()

        def norm(j, _):
            at = pl.ds(pl.multiple_of(i * part + j * step, step), step)
            floats = tokens[at, :].astype(jnp.float32)
            mean = jnp.sum(floats * floats, axis=1, keepdims=True) * (1.0 / width)
            tokens[at, :] = (floats * lax.rsqrt(mean + EPSILON) * gain).astype(jnp.bfloat16)
            return 0

        lax.fori_loop(0, part // step, norm, 0, unroll=True)
    if chunks > 1:
        copies[1].start()
    for first in range(0, width, 512):
        columns = slice(first, first + 512)
        normed[:, columns] = dot(order, tokens[:, columns]).astype(jnp.bfloat16)
    groups, heads = out_ref.shape[0], out_ref.shape[1]
    offsets = [0]
    for i in range(count):
        offsets.append(offsets[-1] + weights_hbm[i].shape[1] // heads)
    for j in range(chunks):
        i, first = origin[j]
        copies[j].wait()
        if j + 2 < chunks:
            copies[j + 2].start()
        product = dot(normed[...], weights[j])
        per_head = offsets[i + 1] - offsets[i]
        for u in range(0, span, HEAD_SIZE):
            values = product[:, u : u + HEAD_SIZE]
            if kinds[i]:
                values = values * cosine + pltpu.roll(values, HEAD_SIZE // 2, 1) * sine
            head, inside = divmod(first + u, per_head)
            inside += offsets[i]
            out_ref[:, head, :, inside : inside + HEAD_SIZE] = values.astype(jnp.bfloat16).reshape(
                groups, rows // groups, HEAD_SIZE
            )


def project(scalars, positions, freq, gain, tokens, weights, kinds, devices, heads):
    rows, width = tokens.shape
    groups = devices // heads
    columns = sum(w.shape[1] for w in weights)
    span = 512
    parts = 4
    flops = 2 * rows * width * columns
    size = 2 * (width * columns + rows * width + rows * columns)
    return pl.pallas_call(
        functools.partial(project_kernel, kinds, devices, heads),
        out_shape=jax.ShapeDtypeStruct((groups, heads, rows // groups, columns // heads), jnp.bfloat16),
        in_specs=[SCALARS] + [WHOLE] * 3 + [IN_PLACE] * (len(weights) + 1),
        out_specs=WHOLE,
        scratch_shapes=[
            pltpu.VMEM((rows, width), jnp.bfloat16),
            pltpu.VMEM((rows, width), jnp.bfloat16),
            pltpu.VMEM((columns // span, width, span), jnp.bfloat16),
            pltpu.SemaphoreType.DMA((parts,)),
            pltpu.SemaphoreType.DMA((columns // span,)),
        ],
        compiler_params=pltpu.CompilerParams(vmem_limit_bytes=56 * MIB),
        cost_estimate=pl.CostEstimate(flops=flops, bytes_accessed=size, transcendentals=0),
    )(scalars, positions, freq, gain, tokens, *weights)


def place_kernel(block, scalar_ref, arrived_ref, slot_ref, ends_ref, *outs):
    outs, order_ref, mask_ref = outs[:-2], outs[-2], outs[-1]
    rows = arrived_ref.shape[0]
    slot = slot_ref[...]
    ends = ends_ref[...]
    first = 0
    for out_ref in outs:
        size = out_ref.shape[0]
        slots = lax.broadcasted_iota(jnp.int32, (size, rows), 0) + first
        chosen = (slots == slot).astype(jnp.bfloat16)
        order_ref[first : first + size, :] = chosen
        out_ref[...] = dot(chosen, arrived_ref[...]).astype(jnp.bfloat16)
        first += size
    _, per_run, _, keys = mask_ref.shape
    for half in range(2):
        for index in range(per_run):
            begin = scalar_ref[half] + index * block
            query_at = lax.broadcasted_iota(jnp.int32, (block, 1), 0) + begin
            key_at = lax.broadcasted_iota(jnp.int32, (1, keys), 1) + (begin + block - keys)
            doc_start = jnp.max(jnp.where(ends <= query_at, ends, 0), axis=1, keepdims=True)
            allowed = (key_at >= doc_start) & (key_at <= query_at)
            mask_ref[half, index] = jnp.where(allowed, jnp.float32(0), jnp.float32(-1e30))


def place(scalars, arrived, slot, ends, sizes, block):
    rows, width = arrived.shape
    per_run = rows // 2 // block
    mask = (2, per_run, block, (REACH_BLOCKS + 1) * block)
    return pl.pallas_call(
        functools.partial(place_kernel, block),
        out_shape=[jax.ShapeDtypeStruct((size, width), jnp.bfloat16) for size in sizes]
        + [jax.ShapeDtypeStruct((rows, rows), jnp.bfloat16), jax.ShapeDtypeStruct(mask, jnp.float32)],
        in_specs=[SCALARS] + [WHOLE] * 3,
        out_specs=[WHOLE] * (len(sizes) + 2),
        compiler_params=pltpu.CompilerParams(vmem_limit_bytes=16 * MIB),
        cost_estimate=pl.CostEstimate(
            flops=2 * rows * rows * width,
            bytes_accessed=4 * arrived.size,
            transcendentals=0,
        ),
    )(scalars, arrived, slot, ends)


def attend_kernel(scalar_ref, query_ref, order_ref, mask_ref, *rest):
    pieces, out_ref, held = rest[:6], rest[6], rest[7]
    target, last = scalar_ref[0], scalar_ref[1]
    heads = query_ref.shape[1] // HEAD_SIZE
    _, per_run, block, keys = mask_ref.shape
    run = per_run * block
    factor = jnp.float32(np.log2(np.e) / HEAD_SIZE**0.5)
    for half in range(2):
        first = 0
        for piece in pieces[3 * half : 3 * half + 3]:
            values = piece[...]
            if half == 1 and first == 0:
                values = jnp.where(last == 1, pieces[2][...], values)
            held[half, first : first + piece.shape[0], :] = values
            first += piece.shape[0]
    indices = (target, per_run - 1 - target)
    at = [pl.multiple_of(index * block, block) for index in indices]
    chosen = [order_ref[pl.ds(pl.multiple_of(at[half] + half * run, block), block), :] for half in range(2)]
    queries = dot(jnp.concatenate(chosen, axis=0), query_ref[...]).astype(jnp.bfloat16)
    here = [slice(half * block, (half + 1) * block) for half in range(2)]
    scores, weights, totals = [], [], []
    for half in range(2):
        stacked = jnp.concatenate(
            [queries[here[half], h * HEAD_SIZE : (h + 1) * HEAD_SIZE] for h in range(heads)], axis=0
        )
        key = held[half, pl.ds(at[half], keys), :HEAD_SIZE]
        scores.append(
            lax.dot_general(stacked, key, (((1,), (1,)), ((), ())), preferred_element_type=jnp.float32)
        )
    for half in range(2):
        masked = scores[half].reshape(heads, block, keys) + mask_ref[half, indices[half]][None]
        masked = masked.reshape(heads * block, keys)
        top = jnp.max(masked, axis=1, keepdims=True)
        exact = jnp.exp2((masked - top) * factor)
        totals.append(jnp.sum(exact, axis=1, keepdims=True))
        weights.append(exact.astype(jnp.bfloat16))
    for half in range(2):
        value = held[half, pl.ds(at[half], keys), HEAD_SIZE:]
        mixed = (dot(weights[half], value) / totals[half]).astype(jnp.bfloat16)
        for h in range(heads):
            out_ref[here[half], h * HEAD_SIZE : (h + 1) * HEAD_SIZE] = mixed[h * block : (h + 1) * block]


def attend(scalars, query, order, mask, pieces):
    rows, width = query.shape
    _, per_run, block, keys = mask.shape
    held = (per_run - 1) * block + keys
    heads = width // HEAD_SIZE
    return pl.pallas_call(
        attend_kernel,
        out_shape=jax.ShapeDtypeStruct((2 * block, width), jnp.bfloat16),
        in_specs=[SCALARS] + [WHOLE] * 9,
        out_specs=WHOLE,
        scratch_shapes=[pltpu.VMEM((2, held, 2 * HEAD_SIZE), jnp.bfloat16)],
        compiler_params=pltpu.CompilerParams(vmem_limit_bytes=16 * MIB),
        cost_estimate=pl.CostEstimate(
            flops=2 * 2 * heads * block * keys * HEAD_SIZE * 2 + 4 * block * rows * width,
            bytes_accessed=2 * query.size + 8 * held * HEAD_SIZE,
            transcendentals=2 * heads * block * keys,
        ),
    )(scalars, query, order, mask, *pieces)


def assemble_kernel(member_ref, *rest):
    count = len(rest) - 2
    pieces, out_hbm, sems = rest[:count], rest[count], rest[count + 1]
    width = pieces[0].shape[1]
    copies = []
    for i, piece in enumerate(pieces):
        at = pl.multiple_of(member_ref[i] * width, width)
        copies.append(pltpu.make_async_copy(piece, out_hbm.at[:, pl.ds(at, width)], sems.at[i]))
        copies[i].start()
    for copy in copies:
        copy.wait()


def assemble(sources, pieces):
    rows, width = pieces[0].shape
    return pl.pallas_call(
        assemble_kernel,
        out_shape=jax.ShapeDtypeStruct((rows, width * len(pieces)), jnp.bfloat16),
        in_specs=[SCALARS] + [WHOLE] * len(pieces),
        out_specs=IN_PLACE,
        scratch_shapes=[pltpu.SemaphoreType.DMA((len(pieces),))],
        compiler_params=pltpu.CompilerParams(vmem_limit_bytes=8 * MIB),
        cost_estimate=pl.CostEstimate(
            flops=0, bytes_accessed=4 * rows * width * len(pieces), transcendentals=0
        ),
    )(sources, *pieces)


def shards(tokens, positions, lengths, gain, w_query, w_key, value_weight):
    devices = lax.axis_size("ctx")
    device = lax.axis_index("ctx")
    rows = tokens.shape[0]
    block = rows // 2
    members = w_key.shape[1] // HEAD_SIZE
    groups = devices // members
    group = device // members
    member = device % members
    run = members * block
    group_rows = rows // groups

    half = HEAD_SIZE // 2
    freq = np.float32(ROPE_THETA ** (-(np.arange(HEAD_SIZE) % half * 2.0 / HEAD_SIZE)))
    operands = (device.reshape(1), positions.reshape(-1, 128), jnp.asarray(freq[None, :]), gain, tokens)

    def exchange(ordered):
        width = ordered.shape[3]
        flat = ordered.reshape(devices, group_rows, width)
        flat = lax.all_to_all(flat, "ctx", split_axis=0, concat_axis=0, tiled=True)
        return flat.reshape(devices * group_rows, width)

    kv = project(*operands, (w_key, value_weight), (True, False), devices, members)
    kv = exchange(kv)
    query = project(*operands, (w_query,), (True,), devices, members)

    table = positions.reshape(devices, rows)
    ours = group_of(table, block, devices, members) == group
    first_run = group * run
    second_run = (2 * devices - members) * block - group * run
    slots = jnp.where(table // run == group, table - first_run, table - second_run + run)
    place_in = jnp.cumsum(ours.astype(jnp.int32), axis=1) - 1
    place_in = jnp.where(ours, place_in, -1)
    wanted = jnp.arange(group_rows, dtype=jnp.int32)[None, :, None] == place_in[:, None, :]
    slot = jnp.sum(jnp.where(wanted, slots[:, None, :], 0), axis=2).reshape(1, devices * group_rows)
    ends = jnp.cumsum(lengths, dtype=jnp.int32)[None, :]

    kv, query = lax.optimization_barrier((kv, query))
    query = exchange(query)
    reach = REACH_BLOCKS * block
    sizes = [run - reach, reach] * 2
    scalars = jnp.stack([first_run, second_run]).astype(jnp.int32)
    early_head, early_tail, late_head, late_tail, order, mask = place(scalars, kv, slot, ends, sizes, block)
    up = [(i, i + members) for i in range(devices - members)]
    down = [(i + members, i) for i in range(devices - members)]
    early_halo = lax.ppermute(early_tail, "ctx", up)
    late_halo = lax.ppermute(late_tail, "ctx", down)
    pieces = (early_halo, early_head, early_tail, late_halo, late_head, late_tail)

    last = group == groups - 1
    lanes = lax.axis_size("dp")
    lane = lax.axis_index("dp")
    farthest = members - 1
    between = list(range(1, farthest))
    turns = [[farthest] + (between if i % 2 == 0 else between[::-1]) + [0] for i in range(lanes)]
    sources, results = [], []
    for turn in range(members):
        distance = jnp.asarray([order_of[turn] for order_of in turns], jnp.int32)[lane]
        scalars = jnp.stack([member ^ distance, last]).astype(jnp.int32)
        out = attend(scalars, query, order, mask, pieces)
        if turn < members - 1:
            route = [
                (i * devices + j, i * devices + (j // members * members + (j % members ^ turns[i][turn])))
                for i in range(lanes)
                for j in range(devices)
            ]
            out = lax.ppermute(out, ("dp", "ctx"), route)
        sources.append(member ^ distance)
        results.append(out)
    return assemble(jnp.stack(sources).astype(jnp.int32), results)


def solution(mesh):
    in_specs = (P(("dp", "ctx"), None), P("dp"), P("dp"), P(), P(), P(), P())
    out_specs = P(("dp", "ctx"), None)
    return jax.shard_map(shards, mesh=mesh, in_specs=in_specs, out_specs=out_specs, check_vma=False)
```

```python
import functools

import jax
import jax.numpy as jnp
import numpy as np
from jax import lax
from jax.experimental import pallas as pl
from jax.experimental.pallas import tpu as pltpu
from jax.sharding import PartitionSpec as P

HEAD_SIZE = 128
REACH_BLOCKS = 3
ROPE_THETA = 500000.0
EPSILON = 1e-05

WHOLE = pl.BlockSpec(memory_space=pltpu.VMEM)
IN_PLACE = pl.BlockSpec(memory_space=pl.ANY)
SCALARS = pl.BlockSpec(memory_space=pltpu.SMEM)
MIB = 1024 * 1024


def dot(a, b):
    return jnp.dot(a, b, preferred_element_type=jnp.float32)


def transposed(row):
    size = row.shape[1]
    here = lax.broadcasted_iota(jnp.int32, (size, size), 0)
    there = lax.broadcasted_iota(jnp.int32, (size, size), 1)
    return jnp.sum(jnp.where(here == there, row, 0), axis=1, keepdims=True)


def group_of(where_at, block, devices, members):
    block_id = where_at // block
    return jnp.minimum(block_id, 2 * devices - 1 - block_id) // members


def project_kernel(kinds, devices, members, scalar_ref, positions_ref, freq_ref, gain_ref, tokens_hbm, *rest):
    count = len(kinds)
    weights_hbm, out_ref = rest[:count], rest[count]
    tokens, normed, weights, token_sems, sems = rest[count + 1 :]
    rows, width = tokens.shape
    chunks, _, span = weights.shape
    parts = token_sems.shape[0]
    part = rows // parts
    token_copies, copies, origin = [], [], []
    for i in range(parts):
        at = pl.ds(i * part, part)
        token_copies.append(pltpu.make_async_copy(tokens_hbm.at[at], tokens.at[at], token_sems.at[i]))
        token_copies[i].start()
    for i in range(count):
        for first in range(0, weights_hbm[i].shape[1], span):
            j = len(copies)
            source = weights_hbm[i].at[:, pl.ds(first, span)]
            copies.append(pltpu.make_async_copy(source, weights.at[j], sems.at[j]))
            origin.append((i, first))

    copies[0].start()
    lanes = positions_ref.shape[1]
    stripes = rows // lanes
    mine = jnp.concatenate(
        [positions_ref[pl.ds(scalar_ref[0] * stripes + i, 1), :] for i in range(stripes)], axis=1
    )
    owner = group_of(mine, rows // 2, devices, members)
    here = lax.broadcasted_iota(jnp.int32, (rows, rows), 0)
    there = lax.broadcasted_iota(jnp.int32, (rows, rows), 1)
    earlier = jnp.where((transposed(owner) == owner) & (here < there), 1, 0)
    rank = owner * (rows * members // devices) + jnp.sum(earlier, axis=0, keepdims=True)
    order = here == rank
    ordered_at = jnp.sum(jnp.where(order, mine, 0), axis=1, keepdims=True)
    angle = ordered_at.astype(jnp.float32) * freq_ref[...]
    lane = lax.broadcasted_iota(jnp.int32, (rows, HEAD_SIZE), 1)
    cosine = jnp.cos(angle)
    sine = jnp.where(lane < HEAD_SIZE // 2, -1.0, 1.0) * jnp.sin(angle)
    order = jnp.where(order, 1.0, 0.0).astype(jnp.bfloat16)
    gain = gain_ref[...].astype(jnp.float32).reshape(1, width)
    step = 32

    for i in range(parts):
        token_copies[i].wait()

        def norm(j, _):
            at = pl.ds(pl.multiple_of(i * part + j * step, step), step)
            floats = tokens[at, :].astype(jnp.float32)
            mean = jnp.sum(floats * floats, axis=1, keepdims=True) * (1.0 / width)
            tokens[at, :] = (floats * lax.rsqrt(mean + EPSILON) * gain).astype(jnp.bfloat16)
            return 0

        lax.fori_loop(0, part // step, norm, 0, unroll=True)
    if chunks > 1:
        copies[1].start()
    for first in range(0, width, 512):
        columns = slice(first, first + 512)
        normed[:, columns] = dot(order, tokens[:, columns]).astype(jnp.bfloat16)
    groups, heads = out_ref.shape[0], out_ref.shape[1]
    offsets = [0]
    for i in range(count):
        offsets.append(offsets[-1] + weights_hbm[i].shape[1] // heads)
    for j in range(chunks):
        i, first = origin[j]
        copies[j].wait()
        if j + 2 < chunks:
            copies[j + 2].start()
        product = dot(normed[...], weights[j])
        per_head = offsets[i + 1] - offsets[i]
        for u in range(0, span, HEAD_SIZE):
            values = product[:, u : u + HEAD_SIZE]
            if kinds[i]:
                values = values * cosine + pltpu.roll(values, HEAD_SIZE // 2, 1) * sine
            head, inside = divmod(first + u, per_head)
            inside += offsets[i]
            out_ref[:, head, :, inside : inside + HEAD_SIZE] = values.astype(jnp.bfloat16).reshape(
                groups, rows // groups, HEAD_SIZE
            )


def project(scalars, positions, freq, gain, tokens, weights, kinds, devices, heads):
    rows, width = tokens.shape
    groups = devices // heads
    columns = sum(w.shape[1] for w in weights)
    span = 512
    parts = 4
    flops = 2 * rows * width * columns
    size = 2 * (width * columns + rows * width + rows * columns)
    return pl.pallas_call(
        functools.partial(project_kernel, kinds, devices, heads),
        out_shape=jax.ShapeDtypeStruct((groups, heads, rows // groups, columns // heads), jnp.bfloat16),
        in_specs=[SCALARS] + [WHOLE] * 3 + [IN_PLACE] * (len(weights) + 1),
        out_specs=WHOLE,
        scratch_shapes=[
            pltpu.VMEM((rows, width), jnp.bfloat16),
            pltpu.VMEM((rows, width), jnp.bfloat16),
            pltpu.VMEM((columns // span, width, span), jnp.bfloat16),
            pltpu.SemaphoreType.DMA((parts,)),
            pltpu.SemaphoreType.DMA((columns // span,)),
        ],
        compiler_params=pltpu.CompilerParams(vmem_limit_bytes=56 * MIB),
        cost_estimate=pl.CostEstimate(flops=flops, bytes_accessed=size, transcendentals=0),
    )(scalars, positions, freq, gain, tokens, *weights)


def place_kernel(arrived_ref, slot_ref, *outs):
    rows = arrived_ref.shape[0]
    first = 0
    for out_ref in outs:
        size = out_ref.shape[0]
        slots = lax.broadcasted_iota(jnp.int32, (size, rows), 0) + first
        chosen = (slots == slot_ref[...]).astype(jnp.bfloat16)
        out_ref[...] = dot(chosen, arrived_ref[...]).astype(jnp.bfloat16)
        first += size


def place(arrived, slot, sizes):
    width = arrived.shape[1]
    return pl.pallas_call(
        place_kernel,
        out_shape=[jax.ShapeDtypeStruct((size, width), jnp.bfloat16) for size in sizes],
        in_specs=[WHOLE, WHOLE],
        out_specs=[WHOLE] * len(sizes),
        compiler_params=pltpu.CompilerParams(vmem_limit_bytes=16 * MIB),
        cost_estimate=pl.CostEstimate(
            flops=2 * sum(sizes) * arrived.shape[0] * width,
            bytes_accessed=4 * arrived.size,
            transcendentals=0,
        ),
    )(arrived, slot)


def attend_kernel(block, scalar_ref, query_ref, slot_ref, ends_ref, *rest):
    pieces, out_ref, held = rest[:6], rest[6], rest[7]
    target, starts, last = scalar_ref[0], (scalar_ref[1], scalar_ref[2]), scalar_ref[3]
    heads = query_ref.shape[1] // HEAD_SIZE
    arrived = query_ref.shape[0]
    run = arrived // 2
    per_run = run // block
    reach = REACH_BLOCKS * block
    keys = reach + block
    slot = slot_ref[...]
    ends = ends_ref[...]
    factor = jnp.float32(np.log2(np.e) / HEAD_SIZE**0.5)
    for half in range(2):
        first = 0
        for piece in pieces[3 * half : 3 * half + 3]:
            values = piece[...]
            if half == 1 and first == 0:
                values = jnp.where(last == 1, pieces[2][...], values)
            held[half, first : first + piece.shape[0], :] = values
            first += piece.shape[0]
    indices = (target, per_run - 1 - target)
    at = [pl.multiple_of(index * block, block) for index in indices]
    iota = lax.broadcasted_iota(jnp.int32, (block, arrived), 0)
    chosen = [(iota + (at[half] + half * run) == slot).astype(jnp.bfloat16) for half in range(2)]
    queries = dot(jnp.concatenate(chosen, axis=0), query_ref[...]).astype(jnp.bfloat16)
    here = [slice(half * block, (half + 1) * block) for half in range(2)]
    scores, weights, totals = [], [], []
    for half in range(2):
        stacked = jnp.concatenate(
            [queries[here[half], h * HEAD_SIZE : (h + 1) * HEAD_SIZE] for h in range(heads)], axis=0
        )
        key = held[half, pl.ds(at[half], keys), :HEAD_SIZE]
        scores.append(
            lax.dot_general(stacked, key, (((1,), (1,)), ((), ())), preferred_element_type=jnp.float32)
        )
    for half in range(2):
        begin = starts[half] + at[half]
        query_at = lax.broadcasted_iota(jnp.int32, (block, 1), 0) + begin
        key_at = lax.broadcasted_iota(jnp.int32, (1, keys), 1) + (begin - reach)
        doc_start = jnp.max(jnp.where(ends <= query_at, ends, 0), axis=1, keepdims=True)
        allowed = (key_at >= doc_start) & (key_at <= query_at)
        masked = jnp.where(allowed[None], scores[half].reshape(heads, block, keys), jnp.float32(-1e30))
        masked = masked.reshape(heads * block, keys)
        top = jnp.max(masked, axis=1, keepdims=True)
        exact = jnp.exp2((masked - top) * factor)
        totals.append(jnp.sum(exact, axis=1, keepdims=True))
        weights.append(exact.astype(jnp.bfloat16))
    for half in range(2):
        value = held[half, pl.ds(at[half], keys), HEAD_SIZE:]
        mixed = (dot(weights[half], value) / totals[half]).astype(jnp.bfloat16)
        for h in range(heads):
            out_ref[here[half], h * HEAD_SIZE : (h + 1) * HEAD_SIZE] = mixed[h * block : (h + 1) * block]


def attend(scalars, query, slot, ends, pieces, block):
    width = query.shape[1]
    held = REACH_BLOCKS * block + query.shape[0] // 2
    heads = width // HEAD_SIZE
    reach = (REACH_BLOCKS + 1) * block
    return pl.pallas_call(
        functools.partial(attend_kernel, block),
        out_shape=jax.ShapeDtypeStruct((2 * block, width), jnp.bfloat16),
        in_specs=[SCALARS] + [WHOLE] * 9,
        out_specs=WHOLE,
        scratch_shapes=[pltpu.VMEM((2, held, 2 * HEAD_SIZE), jnp.bfloat16)],
        compiler_params=pltpu.CompilerParams(vmem_limit_bytes=16 * MIB),
        cost_estimate=pl.CostEstimate(
            flops=2 * 2 * heads * block * reach * HEAD_SIZE * 2 + 4 * block * query.size,
            bytes_accessed=2 * query.size + 8 * held * HEAD_SIZE,
            transcendentals=2 * heads * block * reach,
        ),
    )(scalars, query, slot, ends, *pieces)


def assemble_kernel(source_ref, *rest):
    pieces, out_ref = rest[:-1], rest[-1]
    width = pieces[0].shape[1]
    for i, piece in enumerate(pieces):
        at = pl.multiple_of(source_ref[i] * width, width)
        out_ref[:, pl.ds(at, width)] = piece[...]


def assemble(sources, pieces):
    rows, width = pieces[0].shape
    return pl.pallas_call(
        assemble_kernel,
        out_shape=jax.ShapeDtypeStruct((rows, width * len(pieces)), jnp.bfloat16),
        in_specs=[SCALARS] + [WHOLE] * len(pieces),
        out_specs=WHOLE,
        compiler_params=pltpu.CompilerParams(vmem_limit_bytes=8 * MIB),
        cost_estimate=pl.CostEstimate(
            flops=0, bytes_accessed=4 * rows * width * len(pieces), transcendentals=0
        ),
    )(sources, *pieces)


def shards(tokens, positions, lengths, gain, w_query, w_key, value_weight):
    devices = lax.axis_size("ctx")
    device = lax.axis_index("ctx")
    rows = tokens.shape[0]
    block = rows // 2
    members = w_key.shape[1] // HEAD_SIZE
    groups = devices // members
    group = device // members
    member = device % members
    run = members * block
    group_rows = rows // groups

    half = HEAD_SIZE // 2
    freq = np.float32(ROPE_THETA ** (-(np.arange(HEAD_SIZE) % half * 2.0 / HEAD_SIZE)))
    operands = (device.reshape(1), positions.reshape(-1, 128), jnp.asarray(freq[None, :]), gain, tokens)

    def exchange(ordered):
        width = ordered.shape[3]
        flat = ordered.reshape(devices, group_rows, width)
        flat = lax.all_to_all(flat, "ctx", split_axis=0, concat_axis=0, tiled=True)
        return flat.reshape(devices * group_rows, width)

    kv = project(*operands, (w_key, value_weight), (True, False), devices, members)
    kv = exchange(kv)
    query = project(*operands, (w_query,), (True,), devices, members)

    table = positions.reshape(devices, rows)
    ours = group_of(table, block, devices, members) == group
    first_run = group * run
    second_run = (2 * devices - members) * block - group * run
    slots = jnp.where(table // run == group, table - first_run, table - second_run + run)
    place_in = jnp.cumsum(ours.astype(jnp.int32), axis=1) - 1
    place_in = jnp.where(ours, place_in, -1)
    wanted = jnp.arange(group_rows, dtype=jnp.int32)[None, :, None] == place_in[:, None, :]
    slot = jnp.sum(jnp.where(wanted, slots[:, None, :], 0), axis=2).reshape(1, devices * group_rows)
    ends = jnp.cumsum(lengths, dtype=jnp.int32)[None, :]

    kv, query = lax.optimization_barrier((kv, query))
    query = exchange(query)
    reach = REACH_BLOCKS * block
    sizes = [run - reach, reach] * 2
    early_head, early_tail, late_head, late_tail = place(kv, slot, sizes)
    up = [(i, i + members) for i in range(devices - members)]
    down = [(i + members, i) for i in range(devices - members)]
    early_halo = lax.ppermute(early_tail, "ctx", up)
    late_halo = lax.ppermute(late_tail, "ctx", down)
    pieces = (early_halo, early_head, early_tail, late_halo, late_head, late_tail)

    last = (group == groups - 1).astype(jnp.int32)
    lanes = lax.axis_size("dp")
    odd = lax.axis_index("dp") % 2 == 1
    farthest = members - 1
    between = list(range(1, farthest))
    turns = ([farthest] + between + [0], [farthest] + between[::-1] + [0])
    sources, results = [], []
    for turn in range(members):
        other = member ^ jnp.where(odd, turns[1][turn], turns[0][turn])
        scalars = jnp.stack([other, first_run, second_run, last]).astype(jnp.int32)
        out = attend(scalars, query, slot, ends, pieces, block)
        if turn < farthest:
            route = [
                (i * devices + j, i * devices + j // members * members + (j % members ^ turns[i % 2][turn]))
                for i in range(lanes)
                for j in range(devices)
            ]
            out = lax.ppermute(out, ("dp", "ctx"), route)
        sources.append(other)
        results.append(out)
    return assemble(jnp.stack(sources).astype(jnp.int32), results)


def solution(mesh):
    in_specs = (P(("dp", "ctx"), None), P("dp"), P("dp"), P(), P(), P(), P())
    out_specs = P(("dp", "ctx"), None)
    return jax.shard_map(shards, mesh=mesh, in_specs=in_specs, out_specs=out_specs, check_vma=False)
```

```python
import functools

import jax
import jax.numpy as jnp
import numpy as np
from jax import lax
from jax.experimental import pallas as pl
from jax.experimental.pallas import tpu as pltpu
from jax.sharding import PartitionSpec as P

HEAD_SIZE = 128
REACH_BLOCKS = 3
ROPE_THETA = 500000.0
EPSILON = 1e-05

WHOLE = pl.BlockSpec(memory_space=pltpu.VMEM)
IN_PLACE = pl.BlockSpec(memory_space=pl.ANY)
MIB = 1024 * 1024


def dot(a, b):
    return jnp.dot(a, b, preferred_element_type=jnp.float32)


def transposed(row):
    size = row.shape[1]
    here = lax.broadcasted_iota(jnp.int32, (size, size), 0)
    there = lax.broadcasted_iota(jnp.int32, (size, size), 1)
    return jnp.sum(jnp.where(here == there, row, 0), axis=1, keepdims=True)


def group_of(where_at, block, devices, members):
    block_id = where_at // block
    return jnp.minimum(block_id, 2 * devices - 1 - block_id) // members


def project_kernel(kinds, devices, members, positions_hbm, freq_hbm, gain_hbm, tokens_hbm, *rest):
    count = len(kinds)
    weights_hbm, out_hbm = rest[:count], rest[count]
    positions_ref, freq_ref, gain_ref, tokens, normed, weights, out_ref = rest[count + 1 : count + 8]
    small_sems, token_sems, sems, out_sems = rest[count + 8 :]
    rows, width = tokens.shape
    chunks, _, span = weights.shape
    parts = token_sems.shape[0]
    part = rows // parts
    token_copies, copies, origin = [], [], []
    small_copies = [
        pltpu.make_async_copy(source, target, small_sems.at[i])
        for i, (source, target) in enumerate(
            [(positions_hbm, positions_ref), (freq_hbm, freq_ref), (gain_hbm, gain_ref)]
        )
    ]
    for copy in small_copies:
        copy.start()
    for i in range(parts):
        at = pl.ds(i * part, part)
        token_copies.append(pltpu.make_async_copy(tokens_hbm.at[at], tokens.at[at], token_sems.at[i]))
        token_copies[i].start()
    for i in range(count):
        for first in range(0, weights_hbm[i].shape[1], span):
            j = len(copies)
            source = weights_hbm[i].at[:, pl.ds(first, span)]
            copies.append(pltpu.make_async_copy(source, weights.at[j], sems.at[j]))
            origin.append((i, first))
    copies[0].start()
    for copy in small_copies:
        copy.wait()
    lanes = positions_ref.shape[1]
    stripes = rows // lanes
    mine = jnp.concatenate(
        [positions_ref[pl.ds(lax.axis_index("ctx") * stripes + i, 1), :] for i in range(stripes)], axis=1
    )
    owner = group_of(mine, rows // 2, devices, members)
    here = lax.broadcasted_iota(jnp.int32, (rows, rows), 0)
    there = lax.broadcasted_iota(jnp.int32, (rows, rows), 1)
    earlier = jnp.where((transposed(owner) == owner) & (here < there), 1, 0)
    rank = owner * (rows * members // devices) + jnp.sum(earlier, axis=0, keepdims=True)
    order = here == rank
    ordered_at = jnp.sum(jnp.where(order, mine, 0), axis=1, keepdims=True)
    angle = ordered_at.astype(jnp.float32) * freq_ref[...]
    lane = lax.broadcasted_iota(jnp.int32, (rows, HEAD_SIZE), 1)
    cosine = jnp.cos(angle)
    sine = jnp.where(lane < HEAD_SIZE // 2, -1.0, 1.0) * jnp.sin(angle)
    order = jnp.where(order, 1.0, 0.0).astype(jnp.bfloat16)
    gain = gain_ref[...].astype(jnp.float32).reshape(1, width)
    step = 32

    for i in range(parts):
        token_copies[i].wait()

        def norm(j, _):
            at = pl.ds(pl.multiple_of(i * part + j * step, step), step)
            floats = tokens[at, :].astype(jnp.float32)
            mean = jnp.sum(floats * floats, axis=1, keepdims=True) * (1.0 / width)
            tokens[at, :] = (floats * lax.rsqrt(mean + EPSILON) * gain).astype(jnp.bfloat16)
            return 0

        lax.fori_loop(0, part // step, norm, 0, unroll=True)
    if chunks > 1:
        copies[1].start()
    for first in range(0, width, 512):
        columns = slice(first, first + 512)
        normed[:, columns] = dot(order, tokens[:, columns]).astype(jnp.bfloat16)
    groups, heads = out_ref.shape[:2]
    offsets = [0]
    for i in range(count):
        offsets.append(offsets[-1] + weights_hbm[i].shape[1] // heads)
    written = []
    for j in range(chunks):
        i, first = origin[j]
        copies[j].wait()
        if j + 2 < chunks:
            copies[j + 2].start()
        product = dot(normed[...], weights[j])
        per_head = offsets[i + 1] - offsets[i]
        for u in range(0, span, HEAD_SIZE):
            values = product[:, u : u + HEAD_SIZE]
            if kinds[i]:
                values = values * cosine + pltpu.roll(values, HEAD_SIZE // 2, 1) * sine
            head, inside = divmod(first + u, per_head)
            inside += offsets[i]
            out_ref[:, head, :, inside : inside + HEAD_SIZE] = values.astype(jnp.bfloat16).reshape(
                groups, rows // groups, HEAD_SIZE
            )
        done = (pl.ds(0, groups), pl.ds(first // per_head, max(span // per_head, 1)))
        done += (pl.ds(0, rows // groups), pl.ds(offsets[i] + first % per_head, min(span, per_head)))
        written.append(pltpu.make_async_copy(out_ref.at[done], out_hbm.at[done], out_sems.at[j]))
        written[j].start()
    for copy in written:
        copy.wait()


def project(positions, freq, gain, tokens, weights, kinds, devices, heads):
    rows, width = tokens.shape
    groups = devices // heads
    columns = sum(w.shape[1] for w in weights)
    span = 512
    parts = 4
    flops = 2 * rows * width * columns
    size = 2 * (width * columns + rows * width + rows * columns)
    return pl.pallas_call(
        functools.partial(project_kernel, kinds, devices, heads),
        out_shape=jax.ShapeDtypeStruct((groups, heads, rows // groups, columns // heads), jnp.bfloat16),
        in_specs=[IN_PLACE] * (len(weights) + 4),
        out_specs=IN_PLACE,
        scratch_shapes=[
            pltpu.VMEM(positions.shape, jnp.int32),
            pltpu.VMEM(freq.shape, jnp.float32),
            pltpu.VMEM(gain.shape, jnp.bfloat16),
            pltpu.VMEM((rows, width), jnp.bfloat16),
            pltpu.VMEM((rows, width), jnp.bfloat16),
            pltpu.VMEM((columns // span, width, span), jnp.bfloat16),
            pltpu.VMEM((groups, heads, rows // groups, columns // heads), jnp.bfloat16),
            pltpu.SemaphoreType.DMA((3,)),
            pltpu.SemaphoreType.DMA((parts,)),
            pltpu.SemaphoreType.DMA((columns // span,)),
            pltpu.SemaphoreType.DMA((columns // span,)),
        ],
        compiler_params=pltpu.CompilerParams(vmem_limit_bytes=56 * MIB),
        cost_estimate=pl.CostEstimate(flops=flops, bytes_accessed=size, transcendentals=0),
    )(positions, freq, gain, tokens, *weights)


def place_kernel(arrived_ref, slot_ref, *outs):
    rows = arrived_ref.shape[0]
    first = 0
    for out_ref in outs:
        size = out_ref.shape[0]
        slots = lax.broadcasted_iota(jnp.int32, (size, rows), 0) + first
        chosen = (slots == slot_ref[...]).astype(jnp.bfloat16)
        out_ref[...] = dot(chosen, arrived_ref[...]).astype(jnp.bfloat16)
        first += size


def place(arrived, slot, sizes):
    width = arrived.shape[1]
    return pl.pallas_call(
        place_kernel,
        out_shape=[jax.ShapeDtypeStruct((size, width), jnp.bfloat16) for size in sizes],
        in_specs=[WHOLE, WHOLE],
        out_specs=[WHOLE] * len(sizes),
        compiler_params=pltpu.CompilerParams(vmem_limit_bytes=16 * MIB),
        cost_estimate=pl.CostEstimate(
            flops=2 * sum(sizes) * arrived.shape[0] * width,
            bytes_accessed=4 * arrived.size,
            transcendentals=0,
        ),
    )(arrived, slot)


def taken_at(turn, members):
    distances = distances_at(turn, members)
    odd = lax.axis_index("dp") % 2
    distance = odd * distances[1] + (1 - odd) * distances[0]
    return (lax.axis_index("ctx") % members) ^ distance


def distances_at(turn, members):
    if turn in (0, members - 1):
        return (members - 1 - turn,) * 2
    return (turn, members - 1 - turn)


def attend_kernel(block, turn, members, devices, query_ref, slot_ref, ends_ref, *rest):
    pieces, out_ref, held = rest[:6], rest[6], rest[7]
    target = taken_at(turn, members)
    group = lax.axis_index("ctx") // members
    starts = (group * members * block, (2 * devices - members - group * members) * block)
    last = group == devices // members - 1
    heads = query_ref.shape[1] // HEAD_SIZE
    arrived = query_ref.shape[0]
    run = arrived // 2
    per_run = run // block
    reach = REACH_BLOCKS * block
    keys = reach + block
    slot = slot_ref[...]
    ends = ends_ref[...]
    factor = jnp.float32(np.log2(np.e) / HEAD_SIZE**0.5)
    for half in range(2):
        first = 0
        for piece in pieces[3 * half : 3 * half + 3]:
            values = piece[...]
            if half == 1 and first == 0:
                values = jnp.where(last, pieces[2][...], values)
            held[half, first : first + piece.shape[0], :] = values
            first += piece.shape[0]
    indices = (target, per_run - 1 - target)
    at = [pl.multiple_of(index * block, block) for index in indices]
    iota = lax.broadcasted_iota(jnp.int32, (block, arrived), 0)
    chosen = [(iota + (at[half] + half * run) == slot).astype(jnp.bfloat16) for half in range(2)]
    queries = dot(jnp.concatenate(chosen, axis=0), query_ref[...]).astype(jnp.bfloat16)
    here = [slice(half * block, (half + 1) * block) for half in range(2)]
    scores, weights, totals = [], [], []
    for half in range(2):
        stacked = jnp.concatenate(
            [queries[here[half], h * HEAD_SIZE : (h + 1) * HEAD_SIZE] for h in range(heads)], axis=0
        )
        key = held[half, pl.ds(at[half], keys), :HEAD_SIZE]
        scores.append(
            lax.dot_general(stacked, key, (((1,), (1,)), ((), ())), preferred_element_type=jnp.float32)
        )
    for half in range(2):
        begin = starts[half] + at[half]
        query_at = lax.broadcasted_iota(jnp.int32, (block, 1), 0) + begin
        key_at = lax.broadcasted_iota(jnp.int32, (1, keys), 1) + (begin - reach)
        doc_start = jnp.max(jnp.where(ends <= query_at, ends, 0), axis=1, keepdims=True)
        allowed = (key_at >= doc_start) & (key_at <= query_at)
        masked = jnp.where(allowed[None], scores[half].reshape(heads, block, keys), jnp.float32(-1e30))
        masked = masked.reshape(heads * block, keys)
        top = jnp.max(masked, axis=1, keepdims=True)
        exact = jnp.exp2((masked - top) * factor)
        totals.append(jnp.sum(exact, axis=1, keepdims=True))
        weights.append(exact.astype(jnp.bfloat16))
    for half in range(2):
        value = held[half, pl.ds(at[half], keys), HEAD_SIZE:]
        mixed = (dot(weights[half], value) / totals[half]).astype(jnp.bfloat16)
        for h in range(heads):
            out_ref[here[half], h * HEAD_SIZE : (h + 1) * HEAD_SIZE] = mixed[h * block : (h + 1) * block]


def attend(turn, members, devices, query, slot, ends, pieces, block):
    width = query.shape[1]
    held = REACH_BLOCKS * block + query.shape[0] // 2
    heads = width // HEAD_SIZE
    reach = (REACH_BLOCKS + 1) * block
    return pl.pallas_call(
        functools.partial(attend_kernel, block, turn, members, devices),
        out_shape=jax.ShapeDtypeStruct((2 * block, width), jnp.bfloat16),
        in_specs=[WHOLE] * 9,
        out_specs=WHOLE,
        scratch_shapes=[pltpu.VMEM((2, held, 2 * HEAD_SIZE), jnp.bfloat16)],
        compiler_params=pltpu.CompilerParams(vmem_limit_bytes=16 * MIB),
        cost_estimate=pl.CostEstimate(
            flops=2 * 2 * heads * block * reach * HEAD_SIZE * 2 + 4 * block * query.size,
            bytes_accessed=2 * query.size + 8 * held * HEAD_SIZE,
            transcendentals=2 * heads * block * reach,
        ),
    )(query, slot, ends, *pieces)


def assemble_kernel(*refs):
    pieces, out_ref = refs[:-1], refs[-1]
    width = pieces[0].shape[1]
    for turn, piece in enumerate(pieces):
        at = pl.multiple_of(taken_at(turn, len(pieces)) * width, width)
        out_ref[:, pl.ds(at, width)] = piece[...]


def assemble(pieces):
    rows, width = pieces[0].shape
    return pl.pallas_call(
        assemble_kernel,
        out_shape=jax.ShapeDtypeStruct((rows, width * len(pieces)), jnp.bfloat16),
        in_specs=[WHOLE] * len(pieces),
        out_specs=WHOLE,
        compiler_params=pltpu.CompilerParams(vmem_limit_bytes=8 * MIB),
        cost_estimate=pl.CostEstimate(
            flops=0, bytes_accessed=4 * rows * width * len(pieces), transcendentals=0
        ),
    )(*pieces)


def shards(tokens, positions, lengths, gain, w_query, w_key, value_weight):
    devices = lax.axis_size("ctx")
    device = lax.axis_index("ctx")
    rows = tokens.shape[0]
    block = rows // 2
    members = w_key.shape[1] // HEAD_SIZE
    groups = devices // members
    group = device // members
    run = members * block
    group_rows = rows // groups

    half = HEAD_SIZE // 2
    freq = np.float32(ROPE_THETA ** (-(np.arange(HEAD_SIZE) % half * 2.0 / HEAD_SIZE)))
    operands = (positions.reshape(-1, 128), jnp.asarray(freq[None, :]), gain, tokens)

    def exchange(ordered):
        width = ordered.shape[3]
        flat = ordered.reshape(devices, group_rows, width)
        flat = lax.all_to_all(flat, "ctx", split_axis=0, concat_axis=0, tiled=True)
        return flat.reshape(devices * group_rows, width)

    kv = project(*operands, (w_key, value_weight), (True, False), devices, members)
    kv = exchange(kv)
    query = project(*operands, (w_query,), (True,), devices, members)

    table = positions.reshape(devices, rows)
    ours = group_of(table, block, devices, members) == group
    first_run = group * run
    second_run = (2 * devices - members) * block - group * run
    slots = jnp.where(table // run == group, table - first_run, table - second_run + run)
    place_in = jnp.cumsum(ours.astype(jnp.int32), axis=1) - 1
    place_in = jnp.where(ours, place_in, -1)
    wanted = jnp.arange(group_rows, dtype=jnp.int32)[None, :, None] == place_in[:, None, :]
    slot = jnp.sum(jnp.where(wanted, slots[:, None, :], 0), axis=2).reshape(1, devices * group_rows)
    ends = jnp.cumsum(lengths, dtype=jnp.int32)[None, :]

    kv, query = lax.optimization_barrier((kv, query))
    query = exchange(query)
    reach = REACH_BLOCKS * block
    sizes = [run - reach, reach] * 2
    early_head, early_tail, late_head, late_tail = place(kv, slot, sizes)
    up = [(i, i + members) for i in range(devices - members)]
    down = [(i + members, i) for i in range(devices - members)]
    early_halo = lax.ppermute(early_tail, "ctx", up)
    late_halo = lax.ppermute(late_tail, "ctx", down)
    pieces = (early_halo, early_head, early_tail, late_halo, late_head, late_tail)

    results = []
    for turn in range(members):
        out = attend(turn, members, devices, query, slot, ends, pieces, block)
        if turn < members - 1:
            distances = distances_at(turn, members)
            route = [
                (i * devices + j, i * devices + j // members * members + (j % members ^ distances[i % 2]))
                for i in range(lax.axis_size("dp"))
                for j in range(devices)
            ]
            out = lax.ppermute(out, ("dp", "ctx"), route)
        results.append(out)
    return assemble(results)


def solution(mesh):
    in_specs = (P(("dp", "ctx"), None), P("dp"), P("dp"), P(), P(), P(), P())
    out_specs = P(("dp", "ctx"), None)
    return jax.shard_map(shards, mesh=mesh, in_specs=in_specs, out_specs=out_specs, check_vma=False)
```

```python
import functools

import jax
import jax.numpy as jnp
import numpy as np
from jax import lax
from jax.experimental import pallas as pl
from jax.experimental.pallas import tpu as pltpu
from jax.sharding import PartitionSpec as P

HEAD_SIZE = 128
REACH_BLOCKS = 3
ROPE_THETA = 500000.0
EPSILON = 1e-05

WHOLE = pl.BlockSpec(memory_space=pltpu.VMEM)
IN_PLACE = pl.BlockSpec(memory_space=pl.ANY)
MIB = 1024 * 1024


def dot(a, b):
    return jnp.dot(a, b, preferred_element_type=jnp.float32)


def transposed(row):
    size = row.shape[1]
    here = lax.broadcasted_iota(jnp.int32, (size, size), 0)
    there = lax.broadcasted_iota(jnp.int32, (size, size), 1)
    return jnp.sum(jnp.where(here == there, row, 0), axis=1, keepdims=True)


def group_of(where_at, block, devices, members):
    block_id = where_at // block
    return jnp.minimum(block_id, 2 * devices - 1 - block_id) // members


def project_kernel(kinds, devices, members, apart, positions_hbm, freq_hbm, gain_hbm, tokens_hbm, *rest):
    count = len(kinds)
    weights_hbm, rest = rest[:count], rest[count:]
    outs_hbm, rest = rest[: 1 + apart], (None,) * (count + 1) + rest[1 + apart :]
    positions_ref, freq_ref, gain_ref, tokens, normed, weights, out_ref = rest[count + 1 : count + 8]
    small_sems, token_sems, sems, out_sems = rest[count + 8 :]
    rows, width = tokens.shape
    chunks, _, span = weights.shape
    parts = token_sems.shape[0]
    part = rows // parts
    token_copies, copies, origin = [], [], []
    small_copies = [
        pltpu.make_async_copy(source, target, small_sems.at[i])
        for i, (source, target) in enumerate(
            [(positions_hbm, positions_ref), (freq_hbm, freq_ref), (gain_hbm, gain_ref)]
        )
    ]
    for copy in small_copies:
        copy.start()
    for i in range(parts):
        at = pl.ds(i * part, part)
        token_copies.append(pltpu.make_async_copy(tokens_hbm.at[at], tokens.at[at], token_sems.at[i]))
        token_copies[i].start()
    for i in range(count):
        for first in range(0, weights_hbm[i].shape[1], span):
            j = len(copies)
            source = weights_hbm[i].at[:, pl.ds(first, span)]
            copies.append(pltpu.make_async_copy(source, weights.at[j], sems.at[j]))
            origin.append((i, first))
    copies[0].start()
    for copy in small_copies:
        copy.wait()
    lanes = positions_ref.shape[1]
    stripes = rows // lanes
    mine = jnp.concatenate(
        [positions_ref[pl.ds(lax.axis_index("ctx") * stripes + i, 1), :] for i in range(stripes)], axis=1
    )
    owner = group_of(mine, rows // 2, devices, members)
    here = lax.broadcasted_iota(jnp.int32, (rows, rows), 0)
    there = lax.broadcasted_iota(jnp.int32, (rows, rows), 1)
    earlier = jnp.where((transposed(owner) == owner) & (here < there), 1, 0)
    rank = owner * (rows * members // devices) + jnp.sum(earlier, axis=0, keepdims=True)
    order = here == rank
    ordered_at = jnp.sum(jnp.where(order, mine, 0), axis=1, keepdims=True)
    angle = ordered_at.astype(jnp.float32) * freq_ref[...]
    lane = lax.broadcasted_iota(jnp.int32, (rows, HEAD_SIZE), 1)
    cosine = jnp.cos(angle)
    sine = jnp.where(lane < HEAD_SIZE // 2, -1.0, 1.0) * jnp.sin(angle)
    order = jnp.where(order, 1.0, 0.0).astype(jnp.bfloat16)
    gain = gain_ref[...].astype(jnp.float32).reshape(1, width)
    step = 32

    for i in range(parts):
        token_copies[i].wait()

        def norm(j, _):
            at = pl.ds(pl.multiple_of(i * part + j * step, step), step)
            floats = tokens[at, :].astype(jnp.float32)
            mean = jnp.sum(floats * floats, axis=1, keepdims=True) * (1.0 / width)
            tokens[at, :] = (floats * lax.rsqrt(mean + EPSILON) * gain).astype(jnp.bfloat16)
            return 0

        lax.fori_loop(0, part // step, norm, 0, unroll=True)
    if chunks > 1:
        copies[1].start()
    for first in range(0, width, 512):
        columns = slice(first, first + 512)
        normed[:, columns] = dot(order, tokens[:, columns]).astype(jnp.bfloat16)
    groups, heads = out_ref.shape[:2]
    offsets = [0]
    for i in range(count):
        offsets.append(offsets[-1] + weights_hbm[i].shape[1] // heads)
    written = []
    for j in range(chunks):
        i, first = origin[j]
        copies[j].wait()
        if j + 2 < chunks:
            copies[j + 2].start()
        product = dot(normed[...], weights[j])
        per_head = offsets[i + 1] - offsets[i]
        for u in range(0, span, HEAD_SIZE):
            values = product[:, u : u + HEAD_SIZE]
            if kinds[i]:
                values = values * cosine + pltpu.roll(values, HEAD_SIZE // 2, 1) * sine
            head, inside = divmod(first + u, per_head)
            inside += offsets[i]
            out_ref[:, head, :, inside : inside + HEAD_SIZE] = values.astype(jnp.bfloat16).reshape(
                groups, rows // groups, HEAD_SIZE
            )
        if apart:
            continue
        done = (pl.ds(0, groups), pl.ds(first // per_head, max(span // per_head, 1)))
        done += (pl.ds(0, rows // groups), pl.ds(offsets[i] + first % per_head, min(span, per_head)))
        written.append(pltpu.make_async_copy(out_ref.at[done], outs_hbm[0].at[done], out_sems.at[j]))
        written[j].start()
    if apart:
        me = lax.axis_index("ctx")
        here = pl.ds(me // apart * (groups // 2), groups // 2)
        written.append(pltpu.make_async_copy(out_ref.at[here], outs_hbm[0], out_sems.at[0]))
        for i in range(apart):
            to = me ^ (apart + i)
            source = out_ref.at[to // members, to % members]
            written.append(pltpu.make_async_copy(source, outs_hbm[1 + i], out_sems.at[1 + i]))
        for copy in written:
            copy.start()
    for copy in written:
        copy.wait()


def project(positions, freq, gain, tokens, weights, kinds, devices, heads, apart=0):
    rows, width = tokens.shape
    groups = devices // heads
    columns = sum(w.shape[1] for w in weights)
    span = 512
    parts = 4
    flops = 2 * rows * width * columns
    size = 2 * (width * columns + rows * width + rows * columns)
    out_shape = (groups // 2 if apart else groups, heads, rows // groups, columns // heads)
    out_shapes = [out_shape] + [out_shape[2:]] * apart
    return pl.pallas_call(
        functools.partial(project_kernel, kinds, devices, heads, apart),
        out_shape=[jax.ShapeDtypeStruct(shape, jnp.bfloat16) for shape in out_shapes],
        in_specs=[IN_PLACE] * (len(weights) + 4),
        out_specs=[IN_PLACE] * (1 + apart),
        scratch_shapes=[
            pltpu.VMEM(positions.shape, jnp.int32),
            pltpu.VMEM(freq.shape, jnp.float32),
            pltpu.VMEM(gain.shape, jnp.bfloat16),
            pltpu.VMEM((rows, width), jnp.bfloat16),
            pltpu.VMEM((rows, width), jnp.bfloat16),
            pltpu.VMEM((columns // span, width, span), jnp.bfloat16),
            pltpu.VMEM((groups, heads, rows // groups, columns // heads), jnp.bfloat16),
            pltpu.SemaphoreType.DMA((3,)),
            pltpu.SemaphoreType.DMA((parts,)),
            pltpu.SemaphoreType.DMA((columns // span,)),
            pltpu.SemaphoreType.DMA((max(1 + apart, columns // span),)),
        ],
        compiler_params=pltpu.CompilerParams(vmem_limit_bytes=56 * MIB),
        cost_estimate=pl.CostEstimate(flops=flops, bytes_accessed=size, transcendentals=0),
    )(positions, freq, gain, tokens, *weights)


def place_kernel(arrived_ref, slot_ref, *outs):
    rows = arrived_ref.shape[0]
    first = 0
    for out_ref in outs:
        size = out_ref.shape[0]
        slots = lax.broadcasted_iota(jnp.int32, (size, rows), 0) + first
        chosen = (slots == slot_ref[...]).astype(jnp.bfloat16)
        out_ref[...] = dot(chosen, arrived_ref[...]).astype(jnp.bfloat16)
        first += size


def place(arrived, slot, sizes):
    width = arrived.shape[1]
    return pl.pallas_call(
        place_kernel,
        out_shape=[jax.ShapeDtypeStruct((size, width), jnp.bfloat16) for size in sizes],
        in_specs=[WHOLE, WHOLE],
        out_specs=[WHOLE] * len(sizes),
        compiler_params=pltpu.CompilerParams(vmem_limit_bytes=16 * MIB),
        cost_estimate=pl.CostEstimate(
            flops=2 * sum(sizes) * arrived.shape[0] * width,
            bytes_accessed=4 * arrived.size,
            transcendentals=0,
        ),
    )(arrived, slot)


def taken_at(turn, members):
    distances = distances_at(turn, members)
    odd = lax.axis_index("dp") % 2
    distance = odd * distances[1] + (1 - odd) * distances[0]
    return (lax.axis_index("ctx") % members) ^ distance


def distances_at(turn, members):
    if turn in (0, members - 1):
        return (members - 1 - turn,) * 2
    return (turn, members - 1 - turn)


def attend_kernel(block, turn, members, devices, slot_ref, ends_ref, *rest):
    queries_refs, rest = rest[:-9], rest[-9:]
    pieces, out_ref, held, query_ref = rest[:6], rest[6], rest[7], rest[8]
    first = 0
    for ref in queries_refs:
        query_ref[first : first + ref.shape[0], :] = ref[...]
        first += ref.shape[0]
    target = taken_at(turn, members)
    group = lax.axis_index("ctx") // members
    starts = (group * members * block, (2 * devices - members - group * members) * block)
    last = group == devices // members - 1
    heads = query_ref.shape[1] // HEAD_SIZE
    arrived = query_ref.shape[0]
    run = arrived // 2
    per_run = run // block
    reach = REACH_BLOCKS * block
    keys = reach + block
    slot = slot_ref[...]
    ends = ends_ref[...]
    factor = jnp.float32(np.log2(np.e) / HEAD_SIZE**0.5)
    for half in range(2):
        first = 0
        for piece in pieces[3 * half : 3 * half + 3]:
            values = piece[...]
            if half == 1 and first == 0:
                values = jnp.where(last, pieces[2][...], values)
            held[half, first : first + piece.shape[0], :] = values
            first += piece.shape[0]
    indices = (target, per_run - 1 - target)
    at = [pl.multiple_of(index * block, block) for index in indices]
    iota = lax.broadcasted_iota(jnp.int32, (block, arrived), 0)
    chosen = [(iota + (at[half] + half * run) == slot).astype(jnp.bfloat16) for half in range(2)]
    queries = dot(jnp.concatenate(chosen, axis=0), query_ref[...]).astype(jnp.bfloat16)
    here = [slice(half * block, (half + 1) * block) for half in range(2)]
    scores, weights, totals = [], [], []
    for half in range(2):
        stacked = jnp.concatenate(
            [queries[here[half], h * HEAD_SIZE : (h + 1) * HEAD_SIZE] for h in range(heads)], axis=0
        )
        key = held[half, pl.ds(at[half], keys), :HEAD_SIZE]
        scores.append(
            lax.dot_general(stacked, key, (((1,), (1,)), ((), ())), preferred_element_type=jnp.float32)
        )
    for half in range(2):
        begin = starts[half] + at[half]
        query_at = lax.broadcasted_iota(jnp.int32, (block, 1), 0) + begin
        key_at = lax.broadcasted_iota(jnp.int32, (1, keys), 1) + (begin - reach)
        doc_start = jnp.max(jnp.where(ends <= query_at, ends, 0), axis=1, keepdims=True)
        allowed = (key_at >= doc_start) & (key_at <= query_at)
        masked = jnp.where(allowed[None], scores[half].reshape(heads, block, keys), jnp.float32(-1e30))
        masked = masked.reshape(heads * block, keys)
        top = jnp.max(masked, axis=1, keepdims=True)
        exact = jnp.exp2((masked - top) * factor)
        totals.append(jnp.sum(exact, axis=1, keepdims=True))
        weights.append(exact.astype(jnp.bfloat16))
    for half in range(2):
        value = held[half, pl.ds(at[half], keys), HEAD_SIZE:]
        mixed = (dot(weights[half], value) / totals[half]).astype(jnp.bfloat16)
        for h in range(heads):
            out_ref[here[half], h * HEAD_SIZE : (h + 1) * HEAD_SIZE] = mixed[h * block : (h + 1) * block]


def attend(turn, members, devices, queries, slot, ends, pieces, block):
    rows, width = slot.shape[1], queries[0].shape[1]
    held = REACH_BLOCKS * block + rows // 2
    heads = width // HEAD_SIZE
    reach = (REACH_BLOCKS + 1) * block
    return pl.pallas_call(
        functools.partial(attend_kernel, block, turn, members, devices),
        out_shape=jax.ShapeDtypeStruct((2 * block, width), jnp.bfloat16),
        in_specs=[WHOLE] * (8 + len(queries)),
        out_specs=WHOLE,
        scratch_shapes=[
            pltpu.VMEM((2, held, 2 * HEAD_SIZE), jnp.bfloat16),
            pltpu.VMEM((rows, width), jnp.bfloat16),
        ],
        compiler_params=pltpu.CompilerParams(vmem_limit_bytes=16 * MIB),
        cost_estimate=pl.CostEstimate(
            flops=2 * 2 * heads * block * reach * HEAD_SIZE * 2 + 4 * block * rows * width,
            bytes_accessed=2 * rows * width + 8 * held * HEAD_SIZE,
            transcendentals=2 * heads * block * reach,
        ),
    )(slot, ends, *queries, *pieces)


def assemble_kernel(*refs):
    pieces, out_ref = refs[:-1], refs[-1]
    width = pieces[0].shape[1]
    for turn, piece in enumerate(pieces):
        at = pl.multiple_of(taken_at(turn, len(pieces)) * width, width)
        out_ref[:, pl.ds(at, width)] = piece[...]


def assemble(pieces):
    rows, width = pieces[0].shape
    return pl.pallas_call(
        assemble_kernel,
        out_shape=jax.ShapeDtypeStruct((rows, width * len(pieces)), jnp.bfloat16),
        in_specs=[WHOLE] * len(pieces),
        out_specs=WHOLE,
        compiler_params=pltpu.CompilerParams(vmem_limit_bytes=8 * MIB),
        cost_estimate=pl.CostEstimate(
            flops=0, bytes_accessed=4 * rows * width * len(pieces), transcendentals=0
        ),
    )(*pieces)


def shards(tokens, positions, lengths, gain, w_query, w_key, value_weight):
    devices = lax.axis_size("ctx")
    device = lax.axis_index("ctx")
    rows = tokens.shape[0]
    block = rows // 2
    members = w_key.shape[1] // HEAD_SIZE
    groups = devices // members
    group = device // members
    run = members * block
    group_rows = rows // groups

    half = HEAD_SIZE // 2
    freq = np.float32(ROPE_THETA ** (-(np.arange(HEAD_SIZE) % half * 2.0 / HEAD_SIZE)))
    operands = (positions.reshape(-1, 128), jnp.asarray(freq[None, :]), gain, tokens)

    half_devices = devices // 2
    halves = [list(range(i, i + half_devices)) for i in (0, half_devices)]

    def exchange(ordered, among):
        width = ordered.shape[3]
        flat = ordered.reshape(-1, group_rows, width)
        flat = lax.all_to_all(flat, "ctx", split_axis=0, concat_axis=0, tiled=True, axis_index_groups=among)
        return flat.reshape(-1, width)

    (kv,) = project(*operands, (w_key, value_weight), (True, False), devices, members)
    kv = exchange(kv, None)
    near, *far = project(*operands, (w_query,), (True,), devices, members, half_devices)
    queries = []
    for i, piece in enumerate(far):
        distance = half_devices + i
        queries.append(lax.ppermute(piece, "ctx", [(j, j ^ distance) for j in range(devices)]))

    table = positions.reshape(devices, rows)
    ours = group_of(table, block, devices, members) == group
    first_run = group * run
    second_run = (2 * devices - members) * block - group * run
    slots = jnp.where(table // run == group, table - first_run, table - second_run + run)
    place_in = jnp.cumsum(ours.astype(jnp.int32), axis=1) - 1
    place_in = jnp.where(ours, place_in, -1)
    wanted = jnp.arange(group_rows, dtype=jnp.int32)[None, :, None] == place_in[:, None, :]
    slot = jnp.sum(jnp.where(wanted, slots[:, None, :], 0), axis=2)
    index = jnp.arange(half_devices, dtype=jnp.int32)
    sources = [device // half_devices * half_devices + index, device ^ (half_devices + index)]
    query_slot = slot[jnp.concatenate(sources)].reshape(1, devices * group_rows)
    slot = slot.reshape(1, devices * group_rows)
    ends = jnp.cumsum(lengths, dtype=jnp.int32)[None, :]

    kv, near = lax.optimization_barrier((kv, near))
    queries.insert(0, exchange(near, halves))
    reach = REACH_BLOCKS * block
    sizes = [run - reach, reach] * 2
    early_head, early_tail, late_head, late_tail = place(kv, slot, sizes)
    up = [(i, i + members) for i in range(devices - members)]
    down = [(i + members, i) for i in range(devices - members)]
    early_halo = lax.ppermute(early_tail, "ctx", up)
    late_halo = lax.ppermute(late_tail, "ctx", down)
    pieces = (early_halo, early_head, early_tail, late_halo, late_head, late_tail)

    results = []
    for turn in range(members):
        out = attend(turn, members, devices, queries, query_slot, ends, pieces, block)
        if turn < members - 1:
            distances = distances_at(turn, members)
            route = [
                (i * devices + j, i * devices + j // members * members + (j % members ^ distances[i % 2]))
                for i in range(lax.axis_size("dp"))
                for j in range(devices)
            ]
            out = lax.ppermute(out, ("dp", "ctx"), route)
        results.append(out)
    return assemble(results)


def solution(mesh):
    in_specs = (P(("dp", "ctx"), None), P("dp"), P("dp"), P(), P(), P(), P())
    out_specs = P(("dp", "ctx"), None)
    return jax.shard_map(shards, mesh=mesh, in_specs=in_specs, out_specs=out_specs, check_vma=False)
```

```python
import functools

import jax
import jax.numpy as jnp
import numpy as np
from jax import lax
from jax.experimental import pallas as pl
from jax.experimental.pallas import tpu as pltpu
from jax.sharding import PartitionSpec as P

HEAD_SIZE = 128
REACH_BLOCKS = 3
ROPE_THETA = 500000.0
EPSILON = 1e-05

WHOLE = pl.BlockSpec(memory_space=pltpu.VMEM)
IN_PLACE = pl.BlockSpec(memory_space=pl.ANY)
MIB = 1024 * 1024


def dot(a, b):
    return jnp.dot(a, b, preferred_element_type=jnp.float32)


def transposed(row):
    size = row.shape[1]
    here = lax.broadcasted_iota(jnp.int32, (size, size), 0)
    there = lax.broadcasted_iota(jnp.int32, (size, size), 1)
    return jnp.sum(jnp.where(here == there, row, 0), axis=1, keepdims=True)


def group_of(where_at, block, devices, members):
    block_id = where_at // block
    return jnp.minimum(block_id, 2 * devices - 1 - block_id) // members


def project_kernel(kinds, devices, members, apart, positions_hbm, freq_hbm, gain_hbm, tokens_hbm, *rest):
    count = len(kinds)
    weights_hbm, rest = rest[:count], rest[count:]
    outputs = 1 + len(apart)
    outs_hbm, rest = rest[:outputs], (None,) * (count + 1) + rest[outputs:]
    positions_ref, freq_ref, gain_ref, tokens, normed, weights, out_ref = rest[count + 1 : count + 8]
    small_sems, token_sems, sems, out_sems = rest[count + 8 :]
    rows, width = tokens.shape
    chunks, _, span = weights.shape
    parts = token_sems.shape[0]
    part = rows // parts
    token_copies, copies, origin = [], [], []
    small_copies = [
        pltpu.make_async_copy(source, target, small_sems.at[i])
        for i, (source, target) in enumerate(
            [(positions_hbm, positions_ref), (freq_hbm, freq_ref), (gain_hbm, gain_ref)]
        )
    ]
    for copy in small_copies:
        copy.start()
    for i in range(parts):
        at = pl.ds(i * part, part)
        token_copies.append(pltpu.make_async_copy(tokens_hbm.at[at], tokens.at[at], token_sems.at[i]))
        token_copies[i].start()
    for i in range(count):
        for first in range(0, weights_hbm[i].shape[1], span):
            j = len(copies)
            source = weights_hbm[i].at[:, pl.ds(first, span)]
            copies.append(pltpu.make_async_copy(source, weights.at[j], sems.at[j]))
            origin.append((i, first))
    copies[0].start()
    for copy in small_copies:
        copy.wait()
    lanes = positions_ref.shape[1]
    stripes = rows // lanes
    mine = jnp.concatenate(
        [positions_ref[pl.ds(lax.axis_index("ctx") * stripes + i, 1), :] for i in range(stripes)], axis=1
    )
    owner = group_of(mine, rows // 2, devices, members)
    here = lax.broadcasted_iota(jnp.int32, (rows, rows), 0)
    there = lax.broadcasted_iota(jnp.int32, (rows, rows), 1)
    earlier = jnp.where((transposed(owner) == owner) & (here < there), 1, 0)
    rank = owner * (rows * members // devices) + jnp.sum(earlier, axis=0, keepdims=True)
    order = here == rank
    ordered_at = jnp.sum(jnp.where(order, mine, 0), axis=1, keepdims=True)
    angle = ordered_at.astype(jnp.float32) * freq_ref[...]
    lane = lax.broadcasted_iota(jnp.int32, (rows, HEAD_SIZE), 1)
    cosine = jnp.cos(angle)
    sine = jnp.where(lane < HEAD_SIZE // 2, -1.0, 1.0) * jnp.sin(angle)
    order = jnp.where(order, 1.0, 0.0).astype(jnp.bfloat16)
    gain = gain_ref[...].astype(jnp.float32).reshape(1, width)
    step = 32

    for i in range(parts):
        token_copies[i].wait()

        def norm(j, _):
            at = pl.ds(pl.multiple_of(i * part + j * step, step), step)
            floats = tokens[at, :].astype(jnp.float32)
            mean = jnp.sum(floats * floats, axis=1, keepdims=True) * (1.0 / width)
            tokens[at, :] = (floats * lax.rsqrt(mean + EPSILON) * gain).astype(jnp.bfloat16)
            return 0

        lax.fori_loop(0, part // step, norm, 0, unroll=True)
    if chunks > 1:
        copies[1].start()
    for first in range(0, width, 512):
        columns = slice(first, first + 512)
        normed[:, columns] = dot(order, tokens[:, columns]).astype(jnp.bfloat16)
    groups, heads = out_ref.shape[:2]
    offsets = [0]
    for i in range(count):
        offsets.append(offsets[-1] + weights_hbm[i].shape[1] // heads)
    written = []
    for j in range(chunks):
        i, first = origin[j]
        copies[j].wait()
        if j + 2 < chunks:
            copies[j + 2].start()
        product = dot(normed[...], weights[j])
        per_head = offsets[i + 1] - offsets[i]
        for u in range(0, span, HEAD_SIZE):
            values = product[:, u : u + HEAD_SIZE]
            if kinds[i]:
                values = values * cosine + pltpu.roll(values, HEAD_SIZE // 2, 1) * sine
            head, inside = divmod(first + u, per_head)
            inside += offsets[i]
            out_ref[:, head, :, inside : inside + HEAD_SIZE] = values.astype(jnp.bfloat16).reshape(
                groups, rows // groups, HEAD_SIZE
            )
        if apart:
            continue
        done = (pl.ds(0, groups), pl.ds(first // per_head, max(span // per_head, 1)))
        done += (pl.ds(0, rows // groups), pl.ds(offsets[i] + first % per_head, min(span, per_head)))
        written.append(pltpu.make_async_copy(out_ref.at[done], outs_hbm[0].at[done], out_sems.at[j]))
        written[j].start()
    if apart:
        me = lax.axis_index("ctx")
        quarter = groups // 4
        same = me // members // quarter % 2
        for upper in range(2):
            source = out_ref.at[pl.ds((2 * upper + same) * quarter, quarter)]
            target = outs_hbm[0].at[pl.ds(upper * quarter, quarter)]
            written.append(pltpu.make_async_copy(source, target, out_sems.at[upper]))
        for i, distance in enumerate(apart):
            to = me ^ distance
            source = out_ref.at[to // members, to % members]
            written.append(pltpu.make_async_copy(source, outs_hbm[1 + i], out_sems.at[2 + i]))
        for copy in written:
            copy.start()
    for copy in written:
        copy.wait()


def project(positions, freq, gain, tokens, weights, kinds, devices, heads, apart=()):
    rows, width = tokens.shape
    groups = devices // heads
    columns = sum(w.shape[1] for w in weights)
    span = 512
    parts = 4
    flops = 2 * rows * width * columns
    size = 2 * (width * columns + rows * width + rows * columns)
    out_shape = (groups // 2 if apart else groups, heads, rows // groups, columns // heads)
    out_shapes = [out_shape] + [out_shape[2:]] * len(apart)
    return pl.pallas_call(
        functools.partial(project_kernel, kinds, devices, heads, apart),
        out_shape=[jax.ShapeDtypeStruct(shape, jnp.bfloat16) for shape in out_shapes],
        in_specs=[IN_PLACE] * (len(weights) + 4),
        out_specs=[IN_PLACE] * (1 + len(apart)),
        scratch_shapes=[
            pltpu.VMEM(positions.shape, jnp.int32),
            pltpu.VMEM(freq.shape, jnp.float32),
            pltpu.VMEM(gain.shape, jnp.bfloat16),
            pltpu.VMEM((rows, width), jnp.bfloat16),
            pltpu.VMEM((rows, width), jnp.bfloat16),
            pltpu.VMEM((columns // span, width, span), jnp.bfloat16),
            pltpu.VMEM((groups, heads, rows // groups, columns // heads), jnp.bfloat16),
            pltpu.SemaphoreType.DMA((3,)),
            pltpu.SemaphoreType.DMA((parts,)),
            pltpu.SemaphoreType.DMA((columns // span,)),
            pltpu.SemaphoreType.DMA((max(2 + len(apart), columns // span),)),
        ],
        compiler_params=pltpu.CompilerParams(vmem_limit_bytes=56 * MIB),
        cost_estimate=pl.CostEstimate(flops=flops, bytes_accessed=size, transcendentals=0),
    )(positions, freq, gain, tokens, *weights)


def place_kernel(arrived_ref, slot_ref, *outs):
    rows = arrived_ref.shape[0]
    first = 0
    for out_ref in outs:
        size = out_ref.shape[0]
        slots = lax.broadcasted_iota(jnp.int32, (size, rows), 0) + first
        chosen = (slots == slot_ref[...]).astype(jnp.bfloat16)
        out_ref[...] = dot(chosen, arrived_ref[...]).astype(jnp.bfloat16)
        first += size


def place(arrived, slot, sizes):
    width = arrived.shape[1]
    return pl.pallas_call(
        place_kernel,
        out_shape=[jax.ShapeDtypeStruct((size, width), jnp.bfloat16) for size in sizes],
        in_specs=[WHOLE, WHOLE],
        out_specs=[WHOLE] * len(sizes),
        compiler_params=pltpu.CompilerParams(vmem_limit_bytes=16 * MIB),
        cost_estimate=pl.CostEstimate(
            flops=2 * sum(sizes) * arrived.shape[0] * width,
            bytes_accessed=4 * arrived.size,
            transcendentals=0,
        ),
    )(arrived, slot)


def taken_at(turn, members):
    distances = distances_at(turn, members)
    odd = lax.axis_index("dp") % 2
    distance = odd * distances[1] + (1 - odd) * distances[0]
    return (lax.axis_index("ctx") % members) ^ distance


def distances_at(turn, members):
    if turn in (0, members - 1):
        return (members - 1 - turn,) * 2
    return (turn, members - 1 - turn)


def attend_kernel(block, turn, members, devices, slot_ref, ends_ref, *rest):
    queries_refs, rest = rest[:-9], rest[-9:]
    pieces, out_ref, held, query_ref = rest[:6], rest[6], rest[7], rest[8]
    first = 0
    for ref in queries_refs:
        query_ref[first : first + ref.shape[0], :] = ref[...]
        first += ref.shape[0]
    target = taken_at(turn, members)
    group = lax.axis_index("ctx") // members
    starts = (group * members * block, (2 * devices - members - group * members) * block)
    last = group == devices // members - 1
    heads = query_ref.shape[1] // HEAD_SIZE
    arrived = query_ref.shape[0]
    run = arrived // 2
    per_run = run // block
    reach = REACH_BLOCKS * block
    keys = reach + block
    slot = slot_ref[...]
    ends = ends_ref[...]
    factor = jnp.float32(np.log2(np.e) / HEAD_SIZE**0.5)
    for half in range(2):
        first = 0
        for piece in pieces[3 * half : 3 * half + 3]:
            values = piece[...]
            if half == 1 and first == 0:
                values = jnp.where(last, pieces[2][...], values)
            held[half, first : first + piece.shape[0], :] = values
            first += piece.shape[0]
    indices = (target, per_run - 1 - target)
    at = [pl.multiple_of(index * block, block) for index in indices]
    iota = lax.broadcasted_iota(jnp.int32, (block, arrived), 0)
    chosen = [(iota + (at[half] + half * run) == slot).astype(jnp.bfloat16) for half in range(2)]
    queries = dot(jnp.concatenate(chosen, axis=0), query_ref[...]).astype(jnp.bfloat16)
    here = [slice(half * block, (half + 1) * block) for half in range(2)]
    scores, weights, totals = [], [], []
    for half in range(2):
        stacked = jnp.concatenate(
            [queries[here[half], h * HEAD_SIZE : (h + 1) * HEAD_SIZE] for h in range(heads)], axis=0
        )
        key = held[half, pl.ds(at[half], keys), :HEAD_SIZE]
        scores.append(
            lax.dot_general(stacked, key, (((1,), (1,)), ((), ())), preferred_element_type=jnp.float32)
        )
    for half in range(2):
        begin = starts[half] + at[half]
        query_at = lax.broadcasted_iota(jnp.int32, (block, 1), 0) + begin
        key_at = lax.broadcasted_iota(jnp.int32, (1, keys), 1) + (begin - reach)
        doc_start = jnp.max(jnp.where(ends <= query_at, ends, 0), axis=1, keepdims=True)
        allowed = (key_at >= doc_start) & (key_at <= query_at)
        masked = jnp.where(allowed[None], scores[half].reshape(heads, block, keys), jnp.float32(-1e30))
        masked = masked.reshape(heads * block, keys)
        top = jnp.max(masked, axis=1, keepdims=True)
        exact = jnp.exp2((masked - top) * factor)
        totals.append(jnp.sum(exact, axis=1, keepdims=True))
        weights.append(exact.astype(jnp.bfloat16))
    for half in range(2):
        value = held[half, pl.ds(at[half], keys), HEAD_SIZE:]
        mixed = (dot(weights[half], value) / totals[half]).astype(jnp.bfloat16)
        for h in range(heads):
            out_ref[here[half], h * HEAD_SIZE : (h + 1) * HEAD_SIZE] = mixed[h * block : (h + 1) * block]


def attend(turn, members, devices, queries, slot, ends, pieces, block):
    rows, width = slot.shape[1], queries[0].shape[1]
    held = REACH_BLOCKS * block + rows // 2
    heads = width // HEAD_SIZE
    reach = (REACH_BLOCKS + 1) * block
    return pl.pallas_call(
        functools.partial(attend_kernel, block, turn, members, devices),
        out_shape=jax.ShapeDtypeStruct((2 * block, width), jnp.bfloat16),
        in_specs=[WHOLE] * (8 + len(queries)),
        out_specs=WHOLE,
        scratch_shapes=[
            pltpu.VMEM((2, held, 2 * HEAD_SIZE), jnp.bfloat16),
            pltpu.VMEM((rows, width), jnp.bfloat16),
        ],
        compiler_params=pltpu.CompilerParams(vmem_limit_bytes=16 * MIB),
        cost_estimate=pl.CostEstimate(
            flops=2 * 2 * heads * block * reach * HEAD_SIZE * 2 + 4 * block * rows * width,
            bytes_accessed=2 * rows * width + 8 * held * HEAD_SIZE,
            transcendentals=2 * heads * block * reach,
        ),
    )(slot, ends, *queries, *pieces)


def assemble_kernel(*refs):
    pieces, out_ref = refs[:-1], refs[-1]
    width = pieces[0].shape[1]
    for turn, piece in enumerate(pieces):
        at = pl.multiple_of(taken_at(turn, len(pieces)) * width, width)
        out_ref[:, pl.ds(at, width)] = piece[...]


def assemble(pieces):
    rows, width = pieces[0].shape
    return pl.pallas_call(
        assemble_kernel,
        out_shape=jax.ShapeDtypeStruct((rows, width * len(pieces)), jnp.bfloat16),
        in_specs=[WHOLE] * len(pieces),
        out_specs=WHOLE,
        compiler_params=pltpu.CompilerParams(vmem_limit_bytes=8 * MIB),
        cost_estimate=pl.CostEstimate(
            flops=0, bytes_accessed=4 * rows * width * len(pieces), transcendentals=0
        ),
    )(*pieces)


def shards(tokens, positions, lengths, gain, w_query, w_key, value_weight):
    devices = lax.axis_size("ctx")
    device = lax.axis_index("ctx")
    rows = tokens.shape[0]
    block = rows // 2
    members = w_key.shape[1] // HEAD_SIZE
    groups = devices // members
    group = device // members
    run = members * block
    group_rows = rows // groups

    half = HEAD_SIZE // 2
    freq = np.float32(ROPE_THETA ** (-(np.arange(HEAD_SIZE) % half * 2.0 / HEAD_SIZE)))
    operands = (positions.reshape(-1, 128), jnp.asarray(freq[None, :]), gain, tokens)

    bit = devices // 4
    alike = [[j for j in range(devices) if j // bit % 2 == value] for value in range(2)]
    apart = list(range(3 * bit, 4 * bit)) + list(range(bit, 2 * bit))

    def exchange(ordered, among):
        width = ordered.shape[3]
        flat = ordered.reshape(-1, group_rows, width)
        flat = lax.all_to_all(flat, "ctx", split_axis=0, concat_axis=0, tiled=True, axis_index_groups=among)
        return flat.reshape(-1, width)

    (kv,) = project(*operands, (w_key, value_weight), (True, False), devices, members)
    kv = exchange(kv, None)
    near, *far = project(*operands, (w_query,), (True,), devices, members, apart)
    queries = []
    for distance, piece in zip(apart, far):
        queries.append(lax.ppermute(piece, "ctx", [(j, j ^ distance) for j in range(devices)]))

    table = positions.reshape(devices, rows)
    ours = group_of(table, block, devices, members) == group
    first_run = group * run
    second_run = (2 * devices - members) * block - group * run
    slots = jnp.where(table // run == group, table - first_run, table - second_run + run)
    place_in = jnp.cumsum(ours.astype(jnp.int32), axis=1) - 1
    place_in = jnp.where(ours, place_in, -1)
    wanted = jnp.arange(group_rows, dtype=jnp.int32)[None, :, None] == place_in[:, None, :]
    slot = jnp.sum(jnp.where(wanted, slots[:, None, :], 0), axis=2)
    index = jnp.arange(2 * bit, dtype=jnp.int32)
    sources = [index // bit * 2 * bit + device // bit % 2 * bit + index % bit, device ^ jnp.asarray(np.int32(apart))]
    query_slot = slot[jnp.concatenate(sources)].reshape(1, devices * group_rows)
    slot = slot.reshape(1, devices * group_rows)
    ends = jnp.cumsum(lengths, dtype=jnp.int32)[None, :]

    kv, near = lax.optimization_barrier((kv, near))
    queries.insert(0, exchange(near, alike))
    reach = REACH_BLOCKS * block
    sizes = [run - reach, reach] * 2
    early_head, early_tail, late_head, late_tail = place(kv, slot, sizes)
    up = [(i, i + members) for i in range(devices - members)]
    down = [(i + members, i) for i in range(devices - members)]
    early_halo = lax.ppermute(early_tail, "ctx", up)
    late_halo = lax.ppermute(late_tail, "ctx", down)
    pieces = (early_halo, early_head, early_tail, late_halo, late_head, late_tail)

    results = []
    for turn in range(members):
        out = attend(turn, members, devices, queries, query_slot, ends, pieces, block)
        if turn < members - 1:
            distances = distances_at(turn, members)
            route = [
                (i * devices + j, i * devices + j // members * members + (j % members ^ distances[i % 2]))
                for i in range(lax.axis_size("dp"))
                for j in range(devices)
            ]
            out = lax.ppermute(out, ("dp", "ctx"), route)
        results.append(out)
    return assemble(results)


def solution(mesh):
    in_specs = (P(("dp", "ctx"), None), P("dp"), P("dp"), P(), P(), P(), P())
    out_specs = P(("dp", "ctx"), None)
    return jax.shard_map(shards, mesh=mesh, in_specs=in_specs, out_specs=out_specs, check_vma=False)
```

```python
import functools

import jax
import jax.numpy as jnp
import numpy as np
from jax import lax
from jax.experimental import pallas as pl
from jax.experimental.pallas import tpu as pltpu
from jax.sharding import PartitionSpec as P

HEAD_SIZE = 128
REACH_BLOCKS = 3
ROPE_THETA = 500000.0
EPSILON = 1e-05

WHOLE = pl.BlockSpec(memory_space=pltpu.VMEM)
IN_PLACE = pl.BlockSpec(memory_space=pl.ANY)
MIB = 1024 * 1024


def dot(a, b):
    return jnp.dot(a, b, preferred_element_type=jnp.float32)


def transposed(row):
    size = row.shape[1]
    here = lax.broadcasted_iota(jnp.int32, (size, size), 0)
    there = lax.broadcasted_iota(jnp.int32, (size, size), 1)
    return jnp.sum(jnp.where(here == there, row, 0), axis=1, keepdims=True)


def group_of(where_at, block, devices, members):
    block_id = where_at // block
    return jnp.minimum(block_id, 2 * devices - 1 - block_id) // members


def project_kernel(kinds, devices, members, apart, positions_hbm, freq_hbm, gain_hbm, tokens_hbm, *rest):
    count = len(kinds)
    weights_hbm, rest = rest[:count], rest[count:]
    outs_hbm, rest = rest[: 1 + apart], (None,) * (count + 1) + rest[1 + apart :]
    positions_ref, freq_ref, gain_ref, tokens, normed, weights, out_ref = rest[count + 1 : count + 8]
    small_sems, token_sems, sems, out_sems = rest[count + 8 :]
    rows, width = tokens.shape
    chunks, _, span = weights.shape
    parts = token_sems.shape[0]
    part = rows // parts
    token_copies, copies, origin = [], [], []
    small_copies = [
        pltpu.make_async_copy(source, target, small_sems.at[i])
        for i, (source, target) in enumerate(
            [(positions_hbm, positions_ref), (freq_hbm, freq_ref), (gain_hbm, gain_ref)]
        )
    ]
    for copy in small_copies:
        copy.start()
    for i in range(parts):
        at = pl.ds(i * part, part)
        token_copies.append(pltpu.make_async_copy(tokens_hbm.at[at], tokens.at[at], token_sems.at[i]))
        token_copies[i].start()
    for i in range(count):
        for first in range(0, weights_hbm[i].shape[1], span):
            j = len(copies)
            source = weights_hbm[i].at[:, pl.ds(first, span)]
            copies.append(pltpu.make_async_copy(source, weights.at[j], sems.at[j]))
            origin.append((i, first))
    copies[0].start()
    for copy in small_copies:
        copy.wait()
    lanes = positions_ref.shape[1]
    stripes = rows // lanes
    mine = jnp.concatenate(
        [positions_ref[pl.ds(lax.axis_index("ctx") * stripes + i, 1), :] for i in range(stripes)], axis=1
    )
    owner = group_of(mine, rows // 2, devices, members)
    here = lax.broadcasted_iota(jnp.int32, (rows, rows), 0)
    there = lax.broadcasted_iota(jnp.int32, (rows, rows), 1)
    earlier = jnp.where((transposed(owner) == owner) & (here < there), 1, 0)
    rank = owner * (rows * members // devices) + jnp.sum(earlier, axis=0, keepdims=True)
    order = here == rank
    ordered_at = jnp.sum(jnp.where(order, mine, 0), axis=1, keepdims=True)
    angle = ordered_at.astype(jnp.float32) * freq_ref[...]
    lane = lax.broadcasted_iota(jnp.int32, (rows, HEAD_SIZE), 1)
    cosine = jnp.cos(angle)
    sine = jnp.where(lane < HEAD_SIZE // 2, -1.0, 1.0) * jnp.sin(angle)
    order = jnp.where(order, 1.0, 0.0).astype(jnp.bfloat16)
    gain = gain_ref[...].astype(jnp.float32).reshape(1, width)
    step = 32

    for i in range(parts):
        token_copies[i].wait()

        def norm(j, _):
            at = pl.ds(pl.multiple_of(i * part + j * step, step), step)
            floats = tokens[at, :].astype(jnp.float32)
            mean = jnp.sum(floats * floats, axis=1, keepdims=True) * (1.0 / width)
            tokens[at, :] = (floats * lax.rsqrt(mean + EPSILON) * gain).astype(jnp.bfloat16)
            return 0

        lax.fori_loop(0, part // step, norm, 0, unroll=True)
    if chunks > 1:
        copies[1].start()
    for first in range(0, width, 512):
        columns = slice(first, first + 512)
        normed[:, columns] = dot(order, tokens[:, columns]).astype(jnp.bfloat16)
    groups, heads = out_ref.shape[:2]
    offsets = [0]
    for i in range(count):
        offsets.append(offsets[-1] + weights_hbm[i].shape[1] // heads)
    written = []
    for j in range(chunks):
        i, first = origin[j]
        copies[j].wait()
        if j + 2 < chunks:
            copies[j + 2].start()
        product = dot(normed[...], weights[j])
        per_head = offsets[i + 1] - offsets[i]
        for u in range(0, span, HEAD_SIZE):
            values = product[:, u : u + HEAD_SIZE]
            if kinds[i]:
                values = values * cosine + pltpu.roll(values, HEAD_SIZE // 2, 1) * sine
            head, inside = divmod(first + u, per_head)
            inside += offsets[i]
            out_ref[:, head, :, inside : inside + HEAD_SIZE] = values.astype(jnp.bfloat16).reshape(
                groups, rows // groups, HEAD_SIZE
            )
        if apart:
            continue
        done = (pl.ds(0, groups), pl.ds(first // per_head, max(span // per_head, 1)))
        done += (pl.ds(0, rows // groups), pl.ds(offsets[i] + first % per_head, min(span, per_head)))
        written.append(pltpu.make_async_copy(out_ref.at[done], outs_hbm[0].at[done], out_sems.at[j]))
        written[j].start()
    if apart:
        me = lax.axis_index("ctx")
        here = pl.ds(me // apart * (groups // 2), groups // 2)
        written.append(pltpu.make_async_copy(out_ref.at[here], outs_hbm[0], out_sems.at[0]))
        for i in range(apart):
            to = me ^ (apart + i)
            source = out_ref.at[to // members, to % members]
            written.append(pltpu.make_async_copy(source, outs_hbm[1 + i], out_sems.at[1 + i]))
        for copy in written:
            copy.start()
    for copy in written:
        copy.wait()


def project(positions, freq, gain, tokens, weights, kinds, devices, heads, apart=0):
    rows, width = tokens.shape
    groups = devices // heads
    columns = sum(w.shape[1] for w in weights)
    span = 512
    parts = 4
    flops = 2 * rows * width * columns
    size = 2 * (width * columns + rows * width + rows * columns)
    out_shape = (groups // 2 if apart else groups, heads, rows // groups, columns // heads)
    out_shapes = [out_shape] + [out_shape[2:]] * apart
    return pl.pallas_call(
        functools.partial(project_kernel, kinds, devices, heads, apart),
        out_shape=[jax.ShapeDtypeStruct(shape, jnp.bfloat16) for shape in out_shapes],
        in_specs=[IN_PLACE] * (len(weights) + 4),
        out_specs=[IN_PLACE] * (1 + apart),
        scratch_shapes=[
            pltpu.VMEM(positions.shape, jnp.int32),
            pltpu.VMEM(freq.shape, jnp.float32),
            pltpu.VMEM(gain.shape, jnp.bfloat16),
            pltpu.VMEM((rows, width), jnp.bfloat16),
            pltpu.VMEM((rows, width), jnp.bfloat16),
            pltpu.VMEM((columns // span, width, span), jnp.bfloat16),
            pltpu.VMEM((groups, heads, rows // groups, columns // heads), jnp.bfloat16),
            pltpu.SemaphoreType.DMA((3,)),
            pltpu.SemaphoreType.DMA((parts,)),
            pltpu.SemaphoreType.DMA((columns // span,)),
            pltpu.SemaphoreType.DMA((max(1 + apart, columns // span),)),
        ],
        compiler_params=pltpu.CompilerParams(vmem_limit_bytes=56 * MIB),
        cost_estimate=pl.CostEstimate(flops=flops, bytes_accessed=size, transcendentals=0),
    )(positions, freq, gain, tokens, *weights)


def place_kernel(arrived_ref, slot_ref, *outs):
    rows = arrived_ref.shape[0]
    first = 0
    for out_ref in outs:
        size = out_ref.shape[0]
        slots = lax.broadcasted_iota(jnp.int32, (size, rows), 0) + first
        chosen = (slots == slot_ref[...]).astype(jnp.bfloat16)
        out_ref[...] = dot(chosen, arrived_ref[...]).astype(jnp.bfloat16)
        first += size


def place(arrived, slot, sizes):
    width = arrived.shape[1]
    return pl.pallas_call(
        place_kernel,
        out_shape=[jax.ShapeDtypeStruct((size, width), jnp.bfloat16) for size in sizes],
        in_specs=[WHOLE, WHOLE],
        out_specs=[WHOLE] * len(sizes),
        compiler_params=pltpu.CompilerParams(vmem_limit_bytes=16 * MIB),
        cost_estimate=pl.CostEstimate(
            flops=2 * sum(sizes) * arrived.shape[0] * width,
            bytes_accessed=4 * arrived.size,
            transcendentals=0,
        ),
    )(arrived, slot)


def taken_at(turn, members):
    distances = distances_at(turn, members)
    odd = lax.axis_index("dp") % 2
    distance = odd * distances[1] + (1 - odd) * distances[0]
    return (lax.axis_index("ctx") % members) ^ distance


def distances_at(turn, members):
    if turn in (0, members - 1):
        return (members - 1 - turn,) * 2
    return (turn, members - 1 - turn)


def attend_kernel(block, turn, members, devices, slot_ref, ends_ref, *rest):
    queries_refs, rest = rest[:-9], rest[-9:]
    pieces, out_ref, held, query_ref = rest[:6], rest[6], rest[7], rest[8]
    first = 0
    for ref in queries_refs:
        query_ref[first : first + ref.shape[0], :] = ref[...]
        first += ref.shape[0]
    target = taken_at(turn, members)
    group = lax.axis_index("ctx") // members
    starts = (group * members * block, (2 * devices - members - group * members) * block)
    last = group == devices // members - 1
    heads = query_ref.shape[1] // HEAD_SIZE
    arrived = query_ref.shape[0]
    run = arrived // 2
    per_run = run // block
    reach = REACH_BLOCKS * block
    keys = reach + block
    slot = slot_ref[...]
    ends = ends_ref[...]
    factor = jnp.float32(np.log2(np.e) / HEAD_SIZE**0.5)
    for half in range(2):
        first = 0
        for piece in pieces[3 * half : 3 * half + 3]:
            values = piece[...]
            if half == 1 and first == 0:
                values = jnp.where(last, pieces[2][...], values)
            held[half, first : first + piece.shape[0], :] = values
            first += piece.shape[0]
    indices = (target, per_run - 1 - target)
    at = [pl.multiple_of(index * block, block) for index in indices]
    iota = lax.broadcasted_iota(jnp.int32, (block, arrived), 0)
    chosen = [(iota + (at[half] + half * run) == slot).astype(jnp.bfloat16) for half in range(2)]
    queries = dot(jnp.concatenate(chosen, axis=0), query_ref[...]).astype(jnp.bfloat16)
    here = [slice(half * block, (half + 1) * block) for half in range(2)]
    scores, weights, totals = [], [], []
    for half in range(2):
        stacked = jnp.concatenate(
            [queries[here[half], h * HEAD_SIZE : (h + 1) * HEAD_SIZE] for h in range(heads)], axis=0
        )
        key = held[half, pl.ds(at[half], keys), :HEAD_SIZE]
        scores.append(
            lax.dot_general(stacked, key, (((1,), (1,)), ((), ())), preferred_element_type=jnp.float32)
        )
    for half in range(2):
        begin = starts[half] + at[half]
        query_at = lax.broadcasted_iota(jnp.int32, (block, 1), 0) + begin
        key_at = lax.broadcasted_iota(jnp.int32, (1, keys), 1) + (begin - reach)
        doc_start = jnp.max(jnp.where(ends <= query_at, ends, 0), axis=1, keepdims=True)
        allowed = (key_at >= doc_start) & (key_at <= query_at)
        masked = jnp.where(allowed[None], scores[half].reshape(heads, block, keys), jnp.float32(-1e30))
        masked = masked.reshape(heads * block, keys)
        top = jnp.max(masked, axis=1, keepdims=True)
        exact = jnp.exp2((masked - top) * factor)
        totals.append(jnp.sum(exact, axis=1, keepdims=True))
        weights.append(exact.astype(jnp.bfloat16))
    for half in range(2):
        value = held[half, pl.ds(at[half], keys), HEAD_SIZE:]
        mixed = (dot(weights[half], value) / totals[half]).astype(jnp.bfloat16)
        for h in range(heads):
            out_ref[here[half], h * HEAD_SIZE : (h + 1) * HEAD_SIZE] = mixed[h * block : (h + 1) * block]


def attend(turn, members, devices, queries, slot, ends, pieces, block):
    rows, width = slot.shape[1], queries[0].shape[1]
    held = REACH_BLOCKS * block + rows // 2
    heads = width // HEAD_SIZE
    reach = (REACH_BLOCKS + 1) * block
    return pl.pallas_call(
        functools.partial(attend_kernel, block, turn, members, devices),
        out_shape=jax.ShapeDtypeStruct((2 * block, width), jnp.bfloat16),
        in_specs=[WHOLE] * (8 + len(queries)),
        out_specs=WHOLE,
        scratch_shapes=[
            pltpu.VMEM((2, held, 2 * HEAD_SIZE), jnp.bfloat16),
            pltpu.VMEM((rows, width), jnp.bfloat16),
        ],
        compiler_params=pltpu.CompilerParams(vmem_limit_bytes=16 * MIB),
        cost_estimate=pl.CostEstimate(
            flops=2 * 2 * heads * block * reach * HEAD_SIZE * 2 + 4 * block * rows * width,
            bytes_accessed=2 * rows * width + 8 * held * HEAD_SIZE,
            transcendentals=2 * heads * block * reach,
        ),
    )(slot, ends, *queries, *pieces)


def assemble_kernel(*refs):
    pieces, out_ref = refs[:-1], refs[-1]
    width = pieces[0].shape[1]
    for turn, piece in enumerate(pieces):
        at = pl.multiple_of(taken_at(turn, len(pieces)) * width, width)
        out_ref[:, pl.ds(at, width)] = piece[...]


def assemble(pieces):
    rows, width = pieces[0].shape
    return pl.pallas_call(
        assemble_kernel,
        out_shape=jax.ShapeDtypeStruct((rows, width * len(pieces)), jnp.bfloat16),
        in_specs=[WHOLE] * len(pieces),
        out_specs=WHOLE,
        compiler_params=pltpu.CompilerParams(vmem_limit_bytes=8 * MIB),
        cost_estimate=pl.CostEstimate(
            flops=0, bytes_accessed=4 * rows * width * len(pieces), transcendentals=0
        ),
    )(*pieces)


def shards(tokens, positions, lengths, gain, w_query, w_key, value_weight):
    devices = lax.axis_size("ctx")
    device = lax.axis_index("ctx")
    rows = tokens.shape[0]
    block = rows // 2
    members = w_key.shape[1] // HEAD_SIZE
    groups = devices // members
    group = device // members
    run = members * block
    group_rows = rows // groups

    half = HEAD_SIZE // 2
    freq = np.float32(ROPE_THETA ** (-(np.arange(HEAD_SIZE) % half * 2.0 / HEAD_SIZE)))
    operands = (positions.reshape(-1, 128), jnp.asarray(freq[None, :]), gain, tokens)

    half_devices = devices // 2
    halves = [list(range(i, i + half_devices)) for i in (0, half_devices)]

    def exchange(ordered, among):
        width = ordered.shape[3]
        flat = ordered.reshape(-1, group_rows, width)
        flat = lax.all_to_all(flat, "ctx", split_axis=0, concat_axis=0, tiled=True, axis_index_groups=among)
        return flat.reshape(-1, width)

    (kv,) = project(*operands, (w_key, value_weight), (True, False), devices, members)
    kv = exchange(kv, None)
    near, *far = project(*operands, (w_query,), (True,), devices, members, half_devices)
    queries = []
    for i, piece in enumerate(far):
        distance = half_devices + i
        queries.append(lax.ppermute(piece, "ctx", [(j, j ^ distance) for j in range(devices)]))

    table = positions.reshape(devices, rows)
    ours = group_of(table, block, devices, members) == group
    first_run = group * run
    second_run = (2 * devices - members) * block - group * run
    slots = jnp.where(table // run == group, table - first_run, table - second_run + run)
    place_in = jnp.cumsum(ours.astype(jnp.int32), axis=1) - 1
    place_in = jnp.where(ours, place_in, -1)
    wanted = jnp.arange(group_rows, dtype=jnp.int32)[None, :, None] == place_in[:, None, :]
    slot = jnp.sum(jnp.where(wanted, slots[:, None, :], 0), axis=2)
    index = jnp.arange(half_devices, dtype=jnp.int32)
    sources = [device // half_devices * half_devices + index, device ^ (half_devices + index)]
    query_slot = slot[jnp.concatenate(sources)].reshape(1, devices * group_rows)
    slot = slot.reshape(1, devices * group_rows)
    ends = jnp.cumsum(lengths, dtype=jnp.int32)[None, :]

    kv, near = lax.optimization_barrier((kv, near))
    queries.insert(0, exchange(near, halves))
    kv, *queries[1:6] = lax.optimization_barrier((kv, *queries[1:6]))
    reach = REACH_BLOCKS * block
    sizes = [run - reach, reach] * 2
    early_head, early_tail, late_head, late_tail = place(kv, slot, sizes)
    up = [(i, i + members) for i in range(devices - members)]
    down = [(i + members, i) for i in range(devices - members)]
    early_halo = lax.ppermute(early_tail, "ctx", up)
    late_halo = lax.ppermute(late_tail, "ctx", down)
    pieces = (early_halo, early_head, early_tail, late_halo, late_head, late_tail)

    results = []
    for turn in range(members):
        out = attend(turn, members, devices, queries, query_slot, ends, pieces, block)
        if turn < members - 1:
            distances = distances_at(turn, members)
            route = [
                (i * devices + j, i * devices + j // members * members + (j % members ^ distances[i % 2]))
                for i in range(lax.axis_size("dp"))
                for j in range(devices)
            ]
            out = lax.ppermute(out, ("dp", "ctx"), route)
        results.append(out)
    return assemble(results)


def solution(mesh):
    in_specs = (P(("dp", "ctx"), None), P("dp"), P("dp"), P(), P(), P(), P())
    out_specs = P(("dp", "ctx"), None)
    return jax.shard_map(shards, mesh=mesh, in_specs=in_specs, out_specs=out_specs, check_vma=False)
```

```python
import functools

import jax
import jax.numpy as jnp
import numpy as np
from jax import lax
from jax.experimental import pallas as pl
from jax.experimental.pallas import tpu as pltpu
from jax.sharding import PartitionSpec as P

HEAD_SIZE = 128
REACH_BLOCKS = 3
ROPE_THETA = 500000.0
EPSILON = 1e-05

WHOLE = pl.BlockSpec(memory_space=pltpu.VMEM)
IN_PLACE = pl.BlockSpec(memory_space=pl.ANY)
MIB = 1024 * 1024


def dot(a, b):
    return jnp.dot(a, b, preferred_element_type=jnp.float32)


def transposed(row):
    size = row.shape[1]
    here = lax.broadcasted_iota(jnp.int32, (size, size), 0)
    there = lax.broadcasted_iota(jnp.int32, (size, size), 1)
    return jnp.sum(jnp.where(here == there, row, 0), axis=1, keepdims=True)


def group_of(where_at, block, devices, members):
    block_id = where_at // block
    return jnp.minimum(block_id, 2 * devices - 1 - block_id) // members


def project_kernel(kinds, devices, members, apart, ready, positions_hbm, freq_hbm, gain_hbm, tokens_hbm, *rest):
    count = len(kinds)
    weights_hbm, rest = rest[:count], rest[count:]
    outputs = 1 + len(apart) + (not ready)
    outs_hbm, rest = rest[:outputs], rest[outputs:]
    positions_ref, freq_ref, gain_ref, tokens, normed, weights, out_ref = rest[:7]
    small_sems, token_sems, sems, out_sems = rest[7:]
    rows, width = normed.shape
    chunks, _, span = weights.shape
    parts = token_sems.shape[0]
    part = rows // parts
    token_copies, copies, origin = [], [], []
    small_copies = [
        pltpu.make_async_copy(source, target, small_sems.at[i])
        for i, (source, target) in enumerate(
            [(positions_hbm, positions_ref), (freq_hbm, freq_ref), (gain_hbm, gain_ref)]
        )
    ]
    for copy in small_copies:
        copy.start()
    for i in range(parts):
        at = pl.ds(i * part, part)
        target = normed.at[at] if ready else tokens.at[at]
        token_copies.append(pltpu.make_async_copy(tokens_hbm.at[at], target, token_sems.at[i]))
        token_copies[i].start()
    for i in range(count):
        for first in range(0, weights_hbm[i].shape[1], span):
            j = len(copies)
            source = weights_hbm[i].at[:, pl.ds(first, span)]
            copies.append(pltpu.make_async_copy(source, weights.at[j], sems.at[j]))
            origin.append((i, first))
    copies[0].start()
    if ready and chunks > 1:
        copies[1].start()
    for copy in small_copies:
        copy.wait()
    lanes = positions_ref.shape[1]
    stripes = rows // lanes
    mine = jnp.concatenate(
        [positions_ref[pl.ds(lax.axis_index("ctx") * stripes + i, 1), :] for i in range(stripes)], axis=1
    )
    owner = group_of(mine, rows // 2, devices, members)
    here = lax.broadcasted_iota(jnp.int32, (rows, rows), 0)
    there = lax.broadcasted_iota(jnp.int32, (rows, rows), 1)
    earlier = jnp.where((transposed(owner) == owner) & (here < there), 1, 0)
    rank = owner * (rows * members // devices) + jnp.sum(earlier, axis=0, keepdims=True)
    order = here == rank
    ordered_at = jnp.sum(jnp.where(order, mine, 0), axis=1, keepdims=True)
    angle = ordered_at.astype(jnp.float32) * freq_ref[...]
    lane = lax.broadcasted_iota(jnp.int32, (rows, HEAD_SIZE), 1)
    cosine = jnp.cos(angle)
    sine = jnp.where(lane < HEAD_SIZE // 2, -1.0, 1.0) * jnp.sin(angle)
    order = jnp.where(order, 1.0, 0.0).astype(jnp.bfloat16)
    gain = gain_ref[...].astype(jnp.float32).reshape(1, width)
    step = 32
    written = []

    for i in range(parts):
        token_copies[i].wait()
        for first in range(i * part, (i + 1) * part, step) if not ready else ():
            at = slice(first, first + step)
            floats = tokens[at, :].astype(jnp.float32)
            mean = jnp.sum(floats * floats, axis=1, keepdims=True) * (1.0 / width)
            tokens[at, :] = (floats * lax.rsqrt(mean + EPSILON) * gain).astype(jnp.bfloat16)
    if not ready:
        if chunks > 1:
            copies[1].start()
        for first in range(0, width, 512):
            columns = slice(first, first + 512)
            normed[:, columns] = dot(order, tokens[:, columns]).astype(jnp.bfloat16)
        written.append(pltpu.make_async_copy(normed, outs_hbm[-1], small_sems.at[0]))
        written[0].start()
    groups, heads = out_ref.shape[:2]
    offsets = [0]
    for i in range(count):
        offsets.append(offsets[-1] + weights_hbm[i].shape[1] // heads)
    me = lax.axis_index("ctx")
    far = [
        pltpu.make_async_copy(
            out_ref.at[(me ^ distance) // members, (me ^ distance) % members], outs_hbm[1 + i], out_sems.at[chunks + i]
        )
        for i, distance in enumerate(apart)
    ]
    for j in range(chunks):
        i, first = origin[j]
        copies[j].wait()
        if j + 2 < chunks:
            copies[j + 2].start()
        product = dot(normed[...], weights[j])
        per_head = offsets[i + 1] - offsets[i]
        for u in range(0, span, HEAD_SIZE):
            values = product[:, u : u + HEAD_SIZE]
            if kinds[i]:
                values = values * cosine + pltpu.roll(values, HEAD_SIZE // 2, 1) * sine
            head, inside = divmod(first + u, per_head)
            inside += offsets[i]
            out_ref[:, head, :, inside : inside + HEAD_SIZE] = values.astype(jnp.bfloat16).reshape(
                groups, rows // groups, HEAD_SIZE
            )
        first_head, done_heads = first // per_head, max(span // per_head, 1)
        done = (pl.ds(first_head, done_heads), pl.ds(0, rows // groups))
        done += (pl.ds(offsets[i] + first % per_head, min(span, per_head)),)
        taken = groups // 2 if apart else groups
        start = me // members // taken * taken if apart else 0
        source = out_ref.at[(pl.ds(start, taken),) + done]
        written.append(pltpu.make_async_copy(source, outs_hbm[0].at[(pl.ds(0, taken),) + done], out_sems.at[j]))
        written[-1].start()
        if first % per_head + span >= per_head:
            for distance, copy in zip(apart, far):
                to = (me ^ distance) % members
                pl.when((to >= first_head) & (to < first_head + done_heads))(copy.start)
    for copy in written + far:
        copy.wait()


def project(positions, freq, gain, tokens, weights, kinds, devices, heads, apart=(), ready=False):
    rows, width = tokens.shape
    groups = devices // heads
    columns = sum(w.shape[1] for w in weights)
    span = 512
    parts = 4
    flops = 2 * rows * width * columns
    size = 2 * (width * columns + rows * width + rows * columns)
    out_shape = (groups // 2 if apart else groups, heads, rows // groups, columns // heads)
    out_shapes = [out_shape] + [out_shape[2:]] * len(apart) + [(rows, width)] * (not ready)
    return pl.pallas_call(
        functools.partial(project_kernel, kinds, devices, heads, apart, ready),
        out_shape=[jax.ShapeDtypeStruct(shape, jnp.bfloat16) for shape in out_shapes],
        in_specs=[IN_PLACE] * (len(weights) + 4),
        out_specs=[IN_PLACE] * len(out_shapes),
        scratch_shapes=[
            pltpu.VMEM(positions.shape, jnp.int32),
            pltpu.VMEM(freq.shape, jnp.float32),
            pltpu.VMEM(gain.shape, jnp.bfloat16),
            pltpu.VMEM((8 if ready else rows, width), jnp.bfloat16),
            pltpu.VMEM((rows, width), jnp.bfloat16),
            pltpu.VMEM((columns // span, width, span), jnp.bfloat16),
            pltpu.VMEM((groups, heads, rows // groups, columns // heads), jnp.bfloat16),
            pltpu.SemaphoreType.DMA((3,)),
            pltpu.SemaphoreType.DMA((parts,)),
            pltpu.SemaphoreType.DMA((columns // span,)),
            pltpu.SemaphoreType.DMA((columns // span + len(apart),)),
        ],
        compiler_params=pltpu.CompilerParams(vmem_limit_bytes=56 * MIB),
        cost_estimate=pl.CostEstimate(flops=flops, bytes_accessed=size, transcendentals=0),
    )(positions, freq, gain, tokens, *weights)


def place_kernel(arrived_ref, slot_ref, *outs):
    rows = arrived_ref.shape[0]
    first = 0
    for out_ref in outs:
        size = out_ref.shape[0]
        slots = lax.broadcasted_iota(jnp.int32, (size, rows), 0) + first
        chosen = (slots == slot_ref[...]).astype(jnp.bfloat16)
        out_ref[...] = dot(chosen, arrived_ref[...]).astype(jnp.bfloat16)
        first += size


def place(arrived, slot, sizes):
    width = arrived.shape[1]
    return pl.pallas_call(
        place_kernel,
        out_shape=[jax.ShapeDtypeStruct((size, width), jnp.bfloat16) for size in sizes],
        in_specs=[WHOLE, WHOLE],
        out_specs=[WHOLE] * len(sizes),
        compiler_params=pltpu.CompilerParams(vmem_limit_bytes=16 * MIB),
        cost_estimate=pl.CostEstimate(
            flops=2 * sum(sizes) * arrived.shape[0] * width,
            bytes_accessed=4 * arrived.size,
            transcendentals=0,
        ),
    )(arrived, slot)


def taken_at(turn, members):
    distances = distances_at(turn, members)
    odd = lax.axis_index("dp") % 2
    distance = odd * distances[1] + (1 - odd) * distances[0]
    return (lax.axis_index("ctx") % members) ^ distance


def distances_at(turn, members):
    if turn in (0, members - 1):
        return (members - 1 - turn,) * 2
    return (turn, members - 1 - turn)


def attend_kernel(block, turn, members, devices, slot_ref, ends_ref, *rest):
    queries_refs, rest = rest[:-9], rest[-9:]
    pieces, out_ref, held, query_ref = rest[:6], rest[6], rest[7], rest[8]
    first = 0
    for ref in queries_refs:
        query_ref[first : first + ref.shape[0], :] = ref[...]
        first += ref.shape[0]
    target = taken_at(turn, members)
    group = lax.axis_index("ctx") // members
    starts = (group * members * block, (2 * devices - members - group * members) * block)
    last = group == devices // members - 1
    heads = query_ref.shape[1] // HEAD_SIZE
    arrived = query_ref.shape[0]
    run = arrived // 2
    per_run = run // block
    reach = REACH_BLOCKS * block
    keys = reach + block
    slot = slot_ref[...]
    ends = ends_ref[...]
    factor = jnp.float32(np.log2(np.e) / HEAD_SIZE**0.5)
    for half in range(2):
        first = 0
        for piece in pieces[3 * half : 3 * half + 3]:
            values = piece[...]
            if half == 1 and first == 0:
                values = jnp.where(last, pieces[2][...], values)
            held[half, first : first + piece.shape[0], :] = values
            first += piece.shape[0]
    indices = (target, per_run - 1 - target)
    at = [pl.multiple_of(index * block, block) for index in indices]
    iota = lax.broadcasted_iota(jnp.int32, (block, arrived), 0)
    chosen = [(iota + (at[half] + half * run) == slot).astype(jnp.bfloat16) for half in range(2)]
    queries = dot(jnp.concatenate(chosen, axis=0), query_ref[...]).astype(jnp.bfloat16)
    here = [slice(half * block, (half + 1) * block) for half in range(2)]
    scores, weights, totals = [], [], []
    for half in range(2):
        stacked = jnp.concatenate(
            [queries[here[half], h * HEAD_SIZE : (h + 1) * HEAD_SIZE] for h in range(heads)], axis=0
        )
        key = held[half, pl.ds(at[half], keys), :HEAD_SIZE]
        scores.append(
            lax.dot_general(stacked, key, (((1,), (1,)), ((), ())), preferred_element_type=jnp.float32)
        )
    for half in range(2):
        begin = starts[half] + at[half]
        query_at = lax.broadcasted_iota(jnp.int32, (block, 1), 0) + begin
        key_at = lax.broadcasted_iota(jnp.int32, (1, keys), 1) + (begin - reach)
        doc_start = jnp.max(jnp.where(ends <= query_at, ends, 0), axis=1, keepdims=True)
        allowed = (key_at >= doc_start) & (key_at <= query_at)
        masked = jnp.where(allowed[None], scores[half].reshape(heads, block, keys), jnp.float32(-1e30))
        masked = masked.reshape(heads * block, keys)
        top = jnp.max(masked, axis=1, keepdims=True)
        exact = jnp.exp2((masked - top) * factor)
        totals.append(jnp.sum(exact, axis=1, keepdims=True))
        weights.append(exact.astype(jnp.bfloat16))
    for half in range(2):
        value = held[half, pl.ds(at[half], keys), HEAD_SIZE:]
        mixed = (dot(weights[half], value) / totals[half]).astype(jnp.bfloat16)
        for h in range(heads):
            out_ref[here[half], h * HEAD_SIZE : (h + 1) * HEAD_SIZE] = mixed[h * block : (h + 1) * block]


def attend(turn, members, devices, queries, slot, ends, pieces, block):
    rows, width = slot.shape[1], queries[0].shape[1]
    held = REACH_BLOCKS * block + rows // 2
    heads = width // HEAD_SIZE
    reach = (REACH_BLOCKS + 1) * block
    return pl.pallas_call(
        functools.partial(attend_kernel, block, turn, members, devices),
        out_shape=jax.ShapeDtypeStruct((2 * block, width), jnp.bfloat16),
        in_specs=[WHOLE] * (8 + len(queries)),
        out_specs=WHOLE,
        scratch_shapes=[
            pltpu.VMEM((2, held, 2 * HEAD_SIZE), jnp.bfloat16),
            pltpu.VMEM((rows, width), jnp.bfloat16),
        ],
        compiler_params=pltpu.CompilerParams(vmem_limit_bytes=16 * MIB),
        cost_estimate=pl.CostEstimate(
            flops=2 * 2 * heads * block * reach * HEAD_SIZE * 2 + 4 * block * rows * width,
            bytes_accessed=2 * rows * width + 8 * held * HEAD_SIZE,
            transcendentals=2 * heads * block * reach,
        ),
    )(slot, ends, *queries, *pieces)


def assemble_kernel(*refs):
    pieces, out_ref = refs[:-1], refs[-1]
    width = pieces[0].shape[1]
    for turn, piece in enumerate(pieces):
        at = pl.multiple_of(taken_at(turn, len(pieces)) * width, width)
        out_ref[:, pl.ds(at, width)] = piece[...]


def assemble(pieces):
    rows, width = pieces[0].shape
    return pl.pallas_call(
        assemble_kernel,
        out_shape=jax.ShapeDtypeStruct((rows, width * len(pieces)), jnp.bfloat16),
        in_specs=[WHOLE] * len(pieces),
        out_specs=WHOLE,
        compiler_params=pltpu.CompilerParams(vmem_limit_bytes=8 * MIB),
        cost_estimate=pl.CostEstimate(
            flops=0, bytes_accessed=4 * rows * width * len(pieces), transcendentals=0
        ),
    )(*pieces)


def shards(tokens, positions, lengths, gain, w_query, w_key, value_weight):
    devices = lax.axis_size("ctx")
    device = lax.axis_index("ctx")
    rows = tokens.shape[0]
    block = rows // 2
    members = w_key.shape[1] // HEAD_SIZE
    groups = devices // members
    group = device // members
    run = members * block
    group_rows = rows // groups

    half = HEAD_SIZE // 2
    freq = np.float32(ROPE_THETA ** (-(np.arange(HEAD_SIZE) % half * 2.0 / HEAD_SIZE)))
    operands = (positions.reshape(-1, 128), jnp.asarray(freq[None, :]), gain)

    half_devices = devices // 2
    halves = [list(range(i, i + half_devices)) for i in (0, half_devices)]

    def exchange(ordered, among):
        width = ordered.shape[3]
        flat = ordered.reshape(-1, group_rows, width)
        flat = lax.all_to_all(flat, "ctx", split_axis=0, concat_axis=0, tiled=True, axis_index_groups=among)
        return flat.reshape(-1, width)

    kv, normed = project(*operands, tokens, (w_key, value_weight), (True, False), devices, members)
    kv = exchange(kv, None)
    apart = list(range(half_devices, devices))
    near, *far = project(*operands, normed, (w_query,), (True,), devices, members, apart, True)
    queries = []
    for i, piece in enumerate(far):
        distance = half_devices + i
        queries.append(lax.ppermute(piece, "ctx", [(j, j ^ distance) for j in range(devices)]))

    table = positions.reshape(devices, rows)
    ours = group_of(table, block, devices, members) == group
    first_run = group * run
    second_run = (2 * devices - members) * block - group * run
    slots = jnp.where(table // run == group, table - first_run, table - second_run + run)
    inner = jnp.arange(rows, dtype=jnp.int32)
    before = (inner[:, None] < inner[None, :]).astype(jnp.bfloat16)
    place_in = dot(ours.astype(jnp.bfloat16), before).astype(jnp.int32)
    place_in = jnp.where(ours, place_in, -1)
    wanted = jnp.arange(group_rows, dtype=jnp.int32)[None, :, None] == place_in[:, None, :]
    slot = jnp.sum(jnp.where(wanted, slots[:, None, :], 0), axis=2)
    index = jnp.arange(half_devices, dtype=jnp.int32)
    sources = [device // half_devices * half_devices + index, device ^ (half_devices + index)]
    query_slot = slot[jnp.concatenate(sources)].reshape(1, devices * group_rows)
    slot = slot.reshape(1, devices * group_rows)
    ends = jnp.cumsum(lengths, dtype=jnp.int32)[None, :]

    kv, near = lax.optimization_barrier((kv, near))
    queries.insert(0, exchange(near, halves))
    kv, *queries[1:6] = lax.optimization_barrier((kv, *queries[1:6]))
    reach = REACH_BLOCKS * block
    sizes = [run - reach, reach] * 2
    early_head, early_tail, late_head, late_tail = place(kv, slot, sizes)
    up = [(i, i + members) for i in range(devices - members)]
    down = [(i + members, i) for i in range(devices - members)]
    early_halo = lax.ppermute(early_tail, "ctx", up)
    late_halo = lax.ppermute(late_tail, "ctx", down)
    pieces = (early_halo, early_head, early_tail, late_halo, late_head, late_tail)

    results = []
    for turn in range(members):
        out = attend(turn, members, devices, queries, query_slot, ends, pieces, block)
        if turn < members - 1:
            distances = distances_at(turn, members)
            route = [
                (i * devices + j, i * devices + j // members * members + (j % members ^ distances[i % 2]))
                for i in range(lax.axis_size("dp"))
                for j in range(devices)
            ]
            out = lax.ppermute(out, ("dp", "ctx"), route)
        results.append(out)
    return assemble(results)


def solution(mesh):
    in_specs = (P(("dp", "ctx"), None), P("dp"), P("dp"), P(), P(), P(), P())
    out_specs = P(("dp", "ctx"), None)
    return jax.shard_map(shards, mesh=mesh, in_specs=in_specs, out_specs=out_specs, check_vma=False)
```

```python
import functools

import jax
import jax.numpy as jnp
import numpy as np
from jax import lax
from jax.experimental import pallas as pl
from jax.experimental.pallas import tpu as pltpu
from jax.sharding import PartitionSpec as P

HEAD_SIZE = 128
REACH_BLOCKS = 3
ROPE_THETA = 500000.0
EPSILON = 1e-05

WHOLE = pl.BlockSpec(memory_space=pltpu.VMEM)
IN_PLACE = pl.BlockSpec(memory_space=pl.ANY)
MIB = 1024 * 1024


def dot(a, b):
    return jnp.dot(a, b, preferred_element_type=jnp.float32)


def transposed(row):
    size = row.shape[1]
    here = lax.broadcasted_iota(jnp.int32, (size, size), 0)
    there = lax.broadcasted_iota(jnp.int32, (size, size), 1)
    return jnp.sum(jnp.where(here == there, row, 0), axis=1, keepdims=True)


def group_of(where_at, block, devices, members):
    block_id = where_at // block
    return jnp.minimum(block_id, 2 * devices - 1 - block_id) // members


def project_kernel(kinds, devices, members, apart, positions_hbm, freq_hbm, gain_hbm, tokens_hbm, *rest):
    count = len(kinds)
    weights_hbm, rest = rest[:count], rest[count:]
    outputs = 1 + len(apart)
    outs_hbm, rest = rest[:outputs], rest[outputs:]
    positions_ref, freq_ref, gain_ref, tokens, normed, weights, out_ref = rest[:7]
    small_sems, sems, out_sems = rest[7:]
    rows, width = normed.shape
    chunks, _, span = weights.shape
    copies, origin = [], []
    small_copies = [
        pltpu.make_async_copy(source, target, small_sems.at[i])
        for i, (source, target) in enumerate(
            [(positions_hbm, positions_ref), (freq_hbm, freq_ref), (gain_hbm, gain_ref), (tokens_hbm, tokens)]
        )
    ]
    for copy in small_copies:
        copy.start()
    for i in range(count):
        for first in range(0, weights_hbm[i].shape[1], span):
            j = len(copies)
            source = weights_hbm[i].at[:, pl.ds(first, span)]
            copies.append(pltpu.make_async_copy(source, weights.at[j], sems.at[j]))
            origin.append((i, first))
    copies[0].start()
    for copy in small_copies[:-1]:
        copy.wait()
    lanes = positions_ref.shape[1]
    stripes = rows // lanes
    mine = jnp.concatenate(
        [positions_ref[pl.ds(lax.axis_index("ctx") * stripes + i, 1), :] for i in range(stripes)], axis=1
    )
    owner = group_of(mine, rows // 2, devices, members)
    here = lax.broadcasted_iota(jnp.int32, (rows, rows), 0)
    there = lax.broadcasted_iota(jnp.int32, (rows, rows), 1)
    earlier = jnp.where((transposed(owner) == owner) & (here < there), 1, 0)
    rank = owner * (rows * members // devices) + jnp.sum(earlier, axis=0, keepdims=True)
    order = here == rank
    ordered_at = jnp.sum(jnp.where(order, mine, 0), axis=1, keepdims=True)
    angle = ordered_at.astype(jnp.float32) * freq_ref[...]
    lane = lax.broadcasted_iota(jnp.int32, (rows, HEAD_SIZE), 1)
    cosine = jnp.cos(angle)
    sine = jnp.where(lane < HEAD_SIZE // 2, -1.0, 1.0) * jnp.sin(angle)
    order = jnp.where(order, 1.0, 0.0).astype(jnp.bfloat16)
    gain = gain_ref[...].astype(jnp.float32).reshape(1, width)
    step = 32
    written = []

    small_copies[-1].wait()
    for first in range(0, rows, step):
        at = slice(first, first + step)
        floats = tokens[at, :].astype(jnp.float32)
        mean = jnp.sum(floats * floats, axis=1, keepdims=True) * (1.0 / width)
        tokens[at, :] = (floats * lax.rsqrt(mean + EPSILON) * gain).astype(jnp.bfloat16)
    if chunks > 1:
        copies[1].start()
    for first in range(0, width, 512):
        columns = slice(first, first + 512)
        normed[:, columns] = dot(order, tokens[:, columns]).astype(jnp.bfloat16)
    groups, heads = out_ref.shape[:2]
    offsets = [0]
    for i in range(count):
        offsets.append(offsets[-1] + weights_hbm[i].shape[1] // heads)
    me = lax.axis_index("ctx")
    far = [
        pltpu.make_async_copy(
            out_ref.at[(me ^ distance) // members, (me ^ distance) % members], outs_hbm[1 + i], out_sems.at[chunks + i]
        )
        for i, distance in enumerate(apart)
    ]
    for j in range(chunks):
        i, first = origin[j]
        copies[j].wait()
        if j + 2 < chunks:
            copies[j + 2].start()
        product = dot(normed[...], weights[j])
        per_head = offsets[i + 1] - offsets[i]
        for u in range(0, span, HEAD_SIZE):
            values = product[:, u : u + HEAD_SIZE]
            if kinds[i]:
                values = values * cosine + pltpu.roll(values, HEAD_SIZE // 2, 1) * sine
            head, inside = divmod(first + u, per_head)
            inside += offsets[i]
            out_ref[:, head, :, inside : inside + HEAD_SIZE] = values.astype(jnp.bfloat16).reshape(
                groups, rows // groups, HEAD_SIZE
            )
        first_head, done_heads = first // per_head, max(span // per_head, 1)
        done = (pl.ds(first_head, done_heads), pl.ds(0, rows // groups))
        done += (pl.ds(offsets[i] + first % per_head, min(span, per_head)),)
        taken = groups // 2 if apart else groups
        start = me // members // taken * taken if apart else 0
        source = out_ref.at[(pl.ds(start, taken),) + done]
        written.append(pltpu.make_async_copy(source, outs_hbm[0].at[(pl.ds(0, taken),) + done], out_sems.at[j]))
        written[-1].start()
        if first % per_head + span >= per_head:
            for distance, copy in zip(apart, far):
                to = (me ^ distance) % members
                pl.when((to >= first_head) & (to < first_head + done_heads))(copy.start)
    for copy in written + far:
        copy.wait()


def project(positions, freq, gain, tokens, weights, kinds, devices, heads, apart=()):
    rows, width = tokens.shape
    groups = devices // heads
    columns = sum(w.shape[1] for w in weights)
    span = 512
    flops = 2 * rows * width * columns
    size = 2 * (width * columns + rows * width + rows * columns)
    out_shape = (groups // 2 if apart else groups, heads, rows // groups, columns // heads)
    out_shapes = [out_shape] + [out_shape[2:]] * len(apart)
    return pl.pallas_call(
        functools.partial(project_kernel, kinds, devices, heads, apart),
        out_shape=[jax.ShapeDtypeStruct(shape, jnp.bfloat16) for shape in out_shapes],
        in_specs=[IN_PLACE] * (len(weights) + 4),
        out_specs=[IN_PLACE] * len(out_shapes),
        scratch_shapes=[
            pltpu.VMEM(positions.shape, jnp.int32),
            pltpu.VMEM(freq.shape, jnp.float32),
            pltpu.VMEM(gain.shape, jnp.bfloat16),
            pltpu.VMEM((rows, width), jnp.bfloat16),
            pltpu.VMEM((rows, width), jnp.bfloat16),
            pltpu.VMEM((columns // span, width, span), jnp.bfloat16),
            pltpu.VMEM((groups, heads, rows // groups, columns // heads), jnp.bfloat16),
            pltpu.SemaphoreType.DMA((4,)),
            pltpu.SemaphoreType.DMA((columns // span,)),
            pltpu.SemaphoreType.DMA((columns // span + len(apart),)),
        ],
        compiler_params=pltpu.CompilerParams(vmem_limit_bytes=56 * MIB),
        cost_estimate=pl.CostEstimate(flops=flops, bytes_accessed=size, transcendentals=0),
    )(positions, freq, gain, tokens, *weights)


def place_kernel(arrived_ref, slot_ref, *outs):
    rows = arrived_ref.shape[0]
    first = 0
    for out_ref in outs:
        size = out_ref.shape[0]
        slots = lax.broadcasted_iota(jnp.int32, (size, rows), 0) + first
        chosen = (slots == slot_ref[...]).astype(jnp.bfloat16)
        out_ref[...] = dot(chosen, arrived_ref[...]).astype(jnp.bfloat16)
        first += size


def place(arrived, slot, sizes):
    width = arrived.shape[1]
    return pl.pallas_call(
        place_kernel,
        out_shape=[jax.ShapeDtypeStruct((size, width), jnp.bfloat16) for size in sizes],
        in_specs=[WHOLE, WHOLE],
        out_specs=[WHOLE] * len(sizes),
        compiler_params=pltpu.CompilerParams(vmem_limit_bytes=16 * MIB),
        cost_estimate=pl.CostEstimate(
            flops=2 * sum(sizes) * arrived.shape[0] * width,
            bytes_accessed=4 * arrived.size,
            transcendentals=0,
        ),
    )(arrived, slot)


def taken_at(turn, members):
    distances = distances_at(turn, members)
    odd = lax.axis_index("dp") % 2
    distance = odd * distances[1] + (1 - odd) * distances[0]
    return (lax.axis_index("ctx") % members) ^ distance


def distances_at(turn, members):
    if turn in (0, members - 1):
        return (members - 1 - turn,) * 2
    return (turn, members - 1 - turn)


def attend_kernel(block, turn, members, devices, slot_ref, ends_ref, *rest):
    queries_refs, rest = rest[:-9], rest[-9:]
    pieces, out_ref, held, query_ref = rest[:6], rest[6], rest[7], rest[8]
    first = 0
    for ref in queries_refs:
        query_ref[first : first + ref.shape[0], :] = ref[...]
        first += ref.shape[0]
    target = taken_at(turn, members)
    group = lax.axis_index("ctx") // members
    starts = (group * members * block, (2 * devices - members - group * members) * block)
    last = group == devices // members - 1
    heads = query_ref.shape[1] // HEAD_SIZE
    arrived = query_ref.shape[0]
    run = arrived // 2
    per_run = run // block
    reach = REACH_BLOCKS * block
    keys = reach + block
    slot = slot_ref[...]
    ends = ends_ref[...]
    factor = jnp.float32(np.log2(np.e) / HEAD_SIZE**0.5)
    for half in range(2):
        first = 0
        for piece in pieces[3 * half : 3 * half + 3]:
            values = piece[...]
            if half == 1 and first == 0:
                values = jnp.where(last, pieces[2][...], values)
            held[half, first : first + piece.shape[0], :] = values
            first += piece.shape[0]
    indices = (target, per_run - 1 - target)
    at = [pl.multiple_of(index * block, block) for index in indices]
    iota = lax.broadcasted_iota(jnp.int32, (block, arrived), 0)
    chosen = [(iota + (at[half] + half * run) == slot).astype(jnp.bfloat16) for half in range(2)]
    queries = dot(jnp.concatenate(chosen, axis=0), query_ref[...]).astype(jnp.bfloat16)
    here = [slice(half * block, (half + 1) * block) for half in range(2)]
    scores, weights, totals = [], [], []
    for half in range(2):
        stacked = jnp.concatenate(
            [queries[here[half], h * HEAD_SIZE : (h + 1) * HEAD_SIZE] for h in range(heads)], axis=0
        )
        key = held[half, pl.ds(at[half], keys), :HEAD_SIZE]
        scores.append(
            lax.dot_general(stacked, key, (((1,), (1,)), ((), ())), preferred_element_type=jnp.float32)
        )
    for half in range(2):
        begin = starts[half] + at[half]
        query_at = lax.broadcasted_iota(jnp.int32, (block, 1), 0) + begin
        key_at = lax.broadcasted_iota(jnp.int32, (1, keys), 1) + (begin - reach)
        doc_start = jnp.max(jnp.where(ends <= query_at, ends, 0), axis=1, keepdims=True)
        allowed = (key_at >= doc_start) & (key_at <= query_at)
        masked = jnp.where(allowed[None], scores[half].reshape(heads, block, keys), jnp.float32(-1e30))
        masked = masked.reshape(heads * block, keys)
        top = jnp.max(masked, axis=1, keepdims=True)
        exact = jnp.exp2((masked - top) * factor)
        totals.append(jnp.sum(exact, axis=1, keepdims=True))
        weights.append(exact.astype(jnp.bfloat16))
    for half in range(2):
        value = held[half, pl.ds(at[half], keys), HEAD_SIZE:]
        mixed = (dot(weights[half], value) / totals[half]).astype(jnp.bfloat16)
        for h in range(heads):
            out_ref[here[half], h * HEAD_SIZE : (h + 1) * HEAD_SIZE] = mixed[h * block : (h + 1) * block]


def attend(turn, members, devices, queries, slot, ends, pieces, block):
    rows, width = slot.shape[1], queries[0].shape[1]
    held = REACH_BLOCKS * block + rows // 2
    heads = width // HEAD_SIZE
    reach = (REACH_BLOCKS + 1) * block
    return pl.pallas_call(
        functools.partial(attend_kernel, block, turn, members, devices),
        out_shape=jax.ShapeDtypeStruct((2 * block, width), jnp.bfloat16),
        in_specs=[WHOLE] * (8 + len(queries)),
        out_specs=WHOLE,
        scratch_shapes=[
            pltpu.VMEM((2, held, 2 * HEAD_SIZE), jnp.bfloat16),
            pltpu.VMEM((rows, width), jnp.bfloat16),
        ],
        compiler_params=pltpu.CompilerParams(vmem_limit_bytes=16 * MIB),
        cost_estimate=pl.CostEstimate(
            flops=2 * 2 * heads * block * reach * HEAD_SIZE * 2 + 4 * block * rows * width,
            bytes_accessed=2 * rows * width + 8 * held * HEAD_SIZE,
            transcendentals=2 * heads * block * reach,
        ),
    )(slot, ends, *queries, *pieces)


def assemble_kernel(*refs):
    pieces, out_ref = refs[:-1], refs[-1]
    width = pieces[0].shape[1]
    for turn, piece in enumerate(pieces):
        at = pl.multiple_of(taken_at(turn, len(pieces)) * width, width)
        out_ref[:, pl.ds(at, width)] = piece[...]


def assemble(pieces):
    rows, width = pieces[0].shape
    return pl.pallas_call(
        assemble_kernel,
        out_shape=jax.ShapeDtypeStruct((rows, width * len(pieces)), jnp.bfloat16),
        in_specs=[WHOLE] * len(pieces),
        out_specs=WHOLE,
        compiler_params=pltpu.CompilerParams(vmem_limit_bytes=8 * MIB),
        cost_estimate=pl.CostEstimate(
            flops=0, bytes_accessed=4 * rows * width * len(pieces), transcendentals=0
        ),
    )(*pieces)


def shards(tokens, positions, lengths, gain, w_query, w_key, value_weight):
    devices = lax.axis_size("ctx")
    device = lax.axis_index("ctx")
    rows = tokens.shape[0]
    block = rows // 2
    members = w_key.shape[1] // HEAD_SIZE
    groups = devices // members
    group = device // members
    run = members * block
    group_rows = rows // groups

    half = HEAD_SIZE // 2
    freq = np.float32(ROPE_THETA ** (-(np.arange(HEAD_SIZE) % half * 2.0 / HEAD_SIZE)))
    operands = (positions.reshape(-1, 128), jnp.asarray(freq[None, :]), gain, tokens)

    half_devices = devices // 2
    halves = [list(range(i, i + half_devices)) for i in (0, half_devices)]

    def exchange(ordered, among):
        width = ordered.shape[3]
        flat = ordered.reshape(-1, group_rows, width)
        flat = lax.all_to_all(flat, "ctx", split_axis=0, concat_axis=0, tiled=True, axis_index_groups=among)
        return flat.reshape(-1, width)

    (kv,) = project(*operands, (w_key, value_weight), (True, False), devices, members)
    kv = exchange(kv, None)
    apart = list(range(half_devices, devices))
    near, *far = project(*operands, (w_query,), (True,), devices, members, apart)
    queries = []
    for i, piece in enumerate(far):
        distance = half_devices + i
        queries.append(lax.ppermute(piece, "ctx", [(j, j ^ distance) for j in range(devices)]))

    table = positions.reshape(devices, rows)
    ours = group_of(table, block, devices, members) == group
    first_run = group * run
    second_run = (2 * devices - members) * block - group * run
    slots = jnp.where(table // run == group, table - first_run, table - second_run + run)
    inner = jnp.arange(rows, dtype=jnp.int32)
    before = (inner[:, None] < inner[None, :]).astype(jnp.bfloat16)
    place_in = dot(ours.astype(jnp.bfloat16), before).astype(jnp.int32)
    place_in = jnp.where(ours, place_in, -1)
    wanted = jnp.arange(group_rows, dtype=jnp.int32)[None, :, None] == place_in[:, None, :]
    slot = jnp.sum(jnp.where(wanted, slots[:, None, :], 0), axis=2)
    index = jnp.arange(half_devices, dtype=jnp.int32)
    sources = [device // half_devices * half_devices + index, device ^ (half_devices + index)]
    query_slot = slot[jnp.concatenate(sources)].reshape(1, devices * group_rows)
    slot = slot.reshape(1, devices * group_rows)
    ends = jnp.cumsum(lengths, dtype=jnp.int32)[None, :]

    kv, near = lax.optimization_barrier((kv, near))
    queries.insert(0, exchange(near, halves))
    kv, *queries[1:6] = lax.optimization_barrier((kv, *queries[1:6]))
    reach = REACH_BLOCKS * block
    sizes = [run - reach, reach] * 2
    early_head, early_tail, late_head, late_tail = place(kv, slot, sizes)
    up = [(i, i + members) for i in range(devices - members)]
    down = [(i + members, i) for i in range(devices - members)]
    early_halo = lax.ppermute(early_tail, "ctx", up)
    late_halo = lax.ppermute(late_tail, "ctx", down)
    pieces = (early_halo, early_head, early_tail, late_halo, late_head, late_tail)

    results = []
    for turn in range(members):
        out = attend(turn, members, devices, queries, query_slot, ends, pieces, block)
        if turn < members - 1:
            distances = distances_at(turn, members)
            route = [
                (i * devices + j, i * devices + j // members * members + (j % members ^ distances[i % 2]))
                for i in range(lax.axis_size("dp"))
                for j in range(devices)
            ]
            out = lax.ppermute(out, ("dp", "ctx"), route)
        results.append(out)
    return assemble(results)


def solution(mesh):
    in_specs = (P(("dp", "ctx"), None), P("dp"), P("dp"), P(), P(), P(), P())
    out_specs = P(("dp", "ctx"), None)
    return jax.shard_map(shards, mesh=mesh, in_specs=in_specs, out_specs=out_specs, check_vma=False)
```

```python
import functools

import jax
import jax.numpy as jnp
import numpy as np
from jax import lax
from jax.experimental import pallas as pl
from jax.experimental.pallas import tpu as pltpu
from jax.sharding import PartitionSpec as P

HEAD_SIZE = 128
REACH_BLOCKS = 3
ROPE_THETA = 500000.0
EPSILON = 1e-05

WHOLE = pl.BlockSpec(memory_space=pltpu.VMEM)
IN_PLACE = pl.BlockSpec(memory_space=pl.ANY)
MIB = 1024 * 1024


def dot(a, b):
    return jnp.dot(a, b, preferred_element_type=jnp.float32)


def transposed(row):
    size = row.shape[1]
    here = lax.broadcasted_iota(jnp.int32, (size, size), 0)
    there = lax.broadcasted_iota(jnp.int32, (size, size), 1)
    return jnp.sum(jnp.where(here == there, row, 0), axis=1, keepdims=True)


def group_of(where_at, block, devices, members):
    block_id = where_at // block
    return jnp.minimum(block_id, 2 * devices - 1 - block_id) // members


def project_kernel(kinds, devices, members, apart, positions_hbm, freq_hbm, gain_hbm, tokens_hbm, *rest):
    count = len(kinds)
    weights_hbm, rest = rest[:count], rest[count:]
    groups = devices // members
    outputs = 1 + len(apart) if apart else groups
    outs_hbm, rest = rest[:outputs], rest[outputs:]
    positions_ref, freq_ref, gain_ref, tokens, normed, weights, out_ref = rest[:7]
    small_sems, sems, out_sems = rest[7:]
    rows, width = normed.shape
    chunks, _, span = weights.shape
    copies, origin = [], []
    small_copies = [
        pltpu.make_async_copy(source, target, small_sems.at[i])
        for i, (source, target) in enumerate(
            [(positions_hbm, positions_ref), (freq_hbm, freq_ref), (gain_hbm, gain_ref), (tokens_hbm, tokens)]
        )
    ]
    for copy in small_copies:
        copy.start()
    for i in range(count):
        for first in range(0, weights_hbm[i].shape[1], span):
            j = len(copies)
            source = weights_hbm[i].at[:, pl.ds(first, span)]
            copies.append(pltpu.make_async_copy(source, weights.at[j], sems.at[j]))
            origin.append((i, first))
    copies[0].start()
    for copy in small_copies[:-1]:
        copy.wait()
    lanes = positions_ref.shape[1]
    stripes = rows // lanes
    mine = jnp.concatenate(
        [positions_ref[pl.ds(lax.axis_index("ctx") * stripes + i, 1), :] for i in range(stripes)], axis=1
    )
    owner = group_of(mine, rows // 2, devices, members)
    here = lax.broadcasted_iota(jnp.int32, (rows, rows), 0)
    there = lax.broadcasted_iota(jnp.int32, (rows, rows), 1)
    earlier = jnp.where((transposed(owner) == owner) & (here < there), 1, 0)
    rank = owner * (rows * members // devices) + jnp.sum(earlier, axis=0, keepdims=True)
    order = here == rank
    ordered_at = jnp.sum(jnp.where(order, mine, 0), axis=1, keepdims=True)
    angle = ordered_at.astype(jnp.float32) * freq_ref[...]
    lane = lax.broadcasted_iota(jnp.int32, (rows, HEAD_SIZE), 1)
    cosine = jnp.cos(angle)
    sine = jnp.where(lane < HEAD_SIZE // 2, -1.0, 1.0) * jnp.sin(angle)
    order = jnp.where(order, 1.0, 0.0).astype(jnp.bfloat16)
    gain = gain_ref[...].astype(jnp.float32).reshape(1, width)
    step = 32
    written = []

    small_copies[-1].wait()
    for first in range(0, rows, step):
        at = slice(first, first + step)
        floats = tokens[at, :].astype(jnp.float32)
        mean = jnp.sum(floats * floats, axis=1, keepdims=True) * (1.0 / width)
        tokens[at, :] = (floats * lax.rsqrt(mean + EPSILON) * gain).astype(jnp.bfloat16)
    if chunks > 1:
        copies[1].start()
    for first in range(0, width, 512):
        columns = slice(first, first + 512)
        normed[:, columns] = dot(order, tokens[:, columns]).astype(jnp.bfloat16)
    heads = out_ref.shape[1]
    offsets = [0]
    for i in range(count):
        offsets.append(offsets[-1] + weights_hbm[i].shape[1] // heads)
    me = lax.axis_index("ctx")
    far = [
        pltpu.make_async_copy(
            out_ref.at[(me ^ distance) // members, (me ^ distance) % members], outs_hbm[1 + i], out_sems.at[chunks + i]
        )
        for i, distance in enumerate(apart)
    ]
    for j in range(chunks):
        i, first = origin[j]
        copies[j].wait()
        if j + 2 < chunks:
            copies[j + 2].start()
        product = dot(normed[...], weights[j])
        per_head = offsets[i + 1] - offsets[i]
        for u in range(0, span, HEAD_SIZE):
            values = product[:, u : u + HEAD_SIZE]
            if kinds[i]:
                values = values * cosine + pltpu.roll(values, HEAD_SIZE // 2, 1) * sine
            head, inside = divmod(first + u, per_head)
            inside += offsets[i]
            out_ref[:, head, :, inside : inside + HEAD_SIZE] = values.astype(jnp.bfloat16).reshape(
                groups, rows // groups, HEAD_SIZE
            )
        first_head, done_heads = first // per_head, max(span // per_head, 1)
        done = (pl.ds(first_head, done_heads), pl.ds(0, rows // groups))
        done += (pl.ds(offsets[i] + first % per_head, min(span, per_head)),)
        if apart:
            near = groups // 2
            source = out_ref.at[(pl.ds(me // members // near * near, near),) + done]
            written.append(pltpu.make_async_copy(source, outs_hbm[0].at[(pl.ds(0, near),) + done], out_sems.at[j]))
            written[-1].start()
        for distance in () if apart else range(groups):
            source = out_ref.at[(me // members ^ distance,) + done]
            sem = out_sems.at[j * groups + distance]
            written.append(pltpu.make_async_copy(source, outs_hbm[distance].at[done], sem))
            written[-1].start()
        if first % per_head + span >= per_head:
            for distance, copy in zip(apart, far):
                to = (me ^ distance) % members
                pl.when((to >= first_head) & (to < first_head + done_heads))(copy.start)
    for copy in written + far:
        copy.wait()


def project(positions, freq, gain, tokens, weights, kinds, devices, heads, apart=()):
    rows, width = tokens.shape
    groups = devices // heads
    columns = sum(w.shape[1] for w in weights)
    span = 512
    flops = 2 * rows * width * columns
    size = 2 * (width * columns + rows * width + rows * columns)
    piece = (rows // groups, columns // heads)
    out_shapes = [(groups // 2, heads) + piece] + [piece] * len(apart) if apart else [(heads,) + piece] * groups
    return pl.pallas_call(
        functools.partial(project_kernel, kinds, devices, heads, apart),
        out_shape=[jax.ShapeDtypeStruct(shape, jnp.bfloat16) for shape in out_shapes],
        in_specs=[IN_PLACE] * (len(weights) + 4),
        out_specs=[IN_PLACE] * len(out_shapes),
        scratch_shapes=[
            pltpu.VMEM(positions.shape, jnp.int32),
            pltpu.VMEM(freq.shape, jnp.float32),
            pltpu.VMEM(gain.shape, jnp.bfloat16),
            pltpu.VMEM((rows, width), jnp.bfloat16),
            pltpu.VMEM((rows, width), jnp.bfloat16),
            pltpu.VMEM((columns // span, width, span), jnp.bfloat16),
            pltpu.VMEM((groups, heads, rows // groups, columns // heads), jnp.bfloat16),
            pltpu.SemaphoreType.DMA((4,)),
            pltpu.SemaphoreType.DMA((columns // span,)),
            pltpu.SemaphoreType.DMA((columns // span * groups + len(apart),)),
        ],
        compiler_params=pltpu.CompilerParams(vmem_limit_bytes=56 * MIB),
        cost_estimate=pl.CostEstimate(flops=flops, bytes_accessed=size, transcendentals=0),
    )(positions, freq, gain, tokens, *weights)


def pick_kernel(members, *refs):
    pieces, outs = refs[:-members], refs[-members:]
    rows = pieces[0].shape[1]
    for distance, out_ref in enumerate(outs):
        head = lax.axis_index("ctx") % members ^ distance
        for i, piece in enumerate(pieces):
            out_ref[i * rows : (i + 1) * rows, :] = piece[head]


def pick(pieces):
    members, rows, width = pieces[0].shape
    shape = jax.ShapeDtypeStruct((len(pieces) * rows, width), jnp.bfloat16)
    return pl.pallas_call(
        functools.partial(pick_kernel, members),
        out_shape=[shape] * members,
        in_specs=[WHOLE] * len(pieces),
        out_specs=[WHOLE] * members,
        compiler_params=pltpu.CompilerParams(vmem_limit_bytes=8 * MIB),
        cost_estimate=pl.CostEstimate(
            flops=0, bytes_accessed=4 * len(pieces) * pieces[0].size, transcendentals=0
        ),
    )(*pieces)


def place_kernel(count, slot_ref, *refs):
    arrived, outs = refs[:count], refs[count:]
    slot = slot_ref[...]
    first = 0
    for out_ref in outs:
        size = out_ref.shape[0]
        slots = lax.broadcasted_iota(jnp.int32, (size, slot.shape[1]), 0) + first
        chosen = (slots == slot).astype(jnp.bfloat16)
        total = 0.0
        at = 0
        for ref in arrived:
            total += dot(chosen[:, at : at + ref.shape[0]], ref[...])
            at += ref.shape[0]
        out_ref[...] = total.astype(jnp.bfloat16)
        first += size


def place(arrived, slot, sizes):
    width = arrived[0].shape[1]
    return pl.pallas_call(
        functools.partial(place_kernel, len(arrived)),
        out_shape=[jax.ShapeDtypeStruct((size, width), jnp.bfloat16) for size in sizes],
        in_specs=[WHOLE] * (1 + len(arrived)),
        out_specs=[WHOLE] * len(sizes),
        compiler_params=pltpu.CompilerParams(vmem_limit_bytes=16 * MIB),
        cost_estimate=pl.CostEstimate(
            flops=2 * sum(sizes) * slot.shape[1] * width,
            bytes_accessed=4 * slot.shape[1] * width,
            transcendentals=0,
        ),
    )(slot, *arrived)


def taken_at(turn, members):
    distances = distances_at(turn, members)
    odd = lax.axis_index("dp") % 2
    distance = odd * distances[1] + (1 - odd) * distances[0]
    return (lax.axis_index("ctx") % members) ^ distance


def distances_at(turn, members):
    if turn in (0, members - 1):
        return (members - 1 - turn,) * 2
    return (turn, members - 1 - turn)


def attend_kernel(block, turn, members, devices, slot_ref, ends_ref, *rest):
    queries_refs, rest = rest[:-9], rest[-9:]
    pieces, out_ref, held, query_ref = rest[:6], rest[6], rest[7], rest[8]
    first = 0
    for ref in queries_refs:
        query_ref[first : first + ref.shape[0], :] = ref[...]
        first += ref.shape[0]
    target = taken_at(turn, members)
    group = lax.axis_index("ctx") // members
    starts = (group * members * block, (2 * devices - members - group * members) * block)
    last = group == devices // members - 1
    heads = query_ref.shape[1] // HEAD_SIZE
    arrived = query_ref.shape[0]
    run = arrived // 2
    per_run = run // block
    reach = REACH_BLOCKS * block
    keys = reach + block
    slot = slot_ref[...]
    ends = ends_ref[...]
    factor = jnp.float32(np.log2(np.e) / HEAD_SIZE**0.5)
    for half in range(2):
        first = 0
        for piece in pieces[3 * half : 3 * half + 3]:
            values = piece[...]
            if half == 1 and first == 0:
                values = jnp.where(last, pieces[2][...], values)
            held[half, first : first + piece.shape[0], :] = values
            first += piece.shape[0]
    indices = (target, per_run - 1 - target)
    at = [pl.multiple_of(index * block, block) for index in indices]
    iota = lax.broadcasted_iota(jnp.int32, (block, arrived), 0)
    chosen = [(iota + (at[half] + half * run) == slot).astype(jnp.bfloat16) for half in range(2)]
    queries = dot(jnp.concatenate(chosen, axis=0), query_ref[...]).astype(jnp.bfloat16)
    here = [slice(half * block, (half + 1) * block) for half in range(2)]
    scores, weights, totals = [], [], []
    for half in range(2):
        stacked = jnp.concatenate(
            [queries[here[half], h * HEAD_SIZE : (h + 1) * HEAD_SIZE] for h in range(heads)], axis=0
        )
        key = held[half, pl.ds(at[half], keys), :HEAD_SIZE]
        scores.append(
            lax.dot_general(stacked, key, (((1,), (1,)), ((), ())), preferred_element_type=jnp.float32)
        )
    for half in range(2):
        begin = starts[half] + at[half]
        query_at = lax.broadcasted_iota(jnp.int32, (block, 1), 0) + begin
        key_at = lax.broadcasted_iota(jnp.int32, (1, keys), 1) + (begin - reach)
        doc_start = jnp.max(jnp.where(ends <= query_at, ends, 0), axis=1, keepdims=True)
        allowed = (key_at >= doc_start) & (key_at <= query_at)
        masked = jnp.where(allowed[None], scores[half].reshape(heads, block, keys), jnp.float32(-1e30))
        masked = masked.reshape(heads * block, keys)
        top = jnp.max(masked, axis=1, keepdims=True)
        exact = jnp.exp2((masked - top) * factor)
        totals.append(jnp.sum(exact, axis=1, keepdims=True))
        weights.append(exact.astype(jnp.bfloat16))
    for half in range(2):
        value = held[half, pl.ds(at[half], keys), HEAD_SIZE:]
        mixed = (dot(weights[half], value) / totals[half]).astype(jnp.bfloat16)
        for h in range(heads):
            out_ref[here[half], h * HEAD_SIZE : (h + 1) * HEAD_SIZE] = mixed[h * block : (h + 1) * block]


def attend(turn, members, devices, queries, slot, ends, pieces, block):
    rows, width = slot.shape[1], queries[0].shape[1]
    held = REACH_BLOCKS * block + rows // 2
    heads = width // HEAD_SIZE
    reach = (REACH_BLOCKS + 1) * block
    return pl.pallas_call(
        functools.partial(attend_kernel, block, turn, members, devices),
        out_shape=jax.ShapeDtypeStruct((2 * block, width), jnp.bfloat16),
        in_specs=[WHOLE] * (8 + len(queries)),
        out_specs=WHOLE,
        scratch_shapes=[
            pltpu.VMEM((2, held, 2 * HEAD_SIZE), jnp.bfloat16),
            pltpu.VMEM((rows, width), jnp.bfloat16),
        ],
        compiler_params=pltpu.CompilerParams(vmem_limit_bytes=16 * MIB),
        cost_estimate=pl.CostEstimate(
            flops=2 * 2 * heads * block * reach * HEAD_SIZE * 2 + 4 * block * rows * width,
            bytes_accessed=2 * rows * width + 8 * held * HEAD_SIZE,
            transcendentals=2 * heads * block * reach,
        ),
    )(slot, ends, *queries, *pieces)


def assemble_kernel(*refs):
    pieces, out_ref = refs[:-1], refs[-1]
    width = pieces[0].shape[1]
    for turn, piece in enumerate(pieces):
        at = pl.multiple_of(taken_at(turn, len(pieces)) * width, width)
        out_ref[:, pl.ds(at, width)] = piece[...]


def assemble(pieces):
    rows, width = pieces[0].shape
    return pl.pallas_call(
        assemble_kernel,
        out_shape=jax.ShapeDtypeStruct((rows, width * len(pieces)), jnp.bfloat16),
        in_specs=[WHOLE] * len(pieces),
        out_specs=WHOLE,
        compiler_params=pltpu.CompilerParams(vmem_limit_bytes=8 * MIB),
        cost_estimate=pl.CostEstimate(
            flops=0, bytes_accessed=4 * rows * width * len(pieces), transcendentals=0
        ),
    )(*pieces)


def shards(tokens, positions, lengths, gain, w_query, w_key, value_weight):
    devices = lax.axis_size("ctx")
    device = lax.axis_index("ctx")
    rows = tokens.shape[0]
    block = rows // 2
    members = w_key.shape[1] // HEAD_SIZE
    groups = devices // members
    group = device // members
    run = members * block
    group_rows = rows // groups

    half = HEAD_SIZE // 2
    freq = np.float32(ROPE_THETA ** (-(np.arange(HEAD_SIZE) % half * 2.0 / HEAD_SIZE)))
    operands = (positions.reshape(-1, 128), jnp.asarray(freq[None, :]), gain, tokens)

    half_devices = devices // 2
    halves = [list(range(i, i + half_devices)) for i in (0, half_devices)]

    def permuted(piece, distance):
        return lax.ppermute(piece, "ctx", [(j, j ^ distance) for j in range(devices)])

    pieces = list(project(*operands, (w_key, value_weight), (True, False), devices, members))
    pieces = pieces[:1] + [permuted(piece, i * members) for i, piece in enumerate(pieces) if i]
    apart = list(range(half_devices, devices))
    near, *far = project(*operands, (w_query,), (True,), devices, members, apart)
    queries = [permuted(piece, distance) for distance, piece in zip(apart, far)]

    table = positions.reshape(devices, rows)
    ours = group_of(table, block, devices, members) == group
    first_run = group * run
    second_run = (2 * devices - members) * block - group * run
    slots = jnp.where(table // run == group, table - first_run, table - second_run + run)
    inner = jnp.arange(rows, dtype=jnp.int32)
    before = (inner[:, None] < inner[None, :]).astype(jnp.bfloat16)
    place_in = dot(ours.astype(jnp.bfloat16), before).astype(jnp.int32)
    place_in = jnp.where(ours, place_in, -1)
    wanted = jnp.arange(group_rows, dtype=jnp.int32)[None, :, None] == place_in[:, None, :]
    slot = jnp.sum(jnp.where(wanted, slots[:, None, :], 0), axis=2)
    index = jnp.arange(devices, dtype=jnp.int32)
    kv_order = (device ^ (index // groups)) ^ (index % groups * members)
    index = index[:half_devices]
    query_order = [device // half_devices * half_devices + index, device ^ (half_devices + index)]
    slots = slot[jnp.concatenate([kv_order] + query_order)].reshape(2, 1, devices * group_rows)
    kv_slot, query_slot = slots[0], slots[1]
    ends = jnp.cumsum(lengths, dtype=jnp.int32)[None, :]

    *pieces, queries[0], queries[1] = lax.optimization_barrier((*pieces, queries[0], queries[1]))
    *picked, near = lax.optimization_barrier((*pick(pieces), near))
    kv = picked[:1] + [permuted(piece, i) for i, piece in enumerate(picked) if i]
    flat = near.reshape(half_devices, group_rows, -1)
    flat = lax.all_to_all(flat, "ctx", split_axis=0, concat_axis=0, tiled=True, axis_index_groups=halves)
    kv, queries[:5] = lax.optimization_barrier((kv, queries[:5]))
    queries.insert(0, flat.reshape(half_devices * group_rows, -1))
    reach = REACH_BLOCKS * block
    sizes = [run - reach, reach] * 2
    early_head, early_tail, late_head, late_tail = place(kv, kv_slot, sizes)
    up = [(i, i + members) for i in range(devices - members)]
    down = [(i + members, i) for i in range(devices - members)]
    early_halo = lax.ppermute(early_tail, "ctx", up)
    late_halo = lax.ppermute(late_tail, "ctx", down)
    pieces = (early_halo, early_head, early_tail, late_halo, late_head, late_tail)

    results = []
    for turn in range(members):
        out = attend(turn, members, devices, queries, query_slot, ends, pieces, block)
        if turn < members - 1:
            distances = distances_at(turn, members)
            route = [
                (i * devices + j, i * devices + j // members * members + (j % members ^ distances[i % 2]))
                for i in range(lax.axis_size("dp"))
                for j in range(devices)
            ]
            out = lax.ppermute(out, ("dp", "ctx"), route)
        results.append(out)
    return assemble(results)


def solution(mesh):
    in_specs = (P(("dp", "ctx"), None), P("dp"), P("dp"), P(), P(), P(), P())
    out_specs = P(("dp", "ctx"), None)
    return jax.shard_map(shards, mesh=mesh, in_specs=in_specs, out_specs=out_specs, check_vma=False)
```

```python
import functools

import jax
import jax.numpy as jnp
import numpy as np
from jax import lax
from jax.experimental import pallas as pl
from jax.experimental.pallas import tpu as pltpu
from jax.sharding import PartitionSpec as P

HEAD_SIZE = 128
REACH_BLOCKS = 3
ROPE_THETA = 500000.0
EPSILON = 1e-05

WHOLE = pl.BlockSpec(memory_space=pltpu.VMEM)
IN_PLACE = pl.BlockSpec(memory_space=pl.ANY)
MIB = 1024 * 1024


def dot(a, b):
    return jnp.dot(a, b, preferred_element_type=jnp.float32)


def transposed(row):
    size = row.shape[1]
    here = lax.broadcasted_iota(jnp.int32, (size, size), 0)
    there = lax.broadcasted_iota(jnp.int32, (size, size), 1)
    return jnp.sum(jnp.where(here == there, row, 0), axis=1, keepdims=True)


def group_of(where_at, block, devices, members):
    block_id = where_at // block
    return jnp.minimum(block_id, 2 * devices - 1 - block_id) // members


def project_kernel(kinds, devices, members, apart, positions_hbm, freq_hbm, gain_hbm, tokens_hbm, *rest):
    count = len(kinds)
    weights_hbm, rest = rest[:count], rest[count:]
    outputs = 1 + len(apart)
    outs_hbm, rest = rest[:outputs], rest[outputs:]
    positions_ref, freq_ref, gain_ref, tokens, normed, weights, out_ref = rest[:7]
    small_sems, sems, out_sems = rest[7:]
    rows, width = normed.shape
    chunks, _, span = weights.shape
    copies, origin = [], []
    small_copies = [
        pltpu.make_async_copy(source, target, small_sems.at[i])
        for i, (source, target) in enumerate(
            [(positions_hbm, positions_ref), (freq_hbm, freq_ref), (gain_hbm, gain_ref), (tokens_hbm, tokens)]
        )
    ]
    for copy in small_copies:
        copy.start()
    for i in range(count):
        for first in range(0, weights_hbm[i].shape[1], span):
            j = len(copies)
            source = weights_hbm[i].at[:, pl.ds(first, span)]
            copies.append(pltpu.make_async_copy(source, weights.at[j], sems.at[j]))
            origin.append((i, first))
    copies[0].start()
    for copy in small_copies[:-1]:
        copy.wait()
    lanes = positions_ref.shape[1]
    stripes = rows // lanes
    mine = jnp.concatenate(
        [positions_ref[pl.ds(lax.axis_index("ctx") * stripes + i, 1), :] for i in range(stripes)], axis=1
    )
    owner = group_of(mine, rows // 2, devices, members)
    here = lax.broadcasted_iota(jnp.int32, (rows, rows), 0)
    there = lax.broadcasted_iota(jnp.int32, (rows, rows), 1)
    earlier = jnp.where((transposed(owner) == owner) & (here < there), 1, 0)
    rank = owner * (rows * members // devices) + jnp.sum(earlier, axis=0, keepdims=True)
    order = here == rank
    ordered_at = jnp.sum(jnp.where(order, mine, 0), axis=1, keepdims=True)
    angle = ordered_at.astype(jnp.float32) * freq_ref[...]
    lane = lax.broadcasted_iota(jnp.int32, (rows, HEAD_SIZE), 1)
    cosine = jnp.cos(angle)
    sine = jnp.where(lane < HEAD_SIZE // 2, -1.0, 1.0) * jnp.sin(angle)
    order = jnp.where(order, 1.0, 0.0).astype(jnp.bfloat16)
    gain = gain_ref[...].astype(jnp.float32).reshape(1, width)
    step = 32
    written = []

    small_copies[-1].wait()
    for first in range(0, rows, step):
        at = slice(first, first + step)
        floats = tokens[at, :].astype(jnp.float32)
        mean = jnp.sum(floats * floats, axis=1, keepdims=True) * (1.0 / width)
        tokens[at, :] = (floats * lax.rsqrt(mean + EPSILON) * gain).astype(jnp.bfloat16)
    if chunks > 1:
        copies[1].start()
    for first in range(0, width, 512):
        columns = slice(first, first + 512)
        normed[:, columns] = dot(order, tokens[:, columns]).astype(jnp.bfloat16)
    groups, heads = out_ref.shape[:2]
    offsets = [0]
    for i in range(count):
        offsets.append(offsets[-1] + weights_hbm[i].shape[1] // heads)
    me = lax.axis_index("ctx")
    far = [
        pltpu.make_async_copy(
            out_ref.at[(me ^ distance) // members, (me ^ distance) % members], outs_hbm[1 + i], out_sems.at[chunks + i]
        )
        for i, distance in enumerate(apart)
    ]
    for j in range(chunks):
        i, first = origin[j]
        copies[j].wait()
        if j + 2 < chunks:
            copies[j + 2].start()
        product = dot(normed[...], weights[j])
        per_head = offsets[i + 1] - offsets[i]
        for u in range(0, span, HEAD_SIZE):
            values = product[:, u : u + HEAD_SIZE]
            if kinds[i]:
                values = values * cosine + pltpu.roll(values, HEAD_SIZE // 2, 1) * sine
            head, inside = divmod(first + u, per_head)
            inside += offsets[i]
            out_ref[:, head, :, inside : inside + HEAD_SIZE] = values.astype(jnp.bfloat16).reshape(
                groups, rows // groups, HEAD_SIZE
            )
        first_head, done_heads = first // per_head, max(span // per_head, 1)
        done = (pl.ds(first_head, done_heads), pl.ds(0, rows // groups))
        done += (pl.ds(offsets[i] + first % per_head, min(span, per_head)),)
        taken = groups // 2 if apart else groups
        start = me // members // taken * taken if apart else 0
        source = out_ref.at[(pl.ds(start, taken),) + done]
        written.append(pltpu.make_async_copy(source, outs_hbm[0].at[(pl.ds(0, taken),) + done], out_sems.at[j]))
        written[-1].start()
        if first % per_head + span >= per_head:
            for distance, copy in zip(apart, far):
                to = (me ^ distance) % members
                pl.when((to >= first_head) & (to < first_head + done_heads))(copy.start)
    for copy in written + far:
        copy.wait()


def project(positions, freq, gain, tokens, weights, kinds, devices, heads, apart=()):
    rows, width = tokens.shape
    groups = devices // heads
    columns = sum(w.shape[1] for w in weights)
    span = 512
    flops = 2 * rows * width * columns
    size = 2 * (width * columns + rows * width + rows * columns)
    out_shape = (groups // 2 if apart else groups, heads, rows // groups, columns // heads)
    out_shapes = [out_shape] + [out_shape[2:]] * len(apart)
    return pl.pallas_call(
        functools.partial(project_kernel, kinds, devices, heads, apart),
        out_shape=[jax.ShapeDtypeStruct(shape, jnp.bfloat16) for shape in out_shapes],
        in_specs=[IN_PLACE] * (len(weights) + 4),
        out_specs=[IN_PLACE] * len(out_shapes),
        scratch_shapes=[
            pltpu.VMEM(positions.shape, jnp.int32),
            pltpu.VMEM(freq.shape, jnp.float32),
            pltpu.VMEM(gain.shape, jnp.bfloat16),
            pltpu.VMEM((rows, width), jnp.bfloat16),
            pltpu.VMEM((rows, width), jnp.bfloat16),
            pltpu.VMEM((columns // span, width, span), jnp.bfloat16),
            pltpu.VMEM((groups, heads, rows // groups, columns // heads), jnp.bfloat16),
            pltpu.SemaphoreType.DMA((4,)),
            pltpu.SemaphoreType.DMA((columns // span,)),
            pltpu.SemaphoreType.DMA((columns // span + len(apart),)),
        ],
        compiler_params=pltpu.CompilerParams(vmem_limit_bytes=56 * MIB),
        cost_estimate=pl.CostEstimate(flops=flops, bytes_accessed=size, transcendentals=0),
    )(positions, freq, gain, tokens, *weights)


def place_kernel(arrived_ref, slot_ref, *outs):
    rows = arrived_ref.shape[0]
    first = 0
    for out_ref in outs:
        size = out_ref.shape[0]
        slots = lax.broadcasted_iota(jnp.int32, (size, rows), 0) + first
        chosen = (slots == slot_ref[...]).astype(jnp.bfloat16)
        out_ref[...] = dot(chosen, arrived_ref[...]).astype(jnp.bfloat16)
        first += size


def place(arrived, slot, sizes):
    width = arrived.shape[1]
    return pl.pallas_call(
        place_kernel,
        out_shape=[jax.ShapeDtypeStruct((size, width), jnp.bfloat16) for size in sizes],
        in_specs=[WHOLE, WHOLE],
        out_specs=[WHOLE] * len(sizes),
        compiler_params=pltpu.CompilerParams(vmem_limit_bytes=16 * MIB),
        cost_estimate=pl.CostEstimate(
            flops=2 * sum(sizes) * arrived.shape[0] * width,
            bytes_accessed=4 * arrived.size,
            transcendentals=0,
        ),
    )(arrived, slot)


def taken_at(turn, members):
    distances = distances_at(turn, members)
    odd = lax.axis_index("dp") % 2
    distance = odd * distances[1] + (1 - odd) * distances[0]
    return (lax.axis_index("ctx") % members) ^ distance


def distances_at(turn, members):
    if turn in (0, members - 1):
        return (members - 1 - turn,) * 2
    return (turn, members - 1 - turn)


def attend_kernel(block, turn, members, devices, slot_ref, ends_ref, *rest):
    queries_refs, rest = rest[:-9], rest[-9:]
    pieces, out_ref, held, query_ref = rest[:6], rest[6], rest[7], rest[8]
    first = 0
    for ref in queries_refs:
        query_ref[first : first + ref.shape[0], :] = ref[...]
        first += ref.shape[0]
    target = taken_at(turn, members)
    group = lax.axis_index("ctx") // members
    starts = (group * members * block, (2 * devices - members - group * members) * block)
    last = group == devices // members - 1
    heads = query_ref.shape[1] // HEAD_SIZE
    arrived = query_ref.shape[0]
    run = arrived // 2
    per_run = run // block
    reach = REACH_BLOCKS * block
    keys = reach + block
    slot = slot_ref[...]
    ends = ends_ref[...]
    factor = jnp.float32(np.log2(np.e) / HEAD_SIZE**0.5)
    for half in range(2):
        first = 0
        for piece in pieces[3 * half : 3 * half + 3]:
            values = piece[...]
            if half == 1 and first == 0:
                values = jnp.where(last, pieces[2][...], values)
            held[half, first : first + piece.shape[0], :] = values
            first += piece.shape[0]
    indices = (target, per_run - 1 - target)
    at = [pl.multiple_of(index * block, block) for index in indices]
    iota = lax.broadcasted_iota(jnp.int32, (block, arrived), 0)
    chosen = [(iota + (at[half] + half * run) == slot).astype(jnp.bfloat16) for half in range(2)]
    queries = dot(jnp.concatenate(chosen, axis=0), query_ref[...]).astype(jnp.bfloat16)
    here = [slice(half * block, (half + 1) * block) for half in range(2)]
    scores, weights, totals = [], [], []
    for half in range(2):
        stacked = jnp.concatenate(
            [queries[here[half], h * HEAD_SIZE : (h + 1) * HEAD_SIZE] for h in range(heads)], axis=0
        )
        key = held[half, pl.ds(at[half], keys), :HEAD_SIZE]
        scores.append(
            lax.dot_general(stacked, key, (((1,), (1,)), ((), ())), preferred_element_type=jnp.float32)
        )
    for half in range(2):
        begin = starts[half] + at[half]
        query_at = lax.broadcasted_iota(jnp.int32, (block, 1), 0) + begin
        key_at = lax.broadcasted_iota(jnp.int32, (1, keys), 1) + (begin - reach)
        doc_start = jnp.max(jnp.where(ends <= query_at, ends, 0), axis=1, keepdims=True)
        allowed = (key_at >= doc_start) & (key_at <= query_at)
        masked = jnp.where(allowed[None], scores[half].reshape(heads, block, keys), jnp.float32(-1e30))
        masked = masked.reshape(heads * block, keys)
        top = jnp.max(masked, axis=1, keepdims=True)
        exact = jnp.exp2((masked - top) * factor)
        totals.append(jnp.sum(exact, axis=1, keepdims=True))
        weights.append(exact.astype(jnp.bfloat16))
    for half in range(2):
        value = held[half, pl.ds(at[half], keys), HEAD_SIZE:]
        mixed = (dot(weights[half], value) / totals[half]).astype(jnp.bfloat16)
        for h in range(heads):
            out_ref[here[half], h * HEAD_SIZE : (h + 1) * HEAD_SIZE] = mixed[h * block : (h + 1) * block]


def attend(turn, members, devices, queries, slot, ends, pieces, block):
    rows, width = slot.shape[1], queries[0].shape[1]
    held = REACH_BLOCKS * block + rows // 2
    heads = width // HEAD_SIZE
    reach = (REACH_BLOCKS + 1) * block
    return pl.pallas_call(
        functools.partial(attend_kernel, block, turn, members, devices),
        out_shape=jax.ShapeDtypeStruct((2 * block, width), jnp.bfloat16),
        in_specs=[WHOLE] * (8 + len(queries)),
        out_specs=WHOLE,
        scratch_shapes=[
            pltpu.VMEM((2, held, 2 * HEAD_SIZE), jnp.bfloat16),
            pltpu.VMEM((rows, width), jnp.bfloat16),
        ],
        compiler_params=pltpu.CompilerParams(vmem_limit_bytes=16 * MIB),
        cost_estimate=pl.CostEstimate(
            flops=2 * 2 * heads * block * reach * HEAD_SIZE * 2 + 4 * block * rows * width,
            bytes_accessed=2 * rows * width + 8 * held * HEAD_SIZE,
            transcendentals=2 * heads * block * reach,
        ),
    )(slot, ends, *queries, *pieces)


def assemble_kernel(*refs):
    pieces, out_ref = refs[:-1], refs[-1]
    width = pieces[0].shape[1]
    for turn, piece in enumerate(pieces):
        at = pl.multiple_of(taken_at(turn, len(pieces)) * width, width)
        out_ref[:, pl.ds(at, width)] = piece[...]


def assemble(pieces):
    rows, width = pieces[0].shape
    return pl.pallas_call(
        assemble_kernel,
        out_shape=jax.ShapeDtypeStruct((rows, width * len(pieces)), jnp.bfloat16),
        in_specs=[WHOLE] * len(pieces),
        out_specs=WHOLE,
        compiler_params=pltpu.CompilerParams(vmem_limit_bytes=8 * MIB),
        cost_estimate=pl.CostEstimate(
            flops=0, bytes_accessed=4 * rows * width * len(pieces), transcendentals=0
        ),
    )(*pieces)


def shards(tokens, positions, lengths, gain, w_query, w_key, value_weight):
    devices = lax.axis_size("ctx")
    device = lax.axis_index("ctx")
    rows = tokens.shape[0]
    block = rows // 2
    members = w_key.shape[1] // HEAD_SIZE
    groups = devices // members
    group = device // members
    run = members * block
    group_rows = rows // groups

    half = HEAD_SIZE // 2
    freq = np.float32(ROPE_THETA ** (-(np.arange(HEAD_SIZE) % half * 2.0 / HEAD_SIZE)))
    operands = (positions.reshape(-1, 128), jnp.asarray(freq[None, :]), gain, tokens)

    half_devices = devices // 2
    halves = [list(range(i, i + half_devices)) for i in (0, half_devices)]

    def exchange(ordered, among):
        width = ordered.shape[3]
        flat = ordered.reshape(-1, group_rows, width)
        flat = lax.all_to_all(flat, "ctx", split_axis=0, concat_axis=0, tiled=True, axis_index_groups=among)
        return flat.reshape(-1, width)

    (kv,) = project(*operands, (w_key, value_weight), (True, False), devices, members)
    kv = exchange(kv, None)
    apart = list(range(half_devices, devices))
    near, *far = project(*operands, (w_query,), (True,), devices, members, apart)
    def to_other_half(piece, i):
        return lax.ppermute(piece, "ctx", [(j, j ^ (half_devices + i)) for j in range(devices)])

    held_back = 2
    queries = [to_other_half(piece, i) for i, piece in enumerate(far[:-held_back])]

    table = positions.reshape(devices, rows)
    ours = group_of(table, block, devices, members) == group
    first_run = group * run
    second_run = (2 * devices - members) * block - group * run
    slots = jnp.where(table // run == group, table - first_run, table - second_run + run)
    inner = jnp.arange(rows, dtype=jnp.int32)
    before = (inner[:, None] < inner[None, :]).astype(jnp.bfloat16)
    place_in = dot(ours.astype(jnp.bfloat16), before).astype(jnp.int32)
    place_in = jnp.where(ours, place_in, -1)
    wanted = jnp.arange(group_rows, dtype=jnp.int32)[None, :, None] == place_in[:, None, :]
    slot = jnp.sum(jnp.where(wanted, slots[:, None, :], 0), axis=2)
    index = jnp.arange(half_devices, dtype=jnp.int32)
    sources = [device // half_devices * half_devices + index, device ^ (half_devices + index)]
    query_slot = slot[jnp.concatenate(sources)].reshape(1, devices * group_rows)
    slot = slot.reshape(1, devices * group_rows)
    ends = jnp.cumsum(lengths, dtype=jnp.int32)[None, :]

    kv, near = lax.optimization_barrier((kv, near))
    queries.insert(0, exchange(near, halves))
    kv, *queries[1:6] = lax.optimization_barrier((kv, *queries[1:6]))
    reach = REACH_BLOCKS * block
    sizes = [run - reach, reach] * 2
    early_head, early_tail, late_head, late_tail = place(kv, slot, sizes)
    *late, early_tail, late_tail = lax.optimization_barrier((*far[-held_back:], early_tail, late_tail))
    up = [(i, i + members) for i in range(devices - members)]
    down = [(i + members, i) for i in range(devices - members)]
    early_halo = lax.ppermute(early_tail, "ctx", up)
    late_halo = lax.ppermute(late_tail, "ctx", down)
    for i, piece in enumerate(late):
        queries.append(to_other_half(piece, len(far) - held_back + i))
    pieces = (early_halo, early_head, early_tail, late_halo, late_head, late_tail)

    results = []
    for turn in range(members):
        out = attend(turn, members, devices, queries, query_slot, ends, pieces, block)
        if turn < members - 1:
            distances = distances_at(turn, members)
            route = [
                (i * devices + j, i * devices + j // members * members + (j % members ^ distances[i % 2]))
                for i in range(lax.axis_size("dp"))
                for j in range(devices)
            ]
            out = lax.ppermute(out, ("dp", "ctx"), route)
        results.append(out)
    return assemble(results)


def solution(mesh):
    in_specs = (P(("dp", "ctx"), None), P("dp"), P("dp"), P(), P(), P(), P())
    out_specs = P(("dp", "ctx"), None)
    return jax.shard_map(shards, mesh=mesh, in_specs=in_specs, out_specs=out_specs, check_vma=False)
```

```python
import functools

import jax
import jax.numpy as jnp
import numpy as np
from jax import lax
from jax.experimental import pallas as pl
from jax.experimental.pallas import tpu as pltpu
from jax.sharding import PartitionSpec as P

HEAD_SIZE = 128
REACH_BLOCKS = 3
ROPE_THETA = 500000.0
EPSILON = 1e-05

WHOLE = pl.BlockSpec(memory_space=pltpu.VMEM)
IN_PLACE = pl.BlockSpec(memory_space=pl.ANY)
MIB = 1024 * 1024


def dot(a, b):
    return jnp.dot(a, b, preferred_element_type=jnp.float32)


def transposed(row):
    size = row.shape[1]
    here = lax.broadcasted_iota(jnp.int32, (size, size), 0)
    there = lax.broadcasted_iota(jnp.int32, (size, size), 1)
    return jnp.sum(jnp.where(here == there, row, 0), axis=1, keepdims=True)


def group_of(where_at, block, devices, members):
    block_id = where_at // block
    return jnp.minimum(block_id, 2 * devices - 1 - block_id) // members


def project_kernel(kinds, devices, members, apart, positions_hbm, freq_hbm, gain_hbm, tokens_hbm, *rest):
    count = len(kinds)
    weights_hbm, rest = rest[:count], rest[count:]
    outputs = 1 + len(apart)
    outs_hbm, rest = rest[:outputs], rest[outputs:]
    positions_ref, freq_ref, gain_ref, tokens, normed, weights, out_ref = rest[:7]
    small_sems, sems, out_sems = rest[7:]
    rows, width = normed.shape
    chunks, _, span = weights.shape
    copies, origin = [], []
    small_copies = [
        pltpu.make_async_copy(source, target, small_sems.at[i])
        for i, (source, target) in enumerate(
            [(positions_hbm, positions_ref), (freq_hbm, freq_ref), (gain_hbm, gain_ref), (tokens_hbm, tokens)]
        )
    ]
    for copy in small_copies:
        copy.start()
    for i in range(count):
        for first in range(0, weights_hbm[i].shape[1], span):
            j = len(copies)
            source = weights_hbm[i].at[:, pl.ds(first, span)]
            copies.append(pltpu.make_async_copy(source, weights.at[j], sems.at[j]))
            origin.append((i, first))
    copies[0].start()
    for copy in small_copies[:-1]:
        copy.wait()
    lanes = positions_ref.shape[1]
    stripes = rows // lanes
    mine = jnp.concatenate(
        [positions_ref[pl.ds(lax.axis_index("ctx") * stripes + i, 1), :] for i in range(stripes)], axis=1
    )
    owner = group_of(mine, rows // 2, devices, members)
    here = lax.broadcasted_iota(jnp.int32, (rows, rows), 0)
    there = lax.broadcasted_iota(jnp.int32, (rows, rows), 1)
    earlier = jnp.where((transposed(owner) == owner) & (here < there), 1, 0)
    rank = owner * (rows * members // devices) + jnp.sum(earlier, axis=0, keepdims=True)
    order = here == rank
    ordered_at = jnp.sum(jnp.where(order, mine, 0), axis=1, keepdims=True)
    angle = ordered_at.astype(jnp.float32) * freq_ref[...]
    lane = lax.broadcasted_iota(jnp.int32, (rows, HEAD_SIZE), 1)
    cosine = jnp.cos(angle)
    sine = jnp.where(lane < HEAD_SIZE // 2, -1.0, 1.0) * jnp.sin(angle)
    order = jnp.where(order, 1.0, 0.0).astype(jnp.bfloat16)
    gain = gain_ref[...].astype(jnp.float32).reshape(1, width)
    step = 32
    written = []

    small_copies[-1].wait()
    for first in range(0, rows, step):
        at = slice(first, first + step)
        floats = tokens[at, :].astype(jnp.float32)
        mean = jnp.sum(floats * floats, axis=1, keepdims=True) * (1.0 / width)
        tokens[at, :] = (floats * lax.rsqrt(mean + EPSILON) * gain).astype(jnp.bfloat16)
    if chunks > 1:
        copies[1].start()
    for first in range(0, width, 512):
        columns = slice(first, first + 512)
        normed[:, columns] = dot(order, tokens[:, columns]).astype(jnp.bfloat16)
    groups, heads = out_ref.shape[:2]
    offsets = [0]
    for i in range(count):
        offsets.append(offsets[-1] + weights_hbm[i].shape[1] // heads)
    me = lax.axis_index("ctx")
    far = [
        pltpu.make_async_copy(
            out_ref.at[(me ^ distance) // members, (me ^ distance) % members], outs_hbm[1 + i], out_sems.at[chunks + i]
        )
        for i, distance in enumerate(apart)
    ]
    for j in range(chunks):
        i, first = origin[j]
        copies[j].wait()
        if j + 2 < chunks:
            copies[j + 2].start()
        product = dot(normed[...], weights[j])
        per_head = offsets[i + 1] - offsets[i]
        for u in range(0, span, HEAD_SIZE):
            values = product[:, u : u + HEAD_SIZE]
            if kinds[i]:
                values = values * cosine + pltpu.roll(values, HEAD_SIZE // 2, 1) * sine
            head, inside = divmod(first + u, per_head)
            inside += offsets[i]
            out_ref[:, head, :, inside : inside + HEAD_SIZE] = values.astype(jnp.bfloat16).reshape(
                groups, rows // groups, HEAD_SIZE
            )
        first_head, done_heads = first // per_head, max(span // per_head, 1)
        done = (pl.ds(first_head, done_heads), pl.ds(0, rows // groups))
        done += (pl.ds(offsets[i] + first % per_head, min(span, per_head)),)
        taken = groups // 2 if apart else groups
        start = me // members // taken * taken if apart else 0
        source = out_ref.at[(pl.ds(start, taken),) + done]
        written.append(pltpu.make_async_copy(source, outs_hbm[0].at[(pl.ds(0, taken),) + done], out_sems.at[j]))
        written[-1].start()
        if first % per_head + span >= per_head:
            for distance, copy in zip(apart, far):
                to = (me ^ distance) % members
                pl.when((to >= first_head) & (to < first_head + done_heads))(copy.start)
    for copy in written + far:
        copy.wait()


def project(positions, freq, gain, tokens, weights, kinds, devices, heads, apart=()):
    rows, width = tokens.shape
    groups = devices // heads
    columns = sum(w.shape[1] for w in weights)
    span = 512
    flops = 2 * rows * width * columns
    size = 2 * (width * columns + rows * width + rows * columns)
    out_shape = (groups // 2 if apart else groups, heads, rows // groups, columns // heads)
    out_shapes = [out_shape] + [out_shape[2:]] * len(apart)
    return pl.pallas_call(
        functools.partial(project_kernel, kinds, devices, heads, apart),
        out_shape=[jax.ShapeDtypeStruct(shape, jnp.bfloat16) for shape in out_shapes],
        in_specs=[IN_PLACE] * (len(weights) + 4),
        out_specs=[IN_PLACE] * len(out_shapes),
        scratch_shapes=[
            pltpu.VMEM(positions.shape, jnp.int32),
            pltpu.VMEM(freq.shape, jnp.float32),
            pltpu.VMEM(gain.shape, jnp.bfloat16),
            pltpu.VMEM((rows, width), jnp.bfloat16),
            pltpu.VMEM((rows, width), jnp.bfloat16),
            pltpu.VMEM((columns // span, width, span), jnp.bfloat16),
            pltpu.VMEM((groups, heads, rows // groups, columns // heads), jnp.bfloat16),
            pltpu.SemaphoreType.DMA((4,)),
            pltpu.SemaphoreType.DMA((columns // span,)),
            pltpu.SemaphoreType.DMA((columns // span + len(apart),)),
        ],
        compiler_params=pltpu.CompilerParams(vmem_limit_bytes=56 * MIB),
        cost_estimate=pl.CostEstimate(flops=flops, bytes_accessed=size, transcendentals=0),
    )(positions, freq, gain, tokens, *weights)


def place_kernel(count, slot_ref, *refs):
    pieces, outs, arrived = refs[:count], refs[count:-1], refs[-1]
    rows = arrived.shape[0]
    slot = slot_ref[...]
    first = 0
    for piece in pieces:
        arrived[first : first + piece.shape[0], :] = piece[...]
        first += piece.shape[0]
    first = 0
    for out_ref in outs:
        size = out_ref.shape[0]
        slots = lax.broadcasted_iota(jnp.int32, (size, rows), 0) + first
        chosen = (slots == slot).astype(jnp.bfloat16)
        out_ref[...] = dot(chosen, arrived[...]).astype(jnp.bfloat16)
        first += size


def place(pieces, slot, sizes):
    rows, width = slot.shape[1], pieces[0].shape[1]
    return pl.pallas_call(
        functools.partial(place_kernel, len(pieces)),
        out_shape=[jax.ShapeDtypeStruct((size, width), jnp.bfloat16) for size in sizes],
        in_specs=[WHOLE] * (1 + len(pieces)),
        out_specs=[WHOLE] * len(sizes),
        scratch_shapes=[pltpu.VMEM((rows, width), jnp.bfloat16)],
        compiler_params=pltpu.CompilerParams(vmem_limit_bytes=16 * MIB),
        cost_estimate=pl.CostEstimate(
            flops=2 * sum(sizes) * rows * width,
            bytes_accessed=4 * rows * width,
            transcendentals=0,
        ),
    )(slot, *pieces)


def taken_at(turn, members):
    distances = distances_at(turn, members)
    odd = lax.axis_index("dp") % 2
    distance = odd * distances[1] + (1 - odd) * distances[0]
    return (lax.axis_index("ctx") % members) ^ distance


def distances_at(turn, members):
    if turn in (0, members - 1):
        return (members - 1 - turn,) * 2
    return (turn, members - 1 - turn)


def attend_kernel(block, turn, members, devices, ends_ref, query_ref, *rest):
    pieces, out_ref, held = rest[:6], rest[6], rest[7]
    target = taken_at(turn, members)
    group = lax.axis_index("ctx") // members
    starts = (group * members * block, (2 * devices - members - group * members) * block)
    last = group == devices // members - 1
    heads = query_ref.shape[1] // HEAD_SIZE
    run = query_ref.shape[0] // 2
    per_run = run // block
    reach = REACH_BLOCKS * block
    keys = reach + block
    ends = ends_ref[...]
    factor = jnp.float32(np.log2(np.e) / HEAD_SIZE**0.5)
    for half in range(2):
        first = 0
        for piece in pieces[3 * half : 3 * half + 3]:
            values = piece[...]
            if half == 1 and first == 0:
                values = jnp.where(last, pieces[2][...], values)
            held[half, first : first + piece.shape[0], :] = values
            first += piece.shape[0]
    indices = (target, per_run - 1 - target)
    at = [pl.multiple_of(index * block, block) for index in indices]
    here = [slice(half * block, (half + 1) * block) for half in range(2)]
    scores, weights, totals = [], [], []
    for half in range(2):
        query = query_ref[pl.ds(pl.multiple_of(at[half] + half * run, block), block), :]
        stacked = jnp.concatenate([query[:, h * HEAD_SIZE : (h + 1) * HEAD_SIZE] for h in range(heads)], axis=0)
        key = held[half, pl.ds(at[half], keys), :HEAD_SIZE]
        scores.append(
            lax.dot_general(stacked, key, (((1,), (1,)), ((), ())), preferred_element_type=jnp.float32)
        )
    for half in range(2):
        begin = starts[half] + at[half]
        query_at = lax.broadcasted_iota(jnp.int32, (block, 1), 0) + begin
        key_at = lax.broadcasted_iota(jnp.int32, (1, keys), 1) + (begin - reach)
        doc_start = jnp.max(jnp.where(ends <= query_at, ends, 0), axis=1, keepdims=True)
        allowed = (key_at >= doc_start) & (key_at <= query_at)
        masked = jnp.where(allowed[None], scores[half].reshape(heads, block, keys), jnp.float32(-1e30))
        masked = masked.reshape(heads * block, keys)
        top = jnp.max(masked, axis=1, keepdims=True)
        exact = jnp.exp2((masked - top) * factor)
        totals.append(jnp.sum(exact, axis=1, keepdims=True))
        weights.append(exact.astype(jnp.bfloat16))
    for half in range(2):
        value = held[half, pl.ds(at[half], keys), HEAD_SIZE:]
        mixed = (dot(weights[half], value) / totals[half]).astype(jnp.bfloat16)
        for h in range(heads):
            out_ref[here[half], h * HEAD_SIZE : (h + 1) * HEAD_SIZE] = mixed[h * block : (h + 1) * block]


def attend(turn, members, devices, query, ends, pieces, block):
    rows, width = query.shape
    held = REACH_BLOCKS * block + rows // 2
    heads = width // HEAD_SIZE
    reach = (REACH_BLOCKS + 1) * block
    return pl.pallas_call(
        functools.partial(attend_kernel, block, turn, members, devices),
        out_shape=jax.ShapeDtypeStruct((2 * block, width), jnp.bfloat16),
        in_specs=[WHOLE] * 8,
        out_specs=WHOLE,
        scratch_shapes=[pltpu.VMEM((2, held, 2 * HEAD_SIZE), jnp.bfloat16)],
        compiler_params=pltpu.CompilerParams(vmem_limit_bytes=16 * MIB),
        cost_estimate=pl.CostEstimate(
            flops=2 * 2 * heads * block * reach * HEAD_SIZE * 2,
            bytes_accessed=2 * rows * width + 8 * held * HEAD_SIZE,
            transcendentals=2 * heads * block * reach,
        ),
    )(ends, query, *pieces)


def assemble_kernel(*refs):
    pieces, out_ref = refs[:-1], refs[-1]
    width = pieces[0].shape[1]
    for turn, piece in enumerate(pieces):
        at = pl.multiple_of(taken_at(turn, len(pieces)) * width, width)
        out_ref[:, pl.ds(at, width)] = piece[...]


def assemble(pieces):
    rows, width = pieces[0].shape
    return pl.pallas_call(
        assemble_kernel,
        out_shape=jax.ShapeDtypeStruct((rows, width * len(pieces)), jnp.bfloat16),
        in_specs=[WHOLE] * len(pieces),
        out_specs=WHOLE,
        compiler_params=pltpu.CompilerParams(vmem_limit_bytes=8 * MIB),
        cost_estimate=pl.CostEstimate(
            flops=0, bytes_accessed=4 * rows * width * len(pieces), transcendentals=0
        ),
    )(*pieces)


def shards(tokens, positions, lengths, gain, w_query, w_key, value_weight):
    devices = lax.axis_size("ctx")
    device = lax.axis_index("ctx")
    rows = tokens.shape[0]
    block = rows // 2
    members = w_key.shape[1] // HEAD_SIZE
    groups = devices // members
    group = device // members
    run = members * block
    group_rows = rows // groups

    half = HEAD_SIZE // 2
    freq = np.float32(ROPE_THETA ** (-(np.arange(HEAD_SIZE) % half * 2.0 / HEAD_SIZE)))
    operands = (positions.reshape(-1, 128), jnp.asarray(freq[None, :]), gain, tokens)

    half_devices = devices // 2
    halves = [list(range(i, i + half_devices)) for i in (0, half_devices)]

    def exchange(ordered, among):
        width = ordered.shape[3]
        flat = ordered.reshape(-1, group_rows, width)
        flat = lax.all_to_all(flat, "ctx", split_axis=0, concat_axis=0, tiled=True, axis_index_groups=among)
        return flat.reshape(-1, width)

    (kv,) = project(*operands, (w_key, value_weight), (True, False), devices, members)
    kv = exchange(kv, None)
    apart = list(range(half_devices, devices))
    near, *far = project(*operands, (w_query,), (True,), devices, members, apart)
    queries = []
    for i, piece in enumerate(far):
        distance = half_devices + i
        queries.append(lax.ppermute(piece, "ctx", [(j, j ^ distance) for j in range(devices)]))

    table = positions.reshape(devices, rows)
    ours = group_of(table, block, devices, members) == group
    first_run = group * run
    second_run = (2 * devices - members) * block - group * run
    slots = jnp.where(table // run == group, table - first_run, table - second_run + run)
    inner = jnp.arange(rows, dtype=jnp.int32)
    before = (inner[:, None] < inner[None, :]).astype(jnp.bfloat16)
    place_in = dot(ours.astype(jnp.bfloat16), before).astype(jnp.int32)
    place_in = jnp.where(ours, place_in, -1)
    wanted = jnp.arange(group_rows, dtype=jnp.int32)[None, :, None] == place_in[:, None, :]
    slot = jnp.sum(jnp.where(wanted, slots[:, None, :], 0), axis=2)
    index = jnp.arange(half_devices, dtype=jnp.int32)
    sources = [device // half_devices * half_devices + index, device ^ (half_devices + index)]
    query_slot = slot[jnp.concatenate(sources)].reshape(1, devices * group_rows)
    slot = slot.reshape(1, devices * group_rows)
    ends = jnp.cumsum(lengths, dtype=jnp.int32)[None, :]

    kv, near = lax.optimization_barrier((kv, near))
    queries.insert(0, exchange(near, halves))
    kv, *queries[1:6] = lax.optimization_barrier((kv, *queries[1:6]))
    reach = REACH_BLOCKS * block
    sizes = [run - reach, reach] * 2
    early_head, early_tail, late_head, late_tail = place([kv], slot, sizes)
    up = [(i, i + members) for i in range(devices - members)]
    down = [(i + members, i) for i in range(devices - members)]
    early_halo = lax.ppermute(early_tail, "ctx", up)
    late_halo = lax.ppermute(late_tail, "ctx", down)
    pieces = (early_halo, early_head, early_tail, late_halo, late_head, late_tail)

    (query,) = place(queries, query_slot, [2 * run])
    results = []
    for turn in range(members):
        out = attend(turn, members, devices, query, ends, pieces, block)
        if turn < members - 1:
            distances = distances_at(turn, members)
            route = [
                (i * devices + j, i * devices + j // members * members + (j % members ^ distances[i % 2]))
                for i in range(lax.axis_size("dp"))
                for j in range(devices)
            ]
            out = lax.ppermute(out, ("dp", "ctx"), route)
        results.append(out)
    return assemble(results)


def solution(mesh):
    in_specs = (P(("dp", "ctx"), None), P("dp"), P("dp"), P(), P(), P(), P())
    out_specs = P(("dp", "ctx"), None)
    return jax.shard_map(shards, mesh=mesh, in_specs=in_specs, out_specs=out_specs, check_vma=False)
```

```python
import functools

import jax
import jax.numpy as jnp
import numpy as np
from jax import lax
from jax.experimental import pallas as pl
from jax.experimental.pallas import tpu as pltpu
from jax.sharding import PartitionSpec as P

HEAD_SIZE = 128
REACH_BLOCKS = 3
ROPE_THETA = 500000.0
EPSILON = 1e-05

WHOLE = pl.BlockSpec(memory_space=pltpu.VMEM)
IN_PLACE = pl.BlockSpec(memory_space=pl.ANY)
MIB = 1024 * 1024


def dot(a, b):
    return jnp.dot(a, b, preferred_element_type=jnp.float32)


def transposed(row):
    size = row.shape[1]
    here = lax.broadcasted_iota(jnp.int32, (size, size), 0)
    there = lax.broadcasted_iota(jnp.int32, (size, size), 1)
    return jnp.sum(jnp.where(here == there, row, 0), axis=1, keepdims=True)


def group_of(where_at, block, devices, members):
    block_id = where_at // block
    return jnp.minimum(block_id, 2 * devices - 1 - block_id) // members


def project_kernel(kinds, devices, members, apart, positions_hbm, freq_hbm, gain_hbm, tokens_hbm, *rest):
    count = len(kinds)
    weights_hbm, rest = rest[:count], rest[count:]
    outputs = 1 + len(apart)
    outs_hbm, rest = rest[:outputs], rest[outputs:]
    positions_ref, freq_ref, gain_ref, tokens, normed, weights, out_ref = rest[:7]
    small_sems, sems, out_sems = rest[7:]
    rows, width = normed.shape
    chunks, _, span = weights.shape
    copies, origin = [], []
    small_copies = [
        pltpu.make_async_copy(source, target, small_sems.at[i])
        for i, (source, target) in enumerate(
            [(positions_hbm, positions_ref), (freq_hbm, freq_ref), (gain_hbm, gain_ref), (tokens_hbm, tokens)]
        )
    ]
    for copy in small_copies:
        copy.start()
    for i in range(count):
        for first in range(0, weights_hbm[i].shape[1], span):
            j = len(copies)
            source = weights_hbm[i].at[:, pl.ds(first, span)]
            copies.append(pltpu.make_async_copy(source, weights.at[j], sems.at[j]))
            origin.append((i, first))
    copies[0].start()
    for copy in small_copies[:-1]:
        copy.wait()
    lanes = positions_ref.shape[1]
    stripes = rows // lanes
    mine = jnp.concatenate(
        [positions_ref[pl.ds(lax.axis_index("ctx") * stripes + i, 1), :] for i in range(stripes)], axis=1
    )
    owner = group_of(mine, rows // 2, devices, members)
    here = lax.broadcasted_iota(jnp.int32, (rows, rows), 0)
    there = lax.broadcasted_iota(jnp.int32, (rows, rows), 1)
    earlier = jnp.where((transposed(owner) == owner) & (here < there), 1, 0)
    rank = owner * (rows * members // devices) + jnp.sum(earlier, axis=0, keepdims=True)
    order = here == rank
    ordered_at = jnp.sum(jnp.where(order, mine, 0), axis=1, keepdims=True)
    angle = ordered_at.astype(jnp.float32) * freq_ref[...]
    lane = lax.broadcasted_iota(jnp.int32, (rows, HEAD_SIZE), 1)
    cosine = jnp.cos(angle)
    sine = jnp.where(lane < HEAD_SIZE // 2, -1.0, 1.0) * jnp.sin(angle)
    order = jnp.where(order, 1.0, 0.0).astype(jnp.bfloat16)
    gain = gain_ref[...].astype(jnp.float32).reshape(1, width)
    step = 32
    written = []

    small_copies[-1].wait()
    for first in range(0, rows, step):
        at = slice(first, first + step)
        floats = tokens[at, :].astype(jnp.float32)
        mean = jnp.sum(floats * floats, axis=1, keepdims=True) * (1.0 / width)
        tokens[at, :] = (floats * lax.rsqrt(mean + EPSILON) * gain).astype(jnp.bfloat16)
    if chunks > 1:
        copies[1].start()
    for first in range(0, width, 512):
        columns = slice(first, first + 512)
        normed[:, columns] = dot(order, tokens[:, columns]).astype(jnp.bfloat16)
    groups, heads = out_ref.shape[:2]
    offsets = [0]
    for i in range(count):
        offsets.append(offsets[-1] + weights_hbm[i].shape[1] // heads)
    me = lax.axis_index("ctx")
    far = [
        pltpu.make_async_copy(
            out_ref.at[(me ^ distance) // members, (me ^ distance) % members], outs_hbm[1 + i], out_sems.at[chunks + i]
        )
        for i, distance in enumerate(apart)
    ]
    for j in range(chunks):
        i, first = origin[j]
        copies[j].wait()
        if j + 2 < chunks:
            copies[j + 2].start()
        product = dot(normed[...], weights[j])
        per_head = offsets[i + 1] - offsets[i]
        for u in range(0, span, HEAD_SIZE):
            values = product[:, u : u + HEAD_SIZE]
            if kinds[i]:
                values = values * cosine + pltpu.roll(values, HEAD_SIZE // 2, 1) * sine
            head, inside = divmod(first + u, per_head)
            inside += offsets[i]
            out_ref[:, head, :, inside : inside + HEAD_SIZE] = values.astype(jnp.bfloat16).reshape(
                groups, rows // groups, HEAD_SIZE
            )
        first_head, done_heads = first // per_head, max(span // per_head, 1)
        done = (pl.ds(first_head, done_heads), pl.ds(0, rows // groups))
        done += (pl.ds(offsets[i] + first % per_head, min(span, per_head)),)
        taken = groups // 2 if apart else groups
        start = me // members // taken * taken if apart else 0
        source = out_ref.at[(pl.ds(start, taken),) + done]
        written.append(pltpu.make_async_copy(source, outs_hbm[0].at[(pl.ds(0, taken),) + done], out_sems.at[j]))
        written[-1].start()
        if first % per_head + span >= per_head:
            for distance, copy in zip(apart, far):
                to = (me ^ distance) % members
                pl.when((to >= first_head) & (to < first_head + done_heads))(copy.start)
    for copy in written + far:
        copy.wait()


def project(positions, freq, gain, tokens, weights, kinds, devices, heads, apart=()):
    rows, width = tokens.shape
    groups = devices // heads
    columns = sum(w.shape[1] for w in weights)
    span = 512
    flops = 2 * rows * width * columns
    size = 2 * (width * columns + rows * width + rows * columns)
    out_shape = (groups // 2 if apart else groups, heads, rows // groups, columns // heads)
    out_shapes = [out_shape] + [out_shape[2:]] * len(apart)
    return pl.pallas_call(
        functools.partial(project_kernel, kinds, devices, heads, apart),
        out_shape=[jax.ShapeDtypeStruct(shape, jnp.bfloat16) for shape in out_shapes],
        in_specs=[IN_PLACE] * (len(weights) + 4),
        out_specs=[IN_PLACE] * len(out_shapes),
        scratch_shapes=[
            pltpu.VMEM(positions.shape, jnp.int32),
            pltpu.VMEM(freq.shape, jnp.float32),
            pltpu.VMEM(gain.shape, jnp.bfloat16),
            pltpu.VMEM((rows, width), jnp.bfloat16),
            pltpu.VMEM((rows, width), jnp.bfloat16),
            pltpu.VMEM((columns // span, width, span), jnp.bfloat16),
            pltpu.VMEM((groups, heads, rows // groups, columns // heads), jnp.bfloat16),
            pltpu.SemaphoreType.DMA((4,)),
            pltpu.SemaphoreType.DMA((columns // span,)),
            pltpu.SemaphoreType.DMA((columns // span + len(apart),)),
        ],
        compiler_params=pltpu.CompilerParams(vmem_limit_bytes=56 * MIB),
        cost_estimate=pl.CostEstimate(flops=flops, bytes_accessed=size, transcendentals=0),
    )(positions, freq, gain, tokens, *weights)


def place_kernel(count, members, slot_ref, *refs):
    pieces, outs, arrived = refs[:count], refs[count:-1], refs[-1]
    rows = arrived.shape[0]
    slot = slot_ref[...]
    first = 0
    for piece in pieces:
        arrived[first : first + piece.shape[0], :] = piece[...]
        first += piece.shape[0]
    if members:
        outs, (even_ref, odd_ref) = outs[:-2], outs[-2:]
    first = 0
    for out_ref in outs:
        size = out_ref.shape[0]
        slots = lax.broadcasted_iota(jnp.int32, (size, rows), 0) + first
        chosen = (slots == slot).astype(jnp.bfloat16)
        out_ref[...] = dot(chosen, arrived[...]).astype(jnp.bfloat16)
        first += size
    if members:
        even = lax.axis_index("ctx") // members % 2 == 0
        early, late = outs[1][...], outs[3][...]
        even_ref[...] = jnp.where(even, early, late)
        odd_ref[...] = jnp.where(even, late, early)


def place(pieces, slot, sizes, members=0):
    rows, width = slot.shape[1], pieces[0].shape[1]
    out_sizes = sizes + [sizes[1], sizes[3]] if members else sizes
    return pl.pallas_call(
        functools.partial(place_kernel, len(pieces), members),
        out_shape=[jax.ShapeDtypeStruct((size, width), jnp.bfloat16) for size in out_sizes],
        in_specs=[WHOLE] * (1 + len(pieces)),
        out_specs=[WHOLE] * len(out_sizes),
        scratch_shapes=[pltpu.VMEM((rows, width), jnp.bfloat16)],
        compiler_params=pltpu.CompilerParams(vmem_limit_bytes=16 * MIB),
        cost_estimate=pl.CostEstimate(
            flops=2 * sum(sizes) * rows * width,
            bytes_accessed=4 * rows * width,
            transcendentals=0,
        ),
    )(slot, *pieces)


def taken_at(turn, members):
    distances = distances_at(turn, members)
    odd = lax.axis_index("dp") % 2
    distance = odd * distances[1] + (1 - odd) * distances[0]
    return (lax.axis_index("ctx") % members) ^ distance


def distances_at(turn, members):
    if turn in (0, members - 1):
        return (members - 1 - turn,) * 2
    return (turn, members - 1 - turn)


def attend_kernel(block, turn, members, devices, ends_ref, query_ref, *rest):
    pieces, out_ref, held = rest[:6], rest[6], rest[7]
    target = taken_at(turn, members)
    group = lax.axis_index("ctx") // members
    starts = (group * members * block, (2 * devices - members - group * members) * block)
    last = group == devices // members - 1
    heads = query_ref.shape[1] // HEAD_SIZE
    run = query_ref.shape[0] // 2
    per_run = run // block
    reach = REACH_BLOCKS * block
    keys = reach + block
    ends = ends_ref[...]
    factor = jnp.float32(np.log2(np.e) / HEAD_SIZE**0.5)
    from_even, from_odd, early_head, early_tail, late_head, late_tail = pieces
    second = 1 - group % 2
    held[second, :reach, :] = from_even[...]
    held[1 - second, :reach, :] = jnp.where(last, early_tail[...], from_odd[...])
    for half, (head, tail) in enumerate([(early_head, early_tail), (late_head, late_tail)]):
        cut = reach + head.shape[0]
        held[half, reach:cut, :] = head[...]
        held[half, cut:, :] = tail[...]
    indices = (target, per_run - 1 - target)
    at = [pl.multiple_of(index * block, block) for index in indices]
    here = [slice(half * block, (half + 1) * block) for half in range(2)]
    scores, weights, totals = [], [], []
    for half in range(2):
        query = query_ref[pl.ds(pl.multiple_of(at[half] + half * run, block), block), :]
        stacked = jnp.concatenate([query[:, h * HEAD_SIZE : (h + 1) * HEAD_SIZE] for h in range(heads)], axis=0)
        key = held[half, pl.ds(at[half], keys), :HEAD_SIZE]
        scores.append(
            lax.dot_general(stacked, key, (((1,), (1,)), ((), ())), preferred_element_type=jnp.float32)
        )
    for half in range(2):
        begin = starts[half] + at[half]
        query_at = lax.broadcasted_iota(jnp.int32, (block, 1), 0) + begin
        key_at = lax.broadcasted_iota(jnp.int32, (1, keys), 1) + (begin - reach)
        doc_start = jnp.max(jnp.where(ends <= query_at, ends, 0), axis=1, keepdims=True)
        allowed = (key_at >= doc_start) & (key_at <= query_at)
        masked = jnp.where(allowed[None], scores[half].reshape(heads, block, keys), jnp.float32(-1e30))
        masked = masked.reshape(heads * block, keys)
        top = jnp.max(masked, axis=1, keepdims=True)
        exact = jnp.exp2((masked - top) * factor)
        totals.append(jnp.sum(exact, axis=1, keepdims=True))
        weights.append(exact.astype(jnp.bfloat16))
    for half in range(2):
        value = held[half, pl.ds(at[half], keys), HEAD_SIZE:]
        mixed = (dot(weights[half], value) / totals[half]).astype(jnp.bfloat16)
        for h in range(heads):
            out_ref[here[half], h * HEAD_SIZE : (h + 1) * HEAD_SIZE] = mixed[h * block : (h + 1) * block]


def attend(turn, members, devices, query, ends, pieces, block):
    rows, width = query.shape
    held = REACH_BLOCKS * block + rows // 2
    heads = width // HEAD_SIZE
    reach = (REACH_BLOCKS + 1) * block
    return pl.pallas_call(
        functools.partial(attend_kernel, block, turn, members, devices),
        out_shape=jax.ShapeDtypeStruct((2 * block, width), jnp.bfloat16),
        in_specs=[WHOLE] * 8,
        out_specs=WHOLE,
        scratch_shapes=[pltpu.VMEM((2, held, 2 * HEAD_SIZE), jnp.bfloat16)],
        compiler_params=pltpu.CompilerParams(vmem_limit_bytes=16 * MIB),
        cost_estimate=pl.CostEstimate(
            flops=2 * 2 * heads * block * reach * HEAD_SIZE * 2,
            bytes_accessed=2 * rows * width + 8 * held * HEAD_SIZE,
            transcendentals=2 * heads * block * reach,
        ),
    )(ends, query, *pieces)


def assemble_kernel(*refs):
    pieces, out_ref = refs[:-1], refs[-1]
    width = pieces[0].shape[1]
    for turn, piece in enumerate(pieces):
        at = pl.multiple_of(taken_at(turn, len(pieces)) * width, width)
        out_ref[:, pl.ds(at, width)] = piece[...]


def assemble(pieces):
    rows, width = pieces[0].shape
    return pl.pallas_call(
        assemble_kernel,
        out_shape=jax.ShapeDtypeStruct((rows, width * len(pieces)), jnp.bfloat16),
        in_specs=[WHOLE] * len(pieces),
        out_specs=WHOLE,
        compiler_params=pltpu.CompilerParams(vmem_limit_bytes=8 * MIB),
        cost_estimate=pl.CostEstimate(
            flops=0, bytes_accessed=4 * rows * width * len(pieces), transcendentals=0
        ),
    )(*pieces)


def shards(tokens, positions, lengths, gain, w_query, w_key, value_weight):
    devices = lax.axis_size("ctx")
    device = lax.axis_index("ctx")
    rows = tokens.shape[0]
    block = rows // 2
    members = w_key.shape[1] // HEAD_SIZE
    groups = devices // members
    group = device // members
    run = members * block
    group_rows = rows // groups

    half = HEAD_SIZE // 2
    freq = np.float32(ROPE_THETA ** (-(np.arange(HEAD_SIZE) % half * 2.0 / HEAD_SIZE)))
    operands = (positions.reshape(-1, 128), jnp.asarray(freq[None, :]), gain, tokens)

    half_devices = devices // 2
    halves = [list(range(i, i + half_devices)) for i in (0, half_devices)]

    def exchange(ordered, among):
        width = ordered.shape[3]
        flat = ordered.reshape(-1, group_rows, width)
        flat = lax.all_to_all(flat, "ctx", split_axis=0, concat_axis=0, tiled=True, axis_index_groups=among)
        return flat.reshape(-1, width)

    (kv,) = project(*operands, (w_key, value_weight), (True, False), devices, members)
    kv = exchange(kv, None)
    apart = list(range(half_devices, devices))
    near, *far = project(*operands, (w_query,), (True,), devices, members, apart)
    queries = []
    for i, piece in enumerate(far):
        distance = half_devices + i
        queries.append(lax.ppermute(piece, "ctx", [(j, j ^ distance) for j in range(devices)]))

    table = positions.reshape(devices, rows)
    ours = group_of(table, block, devices, members) == group
    first_run = group * run
    second_run = (2 * devices - members) * block - group * run
    slots = jnp.where(table // run == group, table - first_run, table - second_run + run)
    inner = jnp.arange(rows, dtype=jnp.int32)
    before = (inner[:, None] < inner[None, :]).astype(jnp.bfloat16)
    place_in = dot(ours.astype(jnp.bfloat16), before).astype(jnp.int32)
    place_in = jnp.where(ours, place_in, -1)
    wanted = jnp.arange(group_rows, dtype=jnp.int32)[None, :, None] == place_in[:, None, :]
    slot = jnp.sum(jnp.where(wanted, slots[:, None, :], 0), axis=2)
    index = jnp.arange(half_devices, dtype=jnp.int32)
    sources = [device // half_devices * half_devices + index, device ^ (half_devices + index)]
    query_slot = slot[jnp.concatenate(sources)].reshape(1, devices * group_rows)
    slot = slot.reshape(1, devices * group_rows)
    ends = jnp.cumsum(lengths, dtype=jnp.int32)[None, :]

    kv, near = lax.optimization_barrier((kv, near))
    queries.insert(0, exchange(near, halves))
    kv, *queries[1:6] = lax.optimization_barrier((kv, *queries[1:6]))
    reach = REACH_BLOCKS * block
    sizes = [run - reach, reach] * 2
    *runs, even_out, odd_out = place([kv], slot, sizes, members)
    odd = [i for i in range(1, groups - 1, 2)]
    even = [i for i in range(0, groups, 2)]
    pieces = []
    for lower, out in ((odd, odd_out), (even, even_out)):
        up = [(i * members + j, (i + 1) * members + j) for i in lower for j in range(members)]
        pieces.insert(0, lax.ppermute(out, "ctx", up + [(j, i) for i, j in up]))
    pieces = (*pieces, *runs)

    (query,) = place(queries, query_slot, [2 * run])
    results = []
    for turn in range(members):
        out = attend(turn, members, devices, query, ends, pieces, block)
        if turn < members - 1:
            distances = distances_at(turn, members)
            route = [
                (i * devices + j, i * devices + j // members * members + (j % members ^ distances[i % 2]))
                for i in range(lax.axis_size("dp"))
                for j in range(devices)
            ]
            out = lax.ppermute(out, ("dp", "ctx"), route)
        results.append(out)
    return assemble(results)


def solution(mesh):
    in_specs = (P(("dp", "ctx"), None), P("dp"), P("dp"), P(), P(), P(), P())
    out_specs = P(("dp", "ctx"), None)
    return jax.shard_map(shards, mesh=mesh, in_specs=in_specs, out_specs=out_specs, check_vma=False)
```

```python
import functools

import jax
import jax.numpy as jnp
import numpy as np
from jax import lax
from jax.experimental import pallas as pl
from jax.experimental.pallas import tpu as pltpu
from jax.sharding import PartitionSpec as P

HEAD_SIZE = 128
REACH_BLOCKS = 3
ROPE_THETA = 500000.0
EPSILON = 1e-05

WHOLE = pl.BlockSpec(memory_space=pltpu.VMEM)
IN_PLACE = pl.BlockSpec(memory_space=pl.ANY)
MIB = 1024 * 1024


def dot(a, b):
    return jnp.dot(a, b, preferred_element_type=jnp.float32)


def transposed(row):
    size = row.shape[1]
    here = lax.broadcasted_iota(jnp.int32, (size, size), 0)
    there = lax.broadcasted_iota(jnp.int32, (size, size), 1)
    return jnp.sum(jnp.where(here == there, row, 0), axis=1, keepdims=True)


def group_of(where_at, block, devices, members):
    block_id = where_at // block
    return jnp.minimum(block_id, 2 * devices - 1 - block_id) // members


def project_kernel(kinds, devices, members, apart, positions_hbm, freq_hbm, gain_hbm, tokens_hbm, *rest):
    count = len(kinds)
    weights_hbm, rest = rest[:count], rest[count:]
    outputs = 1 + len(apart)
    outs_hbm, rest = rest[:outputs], rest[outputs:]
    positions_ref, freq_ref, gain_ref, tokens, normed, weights, out_ref = rest[:7]
    small_sems, sems, out_sems = rest[7:]
    rows, width = normed.shape
    chunks, _, span = weights.shape
    copies, origin = [], []
    small_copies = [
        pltpu.make_async_copy(source, target, small_sems.at[i])
        for i, (source, target) in enumerate(
            [(positions_hbm, positions_ref), (freq_hbm, freq_ref), (gain_hbm, gain_ref), (tokens_hbm, tokens)]
        )
    ]
    for copy in small_copies:
        copy.start()
    for i in range(count):
        for first in range(0, weights_hbm[i].shape[1], span):
            j = len(copies)
            source = weights_hbm[i].at[:, pl.ds(first, span)]
            copies.append(pltpu.make_async_copy(source, weights.at[j], sems.at[j]))
            origin.append((i, first))
    copies[0].start()
    for copy in small_copies[:-1]:
        copy.wait()
    lanes = positions_ref.shape[1]
    stripes = rows // lanes
    mine = jnp.concatenate(
        [positions_ref[pl.ds(lax.axis_index("ctx") * stripes + i, 1), :] for i in range(stripes)], axis=1
    )
    owner = group_of(mine, rows // 2, devices, members)
    here = lax.broadcasted_iota(jnp.int32, (rows, rows), 0)
    there = lax.broadcasted_iota(jnp.int32, (rows, rows), 1)
    earlier = jnp.where((transposed(owner) == owner) & (here < there), 1, 0)
    rank = owner * (rows * members // devices) + jnp.sum(earlier, axis=0, keepdims=True)
    order = here == rank
    ordered_at = jnp.sum(jnp.where(order, mine, 0), axis=1, keepdims=True)
    angle = ordered_at.astype(jnp.float32) * freq_ref[...]
    lane = lax.broadcasted_iota(jnp.int32, (rows, HEAD_SIZE), 1)
    cosine = jnp.cos(angle)
    sine = jnp.where(lane < HEAD_SIZE // 2, -1.0, 1.0) * jnp.sin(angle)
    order = jnp.where(order, 1.0, 0.0).astype(jnp.bfloat16)
    gain = gain_ref[...].astype(jnp.float32).reshape(1, width)
    step = 32
    written = []

    small_copies[-1].wait()
    for first in range(0, rows, step):
        at = slice(first, first + step)
        floats = tokens[at, :].astype(jnp.float32)
        mean = jnp.sum(floats * floats, axis=1, keepdims=True) * (1.0 / width)
        tokens[at, :] = (floats * lax.rsqrt(mean + EPSILON) * gain).astype(jnp.bfloat16)
    if chunks > 1:
        copies[1].start()
    for first in range(0, width, 512):
        columns = slice(first, first + 512)
        normed[:, columns] = dot(order, tokens[:, columns]).astype(jnp.bfloat16)
    groups, heads = out_ref.shape[:2]
    offsets = [0]
    for i in range(count):
        offsets.append(offsets[-1] + weights_hbm[i].shape[1] // heads)
    me = lax.axis_index("ctx")
    far = [
        pltpu.make_async_copy(
            out_ref.at[(me ^ distance) // members, (me ^ distance) % members], outs_hbm[1 + i], out_sems.at[chunks + i]
        )
        for i, distance in enumerate(apart)
    ]
    for j in range(chunks):
        i, first = origin[j]
        copies[j].wait()
        if j + 2 < chunks:
            copies[j + 2].start()
        product = dot(normed[...], weights[j])
        per_head = offsets[i + 1] - offsets[i]
        for u in range(0, span, HEAD_SIZE):
            values = product[:, u : u + HEAD_SIZE]
            if kinds[i]:
                values = values * cosine + pltpu.roll(values, HEAD_SIZE // 2, 1) * sine
            head, inside = divmod(first + u, per_head)
            inside += offsets[i]
            out_ref[:, head, :, inside : inside + HEAD_SIZE] = values.astype(jnp.bfloat16).reshape(
                groups, rows // groups, HEAD_SIZE
            )
        first_head, done_heads = first // per_head, max(span // per_head, 1)
        done = (pl.ds(first_head, done_heads), pl.ds(0, rows // groups))
        done += (pl.ds(offsets[i] + first % per_head, min(span, per_head)),)
        taken = groups // 2 if apart else groups
        start = me // members // taken * taken if apart else 0
        source = out_ref.at[(pl.ds(start, taken),) + done]
        written.append(pltpu.make_async_copy(source, outs_hbm[0].at[(pl.ds(0, taken),) + done], out_sems.at[j]))
        written[-1].start()
        if first % per_head + span >= per_head:
            for distance, copy in zip(apart, far):
                to = (me ^ distance) % members
                pl.when((to >= first_head) & (to < first_head + done_heads))(copy.start)
    for copy in written + far:
        copy.wait()


def project(positions, freq, gain, tokens, weights, kinds, devices, heads, apart=()):
    rows, width = tokens.shape
    groups = devices // heads
    columns = sum(w.shape[1] for w in weights)
    span = 512
    flops = 2 * rows * width * columns
    size = 2 * (width * columns + rows * width + rows * columns)
    out_shape = (groups // 2 if apart else groups, heads, rows // groups, columns // heads)
    out_shapes = [out_shape] + [out_shape[2:]] * len(apart)
    return pl.pallas_call(
        functools.partial(project_kernel, kinds, devices, heads, apart),
        out_shape=[jax.ShapeDtypeStruct(shape, jnp.bfloat16) for shape in out_shapes],
        in_specs=[IN_PLACE] * (len(weights) + 4),
        out_specs=[IN_PLACE] * len(out_shapes),
        scratch_shapes=[
            pltpu.VMEM(positions.shape, jnp.int32),
            pltpu.VMEM(freq.shape, jnp.float32),
            pltpu.VMEM(gain.shape, jnp.bfloat16),
            pltpu.VMEM((rows, width), jnp.bfloat16),
            pltpu.VMEM((rows, width), jnp.bfloat16),
            pltpu.VMEM((columns // span, width, span), jnp.bfloat16),
            pltpu.VMEM((groups, heads, rows // groups, columns // heads), jnp.bfloat16),
            pltpu.SemaphoreType.DMA((4,)),
            pltpu.SemaphoreType.DMA((columns // span,)),
            pltpu.SemaphoreType.DMA((columns // span + len(apart),)),
        ],
        compiler_params=pltpu.CompilerParams(vmem_limit_bytes=56 * MIB),
        cost_estimate=pl.CostEstimate(flops=flops, bytes_accessed=size, transcendentals=0),
    )(positions, freq, gain, tokens, *weights)


def place_kernel(count, members, slot_ref, *refs):
    pieces, outs, arrived = refs[:count], refs[count:-1], refs[-1]
    rows = arrived.shape[0]
    slot = slot_ref[...]
    first = 0
    for piece in pieces:
        arrived[first : first + piece.shape[0], :] = piece[...]
        first += piece.shape[0]
    if members:
        outs, (even_ref, odd_ref) = outs[:-2], outs[-2:]
    first = 0
    for out_ref in outs:
        size = out_ref.shape[0]
        slots = lax.broadcasted_iota(jnp.int32, (size, rows), 0) + first
        chosen = (slots == slot).astype(jnp.bfloat16)
        out_ref[...] = dot(chosen, arrived[...]).astype(jnp.bfloat16)
        first += size
    if members:
        even = lax.axis_index("ctx") // members % 2 == 0
        early, late = outs[1][...], outs[3][...]
        even_ref[...] = jnp.where(even, early, late)
        odd_ref[...] = jnp.where(even, late, early)


def place(pieces, slot, sizes, members=0):
    rows, width = slot.shape[1], pieces[0].shape[1]
    out_sizes = sizes + [sizes[1], sizes[3]] if members else sizes
    return pl.pallas_call(
        functools.partial(place_kernel, len(pieces), members),
        out_shape=[jax.ShapeDtypeStruct((size, width), jnp.bfloat16) for size in out_sizes],
        in_specs=[WHOLE] * (1 + len(pieces)),
        out_specs=[WHOLE] * len(out_sizes),
        scratch_shapes=[pltpu.VMEM((rows, width), jnp.bfloat16)],
        compiler_params=pltpu.CompilerParams(vmem_limit_bytes=16 * MIB),
        cost_estimate=pl.CostEstimate(
            flops=2 * sum(sizes) * rows * width,
            bytes_accessed=4 * rows * width,
            transcendentals=0,
        ),
    )(slot, *pieces)


def taken_at(turn, members):
    distances = distances_at(turn, members)
    odd = lax.axis_index("dp") % 2
    distance = odd * distances[1] + (1 - odd) * distances[0]
    return (lax.axis_index("ctx") % members) ^ distance


def distances_at(turn, members):
    if turn in (0, members - 1):
        return (members - 1 - turn,) * 2
    return (turn, members - 1 - turn)


def attend_kernel(block, turn, members, devices, ends_ref, query_ref, *rest):
    pieces, out_ref, held = rest[:6], rest[6], rest[7]
    target = taken_at(turn, members)
    group = lax.axis_index("ctx") // members
    starts = (group * members * block, (2 * devices - members - group * members) * block)
    last = group == devices // members - 1
    heads = query_ref.shape[1] // HEAD_SIZE
    run = query_ref.shape[0] // 2
    per_run = run // block
    reach = REACH_BLOCKS * block
    keys = reach + block
    ends = ends_ref[...]
    factor = jnp.float32(np.log2(np.e) / HEAD_SIZE**0.5)
    from_even, from_odd, early_head, early_tail, late_head, late_tail = pieces
    second = 1 - group % 2
    held[second, :reach, :] = from_even[...]
    held[1 - second, :reach, :] = jnp.where(last, early_tail[...], from_odd[...])
    for half, (head, tail) in enumerate([(early_head, early_tail), (late_head, late_tail)]):
        cut = reach + head.shape[0]
        held[half, reach:cut, :] = head[...]
        held[half, cut:, :] = tail[...]
    indices = (target, per_run - 1 - target)
    at = [pl.multiple_of(index * block, block) for index in indices]
    here = [slice(half * block, (half + 1) * block) for half in range(2)]
    scores, weights, totals = [], [], []
    for half in range(2):
        query = query_ref[pl.ds(pl.multiple_of(at[half] + half * run, block), block), :]
        stacked = jnp.concatenate([query[:, h * HEAD_SIZE : (h + 1) * HEAD_SIZE] for h in range(heads)], axis=0)
        key = held[half, pl.ds(at[half], keys), :HEAD_SIZE]
        scores.append(
            lax.dot_general(stacked, key, (((1,), (1,)), ((), ())), preferred_element_type=jnp.float32)
        )
    for half in range(2):
        begin = starts[half] + at[half]
        query_at = lax.broadcasted_iota(jnp.int32, (block, 1), 0) + begin
        key_at = lax.broadcasted_iota(jnp.int32, (1, keys), 1) + (begin - reach)
        doc_start = jnp.max(jnp.where(ends <= query_at, ends, 0), axis=1, keepdims=True)
        allowed = (key_at >= doc_start) & (key_at <= query_at)
        masked = jnp.where(allowed[None], scores[half].reshape(heads, block, keys), jnp.float32(-1e30))
        masked = masked.reshape(heads * block, keys)
        top = jnp.max(masked, axis=1, keepdims=True)
        exact = jnp.exp2((masked - top) * factor)
        totals.append(jnp.sum(exact, axis=1, keepdims=True))
        weights.append(exact.astype(jnp.bfloat16))
    for half in range(2):
        value = held[half, pl.ds(at[half], keys), HEAD_SIZE:]
        mixed = (dot(weights[half], value) / totals[half]).astype(jnp.bfloat16)
        for h in range(heads):
            out_ref[here[half], h * HEAD_SIZE : (h + 1) * HEAD_SIZE] = mixed[h * block : (h + 1) * block]


def attend(turn, members, devices, query, ends, pieces, block):
    rows, width = query.shape
    held = REACH_BLOCKS * block + rows // 2
    heads = width // HEAD_SIZE
    reach = (REACH_BLOCKS + 1) * block
    return pl.pallas_call(
        functools.partial(attend_kernel, block, turn, members, devices),
        out_shape=jax.ShapeDtypeStruct((2 * block, width), jnp.bfloat16),
        in_specs=[WHOLE] * 8,
        out_specs=WHOLE,
        scratch_shapes=[pltpu.VMEM((2, held, 2 * HEAD_SIZE), jnp.bfloat16)],
        compiler_params=pltpu.CompilerParams(vmem_limit_bytes=16 * MIB),
        cost_estimate=pl.CostEstimate(
            flops=2 * 2 * heads * block * reach * HEAD_SIZE * 2,
            bytes_accessed=2 * rows * width + 8 * held * HEAD_SIZE,
            transcendentals=2 * heads * block * reach,
        ),
    )(ends, query, *pieces)


def assemble_kernel(*refs):
    pieces, out_ref = refs[:-1], refs[-1]
    width = pieces[0].shape[1]
    for turn, piece in enumerate(pieces):
        at = pl.multiple_of(taken_at(turn, len(pieces)) * width, width)
        out_ref[:, pl.ds(at, width)] = piece[...]


def assemble(pieces):
    rows, width = pieces[0].shape
    return pl.pallas_call(
        assemble_kernel,
        out_shape=jax.ShapeDtypeStruct((rows, width * len(pieces)), jnp.bfloat16),
        in_specs=[WHOLE] * len(pieces),
        out_specs=WHOLE,
        compiler_params=pltpu.CompilerParams(vmem_limit_bytes=8 * MIB),
        cost_estimate=pl.CostEstimate(
            flops=0, bytes_accessed=4 * rows * width * len(pieces), transcendentals=0
        ),
    )(*pieces)


def shards(tokens, positions, lengths, gain, w_query, w_key, value_weight):
    devices = lax.axis_size("ctx")
    device = lax.axis_index("ctx")
    rows = tokens.shape[0]
    block = rows // 2
    members = w_key.shape[1] // HEAD_SIZE
    groups = devices // members
    group = device // members
    run = members * block
    group_rows = rows // groups

    half = HEAD_SIZE // 2
    freq = np.float32(ROPE_THETA ** (-(np.arange(HEAD_SIZE) % half * 2.0 / HEAD_SIZE)))
    operands = (positions.reshape(-1, 128), jnp.asarray(freq[None, :]), gain, tokens)

    half_devices = devices // 2
    halves = [list(range(i, i + half_devices)) for i in (0, half_devices)]

    def exchange(ordered, among):
        width = ordered.shape[3]
        flat = ordered.reshape(-1, group_rows, width)
        flat = lax.all_to_all(flat, "ctx", split_axis=0, concat_axis=0, tiled=True, axis_index_groups=among)
        return flat.reshape(-1, width)

    (kv,) = project(*operands, (w_key, value_weight), (True, False), devices, members)
    kv = exchange(kv, None)
    apart = [half_devices + i * members + j for j in range(members)[::-1] for i in range(groups // 2)[::-1]]
    near, *far = project(*operands, (w_query,), (True,), devices, members, apart)
    queries = []
    for distance, piece in zip(apart, far):
        queries.append(lax.ppermute(piece, "ctx", [(j, j ^ distance) for j in range(devices)]))

    table = positions.reshape(devices, rows)
    ours = group_of(table, block, devices, members) == group
    first_run = group * run
    second_run = (2 * devices - members) * block - group * run
    slots = jnp.where(table // run == group, table - first_run, table - second_run + run)
    inner = jnp.arange(rows, dtype=jnp.int32)
    before = (inner[:, None] < inner[None, :]).astype(jnp.bfloat16)
    place_in = dot(ours.astype(jnp.bfloat16), before).astype(jnp.int32)
    place_in = jnp.where(ours, place_in, -1)
    wanted = jnp.arange(group_rows, dtype=jnp.int32)[None, :, None] == place_in[:, None, :]
    slot = jnp.sum(jnp.where(wanted, slots[:, None, :], 0), axis=2)
    index = jnp.arange(half_devices, dtype=jnp.int32)
    sources = [device // half_devices * half_devices + index, device ^ jnp.asarray(np.int32(apart))]
    query_slot = slot[jnp.concatenate(sources)].reshape(1, devices * group_rows)
    slot = slot.reshape(1, devices * group_rows)
    ends = jnp.cumsum(lengths, dtype=jnp.int32)[None, :]

    kv, near = lax.optimization_barrier((kv, near))
    queries.insert(0, exchange(near, halves))
    kv, *queries[1:6] = lax.optimization_barrier((kv, *queries[1:6]))
    reach = REACH_BLOCKS * block
    sizes = [run - reach, reach] * 2
    *runs, even_out, odd_out = place([kv], slot, sizes, members)
    odd = [i for i in range(1, groups - 1, 2)]
    even = [i for i in range(0, groups, 2)]
    pieces = []
    for lower, out in ((even, even_out), (odd, odd_out)):
        up = [(i * members + j, (i + 1) * members + j) for i in lower for j in range(members)]
        pieces.append(lax.ppermute(out, "ctx", up + [(j, i) for i, j in up]))
    pieces = (*pieces, *runs)

    (query,) = place(queries, query_slot, [2 * run])
    results = []
    for turn in range(members):
        out = attend(turn, members, devices, query, ends, pieces, block)
        if turn < members - 1:
            distances = distances_at(turn, members)
            route = [
                (i * devices + j, i * devices + j // members * members + (j % members ^ distances[i % 2]))
                for i in range(lax.axis_size("dp"))
                for j in range(devices)
            ]
            out = lax.ppermute(out, ("dp", "ctx"), route)
        results.append(out)
    return assemble(results)


def solution(mesh):
    in_specs = (P(("dp", "ctx"), None), P("dp"), P("dp"), P(), P(), P(), P())
    out_specs = P(("dp", "ctx"), None)
    return jax.shard_map(shards, mesh=mesh, in_specs=in_specs, out_specs=out_specs, check_vma=False)
```

```python
import functools

import jax
import jax.numpy as jnp
import numpy as np
from jax import lax
from jax.experimental import pallas as pl
from jax.experimental.pallas import tpu as pltpu
from jax.sharding import PartitionSpec as P

HEAD_SIZE = 128
REACH_BLOCKS = 3
ROPE_THETA = 500000.0
EPSILON = 1e-05

WHOLE = pl.BlockSpec(memory_space=pltpu.VMEM)
IN_PLACE = pl.BlockSpec(memory_space=pl.ANY)
MIB = 1024 * 1024


def dot(a, b):
    return jnp.dot(a, b, preferred_element_type=jnp.float32)


def transposed(row):
    size = row.shape[1]
    here = lax.broadcasted_iota(jnp.int32, (size, size), 0)
    there = lax.broadcasted_iota(jnp.int32, (size, size), 1)
    return jnp.sum(jnp.where(here == there, row, 0), axis=1, keepdims=True)


def group_of(where_at, block, devices, members):
    block_id = where_at // block
    return jnp.minimum(block_id, 2 * devices - 1 - block_id) // members


def project_kernel(kinds, devices, members, apart, positions_hbm, freq_hbm, gain_hbm, tokens_hbm, *rest):
    count = len(kinds)
    weights_hbm, rest = rest[:count], rest[count:]
    outputs = 1 + len(apart)
    outs_hbm, rest = rest[:outputs], rest[outputs:]
    positions_ref, freq_ref, gain_ref, tokens, normed, weights, out_ref = rest[:7]
    small_sems, sems, out_sems = rest[7:]
    rows, width = normed.shape
    chunks, _, span = weights.shape
    copies, origin = [], []
    small_copies = [
        pltpu.make_async_copy(source, target, small_sems.at[i])
        for i, (source, target) in enumerate(
            [(positions_hbm, positions_ref), (freq_hbm, freq_ref), (gain_hbm, gain_ref), (tokens_hbm, tokens)]
        )
    ]
    for copy in small_copies:
        copy.start()
    for i in range(count):
        for first in range(0, weights_hbm[i].shape[1], span):
            j = len(copies)
            source = weights_hbm[i].at[:, pl.ds(first, span)]
            copies.append(pltpu.make_async_copy(source, weights.at[j], sems.at[j]))
            origin.append((i, first))
    copies[0].start()
    for copy in small_copies[:-1]:
        copy.wait()
    lanes = positions_ref.shape[1]
    stripes = rows // lanes
    mine = jnp.concatenate(
        [positions_ref[pl.ds(lax.axis_index("ctx") * stripes + i, 1), :] for i in range(stripes)], axis=1
    )
    owner = group_of(mine, rows // 2, devices, members)
    here = lax.broadcasted_iota(jnp.int32, (rows, rows), 0)
    there = lax.broadcasted_iota(jnp.int32, (rows, rows), 1)
    earlier = jnp.where((transposed(owner) == owner) & (here < there), 1, 0)
    rank = owner * (rows * members // devices) + jnp.sum(earlier, axis=0, keepdims=True)
    order = here == rank
    ordered_at = jnp.sum(jnp.where(order, mine, 0), axis=1, keepdims=True)
    angle = ordered_at.astype(jnp.float32) * freq_ref[...]
    lane = lax.broadcasted_iota(jnp.int32, (rows, HEAD_SIZE), 1)
    cosine = jnp.cos(angle)
    sine = jnp.where(lane < HEAD_SIZE // 2, -1.0, 1.0) * jnp.sin(angle)
    order = jnp.where(order, 1.0, 0.0).astype(jnp.bfloat16)
    gain = gain_ref[...].astype(jnp.float32).reshape(1, width)
    step = 32
    written = []

    small_copies[-1].wait()
    for first in range(0, rows, step):
        at = slice(first, first + step)
        floats = tokens[at, :].astype(jnp.float32)
        mean = jnp.sum(floats * floats, axis=1, keepdims=True) * (1.0 / width)
        tokens[at, :] = (floats * lax.rsqrt(mean + EPSILON) * gain).astype(jnp.bfloat16)
    if chunks > 1:
        copies[1].start()
    for first in range(0, width, 512):
        columns = slice(first, first + 512)
        normed[:, columns] = dot(order, tokens[:, columns]).astype(jnp.bfloat16)
    groups, heads = out_ref.shape[:2]
    offsets = [0]
    for i in range(count):
        offsets.append(offsets[-1] + weights_hbm[i].shape[1] // heads)
    me = lax.axis_index("ctx")
    far = [
        pltpu.make_async_copy(
            out_ref.at[(me ^ distance) // members, (me ^ distance) % members], outs_hbm[1 + i], out_sems.at[chunks + i]
        )
        for i, distance in enumerate(apart)
    ]
    for j in range(chunks):
        i, first = origin[j]
        copies[j].wait()
        if j + 2 < chunks:
            copies[j + 2].start()
        product = dot(normed[...], weights[j])
        per_head = offsets[i + 1] - offsets[i]
        for u in range(0, span, HEAD_SIZE):
            values = product[:, u : u + HEAD_SIZE]
            if kinds[i]:
                values = values * cosine + pltpu.roll(values, HEAD_SIZE // 2, 1) * sine
            head, inside = divmod(first + u, per_head)
            inside += offsets[i]
            out_ref[:, head, :, inside : inside + HEAD_SIZE] = values.astype(jnp.bfloat16).reshape(
                groups, rows // groups, HEAD_SIZE
            )
        first_head, done_heads = first // per_head, max(span // per_head, 1)
        done = (pl.ds(first_head, done_heads), pl.ds(0, rows // groups))
        done += (pl.ds(offsets[i] + first % per_head, min(span, per_head)),)
        taken = groups // 2 if apart else groups
        start = me // members // taken * taken if apart else 0
        source = out_ref.at[(pl.ds(start, taken),) + done]
        written.append(pltpu.make_async_copy(source, outs_hbm[0].at[(pl.ds(0, taken),) + done], out_sems.at[j]))
        written[-1].start()
        if first % per_head + span >= per_head:
            for distance, copy in zip(apart, far):
                to = (me ^ distance) % members
                pl.when((to >= first_head) & (to < first_head + done_heads))(copy.start)
    for copy in written + far:
        copy.wait()


def project(positions, freq, gain, tokens, weights, kinds, devices, heads, apart=()):
    rows, width = tokens.shape
    groups = devices // heads
    columns = sum(w.shape[1] for w in weights)
    span = 512
    flops = 2 * rows * width * columns
    size = 2 * (width * columns + rows * width + rows * columns)
    out_shape = (groups // 2 if apart else groups, heads, rows // groups, columns // heads)
    out_shapes = [out_shape] + [out_shape[2:]] * len(apart)
    return pl.pallas_call(
        functools.partial(project_kernel, kinds, devices, heads, apart),
        out_shape=[jax.ShapeDtypeStruct(shape, jnp.bfloat16) for shape in out_shapes],
        in_specs=[IN_PLACE] * (len(weights) + 4),
        out_specs=[IN_PLACE] * len(out_shapes),
        scratch_shapes=[
            pltpu.VMEM(positions.shape, jnp.int32),
            pltpu.VMEM(freq.shape, jnp.float32),
            pltpu.VMEM(gain.shape, jnp.bfloat16),
            pltpu.VMEM((rows, width), jnp.bfloat16),
            pltpu.VMEM((rows, width), jnp.bfloat16),
            pltpu.VMEM((columns // span, width, span), jnp.bfloat16),
            pltpu.VMEM((groups, heads, rows // groups, columns // heads), jnp.bfloat16),
            pltpu.SemaphoreType.DMA((4,)),
            pltpu.SemaphoreType.DMA((columns // span,)),
            pltpu.SemaphoreType.DMA((columns // span + len(apart),)),
        ],
        compiler_params=pltpu.CompilerParams(vmem_limit_bytes=56 * MIB),
        cost_estimate=pl.CostEstimate(flops=flops, bytes_accessed=size, transcendentals=0),
    )(positions, freq, gain, tokens, *weights)


def place_kernel(count, members, slot_ref, *refs):
    pieces, outs, arrived = refs[:count], refs[count:-1], refs[-1]
    rows = arrived.shape[0]
    slot = slot_ref[...]
    first = 0
    for piece in pieces:
        arrived[first : first + piece.shape[0], :] = piece[...]
        first += piece.shape[0]
    if members:
        outs, (even_ref, odd_ref) = outs[:-2], outs[-2:]
    first = 0
    for out_ref in outs:
        size = out_ref.shape[0]
        slots = lax.broadcasted_iota(jnp.int32, (size, rows), 0) + first
        chosen = (slots == slot).astype(jnp.bfloat16)
        out_ref[...] = dot(chosen, arrived[...]).astype(jnp.bfloat16)
        first += size
    if members:
        even = lax.axis_index("ctx") // members % 2 == 0
        early, late = outs[1][...], outs[3][...]
        even_ref[...] = jnp.where(even, early, late)
        odd_ref[...] = jnp.where(even, late, early)


def place(pieces, slot, sizes, members=0):
    rows, width = slot.shape[1], pieces[0].shape[1]
    out_sizes = sizes + [sizes[1], sizes[3]] if members else sizes
    return pl.pallas_call(
        functools.partial(place_kernel, len(pieces), members),
        out_shape=[jax.ShapeDtypeStruct((size, width), jnp.bfloat16) for size in out_sizes],
        in_specs=[WHOLE] * (1 + len(pieces)),
        out_specs=[WHOLE] * len(out_sizes),
        scratch_shapes=[pltpu.VMEM((rows, width), jnp.bfloat16)],
        compiler_params=pltpu.CompilerParams(vmem_limit_bytes=16 * MIB),
        cost_estimate=pl.CostEstimate(
            flops=2 * sum(sizes) * rows * width,
            bytes_accessed=4 * rows * width,
            transcendentals=0,
        ),
    )(slot, *pieces)


def taken_at(turn, members):
    distances = distances_at(turn, members)
    odd = lax.axis_index("dp") % 2
    distance = odd * distances[1] + (1 - odd) * distances[0]
    return (lax.axis_index("ctx") % members) ^ distance


def distances_at(turn, members):
    if turn in (0, members - 1):
        return (members - 1 - turn,) * 2
    return (turn, members - 1 - turn)


def attend_kernel(block, turn, members, devices, ends_ref, query_ref, *rest):
    pieces, out_ref, held = rest[:6], rest[6], rest[7]
    target = taken_at(turn, members)
    group = lax.axis_index("ctx") // members
    starts = (group * members * block, (2 * devices - members - group * members) * block)
    last = group == devices // members - 1
    heads = query_ref.shape[1] // HEAD_SIZE
    run = query_ref.shape[0] // 2
    per_run = run // block
    reach = REACH_BLOCKS * block
    keys = reach + block
    ends = ends_ref[...]
    factor = jnp.float32(np.log2(np.e) / HEAD_SIZE**0.5)
    from_even, from_odd, early_head, early_tail, late_head, late_tail = pieces
    second = 1 - group % 2
    held[second, :reach, :] = from_even[...]
    held[1 - second, :reach, :] = jnp.where(last, early_tail[...], from_odd[...])
    for half, (head, tail) in enumerate([(early_head, early_tail), (late_head, late_tail)]):
        cut = reach + head.shape[0]
        held[half, reach:cut, :] = head[...]
        held[half, cut:, :] = tail[...]
    indices = (target, per_run - 1 - target)
    at = [pl.multiple_of(index * block, block) for index in indices]
    here = [slice(half * block, (half + 1) * block) for half in range(2)]
    scores, weights, totals = [], [], []
    for half in range(2):
        query = query_ref[pl.ds(pl.multiple_of(at[half] + half * run, block), block), :]
        stacked = jnp.concatenate([query[:, h * HEAD_SIZE : (h + 1) * HEAD_SIZE] for h in range(heads)], axis=0)
        key = held[half, pl.ds(at[half], keys), :HEAD_SIZE]
        scores.append(
            lax.dot_general(stacked, key, (((1,), (1,)), ((), ())), preferred_element_type=jnp.float32)
        )
    for half in range(2):
        begin = starts[half] + at[half]
        query_at = lax.broadcasted_iota(jnp.int32, (block, 1), 0) + begin
        key_at = lax.broadcasted_iota(jnp.int32, (1, keys), 1) + (begin - reach)
        doc_start = jnp.max(jnp.where(ends <= query_at, ends, 0), axis=1, keepdims=True)
        allowed = (key_at >= doc_start) & (key_at <= query_at)
        masked = jnp.where(allowed[None], scores[half].reshape(heads, block, keys), jnp.float32(-1e30))
        masked = masked.reshape(heads * block, keys)
        top = jnp.max(masked, axis=1, keepdims=True)
        exact = jnp.exp2((masked - top) * factor)
        totals.append(jnp.sum(exact, axis=1, keepdims=True))
        weights.append(exact.astype(jnp.bfloat16))
    for half in range(2):
        value = held[half, pl.ds(at[half], keys), HEAD_SIZE:]
        mixed = (dot(weights[half], value) / totals[half]).astype(jnp.bfloat16)
        for h in range(heads):
            out_ref[here[half], h * HEAD_SIZE : (h + 1) * HEAD_SIZE] = mixed[h * block : (h + 1) * block]


def attend(turn, members, devices, query, ends, pieces, block):
    rows, width = query.shape
    held = REACH_BLOCKS * block + rows // 2
    heads = width // HEAD_SIZE
    reach = (REACH_BLOCKS + 1) * block
    return pl.pallas_call(
        functools.partial(attend_kernel, block, turn, members, devices),
        out_shape=jax.ShapeDtypeStruct((2 * block, width), jnp.bfloat16),
        in_specs=[WHOLE] * 8,
        out_specs=WHOLE,
        scratch_shapes=[pltpu.VMEM((2, held, 2 * HEAD_SIZE), jnp.bfloat16)],
        compiler_params=pltpu.CompilerParams(vmem_limit_bytes=16 * MIB),
        cost_estimate=pl.CostEstimate(
            flops=2 * 2 * heads * block * reach * HEAD_SIZE * 2,
            bytes_accessed=2 * rows * width + 8 * held * HEAD_SIZE,
            transcendentals=2 * heads * block * reach,
        ),
    )(ends, query, *pieces)


def assemble_kernel(*refs):
    pieces, out_ref = refs[:-1], refs[-1]
    width = pieces[0].shape[1]
    for turn, piece in enumerate(pieces):
        at = pl.multiple_of(taken_at(turn, len(pieces)) * width, width)
        out_ref[:, pl.ds(at, width)] = piece[...]


def assemble(pieces):
    rows, width = pieces[0].shape
    return pl.pallas_call(
        assemble_kernel,
        out_shape=jax.ShapeDtypeStruct((rows, width * len(pieces)), jnp.bfloat16),
        in_specs=[WHOLE] * len(pieces),
        out_specs=WHOLE,
        compiler_params=pltpu.CompilerParams(vmem_limit_bytes=8 * MIB),
        cost_estimate=pl.CostEstimate(
            flops=0, bytes_accessed=4 * rows * width * len(pieces), transcendentals=0
        ),
    )(*pieces)


def shards(tokens, positions, lengths, gain, w_query, w_key, value_weight):
    devices = lax.axis_size("ctx")
    device = lax.axis_index("ctx")
    rows = tokens.shape[0]
    block = rows // 2
    members = w_key.shape[1] // HEAD_SIZE
    groups = devices // members
    group = device // members
    run = members * block
    group_rows = rows // groups

    half = HEAD_SIZE // 2
    freq = np.float32(ROPE_THETA ** (-(np.arange(HEAD_SIZE) % half * 2.0 / HEAD_SIZE)))
    operands = (positions.reshape(-1, 128), jnp.asarray(freq[None, :]), gain, tokens)

    half_devices = devices // 2
    halves = [list(range(i, i + half_devices)) for i in (0, half_devices)]

    def exchange(ordered, among):
        width = ordered.shape[3]
        flat = ordered.reshape(-1, group_rows, width)
        flat = lax.all_to_all(flat, "ctx", split_axis=0, concat_axis=0, tiled=True, axis_index_groups=among)
        return flat.reshape(-1, width)

    (kv,) = project(*operands, (w_key, value_weight), (True, False), devices, members)
    kv = exchange(kv, None)
    apart = list(range(half_devices, devices))
    near, *far = project(*operands, (w_query,), (True,), devices, members, apart)
    table = positions.reshape(devices, rows)
    ours = group_of(table, block, devices, members) == group
    first_run = group * run
    second_run = (2 * devices - members) * block - group * run
    slots = jnp.where(table // run == group, table - first_run, table - second_run + run)
    inner = jnp.arange(rows, dtype=jnp.int32)
    before = (inner[:, None] < inner[None, :]).astype(jnp.bfloat16)
    place_in = dot(ours.astype(jnp.bfloat16), before).astype(jnp.int32)
    place_in = jnp.where(ours, place_in, -1)
    wanted = jnp.arange(group_rows, dtype=jnp.int32)[None, :, None] == place_in[:, None, :]
    slot = jnp.sum(jnp.where(wanted, slots[:, None, :], 0), axis=2)
    index = jnp.arange(half_devices, dtype=jnp.int32)
    sources = [device // half_devices * half_devices + index, device ^ (half_devices + index)]
    query_slot = slot[jnp.concatenate(sources)].reshape(1, devices * group_rows)
    slot = slot.reshape(1, devices * group_rows)
    ends = jnp.cumsum(lengths, dtype=jnp.int32)[None, :]

    *far, slot, query_slot = lax.optimization_barrier((*far, slot, query_slot))
    queries = []
    for i, piece in enumerate(far):
        distance = half_devices + i
        queries.append(lax.ppermute(piece, "ctx", [(j, j ^ distance) for j in range(devices)]))

    kv, near = lax.optimization_barrier((kv, near))
    queries.insert(0, exchange(near, halves))
    kv, *queries[1:6] = lax.optimization_barrier((kv, *queries[1:6]))
    reach = REACH_BLOCKS * block
    sizes = [run - reach, reach] * 2
    *runs, even_out, odd_out = place([kv], slot, sizes, members)
    odd = [i for i in range(1, groups - 1, 2)]
    even = [i for i in range(0, groups, 2)]
    pieces = []
    for lower, out in ((odd, odd_out), (even, even_out)):
        up = [(i * members + j, (i + 1) * members + j) for i in lower for j in range(members)]
        pieces.insert(0, lax.ppermute(out, "ctx", up + [(j, i) for i, j in up]))
    pieces = (*pieces, *runs)

    (query,) = place(queries, query_slot, [2 * run])
    results = []
    for turn in range(members):
        out = attend(turn, members, devices, query, ends, pieces, block)
        if turn < members - 1:
            distances = distances_at(turn, members)
            route = [
                (i * devices + j, i * devices + j // members * members + (j % members ^ distances[i % 2]))
                for i in range(lax.axis_size("dp"))
                for j in range(devices)
            ]
            out = lax.ppermute(out, ("dp", "ctx"), route)
        results.append(out)
    return assemble(results)


def solution(mesh):
    in_specs = (P(("dp", "ctx"), None), P("dp"), P("dp"), P(), P(), P(), P())
    out_specs = P(("dp", "ctx"), None)
    return jax.shard_map(shards, mesh=mesh, in_specs=in_specs, out_specs=out_specs, check_vma=False)
```

```python
import functools

import jax
import jax.numpy as jnp
import numpy as np
from jax import lax
from jax.experimental import pallas as pl
from jax.experimental.pallas import tpu as pltpu
from jax.sharding import PartitionSpec as P

HEAD_SIZE = 128
REACH_BLOCKS = 3
ROPE_THETA = 500000.0
EPSILON = 1e-05

WHOLE = pl.BlockSpec(memory_space=pltpu.VMEM)
IN_PLACE = pl.BlockSpec(memory_space=pl.ANY)
MIB = 1024 * 1024


def dot(a, b):
    return jnp.dot(a, b, preferred_element_type=jnp.float32)


def transposed(row):
    size = row.shape[1]
    here = lax.broadcasted_iota(jnp.int32, (size, size), 0)
    there = lax.broadcasted_iota(jnp.int32, (size, size), 1)
    return jnp.sum(jnp.where(here == there, row, 0), axis=1, keepdims=True)


def group_of(where_at, block, devices, members):
    block_id = where_at // block
    return jnp.minimum(block_id, 2 * devices - 1 - block_id) // members


def project_kernel(kinds, devices, members, apart, positions_hbm, freq_hbm, gain_hbm, tokens_hbm, *rest):
    count = len(kinds)
    weights_hbm, rest = rest[:count], rest[count:]
    outputs = 1 + len(apart)
    outs_hbm, rest = rest[:outputs], rest[outputs:]
    positions_ref, freq_ref, gain_ref, tokens, normed, weights, out_ref = rest[:7]
    small_sems, sems, out_sems = rest[7:]
    rows, width = normed.shape
    chunks, _, span = weights.shape
    copies, origin = [], []
    small_copies = [
        pltpu.make_async_copy(source, target, small_sems.at[i])
        for i, (source, target) in enumerate(
            [(positions_hbm, positions_ref), (freq_hbm, freq_ref), (gain_hbm, gain_ref), (tokens_hbm, tokens)]
        )
    ]
    for copy in small_copies:
        copy.start()
    for i in range(count):
        for first in range(0, weights_hbm[i].shape[1], span):
            j = len(copies)
            source = weights_hbm[i].at[:, pl.ds(first, span)]
            copies.append(pltpu.make_async_copy(source, weights.at[j], sems.at[j]))
            origin.append((i, first))
    copies[0].start()
    for copy in small_copies[:-1]:
        copy.wait()
    lanes = positions_ref.shape[1]
    stripes = rows // lanes
    mine = jnp.concatenate(
        [positions_ref[pl.ds(lax.axis_index("ctx") * stripes + i, 1), :] for i in range(stripes)], axis=1
    )
    owner = group_of(mine, rows // 2, devices, members)
    here = lax.broadcasted_iota(jnp.int32, (rows, rows), 0)
    there = lax.broadcasted_iota(jnp.int32, (rows, rows), 1)
    earlier = jnp.where((transposed(owner) == owner) & (here < there), 1, 0)
    rank = owner * (rows * members // devices) + jnp.sum(earlier, axis=0, keepdims=True)
    order = here == rank
    ordered_at = jnp.sum(jnp.where(order, mine, 0), axis=1, keepdims=True)
    angle = ordered_at.astype(jnp.float32) * freq_ref[...]
    lane = lax.broadcasted_iota(jnp.int32, (rows, HEAD_SIZE), 1)
    cosine = jnp.cos(angle)
    sine = jnp.where(lane < HEAD_SIZE // 2, -1.0, 1.0) * jnp.sin(angle)
    order = jnp.where(order, 1.0, 0.0).astype(jnp.bfloat16)
    gain = gain_ref[...].astype(jnp.float32).reshape(1, width)
    step = 32
    written = []

    small_copies[-1].wait()
    for first in range(0, rows, step):
        at = slice(first, first + step)
        floats = tokens[at, :].astype(jnp.float32)
        mean = jnp.sum(floats * floats, axis=1, keepdims=True) * (1.0 / width)
        tokens[at, :] = (floats * lax.rsqrt(mean + EPSILON) * gain).astype(jnp.bfloat16)
    if chunks > 1:
        copies[1].start()
    for first in range(0, width, 512):
        columns = slice(first, first + 512)
        normed[:, columns] = dot(order, tokens[:, columns]).astype(jnp.bfloat16)
    groups, heads = out_ref.shape[:2]
    offsets = [0]
    for i in range(count):
        offsets.append(offsets[-1] + weights_hbm[i].shape[1] // heads)
    me = lax.axis_index("ctx")
    far = [
        pltpu.make_async_copy(
            out_ref.at[(me ^ distance) // members, (me ^ distance) % members], outs_hbm[1 + i], out_sems.at[chunks + i]
        )
        for i, distance in enumerate(apart)
    ]
    for j in range(chunks):
        i, first = origin[j]
        copies[j].wait()
        if j + 2 < chunks:
            copies[j + 2].start()
        product = dot(normed[...], weights[j])
        per_head = offsets[i + 1] - offsets[i]
        for u in range(0, span, HEAD_SIZE):
            values = product[:, u : u + HEAD_SIZE]
            if kinds[i]:
                values = values * cosine + pltpu.roll(values, HEAD_SIZE // 2, 1) * sine
            head, inside = divmod(first + u, per_head)
            inside += offsets[i]
            out_ref[:, head, :, inside : inside + HEAD_SIZE] = values.astype(jnp.bfloat16).reshape(
                groups, rows // groups, HEAD_SIZE
            )
        first_head, done_heads = first // per_head, max(span // per_head, 1)
        done = (pl.ds(first_head, done_heads), pl.ds(0, rows // groups))
        done += (pl.ds(offsets[i] + first % per_head, min(span, per_head)),)
        taken = groups // 2 if apart else groups
        start = me // members // taken * taken if apart else 0
        source = out_ref.at[(pl.ds(start, taken),) + done]
        written.append(pltpu.make_async_copy(source, outs_hbm[0].at[(pl.ds(0, taken),) + done], out_sems.at[j]))
        written[-1].start()
        if first % per_head + span >= per_head:
            for distance, copy in zip(apart, far):
                to = (me ^ distance) % members
                pl.when((to >= first_head) & (to < first_head + done_heads))(copy.start)
    for copy in written + far:
        copy.wait()


def project(positions, freq, gain, tokens, weights, kinds, devices, heads, apart=()):
    rows, width = tokens.shape
    groups = devices // heads
    columns = sum(w.shape[1] for w in weights)
    span = 512
    flops = 2 * rows * width * columns
    size = 2 * (width * columns + rows * width + rows * columns)
    out_shape = (groups // 2 if apart else groups, heads, rows // groups, columns // heads)
    out_shapes = [out_shape] + [out_shape[2:]] * len(apart)
    return pl.pallas_call(
        functools.partial(project_kernel, kinds, devices, heads, apart),
        out_shape=[jax.ShapeDtypeStruct(shape, jnp.bfloat16) for shape in out_shapes],
        in_specs=[IN_PLACE] * (len(weights) + 4),
        out_specs=[IN_PLACE] * len(out_shapes),
        scratch_shapes=[
            pltpu.VMEM(positions.shape, jnp.int32),
            pltpu.VMEM(freq.shape, jnp.float32),
            pltpu.VMEM(gain.shape, jnp.bfloat16),
            pltpu.VMEM((rows, width), jnp.bfloat16),
            pltpu.VMEM((rows, width), jnp.bfloat16),
            pltpu.VMEM((columns // span, width, span), jnp.bfloat16),
            pltpu.VMEM((groups, heads, rows // groups, columns // heads), jnp.bfloat16),
            pltpu.SemaphoreType.DMA((4,)),
            pltpu.SemaphoreType.DMA((columns // span,)),
            pltpu.SemaphoreType.DMA((columns // span + len(apart),)),
        ],
        compiler_params=pltpu.CompilerParams(vmem_limit_bytes=56 * MIB),
        cost_estimate=pl.CostEstimate(flops=flops, bytes_accessed=size, transcendentals=0),
    )(positions, freq, gain, tokens, *weights)


def place_kernel(count, members, slot_ref, *refs):
    pieces, outs, arrived = refs[:count], refs[count:-1], refs[-1]
    rows = arrived.shape[0]
    slot = slot_ref[...]
    first = 0
    for piece in pieces:
        arrived[first : first + piece.shape[0], :] = piece[...]
        first += piece.shape[0]
    if members:
        outs, (even_ref, odd_ref) = outs[:-2], outs[-2:]
    first = 0
    for out_ref in outs:
        size = out_ref.shape[0]
        slots = lax.broadcasted_iota(jnp.int32, (size, rows), 0) + first
        chosen = (slots == slot).astype(jnp.bfloat16)
        out_ref[...] = dot(chosen, arrived[...]).astype(jnp.bfloat16)
        first += size
    if members:
        even = lax.axis_index("ctx") // members % 2 == 0
        early, late = outs[1][...], outs[3][...]
        even_ref[...] = jnp.where(even, early, late)
        odd_ref[...] = jnp.where(even, late, early)


def place(pieces, slot, sizes, members=0):
    rows, width = slot.shape[1], pieces[0].shape[1]
    out_sizes = sizes + [sizes[1], sizes[3]] if members else sizes
    return pl.pallas_call(
        functools.partial(place_kernel, len(pieces), members),
        out_shape=[jax.ShapeDtypeStruct((size, width), jnp.bfloat16) for size in out_sizes],
        in_specs=[WHOLE] * (1 + len(pieces)),
        out_specs=[WHOLE] * len(out_sizes),
        scratch_shapes=[pltpu.VMEM((rows, width), jnp.bfloat16)],
        compiler_params=pltpu.CompilerParams(vmem_limit_bytes=16 * MIB),
        cost_estimate=pl.CostEstimate(
            flops=2 * sum(sizes) * rows * width,
            bytes_accessed=4 * rows * width,
            transcendentals=0,
        ),
    )(slot, *pieces)


def taken_at(turn, members):
    distances = distances_at(turn, members)
    odd = lax.axis_index("dp") % 2
    distance = odd * distances[1] + (1 - odd) * distances[0]
    return (lax.axis_index("ctx") % members) ^ distance


def distances_at(turn, members):
    if turn in (0, members - 1):
        return (members - 1 - turn,) * 2
    return (turn, members - 1 - turn)


def attend_kernel(block, turn, members, devices, ends_ref, query_ref, *rest):
    pieces, out_ref, held = rest[:6], rest[6], rest[7]
    target = taken_at(turn, members)
    group = lax.axis_index("ctx") // members
    starts = (group * members * block, (2 * devices - members - group * members) * block)
    last = group == devices // members - 1
    heads = query_ref.shape[1] // HEAD_SIZE
    run = query_ref.shape[0] // 2
    per_run = run // block
    reach = REACH_BLOCKS * block
    keys = reach + block
    ends = ends_ref[...]
    factor = jnp.float32(np.log2(np.e) / HEAD_SIZE**0.5)
    from_even, from_odd, early_head, early_tail, late_head, late_tail = pieces
    second = 1 - group % 2
    held[second, :reach, :] = from_even[...]
    held[1 - second, :reach, :] = jnp.where(last, early_tail[...], from_odd[...])
    for half, (head, tail) in enumerate([(early_head, early_tail), (late_head, late_tail)]):
        cut = reach + head.shape[0]
        held[half, reach:cut, :] = head[...]
        held[half, cut:, :] = tail[...]
    indices = (target, per_run - 1 - target)
    at = [pl.multiple_of(index * block, block) for index in indices]
    here = [slice(half * block, (half + 1) * block) for half in range(2)]
    scores, weights, totals = [], [], []
    for half in range(2):
        query = query_ref[pl.ds(pl.multiple_of(at[half] + half * run, block), block), :]
        stacked = jnp.concatenate([query[:, h * HEAD_SIZE : (h + 1) * HEAD_SIZE] for h in range(heads)], axis=0)
        key = held[half, pl.ds(at[half], keys), :HEAD_SIZE]
        scores.append(
            lax.dot_general(stacked, key, (((1,), (1,)), ((), ())), preferred_element_type=jnp.float32)
        )
    for half in range(2):
        begin = starts[half] + at[half]
        query_at = lax.broadcasted_iota(jnp.int32, (block, 1), 0) + begin
        key_at = lax.broadcasted_iota(jnp.int32, (1, keys), 1) + (begin - reach)
        doc_start = jnp.max(jnp.where(ends <= query_at, ends, 0), axis=1, keepdims=True)
        allowed = (key_at >= doc_start) & (key_at <= query_at)
        masked = jnp.where(allowed[None], scores[half].reshape(heads, block, keys), jnp.float32(-1e30))
        masked = masked.reshape(heads * block, keys)
        top = jnp.max(masked, axis=1, keepdims=True)
        exact = jnp.exp2((masked - top) * factor)
        totals.append(jnp.sum(exact, axis=1, keepdims=True))
        weights.append(exact.astype(jnp.bfloat16))
    for half in range(2):
        value = held[half, pl.ds(at[half], keys), HEAD_SIZE:]
        mixed = (dot(weights[half], value) / totals[half]).astype(jnp.bfloat16)
        for h in range(heads):
            out_ref[here[half], h * HEAD_SIZE : (h + 1) * HEAD_SIZE] = mixed[h * block : (h + 1) * block]


def attend(turn, members, devices, query, ends, pieces, block):
    rows, width = query.shape
    held = REACH_BLOCKS * block + rows // 2
    heads = width // HEAD_SIZE
    reach = (REACH_BLOCKS + 1) * block
    return pl.pallas_call(
        functools.partial(attend_kernel, block, turn, members, devices),
        out_shape=jax.ShapeDtypeStruct((2 * block, width), jnp.bfloat16),
        in_specs=[WHOLE] * 8,
        out_specs=WHOLE,
        scratch_shapes=[pltpu.VMEM((2, held, 2 * HEAD_SIZE), jnp.bfloat16)],
        compiler_params=pltpu.CompilerParams(vmem_limit_bytes=16 * MIB),
        cost_estimate=pl.CostEstimate(
            flops=2 * 2 * heads * block * reach * HEAD_SIZE * 2,
            bytes_accessed=2 * rows * width + 8 * held * HEAD_SIZE,
            transcendentals=2 * heads * block * reach,
        ),
    )(ends, query, *pieces)


def assemble_kernel(*refs):
    pieces, out_ref = refs[:-1], refs[-1]
    width = pieces[0].shape[1]
    for turn, piece in enumerate(pieces):
        at = pl.multiple_of(taken_at(turn, len(pieces)) * width, width)
        out_ref[:, pl.ds(at, width)] = piece[...]


def assemble(pieces):
    rows, width = pieces[0].shape
    return pl.pallas_call(
        assemble_kernel,
        out_shape=jax.ShapeDtypeStruct((rows, width * len(pieces)), jnp.bfloat16),
        in_specs=[WHOLE] * len(pieces),
        out_specs=WHOLE,
        compiler_params=pltpu.CompilerParams(vmem_limit_bytes=8 * MIB),
        cost_estimate=pl.CostEstimate(
            flops=0, bytes_accessed=4 * rows * width * len(pieces), transcendentals=0
        ),
    )(*pieces)


def shards(tokens, positions, lengths, gain, w_query, w_key, value_weight):
    devices = lax.axis_size("ctx")
    device = lax.axis_index("ctx")
    rows = tokens.shape[0]
    block = rows // 2
    members = w_key.shape[1] // HEAD_SIZE
    groups = devices // members
    group = device // members
    run = members * block
    group_rows = rows // groups

    half = HEAD_SIZE // 2
    freq = np.float32(ROPE_THETA ** (-(np.arange(HEAD_SIZE) % half * 2.0 / HEAD_SIZE)))
    operands = (positions.reshape(-1, 128), jnp.asarray(freq[None, :]), gain, tokens)

    half_devices = devices // 2
    halves = [list(range(i, i + half_devices)) for i in (0, half_devices)]

    def exchange(ordered, among):
        width = ordered.shape[3]
        flat = ordered.reshape(-1, group_rows, width)
        flat = lax.all_to_all(flat, "ctx", split_axis=0, concat_axis=0, tiled=True, axis_index_groups=among)
        return flat.reshape(-1, width)

    (kv,) = project(*operands, (w_key, value_weight), (True, False), devices, members)
    kv = exchange(kv, None)
    apart = list(range(half_devices, devices))
    near, *far = project(*operands, (w_query,), (True,), devices, members, apart)
    queries = []
    for i, piece in enumerate(far):
        distance = half_devices + i
        queries.append(lax.ppermute(piece, "ctx", [(j, j ^ distance) for j in range(devices)]))

    table = positions.reshape(devices, rows)
    ours = group_of(table, block, devices, members) == group
    first_run = group * run
    second_run = (2 * devices - members) * block - group * run
    slots = jnp.where(table // run == group, table - first_run, table - second_run + run)
    inner = jnp.arange(rows, dtype=jnp.int32)
    before = (inner[:, None] < inner[None, :]).astype(jnp.bfloat16)
    place_in = dot(ours.astype(jnp.bfloat16), before).astype(jnp.int32)
    place_in = jnp.where(ours, place_in, -1)
    wanted = jnp.arange(group_rows, dtype=jnp.int32)[None, :, None] == place_in[:, None, :]
    slot = jnp.sum(jnp.where(wanted, slots[:, None, :], 0), axis=2)
    index = jnp.arange(half_devices, dtype=jnp.int32)
    sources = [device // half_devices * half_devices + index, device ^ (half_devices + index)]
    query_slot = slot[jnp.concatenate(sources)].reshape(1, devices * group_rows)
    slot = slot.reshape(1, devices * group_rows)
    ends = jnp.cumsum(lengths, dtype=jnp.int32)[None, :]

    kv, near = lax.optimization_barrier((kv, near))
    queries.insert(0, exchange(near, halves))
    kv, *queries[1:5] = lax.optimization_barrier((kv, *queries[1:5]))
    reach = REACH_BLOCKS * block
    sizes = [run - reach, reach] * 2
    *runs, even_out, odd_out = place([kv], slot, sizes, members)
    odd = [i for i in range(1, groups - 1, 2)]
    even = [i for i in range(0, groups, 2)]
    pieces = []
    for lower, out in ((odd, odd_out), (even, even_out)):
        up = [(i * members + j, (i + 1) * members + j) for i in lower for j in range(members)]
        pieces.insert(0, lax.ppermute(out, "ctx", up + [(j, i) for i, j in up]))
    pieces = (*pieces, *runs)

    (query,) = place(queries, query_slot, [2 * run])
    results = []
    for turn in range(members):
        out = attend(turn, members, devices, query, ends, pieces, block)
        if turn < members - 1:
            distances = distances_at(turn, members)
            route = [
                (i * devices + j, i * devices + j // members * members + (j % members ^ distances[i % 2]))
                for i in range(lax.axis_size("dp"))
                for j in range(devices)
            ]
            out = lax.ppermute(out, ("dp", "ctx"), route)
        results.append(out)
    return assemble(results)


def solution(mesh):
    in_specs = (P(("dp", "ctx"), None), P("dp"), P("dp"), P(), P(), P(), P())
    out_specs = P(("dp", "ctx"), None)
    return jax.shard_map(shards, mesh=mesh, in_specs=in_specs, out_specs=out_specs, check_vma=False)
```

```python
import functools

import jax
import jax.numpy as jnp
import numpy as np
from jax import lax
from jax.experimental import pallas as pl
from jax.experimental.pallas import tpu as pltpu
from jax.sharding import PartitionSpec as P

HEAD_SIZE = 128
REACH_BLOCKS = 3
ROPE_THETA = 500000.0
EPSILON = 1e-05

WHOLE = pl.BlockSpec(memory_space=pltpu.VMEM)
IN_PLACE = pl.BlockSpec(memory_space=pl.ANY)
MIB = 1024 * 1024


def dot(a, b):
    return jnp.dot(a, b, preferred_element_type=jnp.float32)


def transposed(row):
    size = row.shape[1]
    here = lax.broadcasted_iota(jnp.int32, (size, size), 0)
    there = lax.broadcasted_iota(jnp.int32, (size, size), 1)
    return jnp.sum(jnp.where(here == there, row, 0), axis=1, keepdims=True)


def group_of(where_at, block, devices, members):
    block_id = where_at // block
    return jnp.minimum(block_id, 2 * devices - 1 - block_id) // members


def project_kernel(kinds, devices, members, apart, positions_hbm, freq_hbm, gain_hbm, tokens_hbm, *rest):
    count = len(kinds)
    weights_hbm, rest = rest[:count], rest[count:]
    outputs = 1 + len(apart)
    outs_hbm, rest = rest[:outputs], rest[outputs:]
    positions_ref, freq_ref, gain_ref, tokens, normed, weights, out_ref = rest[:7]
    small_sems, sems, out_sems = rest[7:]
    rows, width = normed.shape
    chunks, _, span = weights.shape
    copies, origin = [], []
    small_copies = [
        pltpu.make_async_copy(source, target, small_sems.at[i])
        for i, (source, target) in enumerate(
            [(positions_hbm, positions_ref), (freq_hbm, freq_ref), (gain_hbm, gain_ref), (tokens_hbm, tokens)]
        )
    ]
    for copy in small_copies:
        copy.start()
    for i in range(count):
        for first in range(0, weights_hbm[i].shape[1], span):
            j = len(copies)
            source = weights_hbm[i].at[:, pl.ds(first, span)]
            copies.append(pltpu.make_async_copy(source, weights.at[j], sems.at[j]))
            origin.append((i, first))
    copies[0].start()
    for copy in small_copies[:-1]:
        copy.wait()
    lanes = positions_ref.shape[1]
    stripes = rows // lanes
    mine = jnp.concatenate(
        [positions_ref[pl.ds(lax.axis_index("ctx") * stripes + i, 1), :] for i in range(stripes)], axis=1
    )
    owner = group_of(mine, rows // 2, devices, members)
    here = lax.broadcasted_iota(jnp.int32, (rows, rows), 0)
    there = lax.broadcasted_iota(jnp.int32, (rows, rows), 1)
    earlier = jnp.where((transposed(owner) == owner) & (here < there), 1, 0)
    rank = owner * (rows * members // devices) + jnp.sum(earlier, axis=0, keepdims=True)
    order = here == rank
    ordered_at = jnp.sum(jnp.where(order, mine, 0), axis=1, keepdims=True)
    angle = ordered_at.astype(jnp.float32) * freq_ref[...]
    lane = lax.broadcasted_iota(jnp.int32, (rows, HEAD_SIZE), 1)
    cosine = jnp.cos(angle)
    sine = jnp.where(lane < HEAD_SIZE // 2, -1.0, 1.0) * jnp.sin(angle)
    order = jnp.where(order, 1.0, 0.0).astype(jnp.bfloat16)
    gain = gain_ref[...].astype(jnp.float32).reshape(1, width)
    step = 32
    written = []

    small_copies[-1].wait()
    for first in range(0, rows, step):
        at = slice(first, first + step)
        floats = tokens[at, :].astype(jnp.float32)
        mean = jnp.sum(floats * floats, axis=1, keepdims=True) * (1.0 / width)
        tokens[at, :] = (floats * lax.rsqrt(mean + EPSILON) * gain).astype(jnp.bfloat16)
    if chunks > 1:
        copies[1].start()
    for first in range(0, width, 512):
        columns = slice(first, first + 512)
        normed[:, columns] = dot(order, tokens[:, columns]).astype(jnp.bfloat16)
    groups, heads = out_ref.shape[:2]
    offsets = [0]
    for i in range(count):
        offsets.append(offsets[-1] + weights_hbm[i].shape[1] // heads)
    me = lax.axis_index("ctx")
    far = [
        pltpu.make_async_copy(
            out_ref.at[(me ^ distance) // members, (me ^ distance) % members], outs_hbm[1 + i], out_sems.at[chunks + i]
        )
        for i, distance in enumerate(apart)
    ]
    for j in range(chunks):
        i, first = origin[j]
        copies[j].wait()
        if j + 2 < chunks:
            copies[j + 2].start()
        product = dot(normed[...], weights[j])
        per_head = offsets[i + 1] - offsets[i]
        for u in range(0, span, HEAD_SIZE):
            values = product[:, u : u + HEAD_SIZE]
            if kinds[i]:
                values = values * cosine + pltpu.roll(values, HEAD_SIZE // 2, 1) * sine
            head, inside = divmod(first + u, per_head)
            inside += offsets[i]
            out_ref[:, head, :, inside : inside + HEAD_SIZE] = values.astype(jnp.bfloat16).reshape(
                groups, rows // groups, HEAD_SIZE
            )
        first_head, done_heads = first // per_head, max(span // per_head, 1)
        done = (pl.ds(first_head, done_heads), pl.ds(0, rows // groups))
        done += (pl.ds(offsets[i] + first % per_head, min(span, per_head)),)
        taken = groups // 2 if apart else groups
        start = me // members // taken * taken if apart else 0
        source = out_ref.at[(pl.ds(start, taken),) + done]
        written.append(pltpu.make_async_copy(source, outs_hbm[0].at[(pl.ds(0, taken),) + done], out_sems.at[j]))
        written[-1].start()
        if first % per_head + span >= per_head:
            for distance, copy in zip(apart, far):
                to = (me ^ distance) % members
                pl.when((to >= first_head) & (to < first_head + done_heads))(copy.start)
    for copy in written + far:
        copy.wait()


def project(positions, freq, gain, tokens, weights, kinds, devices, heads, apart=()):
    rows, width = tokens.shape
    groups = devices // heads
    columns = sum(w.shape[1] for w in weights)
    span = 512
    flops = 2 * rows * width * columns
    size = 2 * (width * columns + rows * width + rows * columns)
    out_shape = (groups // 2 if apart else groups, heads, rows // groups, columns // heads)
    out_shapes = [out_shape] + [out_shape[2:]] * len(apart)
    return pl.pallas_call(
        functools.partial(project_kernel, kinds, devices, heads, apart),
        out_shape=[jax.ShapeDtypeStruct(shape, jnp.bfloat16) for shape in out_shapes],
        in_specs=[IN_PLACE] * (len(weights) + 4),
        out_specs=[IN_PLACE] * len(out_shapes),
        scratch_shapes=[
            pltpu.VMEM(positions.shape, jnp.int32),
            pltpu.VMEM(freq.shape, jnp.float32),
            pltpu.VMEM(gain.shape, jnp.bfloat16),
            pltpu.VMEM((rows, width), jnp.bfloat16),
            pltpu.VMEM((rows, width), jnp.bfloat16),
            pltpu.VMEM((columns // span, width, span), jnp.bfloat16),
            pltpu.VMEM((groups, heads, rows // groups, columns // heads), jnp.bfloat16),
            pltpu.SemaphoreType.DMA((4,)),
            pltpu.SemaphoreType.DMA((columns // span,)),
            pltpu.SemaphoreType.DMA((columns // span + len(apart),)),
        ],
        compiler_params=pltpu.CompilerParams(vmem_limit_bytes=56 * MIB),
        cost_estimate=pl.CostEstimate(flops=flops, bytes_accessed=size, transcendentals=0),
    )(positions, freq, gain, tokens, *weights)


def place_kernel(count, members, slot_ref, *refs):
    pieces, outs, arrived = refs[:count], refs[count:-1], refs[-1]
    rows = arrived.shape[0]
    slot = slot_ref[...]
    first = 0
    for piece in pieces:
        arrived[first : first + piece.shape[0], :] = piece[...]
        first += piece.shape[0]
    if members:
        outs, (even_ref, odd_ref) = outs[:-2], outs[-2:]
    first = 0
    for out_ref in outs:
        size = out_ref.shape[0]
        slots = lax.broadcasted_iota(jnp.int32, (size, rows), 0) + first
        chosen = (slots == slot).astype(jnp.bfloat16)
        out_ref[...] = dot(chosen, arrived[...]).astype(jnp.bfloat16)
        first += size
    if members:
        even = lax.axis_index("ctx") // members % 2 == 0
        early, late = outs[1][...], outs[3][...]
        even_ref[...] = jnp.where(even, early, late)
        odd_ref[...] = jnp.where(even, late, early)


def place(pieces, slot, sizes, members=0):
    rows, width = slot.shape[1], pieces[0].shape[1]
    out_sizes = sizes + [sizes[1], sizes[3]] if members else sizes
    return pl.pallas_call(
        functools.partial(place_kernel, len(pieces), members),
        out_shape=[jax.ShapeDtypeStruct((size, width), jnp.bfloat16) for size in out_sizes],
        in_specs=[WHOLE] * (1 + len(pieces)),
        out_specs=[WHOLE] * len(out_sizes),
        scratch_shapes=[pltpu.VMEM((rows, width), jnp.bfloat16)],
        compiler_params=pltpu.CompilerParams(vmem_limit_bytes=16 * MIB),
        cost_estimate=pl.CostEstimate(
            flops=2 * sum(sizes) * rows * width,
            bytes_accessed=4 * rows * width,
            transcendentals=0,
        ),
    )(slot, *pieces)


def taken_at(turn, members):
    distances = distances_at(turn, members)
    odd = lax.axis_index("dp") % 2
    distance = odd * distances[1] + (1 - odd) * distances[0]
    return (lax.axis_index("ctx") % members) ^ distance


def distances_at(turn, members):
    if turn in (0, members - 1):
        return (members - 1 - turn,) * 2
    return (turn, members - 1 - turn)


def attend_kernel(block, turn, members, devices, ends_ref, query_ref, *rest):
    pieces, out_ref, held = rest[:6], rest[6], rest[7]
    target = taken_at(turn, members)
    group = lax.axis_index("ctx") // members
    starts = (group * members * block, (2 * devices - members - group * members) * block)
    last = group == devices // members - 1
    heads = query_ref.shape[1] // HEAD_SIZE
    run = query_ref.shape[0] // 2
    per_run = run // block
    reach = REACH_BLOCKS * block
    keys = reach + block
    ends = ends_ref[...]
    factor = jnp.float32(np.log2(np.e) / HEAD_SIZE**0.5)
    from_even, from_odd, early_head, early_tail, late_head, late_tail = pieces
    second = 1 - group % 2
    held[second, :reach, :] = from_even[...]
    held[1 - second, :reach, :] = jnp.where(last, early_tail[...], from_odd[...])
    for half, (head, tail) in enumerate([(early_head, early_tail), (late_head, late_tail)]):
        cut = reach + head.shape[0]
        held[half, reach:cut, :] = head[...]
        held[half, cut:, :] = tail[...]
    indices = (target, per_run - 1 - target)
    at = [pl.multiple_of(index * block, block) for index in indices]
    here = [slice(half * block, (half + 1) * block) for half in range(2)]
    scores, weights, totals = [], [], []
    for half in range(2):
        query = query_ref[pl.ds(pl.multiple_of(at[half] + half * run, block), block), :]
        stacked = jnp.concatenate([query[:, h * HEAD_SIZE : (h + 1) * HEAD_SIZE] for h in range(heads)], axis=0)
        key = held[half, pl.ds(at[half], keys), :HEAD_SIZE]
        scores.append(
            lax.dot_general(stacked, key, (((1,), (1,)), ((), ())), preferred_element_type=jnp.float32)
        )
    for half in range(2):
        begin = starts[half] + at[half]
        query_at = lax.broadcasted_iota(jnp.int32, (block, 1), 0) + begin
        key_at = lax.broadcasted_iota(jnp.int32, (1, keys), 1) + (begin - reach)
        doc_start = jnp.max(jnp.where(ends <= query_at, ends, 0), axis=1, keepdims=True)
        allowed = (key_at >= doc_start) & (key_at <= query_at)
        masked = jnp.where(allowed[None], scores[half].reshape(heads, block, keys), jnp.float32(-1e30))
        masked = masked.reshape(heads * block, keys)
        top = jnp.max(masked, axis=1, keepdims=True)
        exact = jnp.exp2((masked - top) * factor)
        totals.append(jnp.sum(exact, axis=1, keepdims=True))
        weights.append(exact.astype(jnp.bfloat16))
    for half in range(2):
        value = held[half, pl.ds(at[half], keys), HEAD_SIZE:]
        mixed = (dot(weights[half], value) / totals[half]).astype(jnp.bfloat16)
        for h in range(heads):
            out_ref[here[half], h * HEAD_SIZE : (h + 1) * HEAD_SIZE] = mixed[h * block : (h + 1) * block]


def attend(turn, members, devices, query, ends, pieces, block):
    rows, width = query.shape
    held = REACH_BLOCKS * block + rows // 2
    heads = width // HEAD_SIZE
    reach = (REACH_BLOCKS + 1) * block
    return pl.pallas_call(
        functools.partial(attend_kernel, block, turn, members, devices),
        out_shape=jax.ShapeDtypeStruct((2 * block, width), jnp.bfloat16),
        in_specs=[WHOLE] * 8,
        out_specs=WHOLE,
        scratch_shapes=[pltpu.VMEM((2, held, 2 * HEAD_SIZE), jnp.bfloat16)],
        compiler_params=pltpu.CompilerParams(vmem_limit_bytes=16 * MIB),
        cost_estimate=pl.CostEstimate(
            flops=2 * 2 * heads * block * reach * HEAD_SIZE * 2,
            bytes_accessed=2 * rows * width + 8 * held * HEAD_SIZE,
            transcendentals=2 * heads * block * reach,
        ),
    )(ends, query, *pieces)


def assemble_kernel(*refs):
    pieces, out_ref = refs[:-1], refs[-1]
    width = pieces[0].shape[1]
    for turn, piece in enumerate(pieces):
        at = pl.multiple_of(taken_at(turn, len(pieces)) * width, width)
        out_ref[:, pl.ds(at, width)] = piece[...]


def assemble(pieces):
    rows, width = pieces[0].shape
    return pl.pallas_call(
        assemble_kernel,
        out_shape=jax.ShapeDtypeStruct((rows, width * len(pieces)), jnp.bfloat16),
        in_specs=[WHOLE] * len(pieces),
        out_specs=WHOLE,
        compiler_params=pltpu.CompilerParams(vmem_limit_bytes=8 * MIB),
        cost_estimate=pl.CostEstimate(
            flops=0, bytes_accessed=4 * rows * width * len(pieces), transcendentals=0
        ),
    )(*pieces)


def shards(tokens, positions, lengths, gain, w_query, w_key, value_weight):
    devices = lax.axis_size("ctx")
    device = lax.axis_index("ctx")
    rows = tokens.shape[0]
    block = rows // 2
    members = w_key.shape[1] // HEAD_SIZE
    groups = devices // members
    group = device // members
    run = members * block
    group_rows = rows // groups

    half = HEAD_SIZE // 2
    freq = np.float32(ROPE_THETA ** (-(np.arange(HEAD_SIZE) % half * 2.0 / HEAD_SIZE)))
    operands = (positions.reshape(-1, 128), jnp.asarray(freq[None, :]), gain, tokens)

    half_devices = devices // 2
    halves = [list(range(i, i + half_devices)) for i in (0, half_devices)]

    def exchange(ordered, among):
        width = ordered.shape[3]
        flat = ordered.reshape(-1, group_rows, width)
        flat = lax.all_to_all(flat, "ctx", split_axis=0, concat_axis=0, tiled=True, axis_index_groups=among)
        return flat.reshape(-1, width)

    (kv,) = project(*operands, (w_key, value_weight), (True, False), devices, members)
    kv = exchange(kv, None)
    apart = list(range(half_devices, devices))
    near, *far = project(*operands, (w_query,), (True,), devices, members, apart)
    queries = []
    for i, piece in enumerate(far):
        distance = half_devices + i
        queries.append(lax.ppermute(piece, "ctx", [(j, j ^ distance) for j in range(devices)]))

    table = positions.reshape(devices, rows)
    ours = group_of(table, block, devices, members) == group
    first_run = group * run
    second_run = (2 * devices - members) * block - group * run
    slots = jnp.where(table // run == group, table - first_run, table - second_run + run)
    inner = jnp.arange(rows, dtype=jnp.int32)
    before = (inner[:, None] < inner[None, :]).astype(jnp.bfloat16)
    place_in = dot(ours.astype(jnp.bfloat16), before).astype(jnp.int32)
    place_in = jnp.where(ours, place_in, -1)
    wanted = jnp.arange(group_rows, dtype=jnp.int32)[None, :, None] == place_in[:, None, :]
    slot = jnp.sum(jnp.where(wanted, slots[:, None, :], 0), axis=2)
    index = jnp.arange(half_devices, dtype=jnp.int32)
    sources = [device // half_devices * half_devices + index, device ^ (half_devices + index)]
    query_slot = slot[jnp.concatenate(sources)].reshape(1, devices * group_rows)
    slot = slot.reshape(1, devices * group_rows)
    ends = jnp.cumsum(lengths, dtype=jnp.int32)[None, :]

    kv, near = lax.optimization_barrier((kv, near))
    queries.insert(0, exchange(near, halves))
    kv, *queries[1:4] = lax.optimization_barrier((kv, *queries[1:4]))
    reach = REACH_BLOCKS * block
    sizes = [run - reach, reach] * 2
    *runs, even_out, odd_out = place([kv], slot, sizes, members)
    odd = [i for i in range(1, groups - 1, 2)]
    even = [i for i in range(0, groups, 2)]
    pieces = []
    for lower, out in ((odd, odd_out), (even, even_out)):
        up = [(i * members + j, (i + 1) * members + j) for i in lower for j in range(members)]
        pieces.insert(0, lax.ppermute(out, "ctx", up + [(j, i) for i, j in up]))
    pieces = (*pieces, *runs)

    (query,) = place(queries, query_slot, [2 * run])
    results = []
    for turn in range(members):
        out = attend(turn, members, devices, query, ends, pieces, block)
        if turn < members - 1:
            distances = distances_at(turn, members)
            route = [
                (i * devices + j, i * devices + j // members * members + (j % members ^ distances[i % 2]))
                for i in range(lax.axis_size("dp"))
                for j in range(devices)
            ]
            out = lax.ppermute(out, ("dp", "ctx"), route)
        results.append(out)
    return assemble(results)


def solution(mesh):
    in_specs = (P(("dp", "ctx"), None), P("dp"), P("dp"), P(), P(), P(), P())
    out_specs = P(("dp", "ctx"), None)
    return jax.shard_map(shards, mesh=mesh, in_specs=in_specs, out_specs=out_specs, check_vma=False)
```

```python
import functools

import jax
import jax.numpy as jnp
import numpy as np
from jax import lax
from jax.experimental import pallas as pl
from jax.experimental.pallas import tpu as pltpu
from jax.sharding import PartitionSpec as P

HEAD_SIZE = 128
REACH_BLOCKS = 3
ROPE_THETA = 500000.0
EPSILON = 1e-05

WHOLE = pl.BlockSpec(memory_space=pltpu.VMEM)
IN_PLACE = pl.BlockSpec(memory_space=pl.ANY)
MIB = 1024 * 1024


def dot(a, b):
    return jnp.dot(a, b, preferred_element_type=jnp.float32)


def transposed(row):
    size = row.shape[1]
    here = lax.broadcasted_iota(jnp.int32, (size, size), 0)
    there = lax.broadcasted_iota(jnp.int32, (size, size), 1)
    return jnp.sum(jnp.where(here == there, row, 0), axis=1, keepdims=True)


def group_of(where_at, block, devices, members):
    block_id = where_at // block
    return jnp.minimum(block_id, 2 * devices - 1 - block_id) // members


def project_kernel(kinds, devices, members, apart, positions_hbm, freq_hbm, gain_hbm, tokens_hbm, *rest):
    count = len(kinds)
    weights_hbm, rest = rest[:count], rest[count:]
    outputs = 1 + len(apart)
    outs_hbm, rest = rest[:outputs], rest[outputs:]
    positions_ref, freq_ref, gain_ref, tokens, normed, weights, out_ref = rest[:7]
    small_sems, sems, out_sems = rest[7:]
    rows, width = normed.shape
    chunks, _, span = weights.shape
    copies, origin = [], []
    small_copies = [
        pltpu.make_async_copy(source, target, small_sems.at[i])
        for i, (source, target) in enumerate(
            [(positions_hbm, positions_ref), (freq_hbm, freq_ref), (gain_hbm, gain_ref), (tokens_hbm, tokens)]
        )
    ]
    for copy in small_copies:
        copy.start()
    for i in range(count):
        for first in range(0, weights_hbm[i].shape[1], span):
            j = len(copies)
            source = weights_hbm[i].at[:, pl.ds(first, span)]
            copies.append(pltpu.make_async_copy(source, weights.at[j], sems.at[j]))
            origin.append((i, first))
    copies[0].start()
    for copy in small_copies[:-1]:
        copy.wait()
    lanes = positions_ref.shape[1]
    stripes = rows // lanes
    mine = jnp.concatenate(
        [positions_ref[pl.ds(lax.axis_index("ctx") * stripes + i, 1), :] for i in range(stripes)], axis=1
    )
    owner = group_of(mine, rows // 2, devices, members)
    here = lax.broadcasted_iota(jnp.int32, (rows, rows), 0)
    there = lax.broadcasted_iota(jnp.int32, (rows, rows), 1)
    earlier = jnp.where((transposed(owner) == owner) & (here < there), 1, 0)
    rank = owner * (rows * members // devices) + jnp.sum(earlier, axis=0, keepdims=True)
    order = here == rank
    ordered_at = jnp.sum(jnp.where(order, mine, 0), axis=1, keepdims=True)
    angle = ordered_at.astype(jnp.float32) * freq_ref[...]
    lane = lax.broadcasted_iota(jnp.int32, (rows, HEAD_SIZE), 1)
    cosine = jnp.cos(angle)
    sine = jnp.where(lane < HEAD_SIZE // 2, -1.0, 1.0) * jnp.sin(angle)
    order = jnp.where(order, 1.0, 0.0).astype(jnp.bfloat16)
    gain = gain_ref[...].astype(jnp.float32).reshape(1, width)
    step = 32
    written = []

    small_copies[-1].wait()
    for first in range(0, rows, step):
        at = slice(first, first + step)
        floats = tokens[at, :].astype(jnp.float32)
        mean = jnp.sum(floats * floats, axis=1, keepdims=True) * (1.0 / width)
        tokens[at, :] = (floats * lax.rsqrt(mean + EPSILON) * gain).astype(jnp.bfloat16)
    if chunks > 1:
        copies[1].start()
    for first in range(0, width, 512):
        columns = slice(first, first + 512)
        normed[:, columns] = dot(order, tokens[:, columns]).astype(jnp.bfloat16)
    groups, heads = out_ref.shape[:2]
    offsets = [0]
    for i in range(count):
        offsets.append(offsets[-1] + weights_hbm[i].shape[1] // heads)
    me = lax.axis_index("ctx")
    far = [
        pltpu.make_async_copy(
            out_ref.at[(me ^ distance) // members, (me ^ distance) % members], outs_hbm[1 + i], out_sems.at[chunks + i]
        )
        for i, distance in enumerate(apart)
    ]
    for j in range(chunks):
        i, first = origin[j]
        copies[j].wait()
        if j + 2 < chunks:
            copies[j + 2].start()
        product = dot(normed[...], weights[j])
        per_head = offsets[i + 1] - offsets[i]
        for u in range(0, span, HEAD_SIZE):
            values = product[:, u : u + HEAD_SIZE]
            if kinds[i]:
                values = values * cosine + pltpu.roll(values, HEAD_SIZE // 2, 1) * sine
            head, inside = divmod(first + u, per_head)
            inside += offsets[i]
            out_ref[:, head, :, inside : inside + HEAD_SIZE] = values.astype(jnp.bfloat16).reshape(
                groups, rows // groups, HEAD_SIZE
            )
        first_head, done_heads = first // per_head, max(span // per_head, 1)
        done = (pl.ds(first_head, done_heads), pl.ds(0, rows // groups))
        done += (pl.ds(offsets[i] + first % per_head, min(span, per_head)),)
        taken = groups // 2 if apart else groups
        start = me // members // taken * taken if apart else 0
        source = out_ref.at[(pl.ds(start, taken),) + done]
        written.append(pltpu.make_async_copy(source, outs_hbm[0].at[(pl.ds(0, taken),) + done], out_sems.at[j]))
        written[-1].start()
        if first % per_head + span >= per_head:
            for distance, copy in zip(apart, far):
                to = (me ^ distance) % members
                pl.when((to >= first_head) & (to < first_head + done_heads))(copy.start)
    for copy in written + far:
        copy.wait()


def project(positions, freq, gain, tokens, weights, kinds, devices, heads, apart=()):
    rows, width = tokens.shape
    groups = devices // heads
    columns = sum(w.shape[1] for w in weights)
    span = 512
    flops = 2 * rows * width * columns
    size = 2 * (width * columns + rows * width + rows * columns)
    out_shape = (groups // 2 if apart else groups, heads, rows // groups, columns // heads)
    out_shapes = [out_shape] + [out_shape[2:]] * len(apart)
    return pl.pallas_call(
        functools.partial(project_kernel, kinds, devices, heads, apart),
        out_shape=[jax.ShapeDtypeStruct(shape, jnp.bfloat16) for shape in out_shapes],
        in_specs=[IN_PLACE] * (len(weights) + 4),
        out_specs=[IN_PLACE] * len(out_shapes),
        scratch_shapes=[
            pltpu.VMEM(positions.shape, jnp.int32),
            pltpu.VMEM(freq.shape, jnp.float32),
            pltpu.VMEM(gain.shape, jnp.bfloat16),
            pltpu.VMEM((rows, width), jnp.bfloat16),
            pltpu.VMEM((rows, width), jnp.bfloat16),
            pltpu.VMEM((columns // span, width, span), jnp.bfloat16),
            pltpu.VMEM((groups, heads, rows // groups, columns // heads), jnp.bfloat16),
            pltpu.SemaphoreType.DMA((4,)),
            pltpu.SemaphoreType.DMA((columns // span,)),
            pltpu.SemaphoreType.DMA((columns // span + len(apart),)),
        ],
        compiler_params=pltpu.CompilerParams(vmem_limit_bytes=56 * MIB),
        cost_estimate=pl.CostEstimate(flops=flops, bytes_accessed=size, transcendentals=0),
    )(positions, freq, gain, tokens, *weights)


def place_kernel(count, members, slot_ref, *refs):
    pieces, outs, arrived = refs[:count], refs[count:-1], refs[-1]
    rows = arrived.shape[0]
    slot = slot_ref[...]
    first = 0
    for piece in pieces:
        arrived[first : first + piece.shape[0], :] = piece[...]
        first += piece.shape[0]
    if members:
        outs, (even_ref, odd_ref) = outs[:-2], outs[-2:]
    first = 0
    for out_ref in outs:
        size = out_ref.shape[0]
        slots = lax.broadcasted_iota(jnp.int32, (size, rows), 0) + first
        chosen = (slots == slot).astype(jnp.bfloat16)
        out_ref[...] = dot(chosen, arrived[...]).astype(jnp.bfloat16)
        first += size
    if members:
        even = lax.axis_index("ctx") // members % 2 == 0
        early, late = outs[1][...], outs[3][...]
        even_ref[...] = jnp.where(even, early, late)
        odd_ref[...] = jnp.where(even, late, early)


def place(pieces, slot, sizes, members=0):
    rows, width = slot.shape[1], pieces[0].shape[1]
    out_sizes = sizes + [sizes[1], sizes[3]] if members else sizes
    return pl.pallas_call(
        functools.partial(place_kernel, len(pieces), members),
        out_shape=[jax.ShapeDtypeStruct((size, width), jnp.bfloat16) for size in out_sizes],
        in_specs=[WHOLE] * (1 + len(pieces)),
        out_specs=[WHOLE] * len(out_sizes),
        scratch_shapes=[pltpu.VMEM((rows, width), jnp.bfloat16)],
        compiler_params=pltpu.CompilerParams(vmem_limit_bytes=16 * MIB),
        cost_estimate=pl.CostEstimate(
            flops=2 * sum(sizes) * rows * width,
            bytes_accessed=4 * rows * width,
            transcendentals=0,
        ),
    )(slot, *pieces)


def taken_at(turn, members):
    distances = distances_at(turn, members)
    odd = lax.axis_index("dp") % 2
    distance = odd * distances[1] + (1 - odd) * distances[0]
    return (lax.axis_index("ctx") % members) ^ distance


def distances_at(turn, members):
    if turn >= members - 2:
        return (members - 1 if turn == members - 2 else 0,) * 2
    return (turn + 1, members - 2 - turn)


def attend_kernel(block, turn, members, devices, ends_ref, query_ref, *rest):
    pieces, out_ref, held = rest[:6], rest[6], rest[7]
    target = taken_at(turn, members)
    group = lax.axis_index("ctx") // members
    starts = (group * members * block, (2 * devices - members - group * members) * block)
    last = group == devices // members - 1
    heads = query_ref.shape[1] // HEAD_SIZE
    run = query_ref.shape[0] // 2
    per_run = run // block
    reach = REACH_BLOCKS * block
    keys = reach + block
    ends = ends_ref[...]
    factor = jnp.float32(np.log2(np.e) / HEAD_SIZE**0.5)
    from_even, from_odd, early_head, early_tail, late_head, late_tail = pieces
    second = 1 - group % 2
    held[second, :reach, :] = from_even[...]
    held[1 - second, :reach, :] = jnp.where(last, early_tail[...], from_odd[...])
    for half, (head, tail) in enumerate([(early_head, early_tail), (late_head, late_tail)]):
        cut = reach + head.shape[0]
        held[half, reach:cut, :] = head[...]
        held[half, cut:, :] = tail[...]
    indices = (target, per_run - 1 - target)
    at = [pl.multiple_of(index * block, block) for index in indices]
    here = [slice(half * block, (half + 1) * block) for half in range(2)]
    scores, weights, totals = [], [], []
    for half in range(2):
        query = query_ref[pl.ds(pl.multiple_of(at[half] + half * run, block), block), :]
        stacked = jnp.concatenate([query[:, h * HEAD_SIZE : (h + 1) * HEAD_SIZE] for h in range(heads)], axis=0)
        key = held[half, pl.ds(at[half], keys), :HEAD_SIZE]
        scores.append(
            lax.dot_general(stacked, key, (((1,), (1,)), ((), ())), preferred_element_type=jnp.float32)
        )
    for half in range(2):
        begin = starts[half] + at[half]
        query_at = lax.broadcasted_iota(jnp.int32, (block, 1), 0) + begin
        key_at = lax.broadcasted_iota(jnp.int32, (1, keys), 1) + (begin - reach)
        doc_start = jnp.max(jnp.where(ends <= query_at, ends, 0), axis=1, keepdims=True)
        allowed = (key_at >= doc_start) & (key_at <= query_at)
        masked = jnp.where(allowed[None], scores[half].reshape(heads, block, keys), jnp.float32(-1e30))
        masked = masked.reshape(heads * block, keys)
        top = jnp.max(masked, axis=1, keepdims=True)
        exact = jnp.exp2((masked - top) * factor)
        totals.append(jnp.sum(exact, axis=1, keepdims=True))
        weights.append(exact.astype(jnp.bfloat16))
    for half in range(2):
        value = held[half, pl.ds(at[half], keys), HEAD_SIZE:]
        mixed = (dot(weights[half], value) / totals[half]).astype(jnp.bfloat16)
        for h in range(heads):
            out_ref[here[half], h * HEAD_SIZE : (h + 1) * HEAD_SIZE] = mixed[h * block : (h + 1) * block]


def attend(turn, members, devices, query, ends, pieces, block):
    rows, width = query.shape
    held = REACH_BLOCKS * block + rows // 2
    heads = width // HEAD_SIZE
    reach = (REACH_BLOCKS + 1) * block
    return pl.pallas_call(
        functools.partial(attend_kernel, block, turn, members, devices),
        out_shape=jax.ShapeDtypeStruct((2 * block, width), jnp.bfloat16),
        in_specs=[WHOLE] * 8,
        out_specs=WHOLE,
        scratch_shapes=[pltpu.VMEM((2, held, 2 * HEAD_SIZE), jnp.bfloat16)],
        compiler_params=pltpu.CompilerParams(vmem_limit_bytes=16 * MIB),
        cost_estimate=pl.CostEstimate(
            flops=2 * 2 * heads * block * reach * HEAD_SIZE * 2,
            bytes_accessed=2 * rows * width + 8 * held * HEAD_SIZE,
            transcendentals=2 * heads * block * reach,
        ),
    )(ends, query, *pieces)


def assemble_kernel(*refs):
    pieces, out_ref = refs[:-1], refs[-1]
    width = pieces[0].shape[1]
    for turn, piece in enumerate(pieces):
        at = pl.multiple_of(taken_at(turn, len(pieces)) * width, width)
        out_ref[:, pl.ds(at, width)] = piece[...]


def assemble(pieces):
    rows, width = pieces[0].shape
    return pl.pallas_call(
        assemble_kernel,
        out_shape=jax.ShapeDtypeStruct((rows, width * len(pieces)), jnp.bfloat16),
        in_specs=[WHOLE] * len(pieces),
        out_specs=WHOLE,
        compiler_params=pltpu.CompilerParams(vmem_limit_bytes=8 * MIB),
        cost_estimate=pl.CostEstimate(
            flops=0, bytes_accessed=4 * rows * width * len(pieces), transcendentals=0
        ),
    )(*pieces)


def shards(tokens, positions, lengths, gain, w_query, w_key, value_weight):
    devices = lax.axis_size("ctx")
    device = lax.axis_index("ctx")
    rows = tokens.shape[0]
    block = rows // 2
    members = w_key.shape[1] // HEAD_SIZE
    groups = devices // members
    group = device // members
    run = members * block
    group_rows = rows // groups

    half = HEAD_SIZE // 2
    freq = np.float32(ROPE_THETA ** (-(np.arange(HEAD_SIZE) % half * 2.0 / HEAD_SIZE)))
    operands = (positions.reshape(-1, 128), jnp.asarray(freq[None, :]), gain, tokens)

    half_devices = devices // 2
    halves = [list(range(i, i + half_devices)) for i in (0, half_devices)]

    def exchange(ordered, among):
        width = ordered.shape[3]
        flat = ordered.reshape(-1, group_rows, width)
        flat = lax.all_to_all(flat, "ctx", split_axis=0, concat_axis=0, tiled=True, axis_index_groups=among)
        return flat.reshape(-1, width)

    (kv,) = project(*operands, (w_key, value_weight), (True, False), devices, members)
    kv = exchange(kv, None)
    apart = list(range(half_devices, devices))
    near, *far = project(*operands, (w_query,), (True,), devices, members, apart)
    queries = []
    for i, piece in enumerate(far):
        distance = half_devices + i
        queries.append(lax.ppermute(piece, "ctx", [(j, j ^ distance) for j in range(devices)]))

    table = positions.reshape(devices, rows)
    ours = group_of(table, block, devices, members) == group
    first_run = group * run
    second_run = (2 * devices - members) * block - group * run
    slots = jnp.where(table // run == group, table - first_run, table - second_run + run)
    inner = jnp.arange(rows, dtype=jnp.int32)
    before = (inner[:, None] < inner[None, :]).astype(jnp.bfloat16)
    place_in = dot(ours.astype(jnp.bfloat16), before).astype(jnp.int32)
    place_in = jnp.where(ours, place_in, -1)
    wanted = jnp.arange(group_rows, dtype=jnp.int32)[None, :, None] == place_in[:, None, :]
    slot = jnp.sum(jnp.where(wanted, slots[:, None, :], 0), axis=2)
    index = jnp.arange(half_devices, dtype=jnp.int32)
    sources = [device // half_devices * half_devices + index, device ^ (half_devices + index)]
    query_slot = slot[jnp.concatenate(sources)].reshape(1, devices * group_rows)
    slot = slot.reshape(1, devices * group_rows)
    ends = jnp.cumsum(lengths, dtype=jnp.int32)[None, :]

    kv, near = lax.optimization_barrier((kv, near))
    queries.insert(0, exchange(near, halves))
    kv, *queries[1:5] = lax.optimization_barrier((kv, *queries[1:5]))
    reach = REACH_BLOCKS * block
    sizes = [run - reach, reach] * 2
    *runs, even_out, odd_out = place([kv], slot, sizes, members)
    odd = [i for i in range(1, groups - 1, 2)]
    even = [i for i in range(0, groups, 2)]
    pieces = []
    for lower, out in ((odd, odd_out), (even, even_out)):
        up = [(i * members + j, (i + 1) * members + j) for i in lower for j in range(members)]
        pieces.insert(0, lax.ppermute(out, "ctx", up + [(j, i) for i, j in up]))
    pieces = (*pieces, *runs)

    (query,) = place(queries, query_slot, [2 * run])
    results = []
    for turn in range(members):
        out = attend(turn, members, devices, query, ends, pieces, block)
        if turn < members - 1:
            distances = distances_at(turn, members)
            route = [
                (i * devices + j, i * devices + j // members * members + (j % members ^ distances[i % 2]))
                for i in range(lax.axis_size("dp"))
                for j in range(devices)
            ]
            out = lax.ppermute(out, ("dp", "ctx"), route)
        results.append(out)
    return assemble(results)


def solution(mesh):
    in_specs = (P(("dp", "ctx"), None), P("dp"), P("dp"), P(), P(), P(), P())
    out_specs = P(("dp", "ctx"), None)
    return jax.shard_map(shards, mesh=mesh, in_specs=in_specs, out_specs=out_specs, check_vma=False)
```

```python
import functools

import jax
import jax.numpy as jnp
import numpy as np
from jax import lax
from jax.experimental import pallas as pl
from jax.experimental.pallas import tpu as pltpu
from jax.sharding import PartitionSpec as P

HEAD_SIZE = 128
REACH_BLOCKS = 3
ROPE_THETA = 500000.0
EPSILON = 1e-05

WHOLE = pl.BlockSpec(memory_space=pltpu.VMEM)
IN_PLACE = pl.BlockSpec(memory_space=pl.ANY)
MIB = 1024 * 1024


def dot(a, b):
    return jnp.dot(a, b, preferred_element_type=jnp.float32)


def transposed(row):
    size = row.shape[1]
    here = lax.broadcasted_iota(jnp.int32, (size, size), 0)
    there = lax.broadcasted_iota(jnp.int32, (size, size), 1)
    return jnp.sum(jnp.where(here == there, row, 0), axis=1, keepdims=True)


def group_of(where_at, block, devices, members):
    block_id = where_at // block
    return jnp.minimum(block_id, 2 * devices - 1 - block_id) // members


def project_kernel(kinds, devices, members, apart, positions_hbm, freq_hbm, gain_hbm, tokens_hbm, *rest):
    count = len(kinds)
    weights_hbm, rest = rest[:count], rest[count:]
    outputs = 1 + len(apart)
    outs_hbm, rest = rest[:outputs], rest[outputs:]
    positions_ref, freq_ref, gain_ref, tokens, normed, weights, out_ref = rest[:7]
    small_sems, sems, out_sems = rest[7:]
    rows, width = normed.shape
    chunks, _, span = weights.shape
    copies, origin = [], []
    small_copies = [
        pltpu.make_async_copy(source, target, small_sems.at[i])
        for i, (source, target) in enumerate(
            [(positions_hbm, positions_ref), (freq_hbm, freq_ref), (gain_hbm, gain_ref), (tokens_hbm, tokens)]
        )
    ]
    for copy in small_copies:
        copy.start()
    for i in range(count):
        for first in range(0, weights_hbm[i].shape[1], span):
            j = len(copies)
            source = weights_hbm[i].at[:, pl.ds(first, span)]
            copies.append(pltpu.make_async_copy(source, weights.at[j], sems.at[j]))
            origin.append((i, first))
    copies[0].start()
    for copy in small_copies[:-1]:
        copy.wait()
    lanes = positions_ref.shape[1]
    stripes = rows // lanes
    mine = jnp.concatenate(
        [positions_ref[pl.ds(lax.axis_index("ctx") * stripes + i, 1), :] for i in range(stripes)], axis=1
    )
    owner = group_of(mine, rows // 2, devices, members)
    here = lax.broadcasted_iota(jnp.int32, (rows, rows), 0)
    there = lax.broadcasted_iota(jnp.int32, (rows, rows), 1)
    earlier = jnp.where((transposed(owner) == owner) & (here < there), 1, 0)
    rank = owner * (rows * members // devices) + jnp.sum(earlier, axis=0, keepdims=True)
    order = here == rank
    ordered_at = jnp.sum(jnp.where(order, mine, 0), axis=1, keepdims=True)
    angle = ordered_at.astype(jnp.float32) * freq_ref[...]
    lane = lax.broadcasted_iota(jnp.int32, (rows, HEAD_SIZE), 1)
    cosine = jnp.cos(angle)
    sine = jnp.where(lane < HEAD_SIZE // 2, -1.0, 1.0) * jnp.sin(angle)
    order = jnp.where(order, 1.0, 0.0).astype(jnp.bfloat16)
    gain = gain_ref[...].astype(jnp.float32).reshape(1, width)
    step = 16
    written = []

    small_copies[-1].wait()
    for first in range(0, rows, step):
        at = slice(first, first + step)
        floats = tokens[at, :].astype(jnp.float32)
        mean = jnp.sum(floats * floats, axis=1, keepdims=True) * (1.0 / width)
        tokens[at, :] = (floats * lax.rsqrt(mean + EPSILON) * gain).astype(jnp.bfloat16)
    if chunks > 1:
        copies[1].start()
    for first in range(0, width, 2048):
        columns = slice(first, first + 2048)
        normed[:, columns] = dot(order, tokens[:, columns]).astype(jnp.bfloat16)
    groups, heads = out_ref.shape[:2]
    offsets = [0]
    for i in range(count):
        offsets.append(offsets[-1] + weights_hbm[i].shape[1] // heads)
    me = lax.axis_index("ctx")
    far = [
        pltpu.make_async_copy(
            out_ref.at[(me ^ distance) // members, (me ^ distance) % members], outs_hbm[1 + i], out_sems.at[chunks + i]
        )
        for i, distance in enumerate(apart)
    ]
    for j in range(chunks):
        i, first = origin[j]
        copies[j].wait()
        if j + 2 < chunks:
            copies[j + 2].start()
        product = dot(normed[...], weights[j])
        per_head = offsets[i + 1] - offsets[i]
        for u in range(0, span, HEAD_SIZE):
            values = product[:, u : u + HEAD_SIZE]
            if kinds[i]:
                values = values * cosine + pltpu.roll(values, HEAD_SIZE // 2, 1) * sine
            head, inside = divmod(first + u, per_head)
            inside += offsets[i]
            out_ref[:, head, :, inside : inside + HEAD_SIZE] = values.astype(jnp.bfloat16).reshape(
                groups, rows // groups, HEAD_SIZE
            )
        first_head, done_heads = first // per_head, max(span // per_head, 1)
        done = (pl.ds(first_head, done_heads), pl.ds(0, rows // groups))
        done += (pl.ds(offsets[i] + first % per_head, min(span, per_head)),)
        taken = groups // 2 if apart else groups
        start = me // members // taken * taken if apart else 0
        source = out_ref.at[(pl.ds(start, taken),) + done]
        written.append(pltpu.make_async_copy(source, outs_hbm[0].at[(pl.ds(0, taken),) + done], out_sems.at[j]))
        written[-1].start()
        if first % per_head + span >= per_head:
            for distance, copy in zip(apart, far):
                to = (me ^ distance) % members
                pl.when((to >= first_head) & (to < first_head + done_heads))(copy.start)
    for copy in written + far:
        copy.wait()


def project(positions, freq, gain, tokens, weights, kinds, devices, heads, apart=()):
    rows, width = tokens.shape
    groups = devices // heads
    columns = sum(w.shape[1] for w in weights)
    span = 512
    flops = 2 * rows * width * columns
    size = 2 * (width * columns + rows * width + rows * columns)
    out_shape = (groups // 2 if apart else groups, heads, rows // groups, columns // heads)
    out_shapes = [out_shape] + [out_shape[2:]] * len(apart)
    return pl.pallas_call(
        functools.partial(project_kernel, kinds, devices, heads, apart),
        out_shape=[jax.ShapeDtypeStruct(shape, jnp.bfloat16) for shape in out_shapes],
        in_specs=[IN_PLACE] * (len(weights) + 4),
        out_specs=[IN_PLACE] * len(out_shapes),
        scratch_shapes=[
            pltpu.VMEM(positions.shape, jnp.int32),
            pltpu.VMEM(freq.shape, jnp.float32),
            pltpu.VMEM(gain.shape, jnp.bfloat16),
            pltpu.VMEM((rows, width), jnp.bfloat16),
            pltpu.VMEM((rows, width), jnp.bfloat16),
            pltpu.VMEM((columns // span, width, span), jnp.bfloat16),
            pltpu.VMEM((groups, heads, rows // groups, columns // heads), jnp.bfloat16),
            pltpu.SemaphoreType.DMA((4,)),
            pltpu.SemaphoreType.DMA((columns // span,)),
            pltpu.SemaphoreType.DMA((columns // span + len(apart),)),
        ],
        compiler_params=pltpu.CompilerParams(vmem_limit_bytes=56 * MIB),
        cost_estimate=pl.CostEstimate(flops=flops, bytes_accessed=size, transcendentals=0),
    )(positions, freq, gain, tokens, *weights)


def place_kernel(count, members, slot_ref, *refs):
    pieces, outs, arrived = refs[:count], refs[count:-1], refs[-1]
    rows = arrived.shape[0]
    slot = slot_ref[...]
    first = 0
    for piece in pieces:
        arrived[first : first + piece.shape[0], :] = piece[...]
        first += piece.shape[0]
    if members:
        outs, (even_ref, odd_ref) = outs[:-2], outs[-2:]
    first = 0
    for out_ref in outs:
        size = out_ref.shape[0]
        slots = lax.broadcasted_iota(jnp.int32, (size, rows), 0) + first
        chosen = (slots == slot).astype(jnp.bfloat16)
        out_ref[...] = dot(chosen, arrived[...]).astype(jnp.bfloat16)
        first += size
    if members:
        even = lax.axis_index("ctx") // members % 2 == 0
        early, late = outs[1][...], outs[3][...]
        even_ref[...] = jnp.where(even, early, late)
        odd_ref[...] = jnp.where(even, late, early)


def place(pieces, slot, sizes, members=0):
    rows, width = slot.shape[1], pieces[0].shape[1]
    out_sizes = sizes + [sizes[1], sizes[3]] if members else sizes
    return pl.pallas_call(
        functools.partial(place_kernel, len(pieces), members),
        out_shape=[jax.ShapeDtypeStruct((size, width), jnp.bfloat16) for size in out_sizes],
        in_specs=[WHOLE] * (1 + len(pieces)),
        out_specs=[WHOLE] * len(out_sizes),
        scratch_shapes=[pltpu.VMEM((rows, width), jnp.bfloat16)],
        compiler_params=pltpu.CompilerParams(vmem_limit_bytes=16 * MIB),
        cost_estimate=pl.CostEstimate(
            flops=2 * sum(sizes) * rows * width,
            bytes_accessed=4 * rows * width,
            transcendentals=0,
        ),
    )(slot, *pieces)


def taken_at(turn, members):
    distances = distances_at(turn, members)
    odd = lax.axis_index("dp") % 2
    distance = odd * distances[1] + (1 - odd) * distances[0]
    return (lax.axis_index("ctx") % members) ^ distance


def distances_at(turn, members):
    if turn in (0, members - 1):
        return (members - 1 - turn,) * 2
    return (turn, members - 1 - turn)


def attend_kernel(block, turn, members, devices, ends_ref, query_ref, *rest):
    pieces, out_ref, held = rest[:6], rest[6], rest[7]
    target = taken_at(turn, members)
    group = lax.axis_index("ctx") // members
    starts = (group * members * block, (2 * devices - members - group * members) * block)
    last = group == devices // members - 1
    heads = query_ref.shape[1] // HEAD_SIZE
    run = query_ref.shape[0] // 2
    per_run = run // block
    reach = REACH_BLOCKS * block
    keys = reach + block
    ends = ends_ref[...]
    factor = jnp.float32(np.log2(np.e) / HEAD_SIZE**0.5)
    from_even, from_odd, early_head, early_tail, late_head, late_tail = pieces
    second = 1 - group % 2
    held[second, :reach, :] = from_even[...]
    held[1 - second, :reach, :] = jnp.where(last, early_tail[...], from_odd[...])
    for half, (head, tail) in enumerate([(early_head, early_tail), (late_head, late_tail)]):
        cut = reach + head.shape[0]
        held[half, reach:cut, :] = head[...]
        held[half, cut:, :] = tail[...]
    indices = (target, per_run - 1 - target)
    at = [pl.multiple_of(index * block, block) for index in indices]
    here = [slice(half * block, (half + 1) * block) for half in range(2)]
    scores, weights, totals = [], [], []
    for half in range(2):
        query = query_ref[pl.ds(pl.multiple_of(at[half] + half * run, block), block), :]
        stacked = jnp.concatenate([query[:, h * HEAD_SIZE : (h + 1) * HEAD_SIZE] for h in range(heads)], axis=0)
        key = held[half, pl.ds(at[half], keys), :HEAD_SIZE]
        scores.append(
            lax.dot_general(stacked, key, (((1,), (1,)), ((), ())), preferred_element_type=jnp.float32)
        )
    for half in range(2):
        begin = starts[half] + at[half]
        query_at = lax.broadcasted_iota(jnp.int32, (block, 1), 0) + begin
        key_at = lax.broadcasted_iota(jnp.int32, (1, keys), 1) + (begin - reach)
        doc_start = jnp.max(jnp.where(ends <= query_at, ends, 0), axis=1, keepdims=True)
        allowed = (key_at >= doc_start) & (key_at <= query_at)
        masked = jnp.where(allowed[None], scores[half].reshape(heads, block, keys), jnp.float32(-1e30))
        masked = masked.reshape(heads * block, keys)
        top = jnp.max(masked, axis=1, keepdims=True)
        exact = jnp.exp2((masked - top) * factor)
        totals.append(jnp.sum(exact, axis=1, keepdims=True))
        weights.append(exact.astype(jnp.bfloat16))
    for half in range(2):
        value = held[half, pl.ds(at[half], keys), HEAD_SIZE:]
        mixed = (dot(weights[half], value) / totals[half]).astype(jnp.bfloat16)
        for h in range(heads):
            out_ref[here[half], h * HEAD_SIZE : (h + 1) * HEAD_SIZE] = mixed[h * block : (h + 1) * block]


def attend(turn, members, devices, query, ends, pieces, block):
    rows, width = query.shape
    held = REACH_BLOCKS * block + rows // 2
    heads = width // HEAD_SIZE
    reach = (REACH_BLOCKS + 1) * block
    return pl.pallas_call(
        functools.partial(attend_kernel, block, turn, members, devices),
        out_shape=jax.ShapeDtypeStruct((2 * block, width), jnp.bfloat16),
        in_specs=[WHOLE] * 8,
        out_specs=WHOLE,
        scratch_shapes=[pltpu.VMEM((2, held, 2 * HEAD_SIZE), jnp.bfloat16)],
        compiler_params=pltpu.CompilerParams(vmem_limit_bytes=16 * MIB),
        cost_estimate=pl.CostEstimate(
            flops=2 * 2 * heads * block * reach * HEAD_SIZE * 2,
            bytes_accessed=2 * rows * width + 8 * held * HEAD_SIZE,
            transcendentals=2 * heads * block * reach,
        ),
    )(ends, query, *pieces)


def assemble_kernel(*refs):
    pieces, out_ref = refs[:-1], refs[-1]
    width = pieces[0].shape[1]
    for turn, piece in enumerate(pieces):
        at = pl.multiple_of(taken_at(turn, len(pieces)) * width, width)
        out_ref[:, pl.ds(at, width)] = piece[...]


def assemble(pieces):
    rows, width = pieces[0].shape
    return pl.pallas_call(
        assemble_kernel,
        out_shape=jax.ShapeDtypeStruct((rows, width * len(pieces)), jnp.bfloat16),
        in_specs=[WHOLE] * len(pieces),
        out_specs=WHOLE,
        compiler_params=pltpu.CompilerParams(vmem_limit_bytes=8 * MIB),
        cost_estimate=pl.CostEstimate(
            flops=0, bytes_accessed=4 * rows * width * len(pieces), transcendentals=0
        ),
    )(*pieces)


def shards(tokens, positions, lengths, gain, w_query, w_key, value_weight):
    devices = lax.axis_size("ctx")
    device = lax.axis_index("ctx")
    rows = tokens.shape[0]
    block = rows // 2
    members = w_key.shape[1] // HEAD_SIZE
    groups = devices // members
    group = device // members
    run = members * block
    group_rows = rows // groups

    half = HEAD_SIZE // 2
    freq = np.float32(ROPE_THETA ** (-(np.arange(HEAD_SIZE) % half * 2.0 / HEAD_SIZE)))
    operands = (positions.reshape(-1, 128), jnp.asarray(freq[None, :]), gain, tokens)

    half_devices = devices // 2
    halves = [list(range(i, i + half_devices)) for i in (0, half_devices)]

    def exchange(ordered, among):
        width = ordered.shape[3]
        flat = ordered.reshape(-1, group_rows, width)
        flat = lax.all_to_all(flat, "ctx", split_axis=0, concat_axis=0, tiled=True, axis_index_groups=among)
        return flat.reshape(-1, width)

    (kv,) = project(*operands, (w_key, value_weight), (True, False), devices, members)
    kv = exchange(kv, None)
    apart = list(range(half_devices, devices))
    near, *far = project(*operands, (w_query,), (True,), devices, members, apart)
    queries = []
    for i, piece in enumerate(far):
        distance = half_devices + i
        queries.append(lax.ppermute(piece, "ctx", [(j, j ^ distance) for j in range(devices)]))

    table = positions.reshape(devices, rows)
    ours = group_of(table, block, devices, members) == group
    first_run = group * run
    second_run = (2 * devices - members) * block - group * run
    slots = jnp.where(table // run == group, table - first_run, table - second_run + run)
    inner = jnp.arange(rows, dtype=jnp.int32)
    before = (inner[:, None] < inner[None, :]).astype(jnp.bfloat16)
    place_in = dot(ours.astype(jnp.bfloat16), before).astype(jnp.int32)
    place_in = jnp.where(ours, place_in, -1)
    wanted = jnp.arange(group_rows, dtype=jnp.int32)[None, :, None] == place_in[:, None, :]
    slot = jnp.sum(jnp.where(wanted, slots[:, None, :], 0), axis=2)
    index = jnp.arange(half_devices, dtype=jnp.int32)
    sources = [device // half_devices * half_devices + index, device ^ (half_devices + index)]
    query_slot = slot[jnp.concatenate(sources)].reshape(1, devices * group_rows)
    slot = slot.reshape(1, devices * group_rows)
    ends = jnp.cumsum(lengths, dtype=jnp.int32)[None, :]

    kv, near = lax.optimization_barrier((kv, near))
    queries.insert(0, exchange(near, halves))
    kv, *queries[1:5] = lax.optimization_barrier((kv, *queries[1:5]))
    reach = REACH_BLOCKS * block
    sizes = [run - reach, reach] * 2
    *runs, even_out, odd_out = place([kv], slot, sizes, members)
    odd = [i for i in range(1, groups - 1, 2)]
    even = [i for i in range(0, groups, 2)]
    pieces = []
    for lower, out in ((odd, odd_out), (even, even_out)):
        up = [(i * members + j, (i + 1) * members + j) for i in lower for j in range(members)]
        pieces.insert(0, lax.ppermute(out, "ctx", up + [(j, i) for i, j in up]))
    pieces = (*pieces, *runs)

    (query,) = place(queries, query_slot, [2 * run])
    results = []
    for turn in range(members):
        out = attend(turn, members, devices, query, ends, pieces, block)
        if turn < members - 1:
            distances = distances_at(turn, members)
            route = [
                (i * devices + j, i * devices + j // members * members + (j % members ^ distances[i % 2]))
                for i in range(lax.axis_size("dp"))
                for j in range(devices)
            ]
            out = lax.ppermute(out, ("dp", "ctx"), route)
        results.append(out)
    return assemble(results)


def solution(mesh):
    in_specs = (P(("dp", "ctx"), None), P("dp"), P("dp"), P(), P(), P(), P())
    out_specs = P(("dp", "ctx"), None)
    return jax.shard_map(shards, mesh=mesh, in_specs=in_specs, out_specs=out_specs, check_vma=False)
```
